32 devices in a mesh: shot: 4 (over y, core), brick: 8 (over z, x).
Axes of the slice: x: 2, y: 2, z: 4, core: 2. Of those that a mesh axis runs over, the one named last changes fastest.
Arguments:
- pressure: float32 [32, 256, 512], P('shot', 'brick'), may hold values from -6 to 6
- auxiliary: float32 [32, 256, 512], P('shot', 'brick'), may hold values from -6 to 6
- pressure_prior: float32 [32, 256, 512], P('shot', 'brick'), may hold values from -6 to 6
- auxiliary_prior: float32 [32, 256, 512], P('shot', 'brick'), may hold values from -6 to 6
- courant_sq: float32 [256, 512], P('brick'), may hold values from 0.05 to 0.2
- thomsen_epsilon: float32 [256, 512], P('brick'), may hold values from 0.1 to 0.35
- thomsen_delta: float32 [256, 512], P('brick'), may hold values from 0 to 0.1
- tilt_angle: float32 [256, 512], P('brick'), may hold values from -3.140625 to 3.140625
- frequencies: float32 [16], replicated, may hold values from 0.05 to 1.5
- spectra: float32 [32, 32, 4096], P('shot', None, 'brick'), may hold values from -6 to 6
- target_cells: int32 [4096], P('brick'), may hold values from 0 to 16383, as said below
- patch_lists: int32 [8, 4, 3, 128], P('brick'), may hold values from 0 to 511, as said below
- patch_counts: int32 [8, 4], P('brick', 'shot'), may hold values from 1 to 3, as said below
Outputs:
- pressure_out: float32 [32, 256, 512], P('shot', 'brick')
- auxiliary_out: float32 [32, 256, 512], P('shot', 'brick')
- spectra_out: float32 [32, 32, 4096], P('shot', None, 'brick')
- gram_tiles: float32 [8, 4, 3, 128, 128], P('brick', 'shot')
The draws below stay inside these ranges and needn't reach their ends.
Inputs may be any that keep to these rules, and one draw needn't show every extreme that they name: `target_cells`: the block of each brick holds distinct cells of that brick. `patch_lists`: target numbers within the owner's brick; the cells of one patch slot are distinct. `patch_counts`: in every brick some owner has all 3 slots live.
All inputs are finite; a program needn't handle non-finite values.
Results may differ from the reference program's by a relative error of at most 0.00077.
Values may be sent and summed in bfloat16 or wider, within the bound.
No kernel may reach another device: no remote copies, remote signals or barrier semaphores. Data moves between devices by JAX's collectives and lax.ppermute only.
A program may use at most 64 MiB of HBM per device.

```python
import math
import jax
import jax.numpy as jnp
from jax import lax

CX = 32
CZ = 512
STEPS = 4
FREQ = 16
TGT_BRICK = 512
PATCH = 128
P_MAX = 3
GROUPS = 4
BRICKS = 8
NX = 256
SHOTS = 32
TARGETS = 4096
FEATURES = 1024


def draw_target_cells(key, part):
    keys = jax.random.split(jax.random.fold_in(key, 11), BRICKS)
    chosen = jax.vmap(lambda single: jax.random.permutation(single, CX * CZ)[:TGT_BRICK])(keys)
    return chosen.reshape(-1).astype(jnp.int32)


def draw_patch_lists(key, part):
    keys = jax.random.split(jax.random.fold_in(key, 23), BRICKS * GROUPS * P_MAX)
    chosen = jax.vmap(lambda single: jax.random.permutation(single, TGT_BRICK)[:PATCH])(keys)
    return chosen.reshape(BRICKS, GROUPS, P_MAX, PATCH).astype(jnp.int32)


def draw_patch_counts(key, part):
    first, second = jax.random.split(jax.random.fold_in(key, 37))
    counts = jax.random.randint(first, (BRICKS, GROUPS), 1, P_MAX + 1)
    fullest = jax.random.randint(second, (BRICKS,), 0, GROUPS)
    places = jnp.arange(GROUPS)[None, :] == fullest[:, None]
    return jnp.where(places, P_MAX, counts).astype(jnp.int32)


def shard_levels(key, extent, pieces, low, top_value):
    loudness = 1.0
    for position, parts in pieces:
        draws = jax.random.uniform(jax.random.fold_in(jax.random.fold_in(key, 6), position), (parts,), jnp.float32, low / len(pieces), top_value / len(pieces))
        loudness = loudness * jnp.repeat(jnp.exp(draws), extent[position] // parts).reshape((-1,) + (1,) * (len(extent) - 1 - position))
    return loudness


def gaussian(rng, dims, spread, most, cuts=(), kind=jnp.bfloat16):
    values = jax.random.normal(rng, dims, jnp.float32) * spread
    if len(cuts) > 0:
        values = shard_levels(rng, dims, cuts, -0.22, 0.18) * values
    return jnp.clip(values, min=-most, max=most).astype(kind)


def setup_inputs(seed: int = 0) -> dict:
    seeds = jax.random.split(jax.random.key(seed), 14)
    return {
        "pressure": gaussian(seeds[0], (SHOTS, NX, CZ), 1.0, 6.0, ((0, 4), (1, 8)), jnp.float32),
        "auxiliary": gaussian(seeds[1], (SHOTS, NX, CZ), 1.0, 6.0, ((0, 4), (1, 8)), jnp.float32),
        "pressure_prior": gaussian(seeds[2], (SHOTS, NX, CZ), 1.0, 6.0, ((0, 4), (1, 8)), jnp.float32),
        "auxiliary_prior": gaussian(seeds[3], (SHOTS, NX, CZ), 1.0, 6.0, ((0, 4), (1, 8)), jnp.float32),
        "courant_sq": jnp.clip(jnp.exp(math.log(0.2) - 1.3862944 * jax.random.uniform(seeds[4], (NX, CZ), jnp.float32) ** shard_levels(seeds[4], (NX, CZ), ((0, 8),), -0.2, 0.2)), 0.05, 0.2),
        "thomsen_epsilon": jnp.clip(0.1 + 0.25 * jax.random.uniform(seeds[5], (NX, CZ), jnp.float32) ** shard_levels(seeds[5], (NX, CZ), ((0, 8),), -0.2, 0.2), 0.1, 0.35),
        "thomsen_delta": jnp.clip(0.1 * jax.random.uniform(seeds[6], (NX, CZ), jnp.float32) ** shard_levels(seeds[6], (NX, CZ), ((0, 8),), -0.2, 0.2), 0.0, 0.1),
        "tilt_angle": jnp.clip(jax.random.uniform(seeds[7], (NX, CZ), jnp.float32, -3.140625, 3.140625), -3.140625, 3.140625),
        "frequencies": jnp.clip(jnp.exp(jax.random.uniform(seeds[8], (FREQ,), jnp.float32, math.log(0.05), math.log(1.5))), 0.05, 1.5),
        "spectra": gaussian(seeds[9], (SHOTS, 2 * FREQ, TARGETS), 1.0, 6.0, ((0, 4), (2, 8)), jnp.float32),
        "target_cells": draw_target_cells(jax.random.fold_in(seeds[13], 71), 0),
        "patch_lists": draw_patch_lists(jax.random.fold_in(seeds[13], 71), 0),
        "patch_counts": draw_patch_counts(jax.random.fold_in(seeds[13], 71), 0),
    }


def tilt_terms(tilt_angle):
    sine = jnp.sin(tilt_angle)
    cosine = jnp.cos(tilt_angle)
    return sine * sine, cosine * cosine, 2.0 * sine * cosine


def derivatives(field, sine_sq, cosine_sq, double_sin):
    widths = [(0, 0)] * (field.ndim - 1) + [(1, 1)]
    padded = jnp.pad(field, widths)
    centre = padded[..., 1:-1, 1:-1]
    second_x = padded[..., 2:, 1:-1] - 2.0 * centre + padded[..., :-2, 1:-1]
    second_z = padded[..., 1:-1, 2:] - 2.0 * centre + padded[..., 1:-1, :-2]
    mixed = 0.25 * (padded[..., 2:, 2:] - padded[..., 2:, :-2] - padded[..., :-2, 2:] + padded[..., :-2, :-2])
    along_axis = sine_sq * second_x + cosine_sq * second_z + double_sin * mixed
    across_axis = second_x + second_z - along_axis
    return along_axis, across_axis


def leapfrog(extended, former, coefficients):
    courant_sq, epsilon, delta_value, sine_sq, cosine_sq, double_sin = coefficients
    along_p, across_p = derivatives(extended[0], sine_sq, cosine_sq, double_sin)
    along_q, across_q = derivatives(extended[1], sine_sq, cosine_sq, double_sin)
    pressure = extended[0][..., 1:-1, :]
    auxiliary = extended[1][..., 1:-1, :]
    pressure_next = 2.0 * pressure - former[0] + courant_sq * ((1.0 + 2.0 * epsilon) * across_p + along_q)
    auxiliary_next = 2.0 * auxiliary - former[1] + courant_sq * ((1.0 + 2.0 * delta_value) * across_p + along_q)
    return jnp.stack([pressure_next, auxiliary_next])


def reference(pressure, auxiliary, pressure_prior, auxiliary_prior, courant_sq, thomsen_epsilon, thomsen_delta, tilt_angle, frequencies, spectra, target_cells, patch_lists, patch_counts):
    sine_sq, cosine_sq, double_sin = tilt_terms(tilt_angle)
    coefficients = (courant_sq, thomsen_epsilon, thomsen_delta, sine_sq, cosine_sq, double_sin)
    brick_of = jnp.arange(TARGETS, dtype=jnp.int32) // TGT_BRICK
    global_cells = (brick_of * (CX * CZ) + target_cells).astype(jnp.int32)

    def propagate(fields):
        current = jnp.stack([fields[0], fields[1]])
        former = jnp.stack([fields[2], fields[3]])
        samples = []
        for moment in range(STEPS):
            extended = jnp.pad(current, ((0, 0), (1, 1), (0, 0)))
            advanced = leapfrog(extended, former, coefficients)
            former = current
            current = advanced
            samples.append(current[0].reshape(-1)[global_cells])
        return current[0], current[1], jnp.stack(samples)

    pressure_out, auxiliary_out, samples = lax.map(propagate, (pressure, auxiliary, pressure_prior, auxiliary_prior))
    spectra_out = spectra
    for moment in range(STEPS):
        angle = frequencies * (moment + 1.0)
        table = jnp.concatenate([jnp.cos(angle), -jnp.sin(angle)])
        spectra_out = spectra_out + table[None, :, None] * samples[:, moment][:, None, :]
    features = spectra_out.astype(jnp.bfloat16).reshape(SHOTS * 2 * FREQ, TARGETS)

    def brick_tiles(brick_index):
        lists = lax.dynamic_index_in_dim(patch_lists, brick_index, 0, keepdims=False)
        columns = (lists + brick_index * TGT_BRICK).astype(jnp.int32).reshape(-1)
        chosen = jnp.take(features, columns, axis=1).astype(jnp.float32).reshape(FEATURES, GROUPS, P_MAX, PATCH)
        grams = jnp.einsum('fgpa,fgpb->gpab', chosen, chosen) / FEATURES
        counts = lax.dynamic_index_in_dim(patch_counts, brick_index, 0, keepdims=False)
        live_slots = (jnp.arange(P_MAX, dtype=jnp.int32)[None, :] < counts[:, None]).astype(jnp.float32)
        return grams * live_slots[:, :, None, None]

    gram_tiles = lax.map(brick_tiles, jnp.arange(BRICKS, dtype=jnp.int32))
    return pressure_out, auxiliary_out, spectra_out, gram_tiles
```

```python
import functools
import math

import jax
import jax.numpy as jnp
from jax import lax
from jax.experimental import pallas as pl
from jax.experimental.pallas import tpu as pltpu
from jax.sharding import PartitionSpec as P

STEPS = 4
MIB = 1024 * 1024
NT = (((1,), (1,)), ((), ()))


TILE = 8
LANES = 128


def tiled(field):
    shots, width, depth = field.shape
    parts = field.reshape(shots, width // TILE, TILE, depth // LANES, LANES)
    return parts.transpose(0, 1, 3, 2, 4)


def untiled(parts):
    shots, across, along, tile, lanes = parts.shape
    return parts.transpose(0, 1, 3, 2, 4).reshape(shots, across * tile, along * lanes)


class ShotRows:
    def __init__(self, ref):
        self.shots, self.across, self.along, tile, lanes = ref.shape
        self.stride = self.across * self.along * tile
        self.flat = ref.reshape(self.shots * self.stride, lanes)

    def place(self, x, j):
        if isinstance(x, int):
            start = (x // TILE * self.along + j) * TILE + x % TILE
        else:
            start = (lax.div(x, TILE) * self.along + j) * TILE + lax.rem(x, TILE)
        return pl.ds(start, self.shots, stride=self.stride)

    def __getitem__(self, x):
        return jnp.concatenate([self.flat[self.place(x, j), :] for j in range(self.along)], 1)

    def __setitem__(self, x, row):
        for j in range(self.along):
            self.flat[self.place(x, j), :] = row[:, j * LANES : (j + 1) * LANES]


def compiler_params(mib):
    return pltpu.CompilerParams(vmem_limit_bytes=mib * MIB)


def tilt_coefficients(courant, epsilon, delta, tilt):
    turns = jnp.round(tilt * (2.0 / math.pi))
    rest = (tilt - turns * 1.5703125) - turns * (math.pi / 2 - 1.5703125)
    odd = turns - 2.0 * jnp.floor(turns * 0.5)
    sign = 1.0 - 2.0 * odd
    double = 2.0 * rest
    square = double * double
    sine = double * (
        1.0
        + square
        * (
            -1.0 / 6
            + square
            * (1.0 / 120 + square * (-1.0 / 5040 + square * (1.0 / 362880 - square / 39916800.0)))
        )
    )
    versine = square * (
        0.5
        + square
        * (
            -1.0 / 24
            + square
            * (1.0 / 720 + square * (-1.0 / 40320 + square * (1.0 / 3628800 - square / 479001600.0)))
        )
    )
    sine_sq = jnp.where(odd > 0.5, 1.0 - 0.5 * versine, 0.5 * versine)
    quarter_sin = 0.25 * sign * sine
    gain_p = courant * (1.0 + 2.0 * epsilon)
    gain_q = courant * (1.0 + 2.0 * delta)
    return sine_sq, quarter_sin, courant, gain_p, gain_q


def depth_terms(row):
    depth = row.shape[-1]
    lane = lax.broadcasted_iota(jnp.int32, row.shape, 1)
    deeper = jnp.where(lane < depth - 1, pltpu.roll(row, depth - 1, 1), 0.0)
    upper = jnp.where(lane > 0, pltpu.roll(row, 1, 1), 0.0)
    return deeper + upper, deeper - upper


def advance(count, p_row, q_row, p_prior, q_prior, coefficient, put):
    p_back, p_here = p_row(-1), p_row(0)
    q_back, q_here = q_row(-1), q_row(0)
    _, p_back_d = depth_terms(p_back)
    _, q_back_d = depth_terms(q_back)
    p_sum, p_here_d = depth_terms(p_here)
    q_sum, q_here_d = depth_terms(q_here)
    for row in range(count):
        p_next, q_next = p_row(row + 1), q_row(row + 1)
        p_next_sum, p_next_d = depth_terms(p_next)
        q_next_sum, q_next_d = depth_terms(q_next)
        sine_sq, quarter_sin, courant, gain_p, gain_q = coefficient(row)
        twice_p, twice_q = p_here + p_here, q_here + q_here
        side = p_next + p_back
        across = (side - twice_p) + sine_sq * (p_sum - side) - quarter_sin * (p_next_d - p_back_d)
        side = q_next + q_back
        along = (q_sum - twice_q) + sine_sq * (side - q_sum) + quarter_sin * (q_next_d - q_back_d)
        along = courant * along
        put(
            row,
            (twice_p - p_prior(row)) + (gain_p * across + along),
            (twice_q - q_prior(row)) + (gain_q * across + along),
        )
        p_back, p_here, p_back_d, p_here_d, p_sum = p_here, p_next, p_here_d, p_next_d, p_next_sum
        q_back, q_here, q_back_d, q_here_d, q_sum = q_here, q_next, q_here_d, q_next_d, q_next_sum


def split_bf16(values):
    high = values.astype(jnp.bfloat16)
    low = (values - high.astype(jnp.float32)).astype(jnp.bfloat16)
    return high, low


def outer_kernel(*refs):
    fields, params, outs = refs[:8], refs[8:16], refs[16:]
    shots, tile = fields[0].shape[0], fields[0].shape[3]
    depth = params[0].shape[1]
    for side in range(2):
        views = [ShotRows(ref) for ref in fields[4 * side : 4 * side + 4]]
        out = outs[side]

        def row(field, distance):
            place = distance if side == 0 else tile - 1 - distance
            return views[field][place]

        position = 0

        def put(first, second):
            nonlocal position
            out[pl.ds(position, 2 * shots), :] = jnp.concatenate([first, second], 0).astype(
                jnp.bfloat16
            )
            position += 2 * shots

        for field in range(4):
            near = row(field, 0)
            put(near, near - near.astype(jnp.bfloat16).astype(jnp.float32))
        for first, second in far_items():
            put(row(*first), row(*second))
        terms = tilt_coefficients(*[ref[...] for ref in params[4 * side : 4 * side + 4]])
        rows = []
        for term in terms:
            for distance in range(STEPS - 1):
                place = distance if side == 0 else tile - 1 - distance
                rows.append(term[place : place + 1, :])
        while len(rows) < 2 * shots:
            rows.append(jnp.zeros((1, depth), jnp.float32))
        out[pl.ds(position, 2 * shots), :] = jnp.concatenate(rows, 0).astype(jnp.bfloat16)


def far_items():
    items = []
    for field in range(2):
        items += [(field, distance) for distance in range(1, STEPS)]
    for field in range(2, 4):
        items += [(field, distance) for distance in range(1, STEPS - 1)]
    return list(zip(items[0::2], items[1::2]))


def outer_rows(fields, params):
    shots, across, along, tile, lanes = fields[0].shape
    depth = along * lanes
    last = across - 1
    field_specs, param_specs = [], []
    for place in (0, last):
        field_specs += [
            pl.BlockSpec((shots, 1, along, tile, lanes), lambda i, place=place: (0, place, 0, 0, 0))
        ] * 4
        param_specs += [pl.BlockSpec((tile, depth), lambda i, place=place: (place, 0))] * 4
    rows = 2 * shots * (4 + len(far_items()) + 1)
    shape = jax.ShapeDtypeStruct((rows, depth), jnp.bfloat16)
    return pl.pallas_call(
        outer_kernel,
        grid=(1,),
        in_specs=field_specs + param_specs,
        out_specs=[pl.BlockSpec((rows, depth), lambda i: (0, 0))] * 2,
        out_shape=[shape, shape],
        compiler_params=compiler_params(16),
        name="outer_rows",
    )(*fields, *fields, *params, *params)


def sample_rows(values, one_hot):
    high, low = split_bf16(values)
    return jnp.dot(jnp.concatenate([high, low], 1), one_hot, preferred_element_type=jnp.float32)


def interior_kernel(
    p_ref,
    q_ref,
    pp_ref,
    qq_ref,
    courant_ref,
    epsilon_ref,
    delta_ref,
    tilt_ref,
    cells_ref,
    lists_ref,
    edge_ref,
    prior_edge_ref,
    coef_edge_ref,
    p_inner_ref,
    q_inner_ref,
    sample_ref,
    depth_hot_ref,
    column_ref,
    list_hot_ref,
    level_ref,
    coef_ref,
):
    shots = p_ref.shape[0]
    width, depth = courant_ref.shape
    p_rows, q_rows, pp_rows, qq_rows = [ShotRows(ref) for ref in (p_ref, q_ref, pp_ref, qq_ref)]

    terms = tilt_coefficients(courant_ref[...], epsilon_ref[...], delta_ref[...], tilt_ref[...])
    for index, term in enumerate(terms):
        for x in range(width):
            coef_ref[index, x] = jnp.broadcast_to(term[x : x + 1, :], (shots, depth))
        flip = -term if index == 1 else term
        coef_edge_ref[0, index] = term[:8, :]
        coef_edge_ref[1, index] = flip[width - 8 :, :]

    @pl.loop(0, width)
    def _(x):
        level_ref[0, 0, x] = p_rows[x]
        level_ref[0, 1, x] = q_rows[x]

    cells = cells_ref[...]
    column = cells // depth
    z_of = cells - column * depth
    column_ref[...] = column
    targets = cells.shape[1]
    for half in range(2):
        for base in range(0, depth, 64):
            lanes = lax.broadcasted_iota(jnp.int32, (64, targets), 0) + base
            depth_hot_ref[pl.ds(half * depth + base, 64), :] = jnp.where(
                lanes == z_of, 1.0, 0.0
            ).astype(jnp.bfloat16)

    owners, slots, patch = lists_ref.shape[1:]
    rows = [lists_ref[0, g, s : s + 1, :] for g in range(owners) for s in range(slots)]
    count = len(rows)
    while len(rows) % 8:
        rows.append(rows[0])
    upright = jnp.transpose(jnp.concatenate(rows, 0).astype(jnp.float32))
    lanes = lax.broadcasted_iota(jnp.int32, (patch, targets), 1).astype(jnp.float32)
    for k in range(count):
        list_hot_ref[pl.ds(k * patch, patch), :] = jnp.where(
            upright[:, k : k + 1] == lanes, 1.0, 0.0
        ).astype(jnp.bfloat16)

    for side in range(2):
        x = 0 if side == 0 else width - 1
        prior_edge_ref[side, 0] = pp_rows[x]
        prior_edge_ref[side, 1] = qq_rows[x]

    chunk = 8
    for step in range(1, STEPS + 1):
        low, high = step, width - step
        chunks = -(-(high - low) // chunk)

        @pl.loop(0, chunks)
        def _(index):
            start = jnp.minimum(low + chunk * index, high - chunk)

            def prior(field):
                if step == 1:
                    rows = (pp_rows, qq_rows)[field]
                    return lambda r: rows[start + r]
                return lambda r: level_ref[step - 2, field, start + r]

            def put(r, p_new, q_new):
                if step < STEPS:
                    level_ref[step, 0, start + r] = p_new
                    level_ref[step, 1, start + r] = q_new
                else:
                    p_inner_ref[start + r - STEPS] = p_new
                    q_inner_ref[start + r - STEPS] = q_new

            advance(
                chunk,
                lambda r: level_ref[step - 1, 0, start + r],
                lambda r: level_ref[step - 1, 1, start + r],
                prior(0),
                prior(1),
                lambda r: [coef_ref[i, start + r] for i in range(5)],
                put,
            )

    for step in range(STEPS):
        for field in range(2):
            for near in range(2):
                edge_ref[0, field, step, near] = level_ref[step, field, step + near]
                edge_ref[1, field, step, near] = level_ref[step, field, width - 1 - step - near]

    for step in range(1, STEPS + 1):
        low, high = step, width - step
        if step < STEPS:
            values = level_ref[step, 0, low:high]
        else:
            values = p_inner_ref[...]
        found = sample_rows(values.reshape((high - low) * shots, depth), depth_hot_ref[...])
        total = jnp.zeros((shots, targets), jnp.float32)
        for r in range(high - low):
            total = total + jnp.where(column == low + r, found[r * shots : (r + 1) * shots], 0.0)
        sample_ref[step - 1] = total


def interior(fields, params, target_cells, patch_lists):
    shots = fields[0].shape[0]
    width, depth = params[0].shape
    targets = target_cells.shape[0]
    _, owners, slots, patch = patch_lists.shape
    f32 = functools.partial(jax.ShapeDtypeStruct, dtype=jnp.float32)
    out_shape = [
        f32((2, 2, STEPS, 2, shots, depth)),
        f32((2, 2, shots, depth)),
        f32((2, 5, 8, depth)),
        f32((width - 2 * STEPS, shots, depth)),
        f32((width - 2 * STEPS, shots, depth)),
        f32((STEPS, shots, targets)),
        jax.ShapeDtypeStruct((2 * depth, targets), jnp.bfloat16),
        jax.ShapeDtypeStruct((1, targets), jnp.int32),
        jax.ShapeDtypeStruct((owners * slots * patch, targets), jnp.bfloat16),
    ]
    vmem = pl.BlockSpec(memory_space=pltpu.VMEM)
    return pl.pallas_call(
        interior_kernel,
        in_specs=[vmem] * 10,
        out_specs=[vmem] * len(out_shape),
        out_shape=out_shape,
        scratch_shapes=[
            pltpu.VMEM((STEPS, 2, width, shots, depth), jnp.float32),
            pltpu.VMEM((5, width, shots, depth), jnp.float32),
        ],
        compiler_params=compiler_params(40),
        cost_estimate=pl.CostEstimate(
            flops=200 * STEPS * shots * width * depth, bytes_accessed=8 * MIB, transcendentals=0
        ),
        name="interior",
    )(*fields, *params, target_cells.reshape(1, targets), patch_lists)


def finish_kernel(
    lower_ref,
    upper_ref,
    edge_ref,
    prior_edge_ref,
    coef_edge_ref,
    sample_ref,
    depth_hot_ref,
    column_ref,
    list_hot_ref,
    spectra_ref,
    table_ref,
    spectra_out_ref,
    packed_ref,
    final_ref,
    level_ref,
    prior_ref,
    coef_ref,
    feature_ref,
    *,
    width,
):
    shots, depth = edge_ref.shape[-2:]
    targets = column_ref.shape[1]
    first = -STEPS
    pair = 2 * shots
    for side, ref in enumerate((lower_ref, upper_ref)):
        for field in range(4):
            both = ref[pl.ds(field * pair, pair), :].astype(jnp.float32)
            value = both[:shots] + both[shots:]
            if field < 2:
                level_ref[side, field, 0, -1 - first] = value
            else:
                prior_ref[side, field - 2, -1 - (1 - STEPS)] = value
        for index, items in enumerate(far_items()):
            both = ref[pl.ds((4 + index) * pair, pair), :].astype(jnp.float32)
            for half, (field, distance) in enumerate(items):
                value = both[half * shots : (half + 1) * shots]
                if field < 2:
                    level_ref[side, field, 0, -1 - distance - first] = value
                else:
                    prior_ref[side, field - 2, -1 - distance - (1 - STEPS)] = value
        params = ref[pl.ds((4 + len(far_items())) * pair, pair), :].astype(jnp.float32)
        for index in range(5):
            for distance in range(STEPS - 1):
                line = index * (STEPS - 1) + distance
                row = params[line : line + 1, :]
                if index == 1 and side == 1:
                    row = -row
                coef_ref[side, index, STEPS - 2 - distance] = jnp.broadcast_to(row, (shots, depth))
            for k in range(STEPS):
                coef_ref[side, index, STEPS - 1 + k] = jnp.broadcast_to(
                    coef_edge_ref[side, index, pl.ds(k if side == 0 else 7 - k, 1), :],
                    (shots, depth),
                )
        for field in range(2):
            prior_ref[side, field, STEPS - 1] = prior_edge_ref[side, field]
            for step in range(STEPS):
                for near in range(2):
                    level_ref[side, field, step, step + near - first] = edge_ref[
                        side, field, step, near
                    ]

    for step in range(1, STEPS + 1):
        low = step - STEPS

        for side in range(2):

            def prior(field):
                if step == 1:
                    return lambda r: prior_ref[side, field, low + r - (1 - STEPS)]
                return lambda r: level_ref[side, field, step - 2, low + r - first]

            def put(r, p_new, q_new):
                if step < STEPS:
                    level_ref[side, 0, step, low + r - first] = p_new
                    level_ref[side, 1, step, low + r - first] = q_new
                else:
                    final_ref[side, 0, r] = p_new
                    final_ref[side, 1, r] = q_new

            advance(
                STEPS,
                lambda r: level_ref[side, 0, step - 1, low + r - first],
                lambda r: level_ref[side, 1, step - 1, low + r - first],
                prior(0),
                prior(1),
                lambda r: [coef_ref[side, i, low + r - (1 - STEPS) + 0] for i in range(5)],
                put,
            )

    column = column_ref[...]
    places, values = [], []
    for step in range(1, STEPS + 1):
        for side in range(2):
            for k in range(step):
                places.append((step, k if side == 0 else width - 1 - k))
                if step < STEPS:
                    values.append(level_ref[side, 0, step, k - first])
                else:
                    values.append(final_ref[side, 0, k])
    found = sample_rows(jnp.concatenate(values, 0), depth_hot_ref[...])
    samples = [sample_ref[step] for step in range(STEPS)]
    for index, (step, x) in enumerate(places):
        samples[step - 1] = samples[step - 1] + jnp.where(
            column == x, found[index * shots : (index + 1) * shots], 0.0
        )

    parts = spectra_ref.shape[0] // shots
    lanes = table_ref.shape[-1]
    for s in range(shots):
        for base in range(0, targets, lanes):
            value = spectra_ref[pl.ds(s * parts, parts), pl.ds(base, lanes)]
            for step in range(STEPS):
                value = value + table_ref[step] * samples[step][s : s + 1, base : base + lanes]
            spectra_out_ref[pl.ds(s * parts, parts), pl.ds(base, lanes)] = value
            feature_ref[pl.ds(s * parts, parts), pl.ds(base, lanes)] = value.astype(jnp.bfloat16)

    owners = packed_ref.shape[0]
    patch = packed_ref.shape[2]
    slots = list_hot_ref.shape[0] // (owners * patch)
    half = patch // 2
    row = lax.broadcasted_iota(jnp.int32, (half, patch), 0)
    lane = lax.broadcasted_iota(jnp.int32, (half, patch), 1)
    from_last = (lane < half) & (row > lane)
    for g in range(owners):
        chosen = lax.dot_general(
            list_hot_ref[pl.ds(g * slots * patch, slots * patch), :],
            feature_ref[...],
            NT,
            preferred_element_type=jnp.float32,
        ).astype(jnp.bfloat16)
        diagonals = []
        for s in range(slots):
            mine = chosen[s * patch : (s + 1) * patch]
            gram = lax.dot_general(mine, mine, NT, preferred_element_type=jnp.float32)
            last = pltpu.roll(gram[half:], half, 1)
            packed_ref[g, pl.ds(s * half, half), :] = jnp.where(from_last, last, gram[:half])
            diagonals.append(jnp.sum(jnp.where(row == lane, last, 0.0), 0, keepdims=True))
        while len(diagonals) % 8:
            diagonals.append(jnp.zeros((1, patch), jnp.float32))
        packed_ref[g, pl.ds(slots * half, len(diagonals)), :] = jnp.concatenate(diagonals, 0)


def finish(lower, upper, inner, spectra, table, width, owners, slots, patch):
    edge, prior_edge, coef_edge, sample, depth_hot, column, list_hot = inner
    shots, depth = edge.shape[-2:]
    targets = column.shape[1]
    features = spectra.shape[0]
    f32 = functools.partial(jax.ShapeDtypeStruct, dtype=jnp.float32)
    rows = slots * (patch // 2) + -(-slots // 8) * 8
    out_shape = [
        f32((features, targets)),
        f32((owners, rows, patch)),
        f32((2, 2, STEPS, shots, depth)),
    ]
    vmem = pl.BlockSpec(memory_space=pltpu.VMEM)
    return pl.pallas_call(
        functools.partial(finish_kernel, width=width),
        in_specs=[vmem] * 11,
        out_specs=[vmem] * len(out_shape),
        out_shape=out_shape,
        scratch_shapes=[
            pltpu.VMEM((2, 2, STEPS, 2 * STEPS + 1, shots, depth), jnp.float32),
            pltpu.VMEM((2, 2, STEPS, shots, depth), jnp.float32),
            pltpu.VMEM((2, 5, 2 * STEPS - 1, shots, depth), jnp.float32),
            pltpu.VMEM((features, targets), jnp.bfloat16),
        ],
        compiler_params=compiler_params(40),
        name="finish",
    )(
        lower,
        upper,
        edge,
        prior_edge,
        coef_edge,
        sample,
        depth_hot,
        column,
        list_hot,
        spectra,
        table,
    )


def assemble_kernel(p_inner_ref, q_inner_ref, final_ref, p_out_ref, q_out_ref):
    width = p_out_ref.shape[1] * TILE
    for field, (inner, out) in enumerate(((p_inner_ref, p_out_ref), (q_inner_ref, q_out_ref))):
        rows = ShotRows(out)
        for k in range(STEPS):
            rows[k] = final_ref[0, field, k]
            rows[width - 1 - k] = final_ref[1, field, k]

        @pl.loop(STEPS, width - STEPS, unroll=4)
        def _(x):
            rows[x] = inner[x - STEPS]


def assemble(p_inner, q_inner, final):
    inner, shots, depth = p_inner.shape
    across, along = (inner + 2 * STEPS) // TILE, depth // LANES
    shape = jax.ShapeDtypeStruct((shots, across, along, TILE, LANES), jnp.float32)
    vmem = pl.BlockSpec(memory_space=pltpu.VMEM)
    return pl.pallas_call(
        assemble_kernel,
        in_specs=[vmem] * 3,
        out_specs=[vmem] * 2,
        out_shape=[shape, shape],
        compiler_params=compiler_params(16),
        cost_estimate=pl.CostEstimate(flops=8 * MIB, bytes_accessed=4 * MIB, transcendentals=0),
        name="assemble",
    )(p_inner, q_inner, final)


def tiles_kernel(received_ref, counts_ref, out_ref, *, features):
    groups = received_ref.shape[0]
    slots, patch = out_ref.shape[2], out_ref.shape[3]
    half = patch // 2
    row = lax.broadcasted_iota(jnp.int32, (half, patch), 0)
    lane = lax.broadcasted_iota(jnp.int32, (half, patch), 1)
    live = counts_ref[0, 0]
    total = received_ref[0]
    for g in range(1, groups):
        total = total + received_ref[g]
    for s in range(slots):
        scale = jnp.where(s < live, 1.0 / features, 0.0)
        packed = total[s * half : (s + 1) * half] * scale
        diagonal = total[slots * half + s : slots * half + s + 1] * scale
        turned = jnp.transpose(jnp.concatenate([packed, packed], 0))
        flipped = turned[:half]
        corner = turned[half:]
        out_ref[0, 0, s, pl.ds(0, half), :] = jnp.where(
            (lane < half) & (row > lane), flipped, packed
        )
        last = jnp.where(row > lane, packed, jnp.where(row == lane, diagonal, flipped))
        out_ref[0, 0, s, pl.ds(half, half), :] = jnp.where(
            lane < half, corner, pltpu.roll(last, half, 1)
        )


def tiles(received, patch_counts, slots, features):
    patch = received.shape[2]
    return pl.pallas_call(
        functools.partial(tiles_kernel, features=features),
        in_specs=[
            pl.BlockSpec(memory_space=pltpu.VMEM),
            pl.BlockSpec(memory_space=pltpu.SMEM),
        ],
        out_specs=pl.BlockSpec(memory_space=pltpu.VMEM),
        out_shape=jax.ShapeDtypeStruct((1, 1, slots, patch, patch), jnp.float32),
        compiler_params=compiler_params(16),
        name="tiles",
    )(received, patch_counts)


def shards(
    pressure,
    auxiliary,
    pressure_prior,
    auxiliary_prior,
    courant_sq,
    thomsen_epsilon,
    thomsen_delta,
    tilt_angle,
    frequencies,
    spectra,
    target_cells,
    patch_lists,
    patch_counts,
):
    shots, width, depth = pressure.shape
    _, owners, slots, patch = patch_lists.shape
    fields = [tiled(item) for item in (pressure, auxiliary, pressure_prior, auxiliary_prior)]
    params = (courant_sq, thomsen_epsilon, thomsen_delta, tilt_angle)
    parts, targets = spectra.shape[1:]

    first_rows, last_rows = outer_rows(fields, params)
    bricks = lax.axis_size("brick")
    upward = [(i, i + 1) for i in range(bricks - 1)]
    downward = [(i + 1, i) for i in range(bricks - 1)]
    lower = lax.ppermute(last_rows, "brick", upward)
    upper = lax.ppermute(first_rows, "brick", downward)

    moments = jnp.arange(1, STEPS + 1, dtype=jnp.float32)
    angle = frequencies[None, :] * moments[:, None]
    table = jnp.concatenate([jnp.cos(angle), -jnp.sin(angle)], 1)
    table = jnp.broadcast_to(table[:, :, None], (STEPS, parts, 128))

    edge, prior_edge, coef_edge, p_inner, q_inner, sample, depth_hot, column, list_hot = interior(
        fields, params, target_cells, patch_lists
    )
    spectra_out, packed, final = finish(
        lower,
        upper,
        (edge, prior_edge, coef_edge, sample, depth_hot, column, list_hot),
        spectra.reshape(shots * parts, targets),
        table,
        width,
        owners,
        slots,
        patch,
    )
    received = lax.all_to_all(packed, "shot", split_axis=0, concat_axis=0, tiled=True)
    pressure_out, auxiliary_out = [untiled(item) for item in assemble(p_inner, q_inner, final)]
    gram_tiles = tiles(received, patch_counts, slots, shots * parts * owners)
    return (pressure_out, auxiliary_out, spectra_out.reshape(spectra.shape), gram_tiles)


def solution(mesh):
    return jax.shard_map(
        shards,
        mesh=mesh,
        in_specs=(
            P("shot", "brick", None),
            P("shot", "brick", None),
            P("shot", "brick", None),
            P("shot", "brick", None),
            P("brick", None),
            P("brick", None),
            P("brick", None),
            P("brick", None),
            P(),
            P("shot", None, "brick"),
            P("brick"),
            P("brick", None, None, None),
            P("brick", "shot"),
        ),
        out_specs=(
            P("shot", "brick", None),
            P("shot", "brick", None),
            P("shot", None, "brick"),
            P("brick", "shot", None, None, None),
        ),
        check_vma=False,
    )
```

```python
import functools
import math

import jax
import jax.numpy as jnp
from jax import lax
from jax.experimental import pallas as pl
from jax.experimental.pallas import tpu as pltpu
from jax.sharding import PartitionSpec as P

STEPS = 4
MIB = 1024 * 1024
NT = (((1,), (1,)), ((), ()))


TILE = 8
LANES = 128


def tiled(field):
    shots, width, depth = field.shape
    parts = field.reshape(shots, width // TILE, TILE, depth // LANES, LANES)
    return parts.transpose(0, 1, 3, 2, 4)


def untiled(parts):
    shots, across, along, tile, lanes = parts.shape
    return parts.transpose(0, 1, 3, 2, 4).reshape(shots, across * tile, along * lanes)


class ShotRows:
    def __init__(self, ref):
        self.shots, self.across, self.along, tile, lanes = ref.shape
        self.stride = self.across * self.along * tile
        self.flat = ref.reshape(self.shots * self.stride, lanes)

    def place(self, x, j):
        if isinstance(x, int):
            start = (x // TILE * self.along + j) * TILE + x % TILE
        else:
            start = (lax.div(x, TILE) * self.along + j) * TILE + lax.rem(x, TILE)
        return pl.ds(start, self.shots, stride=self.stride)

    def __getitem__(self, x):
        return jnp.concatenate([self.flat[self.place(x, j), :] for j in range(self.along)], 1)

    def __setitem__(self, x, row):
        for j in range(self.along):
            self.flat[self.place(x, j), :] = row[:, j * LANES : (j + 1) * LANES]


def compiler_params(mib):
    return pltpu.CompilerParams(vmem_limit_bytes=mib * MIB)


def tilt_coefficients(courant, epsilon, delta, tilt):
    turns = jnp.round(tilt * (2.0 / math.pi))
    rest = (tilt - turns * 1.5703125) - turns * (math.pi / 2 - 1.5703125)
    odd = turns - 2.0 * jnp.floor(turns * 0.5)
    sign = 1.0 - 2.0 * odd
    double = 2.0 * rest
    square = double * double
    sine = double * (
        1.0
        + square
        * (
            -1.0 / 6
            + square
            * (1.0 / 120 + square * (-1.0 / 5040 + square * (1.0 / 362880 - square / 39916800.0)))
        )
    )
    versine = square * (
        0.5
        + square
        * (
            -1.0 / 24
            + square
            * (1.0 / 720 + square * (-1.0 / 40320 + square * (1.0 / 3628800 - square / 479001600.0)))
        )
    )
    sine_sq = jnp.where(odd > 0.5, 1.0 - 0.5 * versine, 0.5 * versine)
    quarter_sin = 0.25 * sign * sine
    gain_p = courant * (1.0 + 2.0 * epsilon)
    gain_q = courant * (1.0 + 2.0 * delta)
    return sine_sq, quarter_sin, courant, gain_p, gain_q


def depth_terms(row):
    depth = row.shape[-1]
    lane = lax.broadcasted_iota(jnp.int32, row.shape, 1)
    deeper = jnp.where(lane < depth - 1, pltpu.roll(row, depth - 1, 1), 0.0)
    upper = jnp.where(lane > 0, pltpu.roll(row, 1, 1), 0.0)
    return deeper + upper, deeper - upper


def advance(count, p_row, q_row, p_prior, q_prior, coefficient, put):
    p_back, p_here = p_row(-1), p_row(0)
    q_back, q_here = q_row(-1), q_row(0)
    _, p_back_d = depth_terms(p_back)
    _, q_back_d = depth_terms(q_back)
    p_sum, p_here_d = depth_terms(p_here)
    q_sum, q_here_d = depth_terms(q_here)
    for row in range(count):
        p_next, q_next = p_row(row + 1), q_row(row + 1)
        p_next_sum, p_next_d = depth_terms(p_next)
        q_next_sum, q_next_d = depth_terms(q_next)
        sine_sq, quarter_sin, courant, gain_p, gain_q = coefficient(row)
        twice_p, twice_q = p_here + p_here, q_here + q_here
        side = p_next + p_back
        across = (side - twice_p) + sine_sq * (p_sum - side) - quarter_sin * (p_next_d - p_back_d)
        side = q_next + q_back
        along = (q_sum - twice_q) + sine_sq * (side - q_sum) + quarter_sin * (q_next_d - q_back_d)
        along = courant * along
        put(
            row,
            (twice_p - p_prior(row)) + (gain_p * across + along),
            (twice_q - q_prior(row)) + (gain_q * across + along),
        )
        p_back, p_here, p_back_d, p_here_d, p_sum = p_here, p_next, p_here_d, p_next_d, p_next_sum
        q_back, q_here, q_back_d, q_here_d, q_sum = q_here, q_next, q_here_d, q_next_d, q_next_sum


def split_bf16(values):
    high = values.astype(jnp.bfloat16)
    low = (values - high.astype(jnp.float32)).astype(jnp.bfloat16)
    return high, low


def outer_kernel(*refs):
    sources, outs, (field_ref, param_ref, field_sem, param_sem) = refs[:8], refs[8:10], refs[10:]
    shots, across, along, tile, lanes = sources[0].shape
    depth = along * lanes
    copies = []
    for side in range(2):
        place = side * (across - 1)
        for i in range(4):
            copies.append(
                pltpu.make_async_copy(
                    sources[i].at[:, pl.ds(place, 1)], field_ref.at[side, i], field_sem.at[side, i]
                )
            )
        for i in range(4):
            copies.append(
                pltpu.make_async_copy(
                    sources[4 + i].at[pl.ds(place * tile, tile)],
                    param_ref.at[side, i],
                    param_sem.at[side, i],
                )
            )
    for copy in copies:
        copy.start()
    for side in range(2):
        for copy in copies[8 * side : 8 * side + 8]:
            copy.wait()
        views = [ShotRows(field_ref.at[side, i]) for i in range(4)]
        out = outs[side]

        def row(field, distance):
            place = distance if side == 0 else tile - 1 - distance
            return views[field][place]

        position = 0

        def put(first, second):
            nonlocal position
            out[pl.ds(position, 2 * shots), :] = jnp.concatenate([first, second], 0).astype(
                jnp.bfloat16
            )
            position += 2 * shots

        for field in range(4):
            near = row(field, 0)
            put(near, near - near.astype(jnp.bfloat16).astype(jnp.float32))
        for first, second in far_items():
            put(row(*first), row(*second))
        terms = tilt_coefficients(*[param_ref[side, i] for i in range(4)])
        rows = []
        for term in terms:
            for distance in range(STEPS - 1):
                place = distance if side == 0 else tile - 1 - distance
                rows.append(term[place : place + 1, :])
        while len(rows) < 2 * shots:
            rows.append(jnp.zeros((1, depth), jnp.float32))
        out[pl.ds(position, 2 * shots), :] = jnp.concatenate(rows, 0).astype(jnp.bfloat16)


def far_items():
    items = []
    for field in range(2):
        items += [(field, distance) for distance in range(1, STEPS)]
    for field in range(2, 4):
        items += [(field, distance) for distance in range(1, STEPS - 1)]
    return list(zip(items[0::2], items[1::2]))


def outer_rows(fields, params):
    shots, across, along, tile, lanes = fields[0].shape
    depth = along * lanes
    rows = 2 * shots * (4 + len(far_items()) + 1)
    shape = jax.ShapeDtypeStruct((rows, depth), jnp.bfloat16)
    return pl.pallas_call(
        outer_kernel,
        in_specs=[pl.BlockSpec(memory_space=pltpu.HBM)] * 8,
        out_specs=[pl.BlockSpec(memory_space=pltpu.VMEM)] * 2,
        out_shape=[shape, shape],
        scratch_shapes=[
            pltpu.VMEM((2, 4, shots, 1, along, tile, lanes), jnp.float32),
            pltpu.VMEM((2, 4, tile, depth), jnp.float32),
            pltpu.SemaphoreType.DMA((2, 4)),
            pltpu.SemaphoreType.DMA((2, 4)),
        ],
        compiler_params=compiler_params(60),
        name="outer_rows",
    )(*fields, *params)


def sample_rows(values, one_hot):
    high, low = split_bf16(values)
    return jnp.dot(jnp.concatenate([high, low], 1), one_hot, preferred_element_type=jnp.float32)


def interior_kernel(
    p_ref,
    q_ref,
    pp_ref,
    qq_ref,
    courant_ref,
    epsilon_ref,
    delta_ref,
    tilt_ref,
    cells_ref,
    lists_ref,
    edge_ref,
    prior_edge_ref,
    coef_edge_ref,
    p_inner_ref,
    q_inner_ref,
    sample_ref,
    depth_hot_ref,
    column_ref,
    list_hot_ref,
    level_ref,
    coef_ref,
):
    shots = p_ref.shape[0]
    width, depth = courant_ref.shape
    p_rows, q_rows, pp_rows, qq_rows = [ShotRows(ref) for ref in (p_ref, q_ref, pp_ref, qq_ref)]

    terms = tilt_coefficients(courant_ref[...], epsilon_ref[...], delta_ref[...], tilt_ref[...])
    for index, term in enumerate(terms):
        for x in range(width):
            coef_ref[index, x] = jnp.broadcast_to(term[x : x + 1, :], (shots, depth))
        flip = -term if index == 1 else term
        coef_edge_ref[0, index] = term[:8, :]
        coef_edge_ref[1, index] = flip[width - 8 :, :]

    @pl.loop(0, width)
    def _(x):
        level_ref[0, 0, x] = p_rows[x]
        level_ref[0, 1, x] = q_rows[x]

    cells = cells_ref[...]
    column = cells // depth
    z_of = cells - column * depth
    column_ref[...] = column
    targets = cells.shape[1]
    for half in range(2):
        for base in range(0, depth, 64):
            lanes = lax.broadcasted_iota(jnp.int32, (64, targets), 0) + base
            depth_hot_ref[pl.ds(half * depth + base, 64), :] = jnp.where(
                lanes == z_of, 1.0, 0.0
            ).astype(jnp.bfloat16)

    owners, slots, patch = lists_ref.shape[1:]
    rows = [lists_ref[0, g, s : s + 1, :] for g in range(owners) for s in range(slots)]
    count = len(rows)
    while len(rows) % 8:
        rows.append(rows[0])
    upright = jnp.transpose(jnp.concatenate(rows, 0).astype(jnp.float32))
    lanes = lax.broadcasted_iota(jnp.int32, (patch, targets), 1).astype(jnp.float32)
    for k in range(count):
        list_hot_ref[pl.ds(k * patch, patch), :] = jnp.where(
            upright[:, k : k + 1] == lanes, 1.0, 0.0
        ).astype(jnp.bfloat16)

    for side in range(2):
        x = 0 if side == 0 else width - 1
        prior_edge_ref[side, 0] = pp_rows[x]
        prior_edge_ref[side, 1] = qq_rows[x]

    chunk = 8
    for step in range(1, STEPS + 1):
        low, high = step, width - step
        chunks = -(-(high - low) // chunk)

        @pl.loop(0, chunks)
        def _(index):
            start = jnp.minimum(low + chunk * index, high - chunk)

            def prior(field):
                if step == 1:
                    rows = (pp_rows, qq_rows)[field]
                    return lambda r: rows[start + r]
                return lambda r: level_ref[step - 2, field, start + r]

            def put(r, p_new, q_new):
                if step < STEPS:
                    level_ref[step, 0, start + r] = p_new
                    level_ref[step, 1, start + r] = q_new
                else:
                    p_inner_ref[start + r - STEPS] = p_new
                    q_inner_ref[start + r - STEPS] = q_new

            advance(
                chunk,
                lambda r: level_ref[step - 1, 0, start + r],
                lambda r: level_ref[step - 1, 1, start + r],
                prior(0),
                prior(1),
                lambda r: [coef_ref[i, start + r] for i in range(5)],
                put,
            )

    for step in range(STEPS):
        for field in range(2):
            for near in range(2):
                edge_ref[0, field, step, near] = level_ref[step, field, step + near]
                edge_ref[1, field, step, near] = level_ref[step, field, width - 1 - step - near]

    for step in range(1, STEPS + 1):
        low, high = step, width - step
        if step < STEPS:
            values = level_ref[step, 0, low:high]
        else:
            values = p_inner_ref[...]
        found = sample_rows(values.reshape((high - low) * shots, depth), depth_hot_ref[...])
        total = jnp.zeros((shots, targets), jnp.float32)
        for r in range(high - low):
            total = total + jnp.where(column == low + r, found[r * shots : (r + 1) * shots], 0.0)
        sample_ref[step - 1] = total


def interior(fields, params, target_cells, patch_lists):
    shots = fields[0].shape[0]
    width, depth = params[0].shape
    targets = target_cells.shape[0]
    _, owners, slots, patch = patch_lists.shape
    f32 = functools.partial(jax.ShapeDtypeStruct, dtype=jnp.float32)
    out_shape = [
        f32((2, 2, STEPS, 2, shots, depth)),
        f32((2, 2, shots, depth)),
        f32((2, 5, 8, depth)),
        f32((width - 2 * STEPS, shots, depth)),
        f32((width - 2 * STEPS, shots, depth)),
        f32((STEPS, shots, targets)),
        jax.ShapeDtypeStruct((2 * depth, targets), jnp.bfloat16),
        jax.ShapeDtypeStruct((1, targets), jnp.int32),
        jax.ShapeDtypeStruct((owners * slots * patch, targets), jnp.bfloat16),
    ]
    vmem = pl.BlockSpec(memory_space=pltpu.VMEM)
    return pl.pallas_call(
        interior_kernel,
        in_specs=[vmem] * 10,
        out_specs=[vmem] * len(out_shape),
        out_shape=out_shape,
        scratch_shapes=[
            pltpu.VMEM((STEPS, 2, width, shots, depth), jnp.float32),
            pltpu.VMEM((5, width, shots, depth), jnp.float32),
        ],
        compiler_params=compiler_params(40),
        cost_estimate=pl.CostEstimate(
            flops=200 * STEPS * shots * width * depth, bytes_accessed=8 * MIB, transcendentals=0
        ),
        name="interior",
    )(*fields, *params, target_cells.reshape(1, targets), patch_lists)


def finish_kernel(
    lower_ref,
    upper_ref,
    edge_ref,
    prior_edge_ref,
    coef_edge_ref,
    sample_ref,
    depth_hot_ref,
    column_ref,
    list_hot_ref,
    spectra_ref,
    table_ref,
    spectra_out_ref,
    packed_ref,
    final_ref,
    level_ref,
    prior_ref,
    coef_ref,
    feature_ref,
    *,
    width,
):
    shots, depth = edge_ref.shape[-2:]
    targets = column_ref.shape[1]
    first = -STEPS
    pair = 2 * shots
    for side, ref in enumerate((lower_ref, upper_ref)):
        for field in range(4):
            both = ref[pl.ds(field * pair, pair), :].astype(jnp.float32)
            value = both[:shots] + both[shots:]
            if field < 2:
                level_ref[side, field, 0, -1 - first] = value
            else:
                prior_ref[side, field - 2, -1 - (1 - STEPS)] = value
        for index, items in enumerate(far_items()):
            both = ref[pl.ds((4 + index) * pair, pair), :].astype(jnp.float32)
            for half, (field, distance) in enumerate(items):
                value = both[half * shots : (half + 1) * shots]
                if field < 2:
                    level_ref[side, field, 0, -1 - distance - first] = value
                else:
                    prior_ref[side, field - 2, -1 - distance - (1 - STEPS)] = value
        params = ref[pl.ds((4 + len(far_items())) * pair, pair), :].astype(jnp.float32)
        for index in range(5):
            for distance in range(STEPS - 1):
                line = index * (STEPS - 1) + distance
                row = params[line : line + 1, :]
                if index == 1 and side == 1:
                    row = -row
                coef_ref[side, index, STEPS - 2 - distance] = jnp.broadcast_to(row, (shots, depth))
            for k in range(STEPS):
                coef_ref[side, index, STEPS - 1 + k] = jnp.broadcast_to(
                    coef_edge_ref[side, index, pl.ds(k if side == 0 else 7 - k, 1), :],
                    (shots, depth),
                )
        for field in range(2):
            prior_ref[side, field, STEPS - 1] = prior_edge_ref[side, field]
            for step in range(STEPS):
                for near in range(2):
                    level_ref[side, field, step, step + near - first] = edge_ref[
                        side, field, step, near
                    ]

    for step in range(1, STEPS + 1):
        low = step - STEPS

        for side in range(2):

            def prior(field):
                if step == 1:
                    return lambda r: prior_ref[side, field, low + r - (1 - STEPS)]
                return lambda r: level_ref[side, field, step - 2, low + r - first]

            def put(r, p_new, q_new):
                if step < STEPS:
                    level_ref[side, 0, step, low + r - first] = p_new
                    level_ref[side, 1, step, low + r - first] = q_new
                else:
                    final_ref[side, 0, r] = p_new
                    final_ref[side, 1, r] = q_new

            advance(
                STEPS,
                lambda r: level_ref[side, 0, step - 1, low + r - first],
                lambda r: level_ref[side, 1, step - 1, low + r - first],
                prior(0),
                prior(1),
                lambda r: [coef_ref[side, i, low + r - (1 - STEPS) + 0] for i in range(5)],
                put,
            )

    column = column_ref[...]
    places, values = [], []
    for step in range(1, STEPS + 1):
        for side in range(2):
            for k in range(step):
                places.append((step, k if side == 0 else width - 1 - k))
                if step < STEPS:
                    values.append(level_ref[side, 0, step, k - first])
                else:
                    values.append(final_ref[side, 0, k])
    found = sample_rows(jnp.concatenate(values, 0), depth_hot_ref[...])
    samples = [sample_ref[step] for step in range(STEPS)]
    for index, (step, x) in enumerate(places):
        samples[step - 1] = samples[step - 1] + jnp.where(
            column == x, found[index * shots : (index + 1) * shots], 0.0
        )

    parts = spectra_ref.shape[0] // shots
    lanes = table_ref.shape[-1]
    for s in range(shots):
        for base in range(0, targets, lanes):
            value = spectra_ref[pl.ds(s * parts, parts), pl.ds(base, lanes)]
            for step in range(STEPS):
                value = value + table_ref[step] * samples[step][s : s + 1, base : base + lanes]
            spectra_out_ref[pl.ds(s * parts, parts), pl.ds(base, lanes)] = value
            feature_ref[pl.ds(s * parts, parts), pl.ds(base, lanes)] = value.astype(jnp.bfloat16)

    owners = packed_ref.shape[0]
    patch = packed_ref.shape[2]
    slots = list_hot_ref.shape[0] // (owners * patch)
    half = patch // 2
    row = lax.broadcasted_iota(jnp.int32, (half, patch), 0)
    lane = lax.broadcasted_iota(jnp.int32, (half, patch), 1)
    from_last = (lane < half) & (row > lane)
    for g in range(owners):
        chosen = lax.dot_general(
            list_hot_ref[pl.ds(g * slots * patch, slots * patch), :],
            feature_ref[...],
            NT,
            preferred_element_type=jnp.float32,
        ).astype(jnp.bfloat16)
        diagonals = []
        for s in range(slots):
            mine = chosen[s * patch : (s + 1) * patch]
            gram = lax.dot_general(mine, mine, NT, preferred_element_type=jnp.float32)
            last = pltpu.roll(gram[half:], half, 1)
            packed_ref[g, pl.ds(s * half, half), :] = jnp.where(from_last, last, gram[:half])
            diagonals.append(jnp.sum(jnp.where(row == lane, last, 0.0), 0, keepdims=True))
        while len(diagonals) % 8:
            diagonals.append(jnp.zeros((1, patch), jnp.float32))
        packed_ref[g, pl.ds(slots * half, len(diagonals)), :] = jnp.concatenate(diagonals, 0)


def finish(lower, upper, inner, spectra, table, width, owners, slots, patch):
    edge, prior_edge, coef_edge, sample, depth_hot, column, list_hot = inner
    shots, depth = edge.shape[-2:]
    targets = column.shape[1]
    features = spectra.shape[0]
    f32 = functools.partial(jax.ShapeDtypeStruct, dtype=jnp.float32)
    rows = slots * (patch // 2) + -(-slots // 8) * 8
    out_shape = [
        f32((features, targets)),
        f32((owners, rows, patch)),
        f32((2, 2, STEPS, shots, depth)),
    ]
    vmem = pl.BlockSpec(memory_space=pltpu.VMEM)
    return pl.pallas_call(
        functools.partial(finish_kernel, width=width),
        in_specs=[vmem] * 11,
        out_specs=[vmem] * len(out_shape),
        out_shape=out_shape,
        scratch_shapes=[
            pltpu.VMEM((2, 2, STEPS, 2 * STEPS + 1, shots, depth), jnp.float32),
            pltpu.VMEM((2, 2, STEPS, shots, depth), jnp.float32),
            pltpu.VMEM((2, 5, 2 * STEPS - 1, shots, depth), jnp.float32),
            pltpu.VMEM((features, targets), jnp.bfloat16),
        ],
        compiler_params=compiler_params(40),
        name="finish",
    )(
        lower,
        upper,
        edge,
        prior_edge,
        coef_edge,
        sample,
        depth_hot,
        column,
        list_hot,
        spectra,
        table,
    )


def assemble_kernel(p_inner_ref, q_inner_ref, final_ref, p_out_ref, q_out_ref):
    width = p_out_ref.shape[1] * TILE
    for field, (inner, out) in enumerate(((p_inner_ref, p_out_ref), (q_inner_ref, q_out_ref))):
        rows = ShotRows(out)
        for k in range(STEPS):
            rows[k] = final_ref[0, field, k]
            rows[width - 1 - k] = final_ref[1, field, k]

        @pl.loop(STEPS, width - STEPS, unroll=4)
        def _(x):
            rows[x] = inner[x - STEPS]


def assemble(p_inner, q_inner, final):
    inner, shots, depth = p_inner.shape
    across, along = (inner + 2 * STEPS) // TILE, depth // LANES
    shape = jax.ShapeDtypeStruct((shots, across, along, TILE, LANES), jnp.float32)
    vmem = pl.BlockSpec(memory_space=pltpu.VMEM)
    return pl.pallas_call(
        assemble_kernel,
        in_specs=[vmem] * 3,
        out_specs=[vmem] * 2,
        out_shape=[shape, shape],
        compiler_params=compiler_params(16),
        cost_estimate=pl.CostEstimate(flops=8 * MIB, bytes_accessed=4 * MIB, transcendentals=0),
        name="assemble",
    )(p_inner, q_inner, final)


def tiles_kernel(received_ref, counts_ref, out_ref, *, features):
    groups = received_ref.shape[0]
    slots, patch = out_ref.shape[2], out_ref.shape[3]
    half = patch // 2
    row = lax.broadcasted_iota(jnp.int32, (half, patch), 0)
    lane = lax.broadcasted_iota(jnp.int32, (half, patch), 1)
    live = counts_ref[0, 0]
    total = received_ref[0]
    for g in range(1, groups):
        total = total + received_ref[g]
    for s in range(slots):
        scale = jnp.where(s < live, 1.0 / features, 0.0)
        packed = total[s * half : (s + 1) * half] * scale
        diagonal = total[slots * half + s : slots * half + s + 1] * scale
        turned = jnp.transpose(jnp.concatenate([packed, packed], 0))
        flipped = turned[:half]
        corner = turned[half:]
        out_ref[0, 0, s, pl.ds(0, half), :] = jnp.where(
            (lane < half) & (row > lane), flipped, packed
        )
        last = jnp.where(row > lane, packed, jnp.where(row == lane, diagonal, flipped))
        out_ref[0, 0, s, pl.ds(half, half), :] = jnp.where(
            lane < half, corner, pltpu.roll(last, half, 1)
        )


def tiles(received, patch_counts, slots, features):
    patch = received.shape[2]
    return pl.pallas_call(
        functools.partial(tiles_kernel, features=features),
        in_specs=[
            pl.BlockSpec(memory_space=pltpu.VMEM),
            pl.BlockSpec(memory_space=pltpu.SMEM),
        ],
        out_specs=pl.BlockSpec(memory_space=pltpu.VMEM),
        out_shape=jax.ShapeDtypeStruct((1, 1, slots, patch, patch), jnp.float32),
        compiler_params=compiler_params(16),
        name="tiles",
    )(received, patch_counts)


def shards(
    pressure,
    auxiliary,
    pressure_prior,
    auxiliary_prior,
    courant_sq,
    thomsen_epsilon,
    thomsen_delta,
    tilt_angle,
    frequencies,
    spectra,
    target_cells,
    patch_lists,
    patch_counts,
):
    shots, width, depth = pressure.shape
    _, owners, slots, patch = patch_lists.shape
    fields = [tiled(item) for item in (pressure, auxiliary, pressure_prior, auxiliary_prior)]
    params = (courant_sq, thomsen_epsilon, thomsen_delta, tilt_angle)
    parts, targets = spectra.shape[1:]

    first_rows, last_rows = outer_rows(fields, params)
    bricks = lax.axis_size("brick")
    upward = [(i, i + 1) for i in range(bricks - 1)]
    downward = [(i + 1, i) for i in range(bricks - 1)]
    lower = lax.ppermute(last_rows, "brick", upward)
    upper = lax.ppermute(first_rows, "brick", downward)

    moments = jnp.arange(1, STEPS + 1, dtype=jnp.float32)
    angle = frequencies[None, :] * moments[:, None]
    table = jnp.concatenate([jnp.cos(angle), -jnp.sin(angle)], 1)
    table = jnp.broadcast_to(table[:, :, None], (STEPS, parts, 128))

    edge, prior_edge, coef_edge, p_inner, q_inner, sample, depth_hot, column, list_hot = interior(
        fields, params, target_cells, patch_lists
    )
    spectra_out, packed, final = finish(
        lower,
        upper,
        (edge, prior_edge, coef_edge, sample, depth_hot, column, list_hot),
        spectra.reshape(shots * parts, targets),
        table,
        width,
        owners,
        slots,
        patch,
    )
    received = lax.all_to_all(packed, "shot", split_axis=0, concat_axis=0, tiled=True)
    pressure_out, auxiliary_out = [untiled(item) for item in assemble(p_inner, q_inner, final)]
    gram_tiles = tiles(received, patch_counts, slots, shots * parts * owners)
    return (pressure_out, auxiliary_out, spectra_out.reshape(spectra.shape), gram_tiles)


def solution(mesh):
    return jax.shard_map(
        shards,
        mesh=mesh,
        in_specs=(
            P("shot", "brick", None),
            P("shot", "brick", None),
            P("shot", "brick", None),
            P("shot", "brick", None),
            P("brick", None),
            P("brick", None),
            P("brick", None),
            P("brick", None),
            P(),
            P("shot", None, "brick"),
            P("brick"),
            P("brick", None, None, None),
            P("brick", "shot"),
        ),
        out_specs=(
            P("shot", "brick", None),
            P("shot", "brick", None),
            P("shot", None, "brick"),
            P("brick", "shot", None, None, None),
        ),
        check_vma=False,
    )
```

```python
import functools
import math

import jax
import jax.numpy as jnp
from jax import lax
from jax.experimental import pallas as pl
from jax.experimental.pallas import tpu as pltpu
from jax.sharding import PartitionSpec as P

STEPS = 4
MIB = 1024 * 1024
NT = (((1,), (1,)), ((), ()))


TILE = 8
LANES = 128


def tiled(field):
    shots, width, depth = field.shape
    parts = field.reshape(shots, width // TILE, TILE, depth // LANES, LANES)
    return parts.transpose(0, 1, 3, 2, 4)


def untiled(parts):
    shots, across, along, tile, lanes = parts.shape
    return parts.transpose(0, 1, 3, 2, 4).reshape(shots, across * tile, along * lanes)


class ShotRows:
    def __init__(self, ref):
        self.shots, self.across, self.along, tile, lanes = ref.shape
        self.stride = self.across * self.along * tile
        self.flat = ref.reshape(self.shots * self.stride, lanes)

    def place(self, x, j):
        if isinstance(x, int):
            start = (x // TILE * self.along + j) * TILE + x % TILE
        else:
            start = (lax.div(x, TILE) * self.along + j) * TILE + lax.rem(x, TILE)
        return pl.ds(start, self.shots, stride=self.stride)

    def __getitem__(self, x):
        return jnp.concatenate([self.flat[self.place(x, j), :] for j in range(self.along)], 1)

    def __setitem__(self, x, row):
        for j in range(self.along):
            self.flat[self.place(x, j), :] = row[:, j * LANES : (j + 1) * LANES]


def compiler_params(mib):
    return pltpu.CompilerParams(vmem_limit_bytes=mib * MIB)


def tilt_coefficients(courant, epsilon, delta, tilt):
    turns = jnp.round(tilt * (2.0 / math.pi))
    rest = (tilt - turns * 1.5703125) - turns * (math.pi / 2 - 1.5703125)
    odd = turns - 2.0 * jnp.floor(turns * 0.5)
    sign = 1.0 - 2.0 * odd
    double = 2.0 * rest
    square = double * double
    sine = double * (
        1.0
        + square
        * (
            -1.0 / 6
            + square
            * (1.0 / 120 + square * (-1.0 / 5040 + square * (1.0 / 362880 - square / 39916800.0)))
        )
    )
    versine = square * (
        0.5
        + square
        * (
            -1.0 / 24
            + square
            * (1.0 / 720 + square * (-1.0 / 40320 + square * (1.0 / 3628800 - square / 479001600.0)))
        )
    )
    sine_sq = jnp.where(odd > 0.5, 1.0 - 0.5 * versine, 0.5 * versine)
    quarter_sin = 0.25 * sign * sine
    gain_p = courant * (1.0 + 2.0 * epsilon)
    gain_q = courant * (1.0 + 2.0 * delta)
    return sine_sq, quarter_sin, courant, gain_p, gain_q


def depth_terms(row):
    depth = row.shape[-1]
    lane = lax.broadcasted_iota(jnp.int32, row.shape, 1)
    deeper = jnp.where(lane < depth - 1, pltpu.roll(row, depth - 1, 1), 0.0)
    upper = jnp.where(lane > 0, pltpu.roll(row, 1, 1), 0.0)
    return deeper + upper, deeper - upper


def advance(count, p_row, q_row, p_prior, q_prior, coefficient, put):
    p_back, p_here = p_row(-1), p_row(0)
    q_back, q_here = q_row(-1), q_row(0)
    _, p_back_d = depth_terms(p_back)
    _, q_back_d = depth_terms(q_back)
    p_sum, p_here_d = depth_terms(p_here)
    q_sum, q_here_d = depth_terms(q_here)
    for row in range(count):
        p_next, q_next = p_row(row + 1), q_row(row + 1)
        p_next_sum, p_next_d = depth_terms(p_next)
        q_next_sum, q_next_d = depth_terms(q_next)
        sine_sq, quarter_sin, courant, gain_p, gain_q = coefficient(row)
        twice_p, twice_q = p_here + p_here, q_here + q_here
        side = p_next + p_back
        across = (side - twice_p) + sine_sq * (p_sum - side) - quarter_sin * (p_next_d - p_back_d)
        side = q_next + q_back
        along = (q_sum - twice_q) + sine_sq * (side - q_sum) + quarter_sin * (q_next_d - q_back_d)
        along = courant * along
        put(
            row,
            (twice_p - p_prior(row)) + (gain_p * across + along),
            (twice_q - q_prior(row)) + (gain_q * across + along),
        )
        p_back, p_here, p_back_d, p_here_d, p_sum = p_here, p_next, p_here_d, p_next_d, p_next_sum
        q_back, q_here, q_back_d, q_here_d, q_sum = q_here, q_next, q_here_d, q_next_d, q_next_sum


def split_bf16(values):
    high = values.astype(jnp.bfloat16)
    low = (values - high.astype(jnp.float32)).astype(jnp.bfloat16)
    return high, low


def outer_kernel(*refs):
    sources, outs, (field_ref, param_ref, field_sem, param_sem) = refs[:8], refs[8:10], refs[10:]
    shots, across, along, tile, lanes = sources[0].shape
    depth = along * lanes
    copies = []
    for side in range(2):
        place = side * (across - 1)
        for i in range(4):
            copies.append(
                pltpu.make_async_copy(
                    sources[i].at[:, pl.ds(place, 1)], field_ref.at[side, i], field_sem.at[side, i]
                )
            )
        for i in range(4):
            copies.append(
                pltpu.make_async_copy(
                    sources[4 + i].at[pl.ds(place * tile, tile)],
                    param_ref.at[side, i],
                    param_sem.at[side, i],
                )
            )
    for copy in copies:
        copy.start()
    for side in range(2):
        for copy in copies[8 * side : 8 * side + 8]:
            copy.wait()
        views = [ShotRows(field_ref.at[side, i]) for i in range(4)]
        out = outs[side]

        def row(field, distance):
            place = distance if side == 0 else tile - 1 - distance
            return views[field][place]

        position = 0

        def put(first, second):
            nonlocal position
            out[pl.ds(position, 2 * shots), :] = jnp.concatenate([first, second], 0).astype(
                jnp.bfloat16
            )
            position += 2 * shots

        for field in range(4):
            near = row(field, 0)
            put(near, near - near.astype(jnp.bfloat16).astype(jnp.float32))
        for first, second in far_items():
            put(row(*first), row(*second))
        terms = tilt_coefficients(*[param_ref[side, i] for i in range(4)])
        rows = []
        for term in terms:
            for distance in range(STEPS - 1):
                place = distance if side == 0 else tile - 1 - distance
                rows.append(term[place : place + 1, :])
        while len(rows) < 2 * shots:
            rows.append(jnp.zeros((1, depth), jnp.float32))
        out[pl.ds(position, 2 * shots), :] = jnp.concatenate(rows, 0).astype(jnp.bfloat16)


def far_items():
    items = []
    for field in range(2):
        items += [(field, distance) for distance in range(1, STEPS)]
    for field in range(2, 4):
        items += [(field, distance) for distance in range(1, STEPS - 1)]
    return list(zip(items[0::2], items[1::2]))


def outer_rows(fields, params):
    shots, across, along, tile, lanes = fields[0].shape
    depth = along * lanes
    rows = 2 * shots * (4 + len(far_items()) + 1)
    shape = jax.ShapeDtypeStruct((rows, depth), jnp.bfloat16)
    return pl.pallas_call(
        outer_kernel,
        in_specs=[pl.BlockSpec(memory_space=pltpu.HBM)] * 8,
        out_specs=[pl.BlockSpec(memory_space=pltpu.VMEM)] * 2,
        out_shape=[shape, shape],
        scratch_shapes=[
            pltpu.VMEM((2, 4, shots, 1, along, tile, lanes), jnp.float32),
            pltpu.VMEM((2, 4, tile, depth), jnp.float32),
            pltpu.SemaphoreType.DMA((2, 4)),
            pltpu.SemaphoreType.DMA((2, 4)),
        ],
        compiler_params=compiler_params(60),
        name="outer_rows",
    )(*fields, *params)


def sample_rows(values, one_hot):
    high, low = split_bf16(values)
    return jnp.dot(jnp.concatenate([high, low], 1), one_hot, preferred_element_type=jnp.float32)


def interior_kernel(
    p_ref,
    q_ref,
    pp_ref,
    qq_ref,
    courant_ref,
    epsilon_ref,
    delta_ref,
    tilt_ref,
    cells_ref,
    lists_ref,
    edge_ref,
    prior_edge_ref,
    coef_edge_ref,
    p_inner_ref,
    q_inner_ref,
    sample_ref,
    depth_hot_ref,
    column_ref,
    list_hot_ref,
    level_ref,
    coef_ref,
):
    shots = p_ref.shape[0]
    width, depth = courant_ref.shape
    p_rows, q_rows, pp_rows, qq_rows = [ShotRows(ref) for ref in (p_ref, q_ref, pp_ref, qq_ref)]

    terms = tilt_coefficients(courant_ref[...], epsilon_ref[...], delta_ref[...], tilt_ref[...])
    for index, term in enumerate(terms):
        for x in range(width):
            coef_ref[index, x] = jnp.broadcast_to(term[x : x + 1, :], (shots, depth))
        flip = -term if index == 1 else term
        coef_edge_ref[0, index] = term[:8, :]
        coef_edge_ref[1, index] = flip[width - 8 :, :]

    @pl.loop(0, width)
    def _(x):
        level_ref[0, 0, x] = p_rows[x]
        level_ref[0, 1, x] = q_rows[x]

    cells = cells_ref[...]
    column = cells // depth
    z_of = cells - column * depth
    column_ref[...] = column
    targets = cells.shape[1]
    for half in range(2):
        for base in range(0, depth, 64):
            lanes = lax.broadcasted_iota(jnp.int32, (64, targets), 0) + base
            depth_hot_ref[pl.ds(half * depth + base, 64), :] = jnp.where(
                lanes == z_of, 1.0, 0.0
            ).astype(jnp.bfloat16)

    owners, slots, patch = lists_ref.shape[1:]
    rows = [lists_ref[0, g, s : s + 1, :] for g in range(owners) for s in range(slots)]
    count = len(rows)
    while len(rows) % 8:
        rows.append(rows[0])
    upright = jnp.transpose(jnp.concatenate(rows, 0).astype(jnp.float32))
    lanes = lax.broadcasted_iota(jnp.int32, (patch, targets), 1).astype(jnp.float32)
    for k in range(count):
        list_hot_ref[pl.ds(k * patch, patch), :] = jnp.where(
            upright[:, k : k + 1] == lanes, 1.0, 0.0
        ).astype(jnp.bfloat16)

    for side in range(2):
        x = 0 if side == 0 else width - 1
        prior_edge_ref[side, 0] = pp_rows[x]
        prior_edge_ref[side, 1] = qq_rows[x]

    chunk = 8
    for step in range(1, STEPS + 1):
        low, high = step, width - step
        chunks = -(-(high - low) // chunk)

        @pl.loop(0, chunks)
        def _(index):
            start = jnp.minimum(low + chunk * index, high - chunk)

            def prior(field):
                if step == 1:
                    rows = (pp_rows, qq_rows)[field]
                    return lambda r: rows[start + r]
                return lambda r: level_ref[step - 2, field, start + r]

            def put(r, p_new, q_new):
                if step < STEPS:
                    level_ref[step, 0, start + r] = p_new
                    level_ref[step, 1, start + r] = q_new
                else:
                    p_inner_ref[start + r - STEPS] = p_new
                    q_inner_ref[start + r - STEPS] = q_new

            advance(
                chunk,
                lambda r: level_ref[step - 1, 0, start + r],
                lambda r: level_ref[step - 1, 1, start + r],
                prior(0),
                prior(1),
                lambda r: [coef_ref[i, start + r] for i in range(5)],
                put,
            )

    for step in range(STEPS):
        for field in range(2):
            for near in range(2):
                edge_ref[0, field, step, near] = level_ref[step, field, step + near]
                edge_ref[1, field, step, near] = level_ref[step, field, width - 1 - step - near]

    for step in range(1, STEPS + 1):
        low, high = step, width - step
        if step < STEPS:
            values = level_ref[step, 0, low:high]
        else:
            values = p_inner_ref[...]
        found = sample_rows(values.reshape((high - low) * shots, depth), depth_hot_ref[...])
        total = jnp.zeros((shots, targets), jnp.float32)
        for r in range(high - low):
            total = total + jnp.where(column == low + r, found[r * shots : (r + 1) * shots], 0.0)
        sample_ref[step - 1] = total


def interior(fields, params, target_cells, patch_lists):
    shots = fields[0].shape[0]
    width, depth = params[0].shape
    targets = target_cells.shape[0]
    _, owners, slots, patch = patch_lists.shape
    f32 = functools.partial(jax.ShapeDtypeStruct, dtype=jnp.float32)
    out_shape = [
        f32((2, 2, STEPS, 2, shots, depth)),
        f32((2, 2, shots, depth)),
        f32((2, 5, 8, depth)),
        f32((width - 2 * STEPS, shots, depth)),
        f32((width - 2 * STEPS, shots, depth)),
        f32((STEPS, shots, targets)),
        jax.ShapeDtypeStruct((2 * depth, targets), jnp.bfloat16),
        jax.ShapeDtypeStruct((1, targets), jnp.int32),
        jax.ShapeDtypeStruct((owners * slots * patch, targets), jnp.bfloat16),
    ]
    vmem = pl.BlockSpec(memory_space=pltpu.VMEM)
    return pl.pallas_call(
        interior_kernel,
        in_specs=[vmem] * 10,
        out_specs=[vmem] * len(out_shape),
        out_shape=out_shape,
        scratch_shapes=[
            pltpu.VMEM((STEPS, 2, width, shots, depth), jnp.float32),
            pltpu.VMEM((5, width, shots, depth), jnp.float32),
        ],
        compiler_params=compiler_params(40),
        cost_estimate=pl.CostEstimate(
            flops=200 * STEPS * shots * width * depth, bytes_accessed=8 * MIB, transcendentals=0
        ),
        name="interior",
    )(*fields, *params, target_cells.reshape(1, targets), patch_lists)


def finish_kernel(
    lower_ref,
    upper_ref,
    edge_ref,
    prior_edge_ref,
    coef_edge_ref,
    sample_ref,
    depth_hot_ref,
    column_ref,
    list_hot_ref,
    spectra_ref,
    table_ref,
    spectra_out_ref,
    packed_ref,
    final_ref,
    level_ref,
    prior_ref,
    coef_ref,
    feature_ref,
    *,
    width,
):
    shots, depth = edge_ref.shape[-2:]
    targets = column_ref.shape[1]
    first = -STEPS
    pair = 2 * shots
    for side, ref in enumerate((lower_ref, upper_ref)):
        for field in range(4):
            both = ref[pl.ds(field * pair, pair), :].astype(jnp.float32)
            value = both[:shots] + both[shots:]
            if field < 2:
                level_ref[side, field, 0, -1 - first] = value
            else:
                prior_ref[side, field - 2, -1 - (1 - STEPS)] = value
        for index, items in enumerate(far_items()):
            both = ref[pl.ds((4 + index) * pair, pair), :].astype(jnp.float32)
            for half, (field, distance) in enumerate(items):
                value = both[half * shots : (half + 1) * shots]
                if field < 2:
                    level_ref[side, field, 0, -1 - distance - first] = value
                else:
                    prior_ref[side, field - 2, -1 - distance - (1 - STEPS)] = value
        params = ref[pl.ds((4 + len(far_items())) * pair, pair), :].astype(jnp.float32)
        for index in range(5):
            for distance in range(STEPS - 1):
                line = index * (STEPS - 1) + distance
                row = params[line : line + 1, :]
                if index == 1 and side == 1:
                    row = -row
                coef_ref[side, index, STEPS - 2 - distance] = jnp.broadcast_to(row, (shots, depth))
            for k in range(STEPS):
                coef_ref[side, index, STEPS - 1 + k] = jnp.broadcast_to(
                    coef_edge_ref[side, index, pl.ds(k if side == 0 else 7 - k, 1), :],
                    (shots, depth),
                )
        for field in range(2):
            prior_ref[side, field, STEPS - 1] = prior_edge_ref[side, field]
            for step in range(STEPS):
                for near in range(2):
                    level_ref[side, field, step, step + near - first] = edge_ref[
                        side, field, step, near
                    ]

    for step in range(1, STEPS + 1):
        low = step - STEPS

        for side in range(2):

            def prior(field):
                if step == 1:
                    return lambda r: prior_ref[side, field, low + r - (1 - STEPS)]
                return lambda r: level_ref[side, field, step - 2, low + r - first]

            def put(r, p_new, q_new):
                if step < STEPS:
                    level_ref[side, 0, step, low + r - first] = p_new
                    level_ref[side, 1, step, low + r - first] = q_new
                else:
                    final_ref[side, 0, r] = p_new
                    final_ref[side, 1, r] = q_new

            advance(
                STEPS,
                lambda r: level_ref[side, 0, step - 1, low + r - first],
                lambda r: level_ref[side, 1, step - 1, low + r - first],
                prior(0),
                prior(1),
                lambda r: [coef_ref[side, i, low + r - (1 - STEPS) + 0] for i in range(5)],
                put,
            )

    column = column_ref[...]
    places, values = [], []
    for step in range(1, STEPS + 1):
        for side in range(2):
            for k in range(step):
                places.append((step, k if side == 0 else width - 1 - k))
                if step < STEPS:
                    values.append(level_ref[side, 0, step, k - first])
                else:
                    values.append(final_ref[side, 0, k])
    found = sample_rows(jnp.concatenate(values, 0), depth_hot_ref[...])
    samples = [sample_ref[step] for step in range(STEPS)]
    for index, (step, x) in enumerate(places):
        samples[step - 1] = samples[step - 1] + jnp.where(
            column == x, found[index * shots : (index + 1) * shots], 0.0
        )

    parts = spectra_ref.shape[0] // shots
    lanes = table_ref.shape[-1]
    for s in range(shots):
        for base in range(0, targets, lanes):
            value = spectra_ref[pl.ds(s * parts, parts), pl.ds(base, lanes)]
            for step in range(STEPS):
                value = value + table_ref[step] * samples[step][s : s + 1, base : base + lanes]
            spectra_out_ref[pl.ds(s * parts, parts), pl.ds(base, lanes)] = value
            feature_ref[pl.ds(s * parts, parts), pl.ds(base, lanes)] = value.astype(jnp.bfloat16)

    owners = packed_ref.shape[0]
    patch = packed_ref.shape[2]
    slots = list_hot_ref.shape[0] // (owners * patch)
    half = patch // 2
    row = lax.broadcasted_iota(jnp.int32, (half, patch), 0)
    lane = lax.broadcasted_iota(jnp.int32, (half, patch), 1)
    from_last = (lane < half) & (row > lane)
    for g in range(owners):
        chosen = lax.dot_general(
            list_hot_ref[pl.ds(g * slots * patch, slots * patch), :],
            feature_ref[...],
            NT,
            preferred_element_type=jnp.float32,
        ).astype(jnp.bfloat16)
        diagonals = []
        for s in range(slots):
            mine = chosen[s * patch : (s + 1) * patch]
            gram = lax.dot_general(mine, mine, NT, preferred_element_type=jnp.float32)
            last = pltpu.roll(gram[half:], half, 1)
            packed_ref[g, pl.ds(s * half, half), :] = jnp.where(from_last, last, gram[:half])
            diagonals.append(jnp.sum(jnp.where(row == lane, last, 0.0), 0, keepdims=True))
        while len(diagonals) % 8:
            diagonals.append(jnp.zeros((1, patch), jnp.float32))
        packed_ref[g, pl.ds(slots * half, len(diagonals)), :] = jnp.concatenate(diagonals, 0)


def finish(lower, upper, inner, spectra, table, width, owners, slots, patch):
    edge, prior_edge, coef_edge, sample, depth_hot, column, list_hot = inner
    shots, depth = edge.shape[-2:]
    targets = column.shape[1]
    features = spectra.shape[0]
    f32 = functools.partial(jax.ShapeDtypeStruct, dtype=jnp.float32)
    rows = slots * (patch // 2) + -(-slots // 8) * 8
    out_shape = [
        f32((features, targets)),
        f32((owners, rows, patch)),
        f32((2, 2, STEPS, shots, depth)),
    ]
    vmem = pl.BlockSpec(memory_space=pltpu.VMEM)
    return pl.pallas_call(
        functools.partial(finish_kernel, width=width),
        in_specs=[vmem] * 11,
        out_specs=[vmem] * len(out_shape),
        out_shape=out_shape,
        scratch_shapes=[
            pltpu.VMEM((2, 2, STEPS, 2 * STEPS + 1, shots, depth), jnp.float32),
            pltpu.VMEM((2, 2, STEPS, shots, depth), jnp.float32),
            pltpu.VMEM((2, 5, 2 * STEPS - 1, shots, depth), jnp.float32),
            pltpu.VMEM((features, targets), jnp.bfloat16),
        ],
        compiler_params=compiler_params(40),
        name="finish",
    )(
        lower,
        upper,
        edge,
        prior_edge,
        coef_edge,
        sample,
        depth_hot,
        column,
        list_hot,
        spectra,
        table,
    )


def assemble_kernel(p_inner_ref, q_inner_ref, final_ref, p_out_ref, q_out_ref):
    width = p_out_ref.shape[1] * TILE
    for field, (inner, out) in enumerate(((p_inner_ref, p_out_ref), (q_inner_ref, q_out_ref))):
        rows = ShotRows(out)
        for k in range(STEPS):
            rows[k] = final_ref[0, field, k]
            rows[width - 1 - k] = final_ref[1, field, k]

        @pl.loop(STEPS, width - STEPS, unroll=4)
        def _(x):
            rows[x] = inner[x - STEPS]


def assemble(p_inner, q_inner, final):
    inner, shots, depth = p_inner.shape
    across, along = (inner + 2 * STEPS) // TILE, depth // LANES
    shape = jax.ShapeDtypeStruct((shots, across, along, TILE, LANES), jnp.float32)
    vmem = pl.BlockSpec(memory_space=pltpu.VMEM)
    return pl.pallas_call(
        assemble_kernel,
        in_specs=[vmem] * 3,
        out_specs=[vmem] * 2,
        out_shape=[shape, shape],
        compiler_params=compiler_params(16),
        cost_estimate=pl.CostEstimate(flops=8 * MIB, bytes_accessed=4 * MIB, transcendentals=0),
        name="assemble",
    )(p_inner, q_inner, final)


def tiles_kernel(received_ref, counts_ref, out_ref, *, features):
    groups = received_ref.shape[0]
    slots, patch = out_ref.shape[2], out_ref.shape[3]
    half = patch // 2
    row = lax.broadcasted_iota(jnp.int32, (half, patch), 0)
    lane = lax.broadcasted_iota(jnp.int32, (half, patch), 1)
    live = counts_ref[0, 0]
    total = received_ref[0]
    for g in range(1, groups):
        total = total + received_ref[g]
    for s in range(slots):
        scale = jnp.where(s < live, 1.0 / features, 0.0)
        packed = total[s * half : (s + 1) * half] * scale
        diagonal = total[slots * half + s : slots * half + s + 1] * scale
        turned = jnp.transpose(jnp.concatenate([packed, packed], 0))
        flipped = turned[:half]
        corner = turned[half:]
        out_ref[0, 0, s, pl.ds(0, half), :] = jnp.where(
            (lane < half) & (row > lane), flipped, packed
        )
        last = jnp.where(row > lane, packed, jnp.where(row == lane, diagonal, flipped))
        out_ref[0, 0, s, pl.ds(half, half), :] = jnp.where(
            lane < half, corner, pltpu.roll(last, half, 1)
        )


def tiles(received, patch_counts, slots, features):
    patch = received.shape[2]
    return pl.pallas_call(
        functools.partial(tiles_kernel, features=features),
        in_specs=[
            pl.BlockSpec(memory_space=pltpu.VMEM),
            pl.BlockSpec(memory_space=pltpu.SMEM),
        ],
        out_specs=pl.BlockSpec(memory_space=pltpu.VMEM),
        out_shape=jax.ShapeDtypeStruct((1, 1, slots, patch, patch), jnp.float32),
        compiler_params=compiler_params(16),
        name="tiles",
    )(received, patch_counts)


def shards(
    pressure,
    auxiliary,
    pressure_prior,
    auxiliary_prior,
    courant_sq,
    thomsen_epsilon,
    thomsen_delta,
    tilt_angle,
    frequencies,
    spectra,
    target_cells,
    patch_lists,
    patch_counts,
):
    shots, width, depth = pressure.shape
    _, owners, slots, patch = patch_lists.shape
    fields = [tiled(item) for item in (pressure, auxiliary, pressure_prior, auxiliary_prior)]
    params = (courant_sq, thomsen_epsilon, thomsen_delta, tilt_angle)
    parts, targets = spectra.shape[1:]

    first_rows, last_rows = outer_rows(fields, params)
    bricks = lax.axis_size("brick")
    upward = [(i, i + 1) for i in range(bricks - 1)]
    downward = [(i + 1, i) for i in range(bricks - 1)]
    lower = lax.ppermute(last_rows, "brick", upward)
    upper = lax.ppermute(first_rows, "brick", downward)

    moments = jnp.arange(1, STEPS + 1, dtype=jnp.float32)
    angle = frequencies[None, :] * moments[:, None]
    table = jnp.concatenate([jnp.cos(angle), -jnp.sin(angle)], 1)
    table = jnp.broadcast_to(table[:, :, None], (STEPS, parts, 128))

    edge, prior_edge, coef_edge, p_inner, q_inner, sample, depth_hot, column, list_hot = interior(
        fields, params, target_cells, patch_lists
    )
    spectra_out, packed, final = finish(
        lower,
        upper,
        (edge, prior_edge, coef_edge, sample, depth_hot, column, list_hot),
        spectra.reshape(shots * parts, targets),
        table,
        width,
        owners,
        slots,
        patch,
    )
    received = lax.psum_scatter(packed, "shot", scatter_dimension=0, tiled=True)
    pressure_out, auxiliary_out = [untiled(item) for item in assemble(p_inner, q_inner, final)]
    gram_tiles = tiles(received, patch_counts, slots, shots * parts * owners)
    return (pressure_out, auxiliary_out, spectra_out.reshape(spectra.shape), gram_tiles)


def solution(mesh):
    return jax.shard_map(
        shards,
        mesh=mesh,
        in_specs=(
            P("shot", "brick", None),
            P("shot", "brick", None),
            P("shot", "brick", None),
            P("shot", "brick", None),
            P("brick", None),
            P("brick", None),
            P("brick", None),
            P("brick", None),
            P(),
            P("shot", None, "brick"),
            P("brick"),
            P("brick", None, None, None),
            P("brick", "shot"),
        ),
        out_specs=(
            P("shot", "brick", None),
            P("shot", "brick", None),
            P("shot", None, "brick"),
            P("brick", "shot", None, None, None),
        ),
        check_vma=False,
    )
```

```python
import functools
import math

import jax
import jax.numpy as jnp
from jax import lax
from jax.experimental import pallas as pl
from jax.experimental.pallas import tpu as pltpu
from jax.sharding import PartitionSpec as P

STEPS = 4
MIB = 1024 * 1024
NT = (((1,), (1,)), ((), ()))


TILE = 8
LANES = 128


def tiled(field):
    shots, width, depth = field.shape
    parts = field.reshape(shots, width // TILE, TILE, depth // LANES, LANES)
    return parts.transpose(0, 1, 3, 2, 4)


def untiled(parts):
    shots, across, along, tile, lanes = parts.shape
    return parts.transpose(0, 1, 3, 2, 4).reshape(shots, across * tile, along * lanes)


class ShotRows:
    def __init__(self, ref):
        self.shots, self.across, self.along, tile, lanes = ref.shape
        self.stride = self.across * self.along * tile
        self.flat = ref.reshape(self.shots * self.stride, lanes)

    def place(self, x, j):
        if isinstance(x, int):
            start = (x // TILE * self.along + j) * TILE + x % TILE
        else:
            start = (lax.div(x, TILE) * self.along + j) * TILE + lax.rem(x, TILE)
        return pl.ds(start, self.shots, stride=self.stride)

    def __getitem__(self, x):
        return jnp.concatenate([self.flat[self.place(x, j), :] for j in range(self.along)], 1)

    def __setitem__(self, x, row):
        for j in range(self.along):
            self.flat[self.place(x, j), :] = row[:, j * LANES : (j + 1) * LANES]


def compiler_params(mib):
    return pltpu.CompilerParams(vmem_limit_bytes=mib * MIB)


def tilt_coefficients(courant, epsilon, delta, tilt):
    turns = jnp.round(tilt * (2.0 / math.pi))
    rest = (tilt - turns * 1.5703125) - turns * (math.pi / 2 - 1.5703125)
    odd = turns - 2.0 * jnp.floor(turns * 0.5)
    sign = 1.0 - 2.0 * odd
    double = 2.0 * rest
    square = double * double
    sine = double * (
        1.0
        + square
        * (
            -1.0 / 6
            + square
            * (1.0 / 120 + square * (-1.0 / 5040 + square * (1.0 / 362880 - square / 39916800.0)))
        )
    )
    versine = square * (
        0.5
        + square
        * (
            -1.0 / 24
            + square
            * (1.0 / 720 + square * (-1.0 / 40320 + square * (1.0 / 3628800 - square / 479001600.0)))
        )
    )
    sine_sq = jnp.where(odd > 0.5, 1.0 - 0.5 * versine, 0.5 * versine)
    quarter_sin = 0.25 * sign * sine
    gain_p = courant * (1.0 + 2.0 * epsilon)
    gain_q = courant * (1.0 + 2.0 * delta)
    return sine_sq, quarter_sin, courant, gain_p, gain_q


def depth_terms(row):
    depth = row.shape[-1]
    lane = lax.broadcasted_iota(jnp.int32, row.shape, 1)
    deeper = jnp.where(lane < depth - 1, pltpu.roll(row, depth - 1, 1), 0.0)
    upper = jnp.where(lane > 0, pltpu.roll(row, 1, 1), 0.0)
    return deeper + upper, deeper - upper


def advance(count, p_row, q_row, p_prior, q_prior, coefficient, put):
    p_back, p_here = p_row(-1), p_row(0)
    q_back, q_here = q_row(-1), q_row(0)
    _, p_back_d = depth_terms(p_back)
    _, q_back_d = depth_terms(q_back)
    p_sum, p_here_d = depth_terms(p_here)
    q_sum, q_here_d = depth_terms(q_here)
    for row in range(count):
        p_next, q_next = p_row(row + 1), q_row(row + 1)
        p_next_sum, p_next_d = depth_terms(p_next)
        q_next_sum, q_next_d = depth_terms(q_next)
        sine_sq, quarter_sin, courant, gain_p, gain_q = coefficient(row)
        twice_p, twice_q = p_here + p_here, q_here + q_here
        side = p_next + p_back
        across = (side - twice_p) + sine_sq * (p_sum - side) - quarter_sin * (p_next_d - p_back_d)
        side = q_next + q_back
        along = (q_sum - twice_q) + sine_sq * (side - q_sum) + quarter_sin * (q_next_d - q_back_d)
        along = courant * along
        put(
            row,
            (twice_p - p_prior(row)) + (gain_p * across + along),
            (twice_q - q_prior(row)) + (gain_q * across + along),
        )
        p_back, p_here, p_back_d, p_here_d, p_sum = p_here, p_next, p_here_d, p_next_d, p_next_sum
        q_back, q_here, q_back_d, q_here_d, q_sum = q_here, q_next, q_here_d, q_next_d, q_next_sum


def split_bf16(values):
    high = values.astype(jnp.bfloat16)
    low = (values - high.astype(jnp.float32)).astype(jnp.bfloat16)
    return high, low


def outer_kernel(*refs):
    sources, outs, (field_ref, param_ref, field_sem, param_sem) = refs[:8], refs[8:10], refs[10:]
    shots, across, along, tile, lanes = sources[0].shape
    depth = along * lanes
    copies = []
    for side in range(2):
        place = side * (across - 1)
        for i in range(4):
            copies.append(
                pltpu.make_async_copy(
                    sources[i].at[:, pl.ds(place, 1)], field_ref.at[side, i], field_sem.at[side, i]
                )
            )
        for i in range(4):
            copies.append(
                pltpu.make_async_copy(
                    sources[4 + i].at[pl.ds(place * tile, tile)],
                    param_ref.at[side, i],
                    param_sem.at[side, i],
                )
            )
    for copy in copies:
        copy.start()
    for side in range(2):
        for copy in copies[8 * side : 8 * side + 8]:
            copy.wait()
        views = [ShotRows(field_ref.at[side, i]) for i in range(4)]
        out = outs[side]

        def row(field, distance):
            place = distance if side == 0 else tile - 1 - distance
            return views[field][place]

        position = 0

        def put(first, second):
            nonlocal position
            out[pl.ds(position, 2 * shots), :] = jnp.concatenate([first, second], 0).astype(
                jnp.bfloat16
            )
            position += 2 * shots

        for field in range(4):
            near = row(field, 0)
            put(near, near - near.astype(jnp.bfloat16).astype(jnp.float32))
        for first, second in far_items():
            put(row(*first), row(*second))
        terms = tilt_coefficients(*[param_ref[side, i] for i in range(4)])
        rows = []
        for term in terms:
            for distance in range(STEPS - 1):
                place = distance if side == 0 else tile - 1 - distance
                rows.append(term[place : place + 1, :])
        while len(rows) < 2 * shots:
            rows.append(jnp.zeros((1, depth), jnp.float32))
        out[pl.ds(position, 2 * shots), :] = jnp.concatenate(rows, 0).astype(jnp.bfloat16)


def far_items():
    items = []
    for field in range(2):
        items += [(field, distance) for distance in range(1, STEPS)]
    for field in range(2, 4):
        items += [(field, distance) for distance in range(1, STEPS - 1)]
    return list(zip(items[0::2], items[1::2]))


def outer_rows(fields, params):
    shots, across, along, tile, lanes = fields[0].shape
    depth = along * lanes
    rows = 2 * shots * (4 + len(far_items()) + 1)
    shape = jax.ShapeDtypeStruct((rows, depth), jnp.bfloat16)
    return pl.pallas_call(
        outer_kernel,
        in_specs=[pl.BlockSpec(memory_space=pltpu.HBM)] * 8,
        out_specs=[pl.BlockSpec(memory_space=pltpu.VMEM)] * 2,
        out_shape=[shape, shape],
        scratch_shapes=[
            pltpu.VMEM((2, 4, shots, 1, along, tile, lanes), jnp.float32),
            pltpu.VMEM((2, 4, tile, depth), jnp.float32),
            pltpu.SemaphoreType.DMA((2, 4)),
            pltpu.SemaphoreType.DMA((2, 4)),
        ],
        compiler_params=compiler_params(60),
        name="outer_rows",
    )(*fields, *params)


def partner(me, k, count):
    if count & (count - 1):
        return (me + k) % count
    return me ^ k


def sample_rows(values, one_hot):
    high, low = split_bf16(values)
    return jnp.dot(jnp.concatenate([high, low], 1), one_hot, preferred_element_type=jnp.float32)


def interior_kernel(
    p_ref,
    q_ref,
    pp_ref,
    qq_ref,
    courant_ref,
    epsilon_ref,
    delta_ref,
    tilt_ref,
    cells_ref,
    lists_ref,
    edge_ref,
    prior_edge_ref,
    coef_edge_ref,
    p_inner_ref,
    q_inner_ref,
    sample_ref,
    depth_hot_ref,
    column_ref,
    list_hot_ref,
    level_ref,
    coef_ref,
):
    shots = p_ref.shape[0]
    width, depth = courant_ref.shape
    p_rows, q_rows, pp_rows, qq_rows = [ShotRows(ref) for ref in (p_ref, q_ref, pp_ref, qq_ref)]

    terms = tilt_coefficients(courant_ref[...], epsilon_ref[...], delta_ref[...], tilt_ref[...])
    for index, term in enumerate(terms):
        for x in range(width):
            coef_ref[index, x] = jnp.broadcast_to(term[x : x + 1, :], (shots, depth))
        flip = -term if index == 1 else term
        coef_edge_ref[0, index] = term[:8, :]
        coef_edge_ref[1, index] = flip[width - 8 :, :]

    @pl.loop(0, width)
    def _(x):
        level_ref[0, 0, x] = p_rows[x]
        level_ref[0, 1, x] = q_rows[x]

    cells = cells_ref[...]
    column = cells // depth
    z_of = cells - column * depth
    column_ref[...] = column
    targets = cells.shape[1]
    for half in range(2):
        for base in range(0, depth, 64):
            lanes = lax.broadcasted_iota(jnp.int32, (64, targets), 0) + base
            depth_hot_ref[pl.ds(half * depth + base, 64), :] = jnp.where(
                lanes == z_of, 1.0, 0.0
            ).astype(jnp.bfloat16)

    owners, slots, patch = lists_ref.shape[1:]
    me = lax.axis_index("shot")
    rows = []
    for k in range(owners):
        lists = lists_ref[0, partner(me, k, owners)]
        rows += [lists[s : s + 1, :] for s in range(slots)]
    count = len(rows)
    while len(rows) % 8:
        rows.append(rows[0])
    upright = jnp.transpose(jnp.concatenate(rows, 0).astype(jnp.float32))
    lanes = lax.broadcasted_iota(jnp.int32, (patch, targets), 1).astype(jnp.float32)
    for k in range(count):
        list_hot_ref[pl.ds(k * patch, patch), :] = jnp.where(
            upright[:, k : k + 1] == lanes, 1.0, 0.0
        ).astype(jnp.bfloat16)

    for side in range(2):
        x = 0 if side == 0 else width - 1
        prior_edge_ref[side, 0] = pp_rows[x]
        prior_edge_ref[side, 1] = qq_rows[x]

    chunk = 8
    for step in range(1, STEPS + 1):
        low, high = step, width - step
        chunks = -(-(high - low) // chunk)

        @pl.loop(0, chunks)
        def _(index):
            start = jnp.minimum(low + chunk * index, high - chunk)

            def prior(field):
                if step == 1:
                    rows = (pp_rows, qq_rows)[field]
                    return lambda r: rows[start + r]
                return lambda r: level_ref[step - 2, field, start + r]

            def put(r, p_new, q_new):
                if step < STEPS:
                    level_ref[step, 0, start + r] = p_new
                    level_ref[step, 1, start + r] = q_new
                else:
                    p_inner_ref[start + r - STEPS] = p_new
                    q_inner_ref[start + r - STEPS] = q_new

            advance(
                chunk,
                lambda r: level_ref[step - 1, 0, start + r],
                lambda r: level_ref[step - 1, 1, start + r],
                prior(0),
                prior(1),
                lambda r: [coef_ref[i, start + r] for i in range(5)],
                put,
            )

    for step in range(STEPS):
        for field in range(2):
            for near in range(2):
                edge_ref[0, field, step, near] = level_ref[step, field, step + near]
                edge_ref[1, field, step, near] = level_ref[step, field, width - 1 - step - near]

    for step in range(1, STEPS + 1):
        low, high = step, width - step
        if step < STEPS:
            values = level_ref[step, 0, low:high]
        else:
            values = p_inner_ref[...]
        found = sample_rows(values.reshape((high - low) * shots, depth), depth_hot_ref[...])
        total = jnp.zeros((shots, targets), jnp.float32)
        for r in range(high - low):
            total = total + jnp.where(column == low + r, found[r * shots : (r + 1) * shots], 0.0)
        sample_ref[step - 1] = total


def interior(fields, params, target_cells, patch_lists):
    shots = fields[0].shape[0]
    width, depth = params[0].shape
    targets = target_cells.shape[0]
    _, owners, slots, patch = patch_lists.shape
    f32 = functools.partial(jax.ShapeDtypeStruct, dtype=jnp.float32)
    out_shape = [
        f32((2, 2, STEPS, 2, shots, depth)),
        f32((2, 2, shots, depth)),
        f32((2, 5, 8, depth)),
        f32((width - 2 * STEPS, shots, depth)),
        f32((width - 2 * STEPS, shots, depth)),
        f32((STEPS, shots, targets)),
        jax.ShapeDtypeStruct((2 * depth, targets), jnp.bfloat16),
        jax.ShapeDtypeStruct((1, targets), jnp.int32),
        jax.ShapeDtypeStruct((owners * slots * patch, targets), jnp.bfloat16),
    ]
    vmem = pl.BlockSpec(memory_space=pltpu.VMEM)
    return pl.pallas_call(
        interior_kernel,
        in_specs=[vmem] * 10,
        out_specs=[vmem] * len(out_shape),
        out_shape=out_shape,
        scratch_shapes=[
            pltpu.VMEM((STEPS, 2, width, shots, depth), jnp.float32),
            pltpu.VMEM((5, width, shots, depth), jnp.float32),
        ],
        compiler_params=compiler_params(40),
        cost_estimate=pl.CostEstimate(
            flops=200 * STEPS * shots * width * depth, bytes_accessed=8 * MIB, transcendentals=0
        ),
        name="interior",
    )(*fields, *params, target_cells.reshape(1, targets), patch_lists)


def finish_kernel(
    lower_ref,
    upper_ref,
    edge_ref,
    prior_edge_ref,
    coef_edge_ref,
    sample_ref,
    depth_hot_ref,
    column_ref,
    list_hot_ref,
    spectra_ref,
    table_ref,
    spectra_out_ref,
    final_ref,
    *rest,
    width,
):
    packed_refs, (level_ref, prior_ref, coef_ref, feature_ref) = rest[:-4], rest[-4:]
    shots, depth = edge_ref.shape[-2:]
    targets = column_ref.shape[1]
    first = -STEPS
    pair = 2 * shots
    for side, ref in enumerate((lower_ref, upper_ref)):
        for field in range(4):
            both = ref[pl.ds(field * pair, pair), :].astype(jnp.float32)
            value = both[:shots] + both[shots:]
            if field < 2:
                level_ref[side, field, 0, -1 - first] = value
            else:
                prior_ref[side, field - 2, -1 - (1 - STEPS)] = value
        for index, items in enumerate(far_items()):
            both = ref[pl.ds((4 + index) * pair, pair), :].astype(jnp.float32)
            for half, (field, distance) in enumerate(items):
                value = both[half * shots : (half + 1) * shots]
                if field < 2:
                    level_ref[side, field, 0, -1 - distance - first] = value
                else:
                    prior_ref[side, field - 2, -1 - distance - (1 - STEPS)] = value
        params = ref[pl.ds((4 + len(far_items())) * pair, pair), :].astype(jnp.float32)
        for index in range(5):
            for distance in range(STEPS - 1):
                line = index * (STEPS - 1) + distance
                row = params[line : line + 1, :]
                if index == 1 and side == 1:
                    row = -row
                coef_ref[side, index, STEPS - 2 - distance] = jnp.broadcast_to(row, (shots, depth))
            for k in range(STEPS):
                coef_ref[side, index, STEPS - 1 + k] = jnp.broadcast_to(
                    coef_edge_ref[side, index, pl.ds(k if side == 0 else 7 - k, 1), :],
                    (shots, depth),
                )
        for field in range(2):
            prior_ref[side, field, STEPS - 1] = prior_edge_ref[side, field]
            for step in range(STEPS):
                for near in range(2):
                    level_ref[side, field, step, step + near - first] = edge_ref[
                        side, field, step, near
                    ]

    for step in range(1, STEPS + 1):
        low = step - STEPS

        for side in range(2):

            def prior(field):
                if step == 1:
                    return lambda r: prior_ref[side, field, low + r - (1 - STEPS)]
                return lambda r: level_ref[side, field, step - 2, low + r - first]

            def put(r, p_new, q_new):
                if step < STEPS:
                    level_ref[side, 0, step, low + r - first] = p_new
                    level_ref[side, 1, step, low + r - first] = q_new
                else:
                    final_ref[side, 0, r] = p_new
                    final_ref[side, 1, r] = q_new

            advance(
                STEPS,
                lambda r: level_ref[side, 0, step - 1, low + r - first],
                lambda r: level_ref[side, 1, step - 1, low + r - first],
                prior(0),
                prior(1),
                lambda r: [coef_ref[side, i, low + r - (1 - STEPS) + 0] for i in range(5)],
                put,
            )

    column = column_ref[...]
    places, values = [], []
    for step in range(1, STEPS + 1):
        for side in range(2):
            for k in range(step):
                places.append((step, k if side == 0 else width - 1 - k))
                if step < STEPS:
                    values.append(level_ref[side, 0, step, k - first])
                else:
                    values.append(final_ref[side, 0, k])
    found = sample_rows(jnp.concatenate(values, 0), depth_hot_ref[...])
    samples = [sample_ref[step] for step in range(STEPS)]
    for index, (step, x) in enumerate(places):
        samples[step - 1] = samples[step - 1] + jnp.where(
            column == x, found[index * shots : (index + 1) * shots], 0.0
        )

    parts = spectra_ref.shape[0] // shots
    lanes = table_ref.shape[-1]
    for s in range(shots):
        for base in range(0, targets, lanes):
            value = spectra_ref[pl.ds(s * parts, parts), pl.ds(base, lanes)]
            for step in range(STEPS):
                value = value + table_ref[step] * samples[step][s : s + 1, base : base + lanes]
            spectra_out_ref[pl.ds(s * parts, parts), pl.ds(base, lanes)] = value
            feature_ref[pl.ds(s * parts, parts), pl.ds(base, lanes)] = value.astype(jnp.bfloat16)

    owners = len(packed_refs)
    patch = packed_refs[0].shape[1]
    slots = list_hot_ref.shape[0] // (owners * patch)
    half = patch // 2
    row = lax.broadcasted_iota(jnp.int32, (half, patch), 0)
    lane = lax.broadcasted_iota(jnp.int32, (half, patch), 1)
    from_last = (lane < half) & (row > lane)
    for g, packed_ref in enumerate(packed_refs):
        chosen = lax.dot_general(
            list_hot_ref[pl.ds(g * slots * patch, slots * patch), :],
            feature_ref[...],
            NT,
            preferred_element_type=jnp.float32,
        ).astype(jnp.bfloat16)
        diagonals = []
        for s in range(slots):
            mine = chosen[s * patch : (s + 1) * patch]
            gram = lax.dot_general(mine, mine, NT, preferred_element_type=jnp.float32)
            last = pltpu.roll(gram[half:], half, 1)
            packed_ref[pl.ds(s * half, half), :] = jnp.where(from_last, last, gram[:half])
            diagonals.append(jnp.sum(jnp.where(row == lane, last, 0.0), 0, keepdims=True))
        while len(diagonals) % 8:
            diagonals.append(jnp.zeros((1, patch), jnp.float32))
        packed_ref[pl.ds(slots * half, len(diagonals)), :] = jnp.concatenate(diagonals, 0)


def finish(lower, upper, inner, spectra, table, width, owners, slots, patch):
    edge, prior_edge, coef_edge, sample, depth_hot, column, list_hot = inner
    shots, depth = edge.shape[-2:]
    targets = column.shape[1]
    features = spectra.shape[0]
    f32 = functools.partial(jax.ShapeDtypeStruct, dtype=jnp.float32)
    rows = slots * (patch // 2) + -(-slots // 8) * 8
    out_shape = [
        f32((features, targets)),
        f32((2, 2, STEPS, shots, depth)),
        *[f32((rows, patch))] * owners,
    ]
    vmem = pl.BlockSpec(memory_space=pltpu.VMEM)
    return pl.pallas_call(
        functools.partial(finish_kernel, width=width),
        in_specs=[vmem] * 11,
        out_specs=[vmem] * len(out_shape),
        out_shape=out_shape,
        scratch_shapes=[
            pltpu.VMEM((2, 2, STEPS, 2 * STEPS + 1, shots, depth), jnp.float32),
            pltpu.VMEM((2, 2, STEPS, shots, depth), jnp.float32),
            pltpu.VMEM((2, 5, 2 * STEPS - 1, shots, depth), jnp.float32),
            pltpu.VMEM((features, targets), jnp.bfloat16),
        ],
        compiler_params=compiler_params(40),
        name="finish",
    )(
        lower,
        upper,
        edge,
        prior_edge,
        coef_edge,
        sample,
        depth_hot,
        column,
        list_hot,
        spectra,
        table,
    )


def assemble_kernel(p_inner_ref, q_inner_ref, final_ref, p_out_ref, q_out_ref):
    width = p_out_ref.shape[1] * TILE
    for field, (inner, out) in enumerate(((p_inner_ref, p_out_ref), (q_inner_ref, q_out_ref))):
        rows = ShotRows(out)
        for k in range(STEPS):
            rows[k] = final_ref[0, field, k]
            rows[width - 1 - k] = final_ref[1, field, k]

        @pl.loop(STEPS, width - STEPS, unroll=4)
        def _(x):
            rows[x] = inner[x - STEPS]


def assemble(p_inner, q_inner, final):
    inner, shots, depth = p_inner.shape
    across, along = (inner + 2 * STEPS) // TILE, depth // LANES
    shape = jax.ShapeDtypeStruct((shots, across, along, TILE, LANES), jnp.float32)
    vmem = pl.BlockSpec(memory_space=pltpu.VMEM)
    return pl.pallas_call(
        assemble_kernel,
        in_specs=[vmem] * 3,
        out_specs=[vmem] * 2,
        out_shape=[shape, shape],
        compiler_params=compiler_params(16),
        cost_estimate=pl.CostEstimate(flops=8 * MIB, bytes_accessed=4 * MIB, transcendentals=0),
        name="assemble",
    )(p_inner, q_inner, final)


def tiles_kernel(counts_ref, *refs, features):
    received, out_ref = refs[:-1], refs[-1]
    slots, patch = out_ref.shape[2], out_ref.shape[3]
    half = patch // 2
    row = lax.broadcasted_iota(jnp.int32, (half, patch), 0)
    lane = lax.broadcasted_iota(jnp.int32, (half, patch), 1)
    live = counts_ref[0, 0]
    total = received[0][...]
    for ref in received[1:]:
        total = total + ref[...]
    for s in range(slots):
        scale = jnp.where(s < live, 1.0 / features, 0.0)
        packed = total[s * half : (s + 1) * half] * scale
        diagonal = total[slots * half + s : slots * half + s + 1] * scale
        turned = jnp.transpose(jnp.concatenate([packed, packed], 0))
        flipped = turned[:half]
        corner = turned[half:]
        out_ref[0, 0, s, pl.ds(0, half), :] = jnp.where(
            (lane < half) & (row > lane), flipped, packed
        )
        last = jnp.where(row > lane, packed, jnp.where(row == lane, diagonal, flipped))
        out_ref[0, 0, s, pl.ds(half, half), :] = jnp.where(
            lane < half, corner, pltpu.roll(last, half, 1)
        )


def tiles(received, patch_counts, slots, features):
    patch = received[0].shape[1]
    return pl.pallas_call(
        functools.partial(tiles_kernel, features=features),
        in_specs=[pl.BlockSpec(memory_space=pltpu.SMEM)]
        + [pl.BlockSpec(memory_space=pltpu.VMEM)] * len(received),
        out_specs=pl.BlockSpec(memory_space=pltpu.VMEM),
        out_shape=jax.ShapeDtypeStruct((1, 1, slots, patch, patch), jnp.float32),
        compiler_params=compiler_params(16),
        name="tiles",
    )(patch_counts, *received)


def shards(
    pressure,
    auxiliary,
    pressure_prior,
    auxiliary_prior,
    courant_sq,
    thomsen_epsilon,
    thomsen_delta,
    tilt_angle,
    frequencies,
    spectra,
    target_cells,
    patch_lists,
    patch_counts,
):
    shots, width, depth = pressure.shape
    _, owners, slots, patch = patch_lists.shape
    fields = [tiled(item) for item in (pressure, auxiliary, pressure_prior, auxiliary_prior)]
    params = (courant_sq, thomsen_epsilon, thomsen_delta, tilt_angle)
    parts, targets = spectra.shape[1:]

    first_rows, last_rows = outer_rows(fields, params)
    bricks = lax.axis_size("brick")
    upward = [(i, i + 1) for i in range(bricks - 1)]
    downward = [(i + 1, i) for i in range(bricks - 1)]
    lower = lax.ppermute(last_rows, "brick", upward)
    upper = lax.ppermute(first_rows, "brick", downward)

    moments = jnp.arange(1, STEPS + 1, dtype=jnp.float32)
    angle = frequencies[None, :] * moments[:, None]
    table = jnp.concatenate([jnp.cos(angle), -jnp.sin(angle)], 1)
    table = jnp.broadcast_to(table[:, :, None], (STEPS, parts, 128))

    edge, prior_edge, coef_edge, p_inner, q_inner, sample, depth_hot, column, list_hot = interior(
        fields, params, target_cells, patch_lists
    )
    spectra_out, final, *packed = finish(
        lower,
        upper,
        (edge, prior_edge, coef_edge, sample, depth_hot, column, list_hot),
        spectra.reshape(shots * parts, targets),
        table,
        width,
        owners,
        slots,
        patch,
    )
    received = packed[:1]
    for k in sorted(range(1, owners), key=lambda k: (k < owners // 2, k)):
        pairs = [(i, int(partner(i, k, owners))) for i in range(owners)]
        received.append(lax.ppermute(packed[k], "shot", pairs))
    pressure_out, auxiliary_out = [untiled(item) for item in assemble(p_inner, q_inner, final)]
    gram_tiles = tiles(received, patch_counts, slots, shots * parts * owners)
    return (pressure_out, auxiliary_out, spectra_out.reshape(spectra.shape), gram_tiles)


def solution(mesh):
    return jax.shard_map(
        shards,
        mesh=mesh,
        in_specs=(
            P("shot", "brick", None),
            P("shot", "brick", None),
            P("shot", "brick", None),
            P("shot", "brick", None),
            P("brick", None),
            P("brick", None),
            P("brick", None),
            P("brick", None),
            P(),
            P("shot", None, "brick"),
            P("brick"),
            P("brick", None, None, None),
            P("brick", "shot"),
        ),
        out_specs=(
            P("shot", "brick", None),
            P("shot", "brick", None),
            P("shot", None, "brick"),
            P("brick", "shot", None, None, None),
        ),
        check_vma=False,
    )
```

```python
import functools
import math

import jax
import jax.numpy as jnp
from jax import lax
from jax.experimental import pallas as pl
from jax.experimental.pallas import tpu as pltpu
from jax.sharding import PartitionSpec as P

STEPS = 4
MIB = 1024 * 1024
NT = (((1,), (1,)), ((), ()))


TILE = 8
LANES = 128


def tiled(field):
    shots, width, depth = field.shape
    parts = field.reshape(shots, width // TILE, TILE, depth // LANES, LANES)
    return parts.transpose(0, 1, 3, 2, 4)


def untiled(parts):
    shots, across, along, tile, lanes = parts.shape
    return parts.transpose(0, 1, 3, 2, 4).reshape(shots, across * tile, along * lanes)


class ShotRows:
    def __init__(self, ref):
        self.shots, self.across, self.along, tile, lanes = ref.shape
        self.stride = self.across * self.along * tile
        self.flat = ref.reshape(self.shots * self.stride, lanes)

    def place(self, x, j):
        if isinstance(x, int):
            start = (x // TILE * self.along + j) * TILE + x % TILE
        else:
            start = (lax.div(x, TILE) * self.along + j) * TILE + lax.rem(x, TILE)
        return pl.ds(start, self.shots, stride=self.stride)

    def __getitem__(self, x):
        return jnp.concatenate([self.flat[self.place(x, j), :] for j in range(self.along)], 1)

    def __setitem__(self, x, row):
        for j in range(self.along):
            self.flat[self.place(x, j), :] = row[:, j * LANES : (j + 1) * LANES]


def compiler_params(mib):
    return pltpu.CompilerParams(vmem_limit_bytes=mib * MIB)


def tilt_coefficients(courant, epsilon, delta, tilt):
    turns = jnp.round(tilt * (2.0 / math.pi))
    rest = (tilt - turns * 1.5703125) - turns * (math.pi / 2 - 1.5703125)
    odd = turns - 2.0 * jnp.floor(turns * 0.5)
    sign = 1.0 - 2.0 * odd
    double = 2.0 * rest
    square = double * double
    sine = double * (
        1.0
        + square
        * (
            -1.0 / 6
            + square
            * (1.0 / 120 + square * (-1.0 / 5040 + square * (1.0 / 362880 - square / 39916800.0)))
        )
    )
    versine = square * (
        0.5
        + square
        * (
            -1.0 / 24
            + square
            * (1.0 / 720 + square * (-1.0 / 40320 + square * (1.0 / 3628800 - square / 479001600.0)))
        )
    )
    sine_sq = jnp.where(odd > 0.5, 1.0 - 0.5 * versine, 0.5 * versine)
    quarter_sin = 0.25 * sign * sine
    gain_p = courant * (1.0 + 2.0 * epsilon)
    gain_q = courant * (1.0 + 2.0 * delta)
    return sine_sq, quarter_sin, courant, gain_p, gain_q


def blocks(row):
    return [row[:, j : j + LANES] for j in range(0, row.shape[1], LANES)]


def depth_terms(row):
    lane = lax.broadcasted_iota(jnp.int32, row[0].shape, 1)
    shallow = [pltpu.roll(block, 1, 1) for block in row]
    deep = [pltpu.roll(block, LANES - 1, 1) for block in row]
    outside = jnp.zeros_like(row[0])
    sums, differences = [], []
    for j in range(len(row)):
        above = jnp.where(lane == 0, shallow[j - 1] if j else outside, shallow[j])
        below = jnp.where(
            lane == LANES - 1, deep[j + 1] if j + 1 < len(row) else outside, deep[j]
        )
        sums.append(below + above)
        differences.append(below - above)
    return sums, differences


def advance(count, p_row, q_row, p_prior, q_prior, coefficient, put):
    p_back, p_here = blocks(p_row(-1)), blocks(p_row(0))
    q_back, q_here = blocks(q_row(-1)), blocks(q_row(0))
    _, p_back_d = depth_terms(p_back)
    _, q_back_d = depth_terms(q_back)
    p_sum, p_here_d = depth_terms(p_here)
    q_sum, q_here_d = depth_terms(q_here)
    for row in range(count):
        p_next, q_next = blocks(p_row(row + 1)), blocks(q_row(row + 1))
        p_next_sum, p_next_d = depth_terms(p_next)
        q_next_sum, q_next_d = depth_terms(q_next)
        p_old, q_old = blocks(p_prior(row)), blocks(q_prior(row))
        p_new, q_new = [], []
        for j in range(len(p_here)):
            sine_sq, quarter_sin, courant, gain_p, gain_q = [coefficient(i, row, j) for i in range(5)]
            twice_p, twice_q = p_here[j] + p_here[j], q_here[j] + q_here[j]
            side = p_next[j] + p_back[j]
            mixed = p_next_d[j] - p_back_d[j]
            across = (side - twice_p) + sine_sq * (p_sum[j] - side) - quarter_sin * mixed
            side = q_next[j] + q_back[j]
            mixed = q_next_d[j] - q_back_d[j]
            along = (q_sum[j] - twice_q) + sine_sq * (side - q_sum[j]) + quarter_sin * mixed
            along = courant * along
            p_new.append((twice_p - p_old[j]) + (gain_p * across + along))
            q_new.append((twice_q - q_old[j]) + (gain_q * across + along))
        put(row, jnp.concatenate(p_new, 1), jnp.concatenate(q_new, 1))
        p_back, p_here, p_back_d, p_here_d, p_sum = p_here, p_next, p_here_d, p_next_d, p_next_sum
        q_back, q_here, q_back_d, q_here_d, q_sum = q_here, q_next, q_here_d, q_next_d, q_next_sum


class CoefficientRows:
    def __init__(self, ref, shots):
        self.shots, (_, self.along, self.rows, lanes) = shots, ref.shape
        self.flat = ref.reshape(ref.shape[0] * self.along * self.rows, lanes)

    def __call__(self, index, row, j):
        place = (index * self.along + j) * self.rows + row
        return self.flat[pl.ds(place, self.shots, stride=0), :]


def split_bf16(values):
    high = values.astype(jnp.bfloat16)
    low = (values - high.astype(jnp.float32)).astype(jnp.bfloat16)
    return high, low


def outer_kernel(*refs):
    sources, outs, (field_ref, param_ref, field_sem, param_sem) = refs[:8], refs[8:10], refs[10:]
    shots, across, along, tile, lanes = sources[0].shape
    depth = along * lanes
    copies = []
    for side in range(2):
        place = side * (across - 1)
        for i in range(4):
            copies.append(
                pltpu.make_async_copy(
                    sources[i].at[:, pl.ds(place, 1), :, pl.ds(side * STEPS, STEPS)],
                    field_ref.at[side, i, :, :, :, pl.ds(side * STEPS, STEPS)],
                    field_sem.at[side, i],
                )
            )
        for i in range(4):
            copies.append(
                pltpu.make_async_copy(
                    sources[4 + i].at[pl.ds(place * tile, tile)],
                    param_ref.at[side, i],
                    param_sem.at[side, i],
                )
            )
    for copy in copies:
        copy.start()
    for side in range(2):
        for copy in copies[8 * side : 8 * side + 8]:
            copy.wait()
        views = [ShotRows(field_ref.at[side, i]) for i in range(4)]
        out = outs[side]

        def row(field, distance):
            place = distance if side == 0 else tile - 1 - distance
            return views[field][place]

        position = 0

        def put(first, second):
            nonlocal position
            out[pl.ds(position, 2 * shots), :] = jnp.concatenate([first, second], 0).astype(
                jnp.bfloat16
            )
            position += 2 * shots

        for field in range(4):
            near = row(field, 0)
            put(near, near - near.astype(jnp.bfloat16).astype(jnp.float32))
        for first, second in far_items():
            put(row(*first), row(*second))
        terms = tilt_coefficients(*[param_ref[side, i] for i in range(4)])
        rows = []
        for index, term in enumerate(terms):
            term = -term if index == 1 and side == 0 else term
            for distance in reversed(range(STEPS - 1)):
                place = distance if side == 0 else tile - 1 - distance
                rows.append(term[place : place + 1, :])
        while len(rows) < 2 * shots:
            rows.append(jnp.zeros((1, depth), jnp.float32))
        out[pl.ds(position, 2 * shots), :] = jnp.concatenate(rows, 0).astype(jnp.bfloat16)


def far_items():
    items = []
    for field in range(2):
        items += [(field, distance) for distance in range(1, STEPS)]
    for field in range(2, 4):
        items += [(field, distance) for distance in range(1, STEPS - 1)]
    return list(zip(items[0::2], items[1::2]))


def outer_rows(fields, params):
    shots, across, along, tile, lanes = fields[0].shape
    depth = along * lanes
    rows = 2 * shots * (4 + len(far_items()) + 1)
    shape = jax.ShapeDtypeStruct((rows, depth), jnp.bfloat16)
    return pl.pallas_call(
        outer_kernel,
        in_specs=[pl.BlockSpec(memory_space=pltpu.HBM)] * 8,
        out_specs=[pl.BlockSpec(memory_space=pltpu.VMEM)] * 2,
        out_shape=[shape, shape],
        scratch_shapes=[
            pltpu.VMEM((2, 4, shots, 1, along, tile, lanes), jnp.float32),
            pltpu.VMEM((2, 4, tile, depth), jnp.float32),
            pltpu.SemaphoreType.DMA((2, 4)),
            pltpu.SemaphoreType.DMA((2, 4)),
        ],
        compiler_params=compiler_params(60),
        name="outer_rows",
    )(*fields, *params)


def partner(me, k, count):
    if count & (count - 1):
        return (me + k) % count
    return me ^ k


def sample_rows(values, one_hot):
    high, low = split_bf16(values)
    return jnp.dot(jnp.concatenate([high, low], 1), one_hot, preferred_element_type=jnp.float32)


def interior_kernel(
    p_ref,
    q_ref,
    pp_ref,
    qq_ref,
    courant_ref,
    epsilon_ref,
    delta_ref,
    tilt_ref,
    cells_ref,
    lists_ref,
    edge_ref,
    prior_edge_ref,
    coef_edge_ref,
    p_inner_ref,
    q_inner_ref,
    sample_ref,
    depth_hot_ref,
    column_ref,
    list_hot_ref,
    level_ref,
    coef_ref,
    split_ref,
    sems,
):
    shots, width, depth = p_ref.shape
    along = depth // LANES
    copies = []
    for i, ref in enumerate((p_ref, q_ref, pp_ref, qq_ref)):
        for s in range(shots):
            copies.append(
                pltpu.make_async_copy(
                    ref.at[s], level_ref.at[1 - i // 2, i % 2, :, s], sems.at[i, s]
                )
            )
    for copy in copies:
        copy.start()

    terms = tilt_coefficients(courant_ref[...], epsilon_ref[...], delta_ref[...], tilt_ref[...])
    for index, term in enumerate(terms):
        for j in range(along):
            coef_ref[index, j] = term[:, j * LANES : (j + 1) * LANES]
        for k in range(STEPS):
            coef_edge_ref[0, index, pl.ds(k, 1), :] = term[k : k + 1, :]
            row = term[width - 1 - k : width - k, :]
            coef_edge_ref[1, index, pl.ds(k, 1), :] = -row if index == 1 else row

    one, zero = jnp.bfloat16(1), jnp.bfloat16(0)
    cells = cells_ref[...]
    column = cells // depth
    column_ref[...] = column
    targets = cells.shape[1]
    z_of = jnp.broadcast_to(cells - column * depth, (16, targets)).astype(jnp.int16)
    places = lax.broadcasted_iota(jnp.int16, (16, targets), 0)
    for base in range(0, depth, 16):
        hot = jnp.where(places + jnp.int16(base) == z_of, one, zero)
        depth_hot_ref[pl.ds(base, 16), :] = hot
        depth_hot_ref[pl.ds(depth + base, 16), :] = hot

    owners, slots, patch = lists_ref.shape[1:]
    me = lax.axis_index("shot")
    rows = []
    for k in range(owners):
        lists = lists_ref[0, partner(me, k, owners)]
        rows += [lists[s : s + 1, :] for s in range(slots)]
    count = len(rows)
    while len(rows) % 8:
        rows.append(rows[0])
    upright = jnp.transpose(jnp.concatenate(rows, 0).astype(jnp.float32)).astype(jnp.int32)
    lanes = lax.broadcasted_iota(jnp.int16, (patch, LANES), 1)
    for k in range(count):
        wanted = jnp.broadcast_to(upright[:, k : k + 1], (patch, LANES)).astype(jnp.int16)
        for base in range(0, targets, LANES):
            list_hot_ref[pl.ds(k * patch, patch), pl.ds(base, LANES)] = jnp.where(
                lanes + jnp.int16(base) == wanted, one, zero
            )

    for copy in copies:
        copy.wait()
    for side in range(2):
        x = 0 if side == 0 else width - 1
        prior_edge_ref[side, 0] = level_ref[0, 0, x]
        prior_edge_ref[side, 1] = level_ref[0, 1, x]

    coefficients = CoefficientRows(coef_ref, shots)
    offsets = [0]
    for step in range(1, STEPS + 1):
        low, high = step, width - step
        chunk = 8 if (high - low) % 8 == 0 else 10
        offset = offsets[-1]
        offsets.append(offset + high - low)

        @pl.loop(0, -(-(high - low) // chunk))
        def _(index):
            at = jnp.minimum(chunk * index, high - low - chunk)
            start = low + at
            held = []

            def put(r, p_new, q_new):
                if step < STEPS:
                    level_ref[step + 1, 0, start + r] = p_new
                    level_ref[step + 1, 1, start + r] = q_new
                else:
                    p_inner_ref[at + r] = p_new
                    q_inner_ref[at + r] = q_new
                held.append(p_new)
                if len(held) == 2:
                    first, rest = split_bf16(jnp.concatenate(held, 0))
                    place = pl.multiple_of((offset + at + r - 1) * shots, 2 * shots)
                    split_ref[pl.ds(place, 2 * shots), pl.ds(0, depth)] = first
                    split_ref[pl.ds(place, 2 * shots), pl.ds(depth, depth)] = rest
                    held.clear()

            advance(
                chunk,
                lambda r: level_ref[step, 0, start + r],
                lambda r: level_ref[step, 1, start + r],
                lambda r: level_ref[step - 1, 0, start + r],
                lambda r: level_ref[step - 1, 1, start + r],
                lambda i, r, j: coefficients(i, start + r, j),
                put,
            )

    for step in range(STEPS):
        for field in range(2):
            for near in range(2):
                edge_ref[0, field, step, near] = level_ref[step + 1, field, step + near]
                edge_ref[1, field, step, near] = level_ref[step + 1, field, width - 1 - step - near]

    found = jnp.dot(split_ref[...], depth_hot_ref[...], preferred_element_type=jnp.float32)
    totals = [jnp.zeros((shots, targets), jnp.float32) for _ in range(STEPS)]
    for x in range(1, width - 1):
        here = column == x
        for step in range(1, STEPS + 1):
            if step <= x < width - step:
                row = (offsets[step - 1] + x - step) * shots
                totals[step - 1] += jnp.where(here, found[row : row + shots], 0.0)
    for step in range(STEPS):
        sample_ref[step] = totals[step]


def interior(fields, params, target_cells, patch_lists):
    shots, width, depth = fields[0].shape
    targets = target_cells.shape[0]
    _, owners, slots, patch = patch_lists.shape
    f32 = functools.partial(jax.ShapeDtypeStruct, dtype=jnp.float32)
    out_shape = [
        f32((2, 2, STEPS, 2, shots, depth)),
        f32((2, 2, shots, depth)),
        f32((2, 5, 8, depth)),
        f32((width - 2 * STEPS, shots, depth)),
        f32((width - 2 * STEPS, shots, depth)),
        f32((STEPS, shots, targets)),
        jax.ShapeDtypeStruct((2 * depth, targets), jnp.bfloat16),
        jax.ShapeDtypeStruct((1, targets), jnp.int32),
        jax.ShapeDtypeStruct((owners * slots * patch, targets), jnp.bfloat16),
    ]
    vmem = pl.BlockSpec(memory_space=pltpu.VMEM)
    return pl.pallas_call(
        interior_kernel,
        in_specs=[pl.BlockSpec(memory_space=pl.ANY)] * 4 + [vmem] * 6,
        out_specs=[vmem] * len(out_shape),
        out_shape=out_shape,
        scratch_shapes=[
            pltpu.VMEM((STEPS + 1, 2, width, shots, depth), jnp.float32),
            pltpu.VMEM((5, depth // LANES, width, LANES), jnp.float32),
            pltpu.VMEM((STEPS * (width - STEPS - 1) * shots, 2 * depth), jnp.bfloat16),
            pltpu.SemaphoreType.DMA((4, shots)),
        ],
        compiler_params=compiler_params(40),
        cost_estimate=pl.CostEstimate(
            flops=200 * STEPS * shots * width * depth, bytes_accessed=8 * MIB, transcendentals=0
        ),
        name="interior",
    )(*fields, *params, target_cells.reshape(1, targets), patch_lists)


def finish_kernel(
    lower_ref,
    upper_ref,
    edge_ref,
    prior_edge_ref,
    coef_edge_ref,
    sample_ref,
    depth_hot_ref,
    column_ref,
    list_hot_ref,
    spectra_ref,
    table_ref,
    spectra_out_ref,
    final_ref,
    *rest,
    width,
):
    packed_refs = rest[:-6]
    level_ref, prior_ref, coef_ref, feature_ref, out_ref, out_sem = rest[-6:]
    shots, depth = edge_ref.shape[-2:]
    targets = column_ref.shape[1]
    first = -STEPS
    pair = 2 * shots
    for side, ref in enumerate((lower_ref, upper_ref)):
        for field in range(4):
            both = ref[pl.ds(field * pair, pair), :].astype(jnp.float32)
            value = both[:shots] + both[shots:]
            if field < 2:
                level_ref[side, field, 0, -1 - first] = value
            else:
                prior_ref[side, field - 2, -1 - (1 - STEPS)] = value
        for index, items in enumerate(far_items()):
            both = ref[pl.ds((4 + index) * pair, pair), :].astype(jnp.float32)
            for half, (field, distance) in enumerate(items):
                value = both[half * shots : (half + 1) * shots]
                if field < 2:
                    level_ref[side, field, 0, -1 - distance - first] = value
                else:
                    prior_ref[side, field - 2, -1 - distance - (1 - STEPS)] = value
        params = ref[pl.ds((4 + len(far_items())) * pair, pair), :].astype(jnp.float32)
        for index in range(5):
            far = params[index * (STEPS - 1) : (index + 1) * (STEPS - 1)]
            near = coef_edge_ref[side, index, pl.ds(0, STEPS), :]
            for j in range(depth // LANES):
                coef_ref[side, index, j, pl.ds(0, STEPS - 1), :] = far[:, j * LANES : (j + 1) * LANES]
                coef_ref[side, index, j, pl.ds(STEPS - 1, STEPS), :] = near[
                    :, j * LANES : (j + 1) * LANES
                ]
        for field in range(2):
            prior_ref[side, field, STEPS - 1] = prior_edge_ref[side, field]
            for step in range(STEPS):
                for near in range(2):
                    level_ref[side, field, step, step + near - first] = edge_ref[
                        side, field, step, near
                    ]

    for step in range(1, STEPS + 1):
        low = step - STEPS

        for side in range(2):
            coefficients = CoefficientRows(coef_ref.at[side], shots)

            def prior(field):
                if step == 1:
                    return lambda r: prior_ref[side, field, low + r - (1 - STEPS)]
                return lambda r: level_ref[side, field, step - 2, low + r - first]

            def put(r, p_new, q_new):
                if step < STEPS:
                    level_ref[side, 0, step, low + r - first] = p_new
                    level_ref[side, 1, step, low + r - first] = q_new
                else:
                    final_ref[side, 0, r] = p_new
                    final_ref[side, 1, r] = q_new

            advance(
                STEPS,
                lambda r: level_ref[side, 0, step - 1, low + r - first],
                lambda r: level_ref[side, 1, step - 1, low + r - first],
                prior(0),
                prior(1),
                lambda i, r, j: coefficients(i, low + r - (1 - STEPS), j),
                put,
            )

    column = column_ref[...]
    places, values = [], []
    for step in range(1, STEPS + 1):
        for side in range(2):
            for k in range(step):
                places.append((step, k if side == 0 else width - 1 - k))
                if step < STEPS:
                    values.append(level_ref[side, 0, step, k - first])
                else:
                    values.append(final_ref[side, 0, k])
    found = sample_rows(jnp.concatenate(values, 0), depth_hot_ref[...])
    samples = [sample_ref[step] for step in range(STEPS)]
    for index, (step, x) in enumerate(places):
        samples[step - 1] = samples[step - 1] + jnp.where(
            column == x, found[index * shots : (index + 1) * shots], 0.0
        )

    parts = spectra_ref.shape[0] // shots
    lanes = table_ref.shape[-1]
    for s in range(shots):
        for base in range(0, targets, lanes):
            value = spectra_ref[pl.ds(s * parts, parts), pl.ds(base, lanes)]
            for step in range(STEPS):
                value = value + table_ref[step] * samples[step][s : s + 1, base : base + lanes]
            out_ref[pl.ds(s * parts, parts), pl.ds(base, lanes)] = value
            feature_ref[pl.ds(s * parts, parts), pl.ds(base, lanes)] = value.astype(jnp.bfloat16)

    out_copy = pltpu.make_async_copy(out_ref, spectra_out_ref, out_sem)
    out_copy.start()

    owners = len(packed_refs)
    patch = packed_refs[0].shape[1]
    slots = list_hot_ref.shape[0] // (owners * patch)
    half = patch // 2
    row = lax.broadcasted_iota(jnp.int32, (half, patch), 0)
    lane = lax.broadcasted_iota(jnp.int32, (half, patch), 1)
    from_last = (lane < half) & (row > lane)
    for g, packed_ref in enumerate(packed_refs):
        chosen = lax.dot_general(
            list_hot_ref[pl.ds(g * slots * patch, slots * patch), :],
            feature_ref[...],
            NT,
            preferred_element_type=jnp.float32,
        ).astype(jnp.bfloat16)
        diagonals = []
        for s in range(slots):
            mine = chosen[s * patch : (s + 1) * patch]
            gram = lax.dot_general(mine, mine, NT, preferred_element_type=jnp.float32)
            last = pltpu.roll(gram[half:], half, 1)
            packed_ref[pl.ds(s * half, half), :] = jnp.where(from_last, last, gram[:half])
            diagonals.append(jnp.sum(jnp.where(row == lane, last, 0.0), 0, keepdims=True))
        while len(diagonals) % 8:
            diagonals.append(jnp.zeros((1, patch), jnp.float32))
        packed_ref[pl.ds(slots * half, len(diagonals)), :] = jnp.concatenate(diagonals, 0)
    out_copy.wait()


def finish(lower, upper, inner, spectra, table, width, owners, slots, patch):
    edge, prior_edge, coef_edge, sample, depth_hot, column, list_hot = inner
    shots, depth = edge.shape[-2:]
    targets = column.shape[1]
    features = spectra.shape[0]
    f32 = functools.partial(jax.ShapeDtypeStruct, dtype=jnp.float32)
    rows = slots * (patch // 2) + -(-slots // 8) * 8
    out_shape = [
        f32((features, targets)),
        f32((2, 2, STEPS, shots, depth)),
        *[f32((rows, patch))] * owners,
    ]
    vmem = pl.BlockSpec(memory_space=pltpu.VMEM)
    return pl.pallas_call(
        functools.partial(finish_kernel, width=width),
        in_specs=[vmem] * 11,
        out_specs=[pl.BlockSpec(memory_space=pl.ANY)] + [vmem] * (len(out_shape) - 1),
        out_shape=out_shape,
        scratch_shapes=[
            pltpu.VMEM((2, 2, STEPS, 2 * STEPS + 1, shots, depth), jnp.float32),
            pltpu.VMEM((2, 2, STEPS, shots, depth), jnp.float32),
            pltpu.VMEM((2, 5, depth // LANES, 2 * STEPS, LANES), jnp.float32),
            pltpu.VMEM((features, targets), jnp.bfloat16),
            pltpu.VMEM((features, targets), jnp.float32),
            pltpu.SemaphoreType.DMA,
        ],
        compiler_params=compiler_params(40),
        name="finish",
    )(
        lower,
        upper,
        edge,
        prior_edge,
        coef_edge,
        sample,
        depth_hot,
        column,
        list_hot,
        spectra,
        table,
    )


def assemble_kernel(p_inner_ref, q_inner_ref, final_ref, p_out_ref, q_out_ref):
    width = p_out_ref.shape[1] * TILE
    for field, (inner, out) in enumerate(((p_inner_ref, p_out_ref), (q_inner_ref, q_out_ref))):
        rows = ShotRows(out)
        for k in range(STEPS):
            rows[k] = final_ref[0, field, k]
            rows[width - 1 - k] = final_ref[1, field, k]

        @pl.loop(STEPS, width - STEPS, unroll=4)
        def _(x):
            rows[x] = inner[x - STEPS]


def assemble(p_inner, q_inner, final):
    inner, shots, depth = p_inner.shape
    across, along = (inner + 2 * STEPS) // TILE, depth // LANES
    shape = jax.ShapeDtypeStruct((shots, across, along, TILE, LANES), jnp.float32)
    vmem = pl.BlockSpec(memory_space=pltpu.VMEM)
    return pl.pallas_call(
        assemble_kernel,
        in_specs=[vmem] * 3,
        out_specs=[vmem] * 2,
        out_shape=[shape, shape],
        compiler_params=compiler_params(16),
        cost_estimate=pl.CostEstimate(flops=8 * MIB, bytes_accessed=4 * MIB, transcendentals=0),
        name="assemble",
    )(p_inner, q_inner, final)


def tiles_kernel(counts_ref, *refs, features):
    received, out_ref = refs[:-1], refs[-1]
    slots, patch = out_ref.shape[2], out_ref.shape[3]
    half = patch // 2
    row = lax.broadcasted_iota(jnp.int32, (half, patch), 0)
    lane = lax.broadcasted_iota(jnp.int32, (half, patch), 1)
    live = counts_ref[0, 0]
    total = received[0][...]
    for ref in received[1:]:
        total = total + ref[...]
    for s in range(slots):
        scale = jnp.where(s < live, 1.0 / features, 0.0)
        packed = total[s * half : (s + 1) * half] * scale
        diagonal = total[slots * half + s : slots * half + s + 1] * scale
        turned = jnp.transpose(jnp.concatenate([packed, packed], 0))
        flipped = turned[:half]
        corner = turned[half:]
        out_ref[0, 0, s, pl.ds(0, half), :] = jnp.where(
            (lane < half) & (row > lane), flipped, packed
        )
        last = jnp.where(row > lane, packed, jnp.where(row == lane, diagonal, flipped))
        out_ref[0, 0, s, pl.ds(half, half), :] = jnp.where(
            lane < half, corner, pltpu.roll(last, half, 1)
        )


def tiles(received, patch_counts, slots, features):
    patch = received[0].shape[1]
    return pl.pallas_call(
        functools.partial(tiles_kernel, features=features),
        in_specs=[pl.BlockSpec(memory_space=pltpu.SMEM)]
        + [pl.BlockSpec(memory_space=pltpu.VMEM)] * len(received),
        out_specs=pl.BlockSpec(memory_space=pltpu.VMEM),
        out_shape=jax.ShapeDtypeStruct((1, 1, slots, patch, patch), jnp.float32),
        compiler_params=compiler_params(16),
        name="tiles",
    )(patch_counts, *received)


def shards(
    pressure,
    auxiliary,
    pressure_prior,
    auxiliary_prior,
    courant_sq,
    thomsen_epsilon,
    thomsen_delta,
    tilt_angle,
    frequencies,
    spectra,
    target_cells,
    patch_lists,
    patch_counts,
):
    shots, width, depth = pressure.shape
    _, owners, slots, patch = patch_lists.shape
    fields = (pressure, auxiliary, pressure_prior, auxiliary_prior)
    params = (courant_sq, thomsen_epsilon, thomsen_delta, tilt_angle)
    parts, targets = spectra.shape[1:]

    first_rows, last_rows = outer_rows([tiled(item) for item in fields], params)
    bricks = lax.axis_size("brick")
    upward = [(i, i + 1) for i in range(bricks - 1)]
    downward = [(i + 1, i) for i in range(bricks - 1)]
    lower = lax.ppermute(last_rows, "brick", upward)
    upper = lax.ppermute(first_rows, "brick", downward)

    moments = jnp.arange(1, STEPS + 1, dtype=jnp.float32)
    angle = frequencies[None, :] * moments[:, None]
    table = jnp.concatenate([jnp.cos(angle), -jnp.sin(angle)], 1)
    table = jnp.broadcast_to(table[:, :, None], (STEPS, parts, 128))

    edge, prior_edge, coef_edge, p_inner, q_inner, sample, depth_hot, column, list_hot = interior(
        fields, params, target_cells, patch_lists
    )
    spectra_out, final, *packed = finish(
        lower,
        upper,
        (edge, prior_edge, coef_edge, sample, depth_hot, column, list_hot),
        spectra.reshape(shots * parts, targets),
        table,
        width,
        owners,
        slots,
        patch,
    )
    received = packed[:1]
    for k in sorted(range(1, owners), key=lambda k: (k < owners // 2, k)):
        pairs = [(i, int(partner(i, k, owners))) for i in range(owners)]
        received.append(lax.ppermute(packed[k], "shot", pairs))
    pressure_out, auxiliary_out = [untiled(item) for item in assemble(p_inner, q_inner, final)]
    gram_tiles = tiles(received, patch_counts, slots, shots * parts * owners)
    return (pressure_out, auxiliary_out, spectra_out.reshape(spectra.shape), gram_tiles)


def solution(mesh):
    return jax.shard_map(
        shards,
        mesh=mesh,
        in_specs=(
            P("shot", "brick", None),
            P("shot", "brick", None),
            P("shot", "brick", None),
            P("shot", "brick", None),
            P("brick", None),
            P("brick", None),
            P("brick", None),
            P("brick", None),
            P(),
            P("shot", None, "brick"),
            P("brick"),
            P("brick", None, None, None),
            P("brick", "shot"),
        ),
        out_specs=(
            P("shot", "brick", None),
            P("shot", "brick", None),
            P("shot", None, "brick"),
            P("brick", "shot", None, None, None),
        ),
        check_vma=False,
    )
```

```python
import functools
import math

import jax
import jax.numpy as jnp
from jax import lax
from jax.experimental import pallas as pl
from jax.experimental.pallas import tpu as pltpu
from jax.sharding import PartitionSpec as P

STEPS = 4
MIB = 1024 * 1024
NT = (((1,), (1,)), ((), ()))


TILE = 8
LANES = 128


def tiled(field):
    shots, width, depth = field.shape
    parts = field.reshape(shots, width // TILE, TILE, depth // LANES, LANES)
    return parts.transpose(0, 1, 3, 2, 4)


def untiled(parts):
    shots, across, along, tile, lanes = parts.shape
    return parts.transpose(0, 1, 3, 2, 4).reshape(shots, across * tile, along * lanes)


class ShotRows:
    def __init__(self, ref):
        self.shots, self.across, self.along, tile, lanes = ref.shape
        self.stride = self.across * self.along * tile
        self.flat = ref.reshape(self.shots * self.stride, lanes)

    def place(self, x, j):
        if isinstance(x, int):
            start = (x // TILE * self.along + j) * TILE + x % TILE
        else:
            start = (lax.div(x, TILE) * self.along + j) * TILE + lax.rem(x, TILE)
        return pl.ds(start, self.shots, stride=self.stride)

    def __getitem__(self, x):
        return jnp.concatenate([self.flat[self.place(x, j), :] for j in range(self.along)], 1)

    def __setitem__(self, x, row):
        for j in range(self.along):
            self.flat[self.place(x, j), :] = row[:, j * LANES : (j + 1) * LANES]


def compiler_params(mib):
    return pltpu.CompilerParams(vmem_limit_bytes=mib * MIB)


def tilt_coefficients(courant, epsilon, delta, tilt):
    turns = jnp.round(tilt * (2.0 / math.pi))
    rest = (tilt - turns * 1.5703125) - turns * (math.pi / 2 - 1.5703125)
    odd = turns - 2.0 * jnp.floor(turns * 0.5)
    sign = 1.0 - 2.0 * odd
    double = 2.0 * rest
    square = double * double
    sine = double * (
        1.0
        + square
        * (
            -1.0 / 6
            + square
            * (1.0 / 120 + square * (-1.0 / 5040 + square * (1.0 / 362880 - square / 39916800.0)))
        )
    )
    versine = square * (
        0.5
        + square
        * (
            -1.0 / 24
            + square
            * (1.0 / 720 + square * (-1.0 / 40320 + square * (1.0 / 3628800 - square / 479001600.0)))
        )
    )
    sine_sq = jnp.where(odd > 0.5, 1.0 - 0.5 * versine, 0.5 * versine)
    quarter_sin = 0.25 * sign * sine
    gain_p = courant * (1.0 + 2.0 * epsilon)
    gain_q = courant * (1.0 + 2.0 * delta)
    return sine_sq, quarter_sin, courant, gain_p, gain_q


def blocks(row):
    return [row[:, j : j + LANES] for j in range(0, row.shape[1], LANES)]


def depth_terms(row):
    lane = lax.broadcasted_iota(jnp.int32, row[0].shape, 1)
    shallow = [pltpu.roll(block, 1, 1) for block in row]
    deep = [pltpu.roll(block, LANES - 1, 1) for block in row]
    outside = jnp.zeros_like(row[0])
    sums, differences = [], []
    for j in range(len(row)):
        above = jnp.where(lane == 0, shallow[j - 1] if j else outside, shallow[j])
        below = jnp.where(
            lane == LANES - 1, deep[j + 1] if j + 1 < len(row) else outside, deep[j]
        )
        sums.append(below + above)
        differences.append(below - above)
    return sums, differences


def advance(count, p_row, q_row, p_prior, q_prior, coefficient, put):
    p_back, p_here = blocks(p_row(-1)), blocks(p_row(0))
    q_back, q_here = blocks(q_row(-1)), blocks(q_row(0))
    _, p_back_d = depth_terms(p_back)
    _, q_back_d = depth_terms(q_back)
    p_sum, p_here_d = depth_terms(p_here)
    q_sum, q_here_d = depth_terms(q_here)
    for row in range(count):
        p_next, q_next = blocks(p_row(row + 1)), blocks(q_row(row + 1))
        p_next_sum, p_next_d = depth_terms(p_next)
        q_next_sum, q_next_d = depth_terms(q_next)
        p_old, q_old = blocks(p_prior(row)), blocks(q_prior(row))
        p_new, q_new = [], []
        for j in range(len(p_here)):
            sine_sq, quarter_sin, courant, gain_p, gain_q = [coefficient(i, row, j) for i in range(5)]
            twice_p, twice_q = p_here[j] + p_here[j], q_here[j] + q_here[j]
            side = p_next[j] + p_back[j]
            mixed = p_next_d[j] - p_back_d[j]
            across = (side - twice_p) + sine_sq * (p_sum[j] - side) - quarter_sin * mixed
            side = q_next[j] + q_back[j]
            mixed = q_next_d[j] - q_back_d[j]
            along = (q_sum[j] - twice_q) + sine_sq * (side - q_sum[j]) + quarter_sin * mixed
            along = courant * along
            p_new.append((twice_p - p_old[j]) + (gain_p * across + along))
            q_new.append((twice_q - q_old[j]) + (gain_q * across + along))
        put(row, jnp.concatenate(p_new, 1), jnp.concatenate(q_new, 1))
        p_back, p_here, p_back_d, p_here_d, p_sum = p_here, p_next, p_here_d, p_next_d, p_next_sum
        q_back, q_here, q_back_d, q_here_d, q_sum = q_here, q_next, q_here_d, q_next_d, q_next_sum


class CoefficientRows:
    def __init__(self, ref, shots):
        self.shots, (_, self.along, self.rows, lanes) = shots, ref.shape
        self.flat = ref.reshape(ref.shape[0] * self.along * self.rows, lanes)

    def __call__(self, index, row, j):
        place = (index * self.along + j) * self.rows + row
        return self.flat[pl.ds(place, self.shots, stride=0), :]


def split_bf16(values):
    high = values.astype(jnp.bfloat16)
    low = (values - high.astype(jnp.float32)).astype(jnp.bfloat16)
    return high, low


def outer_kernel(*refs):
    sources, outs, (field_ref, param_ref, field_sem, param_sem) = refs[:8], refs[8:10], refs[10:]
    shots, across, along, tile, lanes = sources[0].shape
    depth = along * lanes
    copies = []
    for side in range(2):
        place = side * (across - 1)
        for i in range(4):
            copies.append(
                pltpu.make_async_copy(
                    sources[i].at[:, pl.ds(place, 1), :, pl.ds(side * STEPS, STEPS)],
                    field_ref.at[side, i, :, :, :, pl.ds(side * STEPS, STEPS)],
                    field_sem.at[side, i],
                )
            )
        for i in range(4):
            copies.append(
                pltpu.make_async_copy(
                    sources[4 + i].at[pl.ds(place * tile, tile)],
                    param_ref.at[side, i],
                    param_sem.at[side, i],
                )
            )
    for copy in copies:
        copy.start()
    for side in range(2):
        for copy in copies[8 * side : 8 * side + 8]:
            copy.wait()
        views = [ShotRows(field_ref.at[side, i]) for i in range(4)]
        out = outs[side]

        def row(field, distance):
            place = distance if side == 0 else tile - 1 - distance
            return views[field][place]

        position = 0

        def put(first, second):
            nonlocal position
            out[pl.ds(position, 2 * shots), :] = jnp.concatenate([first, second], 0).astype(
                jnp.bfloat16
            )
            position += 2 * shots

        for field in range(4):
            near = row(field, 0)
            put(near, near - near.astype(jnp.bfloat16).astype(jnp.float32))
        for first, second in far_items():
            put(row(*first), row(*second))
        terms = tilt_coefficients(*[param_ref[side, i] for i in range(4)])
        rows = []
        for index, term in enumerate(terms):
            term = -term if index == 1 and side == 0 else term
            for distance in reversed(range(STEPS - 1)):
                place = distance if side == 0 else tile - 1 - distance
                rows.append(term[place : place + 1, :])
        while len(rows) < 2 * shots:
            rows.append(jnp.zeros((1, depth), jnp.float32))
        out[pl.ds(position, 2 * shots), :] = jnp.concatenate(rows, 0).astype(jnp.bfloat16)


def far_items():
    items = []
    for field in range(2):
        items += [(field, distance) for distance in range(1, STEPS)]
    for field in range(2, 4):
        items += [(field, distance) for distance in range(1, STEPS - 1)]
    return list(zip(items[0::2], items[1::2]))


def outer_rows(fields, params):
    shots, across, along, tile, lanes = fields[0].shape
    depth = along * lanes
    rows = 2 * shots * (4 + len(far_items()) + 1)
    shape = jax.ShapeDtypeStruct((rows, depth), jnp.bfloat16)
    return pl.pallas_call(
        outer_kernel,
        in_specs=[pl.BlockSpec(memory_space=pltpu.HBM)] * 8,
        out_specs=[pl.BlockSpec(memory_space=pltpu.VMEM)] * 2,
        out_shape=[shape, shape],
        scratch_shapes=[
            pltpu.VMEM((2, 4, shots, 1, along, tile, lanes), jnp.float32),
            pltpu.VMEM((2, 4, tile, depth), jnp.float32),
            pltpu.SemaphoreType.DMA((2, 4)),
            pltpu.SemaphoreType.DMA((2, 4)),
        ],
        compiler_params=compiler_params(60),
        name="outer_rows",
    )(*fields, *params)


def partner(me, k, count):
    if count & (count - 1):
        return (me + k) % count
    return me ^ k


def sample_rows(values, one_hot):
    high, low = split_bf16(values)
    return jnp.dot(jnp.concatenate([high, low], 1), one_hot, preferred_element_type=jnp.float32)


def interior_kernel(
    p_ref,
    q_ref,
    pp_ref,
    qq_ref,
    courant_ref,
    epsilon_ref,
    delta_ref,
    tilt_ref,
    cells_ref,
    lists_ref,
    edge_ref,
    prior_edge_ref,
    coef_edge_ref,
    p_inner_ref,
    q_inner_ref,
    sample_ref,
    depth_hot_ref,
    column_ref,
    list_hot_ref,
    level_ref,
    coef_ref,
    split_ref,
):
    shots = p_ref.shape[0]
    width, depth = courant_ref.shape
    along = depth // LANES
    p_rows, q_rows, pp_rows, qq_rows = [ShotRows(ref) for ref in (p_ref, q_ref, pp_ref, qq_ref)]

    @pl.loop(0, width, unroll=4)
    def _(x):
        level_ref[0, 0, x] = p_rows[x]
        level_ref[0, 1, x] = q_rows[x]

    terms = tilt_coefficients(courant_ref[...], epsilon_ref[...], delta_ref[...], tilt_ref[...])
    for index, term in enumerate(terms):
        for j in range(along):
            coef_ref[index, j] = term[:, j * LANES : (j + 1) * LANES]
        for k in range(STEPS):
            coef_edge_ref[0, index, pl.ds(k, 1), :] = term[k : k + 1, :]
            row = term[width - 1 - k : width - k, :]
            coef_edge_ref[1, index, pl.ds(k, 1), :] = -row if index == 1 else row

    one, zero = jnp.bfloat16(1), jnp.bfloat16(0)
    cells = cells_ref[...]
    column = cells // depth
    column_ref[...] = column
    targets = cells.shape[1]
    z_of = jnp.broadcast_to(cells - column * depth, (16, targets)).astype(jnp.int16)
    places = lax.broadcasted_iota(jnp.int16, (16, targets), 0)
    for base in range(0, depth, 16):
        hot = jnp.where(places + jnp.int16(base) == z_of, one, zero)
        depth_hot_ref[pl.ds(base, 16), :] = hot
        depth_hot_ref[pl.ds(depth + base, 16), :] = hot

    owners, slots, patch = lists_ref.shape[1:]
    me = lax.axis_index("shot")
    rows = []
    for k in range(owners):
        lists = lists_ref[0, partner(me, k, owners)]
        rows += [lists[s : s + 1, :] for s in range(slots)]
    count = len(rows)
    while len(rows) % 8:
        rows.append(rows[0])
    upright = jnp.transpose(jnp.concatenate(rows, 0).astype(jnp.float32)).astype(jnp.int32)
    lanes = lax.broadcasted_iota(jnp.int16, (patch, LANES), 1)
    for k in range(count):
        wanted = jnp.broadcast_to(upright[:, k : k + 1], (patch, LANES)).astype(jnp.int16)
        for base in range(0, targets, LANES):
            list_hot_ref[pl.ds(k * patch, patch), pl.ds(base, LANES)] = jnp.where(
                lanes + jnp.int16(base) == wanted, one, zero
            )

    for side in range(2):
        x = 0 if side == 0 else width - 1
        prior_edge_ref[side, 0] = pp_rows[x]
        prior_edge_ref[side, 1] = qq_rows[x]

    coefficients = CoefficientRows(coef_ref, shots)
    offsets = [0]
    for step in range(1, STEPS + 1):
        low, high = step, width - step
        chunk = 8 if (high - low) % 8 == 0 else 10
        offset = offsets[-1]
        offsets.append(offset + high - low)

        @pl.loop(0, -(-(high - low) // chunk))
        def _(index):
            at = jnp.minimum(chunk * index, high - low - chunk)
            start = low + at
            held = []

            def put(r, p_new, q_new):
                if step < STEPS:
                    level_ref[step, 0, start + r] = p_new
                    level_ref[step, 1, start + r] = q_new
                else:
                    p_inner_ref[at + r] = p_new
                    q_inner_ref[at + r] = q_new
                held.append(p_new)
                if len(held) == 2:
                    first, rest = split_bf16(jnp.concatenate(held, 0))
                    place = pl.multiple_of((offset + at + r - 1) * shots, 2 * shots)
                    split_ref[pl.ds(place, 2 * shots), pl.ds(0, depth)] = first
                    split_ref[pl.ds(place, 2 * shots), pl.ds(depth, depth)] = rest
                    held.clear()

            advance(
                chunk,
                lambda r: level_ref[step - 1, 0, start + r],
                lambda r: level_ref[step - 1, 1, start + r],
                lambda r: pp_rows[start + r] if step == 1 else level_ref[step - 2, 0, start + r],
                lambda r: qq_rows[start + r] if step == 1 else level_ref[step - 2, 1, start + r],
                lambda i, r, j: coefficients(i, start + r, j),
                put,
            )

    for step in range(STEPS):
        for field in range(2):
            for near in range(2):
                edge_ref[0, field, step, near] = level_ref[step, field, step + near]
                edge_ref[1, field, step, near] = level_ref[step, field, width - 1 - step - near]

    found = jnp.dot(split_ref[...], depth_hot_ref[...], preferred_element_type=jnp.float32)
    totals = [jnp.zeros((shots, targets), jnp.float32) for _ in range(STEPS)]
    for x in range(1, width - 1):
        here = column == x
        for step in range(1, STEPS + 1):
            if step <= x < width - step:
                row = (offsets[step - 1] + x - step) * shots
                totals[step - 1] += jnp.where(here, found[row : row + shots], 0.0)
    for step in range(STEPS):
        sample_ref[step] = totals[step]


def interior(fields, params, target_cells, patch_lists):
    shots = fields[0].shape[0]
    width, depth = params[0].shape
    targets = target_cells.shape[0]
    _, owners, slots, patch = patch_lists.shape
    f32 = functools.partial(jax.ShapeDtypeStruct, dtype=jnp.float32)
    out_shape = [
        f32((2, 2, STEPS, 2, shots, depth)),
        f32((2, 2, shots, depth)),
        f32((2, 5, 8, depth)),
        f32((width - 2 * STEPS, shots, depth)),
        f32((width - 2 * STEPS, shots, depth)),
        f32((STEPS, shots, targets)),
        jax.ShapeDtypeStruct((2 * depth, targets), jnp.bfloat16),
        jax.ShapeDtypeStruct((1, targets), jnp.int32),
        jax.ShapeDtypeStruct((owners * slots * patch, targets), jnp.bfloat16),
    ]
    vmem = pl.BlockSpec(memory_space=pltpu.VMEM)
    return pl.pallas_call(
        interior_kernel,
        in_specs=[vmem] * 10,
        out_specs=[vmem] * len(out_shape),
        out_shape=out_shape,
        scratch_shapes=[
            pltpu.VMEM((STEPS, 2, width, shots, depth), jnp.float32),
            pltpu.VMEM((5, depth // LANES, width, LANES), jnp.float32),
            pltpu.VMEM((STEPS * (width - STEPS - 1) * shots, 2 * depth), jnp.bfloat16),
        ],
        compiler_params=compiler_params(40),
        cost_estimate=pl.CostEstimate(
            flops=200 * STEPS * shots * width * depth, bytes_accessed=8 * MIB, transcendentals=0
        ),
        name="interior",
    )(*fields, *params, target_cells.reshape(1, targets), patch_lists)


def finish_kernel(
    lower_ref,
    upper_ref,
    edge_ref,
    prior_edge_ref,
    coef_edge_ref,
    sample_ref,
    depth_hot_ref,
    column_ref,
    list_hot_ref,
    spectra_ref,
    table_ref,
    spectra_out_ref,
    final_ref,
    *rest,
    width,
):
    packed_refs = rest[:-6]
    level_ref, prior_ref, coef_ref, feature_ref, out_ref, out_sem = rest[-6:]
    shots, depth = edge_ref.shape[-2:]
    targets = column_ref.shape[1]
    first = -STEPS
    pair = 2 * shots
    for side, ref in enumerate((lower_ref, upper_ref)):
        for field in range(4):
            both = ref[pl.ds(field * pair, pair), :].astype(jnp.float32)
            value = both[:shots] + both[shots:]
            if field < 2:
                level_ref[side, field, 0, -1 - first] = value
            else:
                prior_ref[side, field - 2, -1 - (1 - STEPS)] = value
        for index, items in enumerate(far_items()):
            both = ref[pl.ds((4 + index) * pair, pair), :].astype(jnp.float32)
            for half, (field, distance) in enumerate(items):
                value = both[half * shots : (half + 1) * shots]
                if field < 2:
                    level_ref[side, field, 0, -1 - distance - first] = value
                else:
                    prior_ref[side, field - 2, -1 - distance - (1 - STEPS)] = value
        params = ref[pl.ds((4 + len(far_items())) * pair, pair), :].astype(jnp.float32)
        for index in range(5):
            far = params[index * (STEPS - 1) : (index + 1) * (STEPS - 1)]
            near = coef_edge_ref[side, index, pl.ds(0, STEPS), :]
            for j in range(depth // LANES):
                coef_ref[side, index, j, pl.ds(0, STEPS - 1), :] = far[:, j * LANES : (j + 1) * LANES]
                coef_ref[side, index, j, pl.ds(STEPS - 1, STEPS), :] = near[
                    :, j * LANES : (j + 1) * LANES
                ]
        for field in range(2):
            prior_ref[side, field, STEPS - 1] = prior_edge_ref[side, field]
            for step in range(STEPS):
                for near in range(2):
                    level_ref[side, field, step, step + near - first] = edge_ref[
                        side, field, step, near
                    ]

    for step in range(1, STEPS + 1):
        low = step - STEPS

        for side in range(2):
            coefficients = CoefficientRows(coef_ref.at[side], shots)

            def prior(field):
                if step == 1:
                    return lambda r: prior_ref[side, field, low + r - (1 - STEPS)]
                return lambda r: level_ref[side, field, step - 2, low + r - first]

            def put(r, p_new, q_new):
                if step < STEPS:
                    level_ref[side, 0, step, low + r - first] = p_new
                    level_ref[side, 1, step, low + r - first] = q_new
                else:
                    final_ref[side, 0, r] = p_new
                    final_ref[side, 1, r] = q_new

            advance(
                STEPS,
                lambda r: level_ref[side, 0, step - 1, low + r - first],
                lambda r: level_ref[side, 1, step - 1, low + r - first],
                prior(0),
                prior(1),
                lambda i, r, j: coefficients(i, low + r - (1 - STEPS), j),
                put,
            )

    column = column_ref[...]
    places, values = [], []
    for step in range(1, STEPS + 1):
        for side in range(2):
            for k in range(step):
                places.append((step, k if side == 0 else width - 1 - k))
                if step < STEPS:
                    values.append(level_ref[side, 0, step, k - first])
                else:
                    values.append(final_ref[side, 0, k])
    found = sample_rows(jnp.concatenate(values, 0), depth_hot_ref[...])
    samples = [sample_ref[step] for step in range(STEPS)]
    for index, (step, x) in enumerate(places):
        samples[step - 1] = samples[step - 1] + jnp.where(
            column == x, found[index * shots : (index + 1) * shots], 0.0
        )

    parts = spectra_ref.shape[0] // shots
    lanes = table_ref.shape[-1]
    for s in range(shots):
        for base in range(0, targets, lanes):
            value = spectra_ref[pl.ds(s * parts, parts), pl.ds(base, lanes)]
            for step in range(STEPS):
                value = value + table_ref[step] * samples[step][s : s + 1, base : base + lanes]
            out_ref[pl.ds(s * parts, parts), pl.ds(base, lanes)] = value
            feature_ref[pl.ds(s * parts, parts), pl.ds(base, lanes)] = value.astype(jnp.bfloat16)

    out_copy = pltpu.make_async_copy(out_ref, spectra_out_ref, out_sem)
    out_copy.start()

    owners = len(packed_refs)
    patch = packed_refs[0].shape[1]
    slots = list_hot_ref.shape[0] // (owners * patch)
    half = patch // 2
    row = lax.broadcasted_iota(jnp.int32, (half, patch), 0)
    lane = lax.broadcasted_iota(jnp.int32, (half, patch), 1)
    from_last = (lane < half) & (row > lane)
    for g, packed_ref in enumerate(packed_refs):
        chosen = lax.dot_general(
            list_hot_ref[pl.ds(g * slots * patch, slots * patch), :],
            feature_ref[...],
            NT,
            preferred_element_type=jnp.float32,
        ).astype(jnp.bfloat16)
        diagonals = []
        for s in range(slots):
            mine = chosen[s * patch : (s + 1) * patch]
            gram = lax.dot_general(mine, mine, NT, preferred_element_type=jnp.float32)
            last = pltpu.roll(gram[half:], half, 1)
            packed_ref[pl.ds(s * half, half), :] = jnp.where(from_last, last, gram[:half])
            diagonals.append(jnp.sum(jnp.where(row == lane, last, 0.0), 0, keepdims=True))
        while len(diagonals) % 8:
            diagonals.append(jnp.zeros((1, patch), jnp.float32))
        packed_ref[pl.ds(slots * half, len(diagonals)), :] = jnp.concatenate(diagonals, 0)
    out_copy.wait()


def finish(lower, upper, inner, spectra, table, width, owners, slots, patch):
    edge, prior_edge, coef_edge, sample, depth_hot, column, list_hot = inner
    shots, depth = edge.shape[-2:]
    targets = column.shape[1]
    features = spectra.shape[0]
    f32 = functools.partial(jax.ShapeDtypeStruct, dtype=jnp.float32)
    rows = slots * (patch // 2) + -(-slots // 8) * 8
    out_shape = [
        f32((features, targets)),
        f32((2, 2, STEPS, shots, depth)),
        *[f32((rows, patch))] * owners,
    ]
    vmem = pl.BlockSpec(memory_space=pltpu.VMEM)
    return pl.pallas_call(
        functools.partial(finish_kernel, width=width),
        in_specs=[vmem] * 11,
        out_specs=[pl.BlockSpec(memory_space=pl.ANY)] + [vmem] * (len(out_shape) - 1),
        out_shape=out_shape,
        scratch_shapes=[
            pltpu.VMEM((2, 2, STEPS, 2 * STEPS + 1, shots, depth), jnp.float32),
            pltpu.VMEM((2, 2, STEPS, shots, depth), jnp.float32),
            pltpu.VMEM((2, 5, depth // LANES, 2 * STEPS, LANES), jnp.float32),
            pltpu.VMEM((features, targets), jnp.bfloat16),
            pltpu.VMEM((features, targets), jnp.float32),
            pltpu.SemaphoreType.DMA,
        ],
        compiler_params=compiler_params(40),
        name="finish",
    )(
        lower,
        upper,
        edge,
        prior_edge,
        coef_edge,
        sample,
        depth_hot,
        column,
        list_hot,
        spectra,
        table,
    )


def assemble_kernel(p_inner_ref, q_inner_ref, final_ref, p_out_ref, q_out_ref):
    width = p_out_ref.shape[1] * TILE
    for field, (inner, out) in enumerate(((p_inner_ref, p_out_ref), (q_inner_ref, q_out_ref))):
        rows = ShotRows(out)
        for k in range(STEPS):
            rows[k] = final_ref[0, field, k]
            rows[width - 1 - k] = final_ref[1, field, k]

        @pl.loop(STEPS, width - STEPS, unroll=4)
        def _(x):
            rows[x] = inner[x - STEPS]


def assemble(p_inner, q_inner, final):
    inner, shots, depth = p_inner.shape
    across, along = (inner + 2 * STEPS) // TILE, depth // LANES
    shape = jax.ShapeDtypeStruct((shots, across, along, TILE, LANES), jnp.float32)
    vmem = pl.BlockSpec(memory_space=pltpu.VMEM)
    return pl.pallas_call(
        assemble_kernel,
        in_specs=[vmem] * 3,
        out_specs=[vmem] * 2,
        out_shape=[shape, shape],
        compiler_params=compiler_params(16),
        cost_estimate=pl.CostEstimate(flops=8 * MIB, bytes_accessed=4 * MIB, transcendentals=0),
        name="assemble",
    )(p_inner, q_inner, final)


def tiles_kernel(counts_ref, *refs, features):
    received, out_ref = refs[:-1], refs[-1]
    slots, patch = out_ref.shape[2], out_ref.shape[3]
    half = patch // 2
    row = lax.broadcasted_iota(jnp.int32, (half, patch), 0)
    lane = lax.broadcasted_iota(jnp.int32, (half, patch), 1)
    live = counts_ref[0, 0]
    total = received[0][...]
    for ref in received[1:]:
        total = total + ref[...]
    for s in range(slots):
        scale = jnp.where(s < live, 1.0 / features, 0.0)
        packed = total[s * half : (s + 1) * half] * scale
        diagonal = total[slots * half + s : slots * half + s + 1] * scale
        turned = jnp.transpose(jnp.concatenate([packed, packed], 0))
        flipped = turned[:half]
        corner = turned[half:]
        out_ref[0, 0, s, pl.ds(0, half), :] = jnp.where(
            (lane < half) & (row > lane), flipped, packed
        )
        last = jnp.where(row > lane, packed, jnp.where(row == lane, diagonal, flipped))
        out_ref[0, 0, s, pl.ds(half, half), :] = jnp.where(
            lane < half, corner, pltpu.roll(last, half, 1)
        )


def tiles(received, patch_counts, slots, features):
    patch = received[0].shape[1]
    return pl.pallas_call(
        functools.partial(tiles_kernel, features=features),
        in_specs=[pl.BlockSpec(memory_space=pltpu.SMEM)]
        + [pl.BlockSpec(memory_space=pltpu.VMEM)] * len(received),
        out_specs=pl.BlockSpec(memory_space=pltpu.VMEM),
        out_shape=jax.ShapeDtypeStruct((1, 1, slots, patch, patch), jnp.float32),
        compiler_params=compiler_params(16),
        name="tiles",
    )(patch_counts, *received)


def shards(
    pressure,
    auxiliary,
    pressure_prior,
    auxiliary_prior,
    courant_sq,
    thomsen_epsilon,
    thomsen_delta,
    tilt_angle,
    frequencies,
    spectra,
    target_cells,
    patch_lists,
    patch_counts,
):
    shots, width, depth = pressure.shape
    _, owners, slots, patch = patch_lists.shape
    fields = [tiled(item) for item in (pressure, auxiliary, pressure_prior, auxiliary_prior)]
    params = (courant_sq, thomsen_epsilon, thomsen_delta, tilt_angle)
    parts, targets = spectra.shape[1:]

    first_rows, last_rows = outer_rows(fields, params)
    bricks = lax.axis_size("brick")
    upward = [(i, i + 1) for i in range(bricks - 1)]
    downward = [(i + 1, i) for i in range(bricks - 1)]
    lower = lax.ppermute(last_rows, "brick", upward)
    upper = lax.ppermute(first_rows, "brick", downward)

    moments = jnp.arange(1, STEPS + 1, dtype=jnp.float32)
    angle = frequencies[None, :] * moments[:, None]
    table = jnp.concatenate([jnp.cos(angle), -jnp.sin(angle)], 1)
    table = jnp.broadcast_to(table[:, :, None], (STEPS, parts, 128))

    edge, prior_edge, coef_edge, p_inner, q_inner, sample, depth_hot, column, list_hot = interior(
        fields, params, target_cells, patch_lists
    )
    spectra_out, final, *packed = finish(
        lower,
        upper,
        (edge, prior_edge, coef_edge, sample, depth_hot, column, list_hot),
        spectra.reshape(shots * parts, targets),
        table,
        width,
        owners,
        slots,
        patch,
    )
    received = packed[:1]
    for k in sorted(range(1, owners), key=lambda k: (k < owners // 2, k)):
        pairs = [(i, int(partner(i, k, owners))) for i in range(owners)]
        received.append(lax.ppermute(packed[k], "shot", pairs))
    pressure_out, auxiliary_out = [untiled(item) for item in assemble(p_inner, q_inner, final)]
    gram_tiles = tiles(received, patch_counts, slots, shots * parts * owners)
    return (pressure_out, auxiliary_out, spectra_out.reshape(spectra.shape), gram_tiles)


def solution(mesh):
    return jax.shard_map(
        shards,
        mesh=mesh,
        in_specs=(
            P("shot", "brick", None),
            P("shot", "brick", None),
            P("shot", "brick", None),
            P("shot", "brick", None),
            P("brick", None),
            P("brick", None),
            P("brick", None),
            P("brick", None),
            P(),
            P("shot", None, "brick"),
            P("brick"),
            P("brick", None, None, None),
            P("brick", "shot"),
        ),
        out_specs=(
            P("shot", "brick", None),
            P("shot", "brick", None),
            P("shot", None, "brick"),
            P("brick", "shot", None, None, None),
        ),
        check_vma=False,
    )
```

```python
import functools
import math

import jax
import jax.numpy as jnp
from jax import lax
from jax.experimental import pallas as pl
from jax.experimental.pallas import tpu as pltpu
from jax.sharding import PartitionSpec as P

STEPS = 4
MIB = 1024 * 1024
NT = (((1,), (1,)), ((), ()))


TILE = 8
LANES = 128


def tiled(field):
    shots, width, depth = field.shape
    parts = field.reshape(shots, width // TILE, TILE, depth // LANES, LANES)
    return parts.transpose(0, 1, 3, 2, 4)


def untiled(parts):
    shots, across, along, tile, lanes = parts.shape
    return parts.transpose(0, 1, 3, 2, 4).reshape(shots, across * tile, along * lanes)


class ShotRows:
    def __init__(self, ref):
        self.shots, self.across, self.along, tile, lanes = ref.shape
        self.stride = self.across * self.along * tile
        self.flat = ref.reshape(self.shots * self.stride, lanes)

    def place(self, x, j):
        if isinstance(x, int):
            start = (x // TILE * self.along + j) * TILE + x % TILE
        else:
            start = (lax.div(x, TILE) * self.along + j) * TILE + lax.rem(x, TILE)
        return pl.ds(start, self.shots, stride=self.stride)

    def __getitem__(self, x):
        return jnp.concatenate([self.flat[self.place(x, j), :] for j in range(self.along)], 1)

    def __setitem__(self, x, row):
        for j in range(self.along):
            self.flat[self.place(x, j), :] = row[:, j * LANES : (j + 1) * LANES]


def compiler_params(mib):
    return pltpu.CompilerParams(vmem_limit_bytes=mib * MIB)


def tilt_coefficients(courant, epsilon, delta, tilt):
    turns = jnp.round(tilt * (2.0 / math.pi))
    rest = (tilt - turns * 1.5703125) - turns * (math.pi / 2 - 1.5703125)
    odd = turns - 2.0 * jnp.floor(turns * 0.5)
    sign = 1.0 - 2.0 * odd
    double = 2.0 * rest
    square = double * double
    sine = double * (
        1.0
        + square
        * (
            -1.0 / 6
            + square
            * (1.0 / 120 + square * (-1.0 / 5040 + square * (1.0 / 362880 - square / 39916800.0)))
        )
    )
    versine = square * (
        0.5
        + square
        * (
            -1.0 / 24
            + square
            * (1.0 / 720 + square * (-1.0 / 40320 + square * (1.0 / 3628800 - square / 479001600.0)))
        )
    )
    sine_sq = jnp.where(odd > 0.5, 1.0 - 0.5 * versine, 0.5 * versine)
    quarter_sin = 0.25 * sign * sine
    gain_p = courant * (1.0 + 2.0 * epsilon)
    gain_q = courant * (1.0 + 2.0 * delta)
    return sine_sq, quarter_sin, courant, gain_p, gain_q


def blocks(row):
    return [row[:, j : j + LANES] for j in range(0, row.shape[1], LANES)]


def depth_terms(row):
    lane = lax.broadcasted_iota(jnp.int32, row[0].shape, 1)
    shallow = [pltpu.roll(block, 1, 1) for block in row]
    deep = [pltpu.roll(block, LANES - 1, 1) for block in row]
    outside = jnp.zeros_like(row[0])
    sums, differences = [], []
    for j in range(len(row)):
        above = jnp.where(lane == 0, shallow[j - 1] if j else outside, shallow[j])
        below = jnp.where(
            lane == LANES - 1, deep[j + 1] if j + 1 < len(row) else outside, deep[j]
        )
        sums.append(below + above)
        differences.append(below - above)
    return sums, differences


def advance(count, p_row, q_row, p_prior, q_prior, coefficient, put):
    p_back, p_here = blocks(p_row(-1)), blocks(p_row(0))
    q_back, q_here = blocks(q_row(-1)), blocks(q_row(0))
    _, p_back_d = depth_terms(p_back)
    _, q_back_d = depth_terms(q_back)
    p_sum, p_here_d = depth_terms(p_here)
    q_sum, q_here_d = depth_terms(q_here)
    for row in range(count):
        p_next, q_next = blocks(p_row(row + 1)), blocks(q_row(row + 1))
        p_next_sum, p_next_d = depth_terms(p_next)
        q_next_sum, q_next_d = depth_terms(q_next)
        p_old, q_old = blocks(p_prior(row)), blocks(q_prior(row))
        p_new, q_new = [], []
        for j in range(len(p_here)):
            sine_sq, quarter_sin, courant, gain_p, gain_q = [coefficient(i, row, j) for i in range(5)]
            twice_p, twice_q = p_here[j] + p_here[j], q_here[j] + q_here[j]
            side = p_next[j] + p_back[j]
            mixed = p_next_d[j] - p_back_d[j]
            across = (side - twice_p) + sine_sq * (p_sum[j] - side) - quarter_sin * mixed
            side = q_next[j] + q_back[j]
            mixed = q_next_d[j] - q_back_d[j]
            along = (q_sum[j] - twice_q) + sine_sq * (side - q_sum[j]) + quarter_sin * mixed
            along = courant * along
            p_new.append((twice_p - p_old[j]) + (gain_p * across + along))
            q_new.append((twice_q - q_old[j]) + (gain_q * across + along))
        put(row, jnp.concatenate(p_new, 1), jnp.concatenate(q_new, 1))
        p_back, p_here, p_back_d, p_here_d, p_sum = p_here, p_next, p_here_d, p_next_d, p_next_sum
        q_back, q_here, q_back_d, q_here_d, q_sum = q_here, q_next, q_here_d, q_next_d, q_next_sum


class CoefficientRows:
    def __init__(self, ref, shots):
        self.shots, (_, self.along, self.rows, lanes) = shots, ref.shape
        self.flat = ref.reshape(ref.shape[0] * self.along * self.rows, lanes)

    def __call__(self, index, row, j):
        place = (index * self.along + j) * self.rows + row
        return self.flat[pl.ds(place, self.shots, stride=0), :]


def split_bf16(values):
    high = values.astype(jnp.bfloat16)
    low = (values - high.astype(jnp.float32)).astype(jnp.bfloat16)
    return high, low


def outer_kernel(*refs):
    sources, outs, (field_ref, param_ref, field_sem, param_sem) = refs[:8], refs[8:10], refs[10:]
    shots, across, along, tile, lanes = sources[0].shape
    depth = along * lanes
    copies = []
    for side in range(2):
        place = side * (across - 1)
        for i in range(4):
            copies.append(
                pltpu.make_async_copy(
                    sources[i].at[:, pl.ds(place, 1), :, pl.ds(side * STEPS, STEPS)],
                    field_ref.at[side, i, :, :, :, pl.ds(side * STEPS, STEPS)],
                    field_sem.at[side, i],
                )
            )
        for i in range(4):
            copies.append(
                pltpu.make_async_copy(
                    sources[4 + i].at[pl.ds(place * tile, tile)],
                    param_ref.at[side, i],
                    param_sem.at[side, i],
                )
            )
    for copy in copies:
        copy.start()
    tiles_by_side = []
    for side in range(2):
        for copy in copies[8 * side : 8 * side + 8]:
            copy.wait()
        terms = tilt_coefficients(*[param_ref[side, i] for i in range(4)])
        rows = []
        for index, term in enumerate(terms):
            term = -term if index == 1 and side == 0 else term
            for distance in reversed(range(STEPS - 1)):
                place = distance if side == 0 else tile - 1 - distance
                rows.append(term[place : place + 1, :])
        while len(rows) < 2 * shots:
            rows.append(jnp.zeros((1, depth), jnp.float32))
        tiles_by_side.append(jnp.concatenate(rows, 0))

    stride = along * tile
    flat = field_ref.reshape(2 * 4 * shots * stride, lanes)
    for turn in range(2):
        side = outer_side(turn)
        out = outs[turn]

        def row(field, distance):
            base = (side * 4 + field) * shots * stride + distance + side * (tile - 1 - 2 * distance)
            return jnp.concatenate(
                [flat[pl.ds(base + j * tile, shots, stride=stride), :] for j in range(along)], 1
            )

        position = 0

        def put(first, second):
            nonlocal position
            out[pl.ds(position, 2 * shots), :] = jnp.concatenate([first, second], 0).astype(
                jnp.bfloat16
            )
            position += 2 * shots

        for field in range(4):
            near = row(field, 0)
            put(near, near - near.astype(jnp.bfloat16).astype(jnp.float32))
        for first, second in far_items():
            put(row(*first), row(*second))
        out[pl.ds(position, 2 * shots), :] = jnp.where(
            side == 1, tiles_by_side[1], tiles_by_side[0]
        ).astype(jnp.bfloat16)


def outer_side(turn):
    return jnp.where(lax.axis_index("brick") % 2 == turn, 1, 0)


def far_items():
    items = []
    for field in range(2):
        items += [(field, distance) for distance in range(1, STEPS)]
    for field in range(2, 4):
        items += [(field, distance) for distance in range(1, STEPS - 1)]
    return list(zip(items[0::2], items[1::2]))


def outer_rows(fields, params):
    shots, across, along, tile, lanes = fields[0].shape
    depth = along * lanes
    rows = 2 * shots * (4 + len(far_items()) + 1)
    shape = jax.ShapeDtypeStruct((rows, depth), jnp.bfloat16)
    return pl.pallas_call(
        outer_kernel,
        in_specs=[pl.BlockSpec(memory_space=pltpu.HBM)] * 8,
        out_specs=[pl.BlockSpec(memory_space=pltpu.VMEM)] * 2,
        out_shape=[shape, shape],
        scratch_shapes=[
            pltpu.VMEM((2, 4, shots, 1, along, tile, lanes), jnp.float32),
            pltpu.VMEM((2, 4, tile, depth), jnp.float32),
            pltpu.SemaphoreType.DMA((2, 4)),
            pltpu.SemaphoreType.DMA((2, 4)),
        ],
        compiler_params=compiler_params(60),
        name="outer_rows",
    )(*fields, *params)


def partner(me, k, count):
    if count & (count - 1):
        return (me + k) % count
    return me ^ k


def sample_rows(values, one_hot):
    high, low = split_bf16(values)
    return jnp.dot(jnp.concatenate([high, low], 1), one_hot, preferred_element_type=jnp.float32)


def interior_kernel(
    p_ref,
    q_ref,
    pp_ref,
    qq_ref,
    courant_ref,
    epsilon_ref,
    delta_ref,
    tilt_ref,
    cells_ref,
    lists_ref,
    edge_ref,
    prior_edge_ref,
    coef_edge_ref,
    p_inner_ref,
    q_inner_ref,
    sample_ref,
    depth_hot_ref,
    column_ref,
    list_hot_ref,
    level_ref,
    coef_ref,
    split_ref,
):
    shots = p_ref.shape[0]
    width, depth = courant_ref.shape
    along = depth // LANES
    p_rows, q_rows, pp_rows, qq_rows = [ShotRows(ref) for ref in (p_ref, q_ref, pp_ref, qq_ref)]

    @pl.loop(0, width, unroll=4)
    def _(x):
        level_ref[0, 0, x] = p_rows[x]
        level_ref[0, 1, x] = q_rows[x]

    terms = tilt_coefficients(courant_ref[...], epsilon_ref[...], delta_ref[...], tilt_ref[...])
    for index, term in enumerate(terms):
        for j in range(along):
            coef_ref[index, j] = term[:, j * LANES : (j + 1) * LANES]
        for k in range(STEPS):
            coef_edge_ref[0, index, pl.ds(k, 1), :] = term[k : k + 1, :]
            row = term[width - 1 - k : width - k, :]
            coef_edge_ref[1, index, pl.ds(k, 1), :] = -row if index == 1 else row

    one, zero = jnp.bfloat16(1), jnp.bfloat16(0)
    cells = cells_ref[...]
    column = cells // depth
    column_ref[...] = column
    targets = cells.shape[1]
    z_of = jnp.broadcast_to(cells - column * depth, (16, targets)).astype(jnp.int16)
    places = lax.broadcasted_iota(jnp.int16, (16, targets), 0)
    for base in range(0, depth, 16):
        hot = jnp.where(places + jnp.int16(base) == z_of, one, zero)
        depth_hot_ref[pl.ds(base, 16), :] = hot
        depth_hot_ref[pl.ds(depth + base, 16), :] = hot

    owners, slots, patch = lists_ref.shape[1:]
    me = lax.axis_index("shot")
    rows = []
    for k in range(owners):
        lists = lists_ref[0, partner(me, k, owners)]
        rows += [lists[s : s + 1, :] for s in range(slots)]
    count = len(rows)
    while len(rows) % 8:
        rows.append(rows[0])
    upright = jnp.transpose(jnp.concatenate(rows, 0).astype(jnp.float32)).astype(jnp.int32)
    lanes = lax.broadcasted_iota(jnp.int16, (patch, LANES), 1)
    for k in range(count):
        wanted = jnp.broadcast_to(upright[:, k : k + 1], (patch, LANES)).astype(jnp.int16)
        for base in range(0, targets, LANES):
            list_hot_ref[pl.ds(k * patch, patch), pl.ds(base, LANES)] = jnp.where(
                lanes + jnp.int16(base) == wanted, one, zero
            )

    for side in range(2):
        x = 0 if side == 0 else width - 1
        prior_edge_ref[side, 0] = pp_rows[x]
        prior_edge_ref[side, 1] = qq_rows[x]

    coefficients = CoefficientRows(coef_ref, shots)
    offsets = [0]
    for step in range(1, STEPS + 1):
        low, high = step, width - step
        chunk = 8 if (high - low) % 8 == 0 else 10
        offset = offsets[-1]
        offsets.append(offset + high - low)

        @pl.loop(0, -(-(high - low) // chunk))
        def _(index):
            at = jnp.minimum(chunk * index, high - low - chunk)
            start = low + at
            held = []

            def put(r, p_new, q_new):
                if step < STEPS:
                    level_ref[step, 0, start + r] = p_new
                    level_ref[step, 1, start + r] = q_new
                else:
                    p_inner_ref[at + r] = p_new
                    q_inner_ref[at + r] = q_new
                held.append(p_new)
                if len(held) == 2:
                    first, rest = split_bf16(jnp.concatenate(held, 0))
                    place = pl.multiple_of((offset + at + r - 1) * shots, 2 * shots)
                    split_ref[pl.ds(place, 2 * shots), pl.ds(0, depth)] = first
                    split_ref[pl.ds(place, 2 * shots), pl.ds(depth, depth)] = rest
                    held.clear()

            advance(
                chunk,
                lambda r: level_ref[step - 1, 0, start + r],
                lambda r: level_ref[step - 1, 1, start + r],
                lambda r: pp_rows[start + r] if step == 1 else level_ref[step - 2, 0, start + r],
                lambda r: qq_rows[start + r] if step == 1 else level_ref[step - 2, 1, start + r],
                lambda i, r, j: coefficients(i, start + r, j),
                put,
            )

    for step in range(STEPS):
        for field in range(2):
            for near in range(2):
                edge_ref[0, field, step, near] = level_ref[step, field, step + near]
                edge_ref[1, field, step, near] = level_ref[step, field, width - 1 - step - near]

    found = jnp.dot(split_ref[...], depth_hot_ref[...], preferred_element_type=jnp.float32)
    totals = [jnp.zeros((shots, targets), jnp.float32) for _ in range(STEPS)]
    for x in range(1, width - 1):
        here = column == x
        for step in range(1, STEPS + 1):
            if step <= x < width - step:
                row = (offsets[step - 1] + x - step) * shots
                totals[step - 1] += jnp.where(here, found[row : row + shots], 0.0)
    for step in range(STEPS):
        sample_ref[step] = totals[step]


def interior(fields, params, target_cells, patch_lists):
    shots = fields[0].shape[0]
    width, depth = params[0].shape
    targets = target_cells.shape[0]
    _, owners, slots, patch = patch_lists.shape
    f32 = functools.partial(jax.ShapeDtypeStruct, dtype=jnp.float32)
    out_shape = [
        f32((2, 2, STEPS, 2, shots, depth)),
        f32((2, 2, shots, depth)),
        f32((2, 5, 8, depth)),
        f32((width - 2 * STEPS, shots, depth)),
        f32((width - 2 * STEPS, shots, depth)),
        f32((STEPS, shots, targets)),
        jax.ShapeDtypeStruct((2 * depth, targets), jnp.bfloat16),
        jax.ShapeDtypeStruct((1, targets), jnp.int32),
        jax.ShapeDtypeStruct((owners * slots * patch, targets), jnp.bfloat16),
    ]
    vmem = pl.BlockSpec(memory_space=pltpu.VMEM)
    return pl.pallas_call(
        interior_kernel,
        in_specs=[vmem] * 10,
        out_specs=[vmem] * len(out_shape),
        out_shape=out_shape,
        scratch_shapes=[
            pltpu.VMEM((STEPS, 2, width, shots, depth), jnp.float32),
            pltpu.VMEM((5, depth // LANES, width, LANES), jnp.float32),
            pltpu.VMEM((STEPS * (width - STEPS - 1) * shots, 2 * depth), jnp.bfloat16),
        ],
        compiler_params=compiler_params(40),
        cost_estimate=pl.CostEstimate(
            flops=200 * STEPS * shots * width * depth, bytes_accessed=8 * MIB, transcendentals=0
        ),
        name="interior",
    )(*fields, *params, target_cells.reshape(1, targets), patch_lists)


def finish_kernel(
    even_ref,
    odd_ref,
    edge_ref,
    prior_edge_ref,
    coef_edge_ref,
    sample_ref,
    depth_hot_ref,
    column_ref,
    list_hot_ref,
    spectra_ref,
    table_ref,
    spectra_out_ref,
    final_ref,
    *rest,
    width,
):
    packed_refs = rest[:-6]
    level_ref, prior_ref, coef_ref, feature_ref, out_ref, out_sem = rest[-6:]
    shots, depth = edge_ref.shape[-2:]
    targets = column_ref.shape[1]
    first = -STEPS
    pair = 2 * shots
    for turn, ref in enumerate((even_ref, odd_ref)):
        side = outer_side(turn)
        for field in range(4):
            both = ref[pl.ds(field * pair, pair), :].astype(jnp.float32)
            value = both[:shots] + both[shots:]
            if field < 2:
                level_ref[side, field, 0, -1 - first] = value
            else:
                prior_ref[side, field - 2, -1 - (1 - STEPS)] = value
        for index, items in enumerate(far_items()):
            both = ref[pl.ds((4 + index) * pair, pair), :].astype(jnp.float32)
            for half, (field, distance) in enumerate(items):
                value = both[half * shots : (half + 1) * shots]
                if field < 2:
                    level_ref[side, field, 0, -1 - distance - first] = value
                else:
                    prior_ref[side, field - 2, -1 - distance - (1 - STEPS)] = value
        params = ref[pl.ds((4 + len(far_items())) * pair, pair), :].astype(jnp.float32)
        for index in range(5):
            far = params[index * (STEPS - 1) : (index + 1) * (STEPS - 1)]
            for j, block in enumerate(blocks(far)):
                coef_ref[side, index, j, pl.ds(0, STEPS - 1), :] = block
    for side in range(2):
        for index in range(5):
            near = coef_edge_ref[side, index, pl.ds(0, STEPS), :]
            for j, block in enumerate(blocks(near)):
                coef_ref[side, index, j, pl.ds(STEPS - 1, STEPS), :] = block
        for field in range(2):
            prior_ref[side, field, STEPS - 1] = prior_edge_ref[side, field]
            for step in range(STEPS):
                for near in range(2):
                    level_ref[side, field, step, step + near - first] = edge_ref[
                        side, field, step, near
                    ]

    for step in range(1, STEPS + 1):
        low = step - STEPS

        for side in range(2):
            coefficients = CoefficientRows(coef_ref.at[side], shots)

            def prior(field):
                if step == 1:
                    return lambda r: prior_ref[side, field, low + r - (1 - STEPS)]
                return lambda r: level_ref[side, field, step - 2, low + r - first]

            def put(r, p_new, q_new):
                if step < STEPS:
                    level_ref[side, 0, step, low + r - first] = p_new
                    level_ref[side, 1, step, low + r - first] = q_new
                else:
                    final_ref[side, 0, r] = p_new
                    final_ref[side, 1, r] = q_new

            advance(
                STEPS,
                lambda r: level_ref[side, 0, step - 1, low + r - first],
                lambda r: level_ref[side, 1, step - 1, low + r - first],
                prior(0),
                prior(1),
                lambda i, r, j: coefficients(i, low + r - (1 - STEPS), j),
                put,
            )

    column = column_ref[...]
    places, values = [], []
    for step in range(1, STEPS + 1):
        for side in range(2):
            for k in range(step):
                places.append((step, k if side == 0 else width - 1 - k))
                if step < STEPS:
                    values.append(level_ref[side, 0, step, k - first])
                else:
                    values.append(final_ref[side, 0, k])
    found = sample_rows(jnp.concatenate(values, 0), depth_hot_ref[...])
    samples = [sample_ref[step] for step in range(STEPS)]
    for index, (step, x) in enumerate(places):
        samples[step - 1] = samples[step - 1] + jnp.where(
            column == x, found[index * shots : (index + 1) * shots], 0.0
        )

    parts = spectra_ref.shape[0] // shots
    lanes = table_ref.shape[-1]
    for s in range(shots):
        for base in range(0, targets, lanes):
            value = spectra_ref[pl.ds(s * parts, parts), pl.ds(base, lanes)]
            for step in range(STEPS):
                value = value + table_ref[step] * samples[step][s : s + 1, base : base + lanes]
            out_ref[pl.ds(s * parts, parts), pl.ds(base, lanes)] = value
            feature_ref[pl.ds(s * parts, parts), pl.ds(base, lanes)] = value.astype(jnp.bfloat16)

    out_copy = pltpu.make_async_copy(out_ref, spectra_out_ref, out_sem)
    out_copy.start()

    owners = len(packed_refs)
    patch = packed_refs[0].shape[1]
    slots = list_hot_ref.shape[0] // (owners * patch)
    half = patch // 2
    row = lax.broadcasted_iota(jnp.int32, (half, patch), 0)
    lane = lax.broadcasted_iota(jnp.int32, (half, patch), 1)
    from_last = (lane < half) & (row > lane)
    for g, packed_ref in enumerate(packed_refs):
        chosen = lax.dot_general(
            list_hot_ref[pl.ds(g * slots * patch, slots * patch), :],
            feature_ref[...],
            NT,
            preferred_element_type=jnp.float32,
        ).astype(jnp.bfloat16)
        diagonals = []
        for s in range(slots):
            mine = chosen[s * patch : (s + 1) * patch]
            gram = lax.dot_general(mine, mine, NT, preferred_element_type=jnp.float32)
            last = pltpu.roll(gram[half:], half, 1)
            packed_ref[pl.ds(s * half, half), :] = jnp.where(from_last, last, gram[:half])
            diagonals.append(jnp.sum(jnp.where(row == lane, last, 0.0), 0, keepdims=True))
        while len(diagonals) % 8:
            diagonals.append(jnp.zeros((1, patch), jnp.float32))
        packed_ref[pl.ds(slots * half, len(diagonals)), :] = jnp.concatenate(diagonals, 0)
    out_copy.wait()


def finish(even, odd, inner, spectra, table, width, owners, slots, patch):
    edge, prior_edge, coef_edge, sample, depth_hot, column, list_hot = inner
    shots, depth = edge.shape[-2:]
    targets = column.shape[1]
    features = spectra.shape[0]
    f32 = functools.partial(jax.ShapeDtypeStruct, dtype=jnp.float32)
    rows = slots * (patch // 2) + -(-slots // 8) * 8
    out_shape = [
        f32((features, targets)),
        f32((2, 2, STEPS, shots, depth)),
        *[f32((rows, patch))] * owners,
    ]
    vmem = pl.BlockSpec(memory_space=pltpu.VMEM)
    return pl.pallas_call(
        functools.partial(finish_kernel, width=width),
        in_specs=[vmem] * 11,
        out_specs=[pl.BlockSpec(memory_space=pl.ANY)] + [vmem] * (len(out_shape) - 1),
        out_shape=out_shape,
        scratch_shapes=[
            pltpu.VMEM((2, 2, STEPS, 2 * STEPS + 1, shots, depth), jnp.float32),
            pltpu.VMEM((2, 2, STEPS, shots, depth), jnp.float32),
            pltpu.VMEM((2, 5, depth // LANES, 2 * STEPS, LANES), jnp.float32),
            pltpu.VMEM((features, targets), jnp.bfloat16),
            pltpu.VMEM((features, targets), jnp.float32),
            pltpu.SemaphoreType.DMA,
        ],
        compiler_params=compiler_params(40),
        name="finish",
    )(
        even,
        odd,
        edge,
        prior_edge,
        coef_edge,
        sample,
        depth_hot,
        column,
        list_hot,
        spectra,
        table,
    )


def assemble_kernel(p_inner_ref, q_inner_ref, final_ref, p_out_ref, q_out_ref):
    width = p_out_ref.shape[1] * TILE
    for field, (inner, out) in enumerate(((p_inner_ref, p_out_ref), (q_inner_ref, q_out_ref))):
        rows = ShotRows(out)
        for k in range(STEPS):
            rows[k] = final_ref[0, field, k]
            rows[width - 1 - k] = final_ref[1, field, k]

        @pl.loop(STEPS, width - STEPS, unroll=4)
        def _(x):
            rows[x] = inner[x - STEPS]


def assemble(p_inner, q_inner, final):
    inner, shots, depth = p_inner.shape
    across, along = (inner + 2 * STEPS) // TILE, depth // LANES
    shape = jax.ShapeDtypeStruct((shots, across, along, TILE, LANES), jnp.float32)
    vmem = pl.BlockSpec(memory_space=pltpu.VMEM)
    return pl.pallas_call(
        assemble_kernel,
        in_specs=[vmem] * 3,
        out_specs=[vmem] * 2,
        out_shape=[shape, shape],
        compiler_params=compiler_params(16),
        cost_estimate=pl.CostEstimate(flops=8 * MIB, bytes_accessed=4 * MIB, transcendentals=0),
        name="assemble",
    )(p_inner, q_inner, final)


def tiles_kernel(counts_ref, *refs, features):
    received, out_ref = refs[:-1], refs[-1]
    slots, patch = out_ref.shape[2], out_ref.shape[3]
    half = patch // 2
    row = lax.broadcasted_iota(jnp.int32, (half, patch), 0)
    lane = lax.broadcasted_iota(jnp.int32, (half, patch), 1)
    live = counts_ref[0, 0]
    total = received[0][...]
    for ref in received[1:]:
        total = total + ref[...]
    for s in range(slots):
        scale = jnp.where(s < live, 1.0 / features, 0.0)
        packed = total[s * half : (s + 1) * half] * scale
        diagonal = total[slots * half + s : slots * half + s + 1] * scale
        turned = jnp.transpose(jnp.concatenate([packed, packed], 0))
        flipped = turned[:half]
        corner = turned[half:]
        out_ref[0, 0, s, pl.ds(0, half), :] = jnp.where(
            (lane < half) & (row > lane), flipped, packed
        )
        last = jnp.where(row > lane, packed, jnp.where(row == lane, diagonal, flipped))
        out_ref[0, 0, s, pl.ds(half, half), :] = jnp.where(
            lane < half, corner, pltpu.roll(last, half, 1)
        )


def tiles(received, patch_counts, slots, features):
    patch = received[0].shape[1]
    return pl.pallas_call(
        functools.partial(tiles_kernel, features=features),
        in_specs=[pl.BlockSpec(memory_space=pltpu.SMEM)]
        + [pl.BlockSpec(memory_space=pltpu.VMEM)] * len(received),
        out_specs=pl.BlockSpec(memory_space=pltpu.VMEM),
        out_shape=jax.ShapeDtypeStruct((1, 1, slots, patch, patch), jnp.float32),
        compiler_params=compiler_params(16),
        name="tiles",
    )(patch_counts, *received)


def shards(
    pressure,
    auxiliary,
    pressure_prior,
    auxiliary_prior,
    courant_sq,
    thomsen_epsilon,
    thomsen_delta,
    tilt_angle,
    frequencies,
    spectra,
    target_cells,
    patch_lists,
    patch_counts,
):
    shots, width, depth = pressure.shape
    _, owners, slots, patch = patch_lists.shape
    fields = [tiled(item) for item in (pressure, auxiliary, pressure_prior, auxiliary_prior)]
    params = (courant_sq, thomsen_epsilon, thomsen_delta, tilt_angle)
    parts, targets = spectra.shape[1:]

    bricks = lax.axis_size("brick")
    swapped = []
    for turn, rows in enumerate(outer_rows(fields, params)):
        pairs = []
        for i in range(turn, bricks - 1, 2):
            pairs += [(i, i + 1), (i + 1, i)]
        swapped.append(lax.ppermute(rows, "brick", pairs))
    even, odd = swapped

    moments = jnp.arange(1, STEPS + 1, dtype=jnp.float32)
    angle = frequencies[None, :] * moments[:, None]
    table = jnp.concatenate([jnp.cos(angle), -jnp.sin(angle)], 1)
    table = jnp.broadcast_to(table[:, :, None], (STEPS, parts, 128))

    edge, prior_edge, coef_edge, p_inner, q_inner, sample, depth_hot, column, list_hot = interior(
        fields, params, target_cells, patch_lists
    )
    spectra_out, final, *packed = finish(
        even,
        odd,
        (edge, prior_edge, coef_edge, sample, depth_hot, column, list_hot),
        spectra.reshape(shots * parts, targets),
        table,
        width,
        owners,
        slots,
        patch,
    )
    received = packed[:1]
    for k in sorted(range(1, owners), key=lambda k: (k < owners // 2, k)):
        pairs = [(i, int(partner(i, k, owners))) for i in range(owners)]
        received.append(lax.ppermute(packed[k], "shot", pairs))
    pressure_out, auxiliary_out = [untiled(item) for item in assemble(p_inner, q_inner, final)]
    gram_tiles = tiles(received, patch_counts, slots, shots * parts * owners)
    return (pressure_out, auxiliary_out, spectra_out.reshape(spectra.shape), gram_tiles)


def solution(mesh):
    return jax.shard_map(
        shards,
        mesh=mesh,
        in_specs=(
            P("shot", "brick", None),
            P("shot", "brick", None),
            P("shot", "brick", None),
            P("shot", "brick", None),
            P("brick", None),
            P("brick", None),
            P("brick", None),
            P("brick", None),
            P(),
            P("shot", None, "brick"),
            P("brick"),
            P("brick", None, None, None),
            P("brick", "shot"),
        ),
        out_specs=(
            P("shot", "brick", None),
            P("shot", "brick", None),
            P("shot", None, "brick"),
            P("brick", "shot", None, None, None),
        ),
        check_vma=False,
    )
```

```python
import functools
import math

import jax
import jax.numpy as jnp
from jax import lax
from jax.experimental import pallas as pl
from jax.experimental.pallas import tpu as pltpu
from jax.sharding import PartitionSpec as P

STEPS = 4
MIB = 1024 * 1024
NT = (((1,), (1,)), ((), ()))


TILE = 8
LANES = 128


def tiled(field):
    shots, width, depth = field.shape
    parts = field.reshape(shots, width // TILE, TILE, depth // LANES, LANES)
    return parts.transpose(0, 1, 3, 2, 4)


def untiled(parts):
    shots, across, along, tile, lanes = parts.shape
    return parts.transpose(0, 1, 3, 2, 4).reshape(shots, across * tile, along * lanes)


class ShotRows:
    def __init__(self, ref):
        self.shots, self.across, self.along, tile, lanes = ref.shape
        self.stride = self.across * self.along * tile
        self.flat = ref.reshape(self.shots * self.stride, lanes)

    def place(self, x, j):
        if isinstance(x, int):
            start = (x // TILE * self.along + j) * TILE + x % TILE
        else:
            start = (lax.div(x, TILE) * self.along + j) * TILE + lax.rem(x, TILE)
        return pl.ds(start, self.shots, stride=self.stride)

    def __getitem__(self, x):
        return jnp.concatenate([self.flat[self.place(x, j), :] for j in range(self.along)], 1)

    def __setitem__(self, x, row):
        for j in range(self.along):
            self.flat[self.place(x, j), :] = row[:, j * LANES : (j + 1) * LANES]


def compiler_params(mib):
    return pltpu.CompilerParams(vmem_limit_bytes=mib * MIB)


def tilt_coefficients(courant, epsilon, delta, tilt):
    turns = jnp.round(tilt * (2.0 / math.pi))
    rest = (tilt - turns * 1.5703125) - turns * (math.pi / 2 - 1.5703125)
    odd = turns - 2.0 * jnp.floor(turns * 0.5)
    sign = 1.0 - 2.0 * odd
    double = 2.0 * rest
    square = double * double
    sine = double * (
        1.0
        + square
        * (
            -1.0 / 6
            + square
            * (1.0 / 120 + square * (-1.0 / 5040 + square * (1.0 / 362880 - square / 39916800.0)))
        )
    )
    versine = square * (
        0.5
        + square
        * (
            -1.0 / 24
            + square
            * (1.0 / 720 + square * (-1.0 / 40320 + square * (1.0 / 3628800 - square / 479001600.0)))
        )
    )
    sine_sq = jnp.where(odd > 0.5, 1.0 - 0.5 * versine, 0.5 * versine)
    quarter_sin = 0.25 * sign * sine
    gain_p = courant * (1.0 + 2.0 * epsilon)
    gain_q = courant * (1.0 + 2.0 * delta)
    return sine_sq, quarter_sin, courant, gain_p, gain_q


def blocks(row):
    return [row[:, j : j + LANES] for j in range(0, row.shape[1], LANES)]


def depth_terms(row):
    lane = lax.broadcasted_iota(jnp.int32, row[0].shape, 1)
    shallow = [pltpu.roll(block, 1, 1) for block in row]
    deep = [pltpu.roll(block, LANES - 1, 1) for block in row]
    outside = jnp.zeros_like(row[0])
    sums, differences = [], []
    for j in range(len(row)):
        above = jnp.where(lane == 0, shallow[j - 1] if j else outside, shallow[j])
        below = jnp.where(
            lane == LANES - 1, deep[j + 1] if j + 1 < len(row) else outside, deep[j]
        )
        sums.append(below + above)
        differences.append(below - above)
    return sums, differences


def advance(count, p_row, q_row, p_prior, q_prior, coefficient, put):
    p_back, p_here = blocks(p_row(-1)), blocks(p_row(0))
    q_back, q_here = blocks(q_row(-1)), blocks(q_row(0))
    _, p_back_d = depth_terms(p_back)
    _, q_back_d = depth_terms(q_back)
    p_sum, p_here_d = depth_terms(p_here)
    q_sum, q_here_d = depth_terms(q_here)
    for row in range(count):
        p_next, q_next = blocks(p_row(row + 1)), blocks(q_row(row + 1))
        p_next_sum, p_next_d = depth_terms(p_next)
        q_next_sum, q_next_d = depth_terms(q_next)
        p_old, q_old = blocks(p_prior(row)), blocks(q_prior(row))
        p_new, q_new = [], []
        for j in range(len(p_here)):
            sine_sq, quarter_sin, courant, gain_p, gain_q = [coefficient(i, row, j) for i in range(5)]
            twice_p, twice_q = p_here[j] + p_here[j], q_here[j] + q_here[j]
            side = p_next[j] + p_back[j]
            mixed = p_next_d[j] - p_back_d[j]
            across = (side - twice_p) + sine_sq * (p_sum[j] - side) - quarter_sin * mixed
            side = q_next[j] + q_back[j]
            mixed = q_next_d[j] - q_back_d[j]
            along = (q_sum[j] - twice_q) + sine_sq * (side - q_sum[j]) + quarter_sin * mixed
            along = courant * along
            p_new.append((twice_p - p_old[j]) + (gain_p * across + along))
            q_new.append((twice_q - q_old[j]) + (gain_q * across + along))
        put(row, jnp.concatenate(p_new, 1), jnp.concatenate(q_new, 1))
        p_back, p_here, p_back_d, p_here_d, p_sum = p_here, p_next, p_here_d, p_next_d, p_next_sum
        q_back, q_here, q_back_d, q_here_d, q_sum = q_here, q_next, q_here_d, q_next_d, q_next_sum


class CoefficientRows:
    def __init__(self, ref, shots):
        self.shots, (_, self.along, self.rows, lanes) = shots, ref.shape
        self.flat = ref.reshape(ref.shape[0] * self.along * self.rows, lanes)

    def __call__(self, index, row, j):
        place = (index * self.along + j) * self.rows + row
        return self.flat[pl.ds(place, self.shots, stride=0), :]


def split_bf16(values):
    high = values.astype(jnp.bfloat16)
    low = (values - high.astype(jnp.float32)).astype(jnp.bfloat16)
    return high, low


def pack_message(out, side, row, terms):
    size, depth = out.shape
    pair = size // (len(far_items()) + 5)
    items = []
    for field in range(4):
        near = row(field, 0)
        items.append((near, near - near.astype(jnp.bfloat16).astype(jnp.float32)))
    for first, second in far_items():
        items.append((row(*first), row(*second)))
    for position, both in enumerate(items):
        out[pl.ds(position * pair, pair), :] = jnp.concatenate(both, 0).astype(jnp.bfloat16)
    lines = []
    for index, term in enumerate(terms):
        last = term.shape[0] - 1
        for distance in reversed(range(STEPS - 1)):
            low = term[distance : distance + 1, :]
            high = term[last - distance : last - distance + 1, :]
            lines.append(jnp.where(side == 1, high, -low if index == 1 else low))
    while len(lines) < pair:
        lines.append(jnp.zeros((1, depth), jnp.float32))
    out[pl.ds(len(items) * pair, pair), :] = jnp.concatenate(lines, 0).astype(jnp.bfloat16)


def message_shape(shots, depth):
    return jax.ShapeDtypeStruct((2 * shots * (len(far_items()) + 5), depth), jnp.bfloat16)


def outer_kernel(*refs):
    sources, out, (field_ref, param_ref, field_sem, param_sem) = refs[:8], refs[8], refs[9:]
    shots, across, along, tile, lanes = sources[0].shape
    side = outer_side(0)
    place = side * (across - 1)
    copies = []
    for i in range(4):
        copies.append(
            pltpu.make_async_copy(
                sources[4 + i].at[pl.ds(pl.multiple_of(place * tile, tile), tile)],
                param_ref.at[i],
                param_sem.at[i],
            )
        )
    for i in range(4):
        copies.append(
            pltpu.make_async_copy(
                sources[i].at[:, pl.ds(place, 1)], field_ref.at[i], field_sem.at[i]
            )
        )
    for copy in copies:
        copy.start()
    for copy in copies[:4]:
        copy.wait()
    terms = tilt_coefficients(*[param_ref[i] for i in range(4)])
    for copy in copies[4:]:
        copy.wait()
    views = [ShotRows(field_ref.at[i]) for i in range(4)]
    pack_message(
        out,
        side,
        lambda field, distance: views[field][distance + side * (tile - 1 - 2 * distance)],
        terms,
    )


def outer_side(turn):
    return jnp.where(lax.axis_index("brick") % 2 == turn, 1, 0)


def far_items():
    items = []
    for field in range(2):
        items += [(field, distance) for distance in range(1, STEPS)]
    for field in range(2, 4):
        items += [(field, distance) for distance in range(1, STEPS - 1)]
    return list(zip(items[0::2], items[1::2]))


def outer_rows(fields, params):
    shots, across, along, tile, lanes = fields[0].shape
    depth = along * lanes
    return pl.pallas_call(
        outer_kernel,
        in_specs=[pl.BlockSpec(memory_space=pltpu.HBM)] * 8,
        out_specs=pl.BlockSpec(memory_space=pltpu.VMEM),
        out_shape=message_shape(shots, depth),
        scratch_shapes=[
            pltpu.VMEM((4, shots, 1, along, tile, lanes), jnp.float32),
            pltpu.VMEM((4, tile, depth), jnp.float32),
            pltpu.SemaphoreType.DMA((4,)),
            pltpu.SemaphoreType.DMA((4,)),
        ],
        compiler_params=compiler_params(60),
        name="outer_rows",
    )(*fields, *params)


def partner(me, k, count):
    if count & (count - 1):
        return (me + k) % count
    return me ^ k


def sample_rows(values, one_hot):
    high, low = split_bf16(values)
    return jnp.dot(jnp.concatenate([high, low], 1), one_hot, preferred_element_type=jnp.float32)


def run_step(step, width, level, prior, coefficients, put_row, split_ref, offset):
    low, high = step, width - step
    chunk = 8 if (high - low) % 8 == 0 else 10
    here = level(step - 1)
    shots, depth = here.shape[-2:]

    @pl.loop(0, -(-(high - low) // chunk))
    def _(index):
        at = jnp.minimum(chunk * index, high - low - chunk)
        start = low + at
        held = []

        def put(r, p_new, q_new):
            put_row(start + r, p_new, q_new)
            held.append(p_new)
            if len(held) == 2:
                first, rest = split_bf16(jnp.concatenate(held, 0))
                place = pl.multiple_of((offset + at + r - 1) * shots, 2 * shots)
                split_ref[pl.ds(place, 2 * shots), pl.ds(0, depth)] = first
                split_ref[pl.ds(place, 2 * shots), pl.ds(depth, depth)] = rest
                held.clear()

        advance(
            chunk,
            lambda r: here[0, start + r],
            lambda r: here[1, start + r],
            lambda r: prior(0, start + r),
            lambda r: prior(1, start + r),
            lambda i, r, j: coefficients(i, start + r, j),
            put,
        )


def begin_kernel(
    p_ref,
    q_ref,
    pp_ref,
    qq_ref,
    courant_ref,
    epsilon_ref,
    delta_ref,
    tilt_ref,
    cells_ref,
    lists_ref,
    sent_ref,
    message_ref,
    prior_edge_ref,
    coef_edge_ref,
    depth_hot_ref,
    column_ref,
    list_hot_ref,
    level_ref,
    coef_ref,
    split_ref,
):
    shots = p_ref.shape[0]
    width, depth = courant_ref.shape
    along = depth // LANES
    p_rows, q_rows, pp_rows, qq_rows = [ShotRows(ref) for ref in (p_ref, q_ref, pp_ref, qq_ref)]

    @pl.loop(0, width, unroll=4)
    def _(x):
        level_ref[0, 0, x] = p_rows[x]
        level_ref[0, 1, x] = q_rows[x]

    terms = tilt_coefficients(courant_ref[...], epsilon_ref[...], delta_ref[...], tilt_ref[...])
    for index, term in enumerate(terms):
        for j in range(along):
            coef_ref[index, j] = term[:, j * LANES : (j + 1) * LANES]
        for k in range(STEPS):
            coef_edge_ref[0, index, pl.ds(k, 1), :] = term[k : k + 1, :]
            row = term[width - 1 - k : width - k, :]
            coef_edge_ref[1, index, pl.ds(k, 1), :] = -row if index == 1 else row

    one, zero = jnp.bfloat16(1), jnp.bfloat16(0)
    cells = cells_ref[...]
    column = cells // depth
    column_ref[...] = column
    targets = cells.shape[1]
    z_of = jnp.broadcast_to(cells - column * depth, (16, targets)).astype(jnp.int16)
    places = lax.broadcasted_iota(jnp.int16, (16, targets), 0)
    for base in range(0, depth, 16):
        hot = jnp.where(places + jnp.int16(base) == z_of, one, zero)
        depth_hot_ref[pl.ds(base, 16), :] = hot
        depth_hot_ref[pl.ds(depth + base, 16), :] = hot

    owners, slots, patch = lists_ref.shape[1:]
    me = lax.axis_index("shot")
    rows = []
    for k in range(owners):
        lists = lists_ref[0, partner(me, k, owners)]
        rows += [lists[s : s + 1, :] for s in range(slots)]
    count = len(rows)
    while len(rows) % 8:
        rows.append(rows[0])
    upright = jnp.transpose(jnp.concatenate(rows, 0).astype(jnp.float32)).astype(jnp.int32)
    lanes = lax.broadcasted_iota(jnp.int16, (patch, LANES), 1)
    for k in range(count):
        wanted = jnp.broadcast_to(upright[:, k : k + 1], (patch, LANES)).astype(jnp.int16)
        for base in range(0, targets, LANES):
            list_hot_ref[pl.ds(k * patch, patch), pl.ds(base, LANES)] = jnp.where(
                lanes + jnp.int16(base) == wanted, one, zero
            )

    for side in range(2):
        x = 0 if side == 0 else width - 1
        prior_edge_ref[side, 0] = pp_rows[x]
        prior_edge_ref[side, 1] = qq_rows[x]

    views = (p_rows, q_rows, pp_rows, qq_rows)
    side = outer_side(1)
    pack_message(
        message_ref,
        side,
        lambda field, distance: views[field][distance + side * (width - 1 - 2 * distance)],
        terms,
    )

    def put_row(x, p_new, q_new):
        level_ref[1, 0, x] = p_new
        level_ref[1, 1, x] = q_new

    run_step(
        1,
        width,
        lambda m: level_ref.at[m],
        lambda field, x: views[2 + field][x],
        CoefficientRows(coef_ref, shots),
        put_row,
        split_ref,
        0,
    )


def begin(fields, params, target_cells, patch_lists, sent):
    shots = fields[0].shape[0]
    width, depth = params[0].shape
    targets = target_cells.shape[0]
    _, owners, slots, patch = patch_lists.shape
    f32 = functools.partial(jax.ShapeDtypeStruct, dtype=jnp.float32)
    bf16 = functools.partial(jax.ShapeDtypeStruct, dtype=jnp.bfloat16)
    out_shape = [
        message_shape(shots, depth),
        f32((2, 2, shots, depth)),
        f32((2, 5, 8, depth)),
        bf16((2 * depth, targets)),
        jax.ShapeDtypeStruct((1, targets), jnp.int32),
        bf16((owners * slots * patch, targets)),
        f32((2, 2, width, shots, depth)),
        f32((5, depth // LANES, width, LANES)),
        bf16(((width - 2) * shots, 2 * depth)),
    ]
    vmem = pl.BlockSpec(memory_space=pltpu.VMEM)
    return pl.pallas_call(
        begin_kernel,
        in_specs=[vmem] * 10 + [pl.BlockSpec(memory_space=pl.ANY)],
        out_specs=[vmem] * len(out_shape),
        out_shape=out_shape,
        compiler_params=compiler_params(32),
        cost_estimate=pl.CostEstimate(
            flops=4000 * STEPS * shots * width * depth, bytes_accessed=32 * MIB, transcendentals=0
        ),
        name="begin",
    )(*fields, *params, target_cells.reshape(1, targets), patch_lists, sent)


def interior_kernel(
    begun_ref,
    coef_ref,
    begun_split_ref,
    depth_hot_ref,
    column_ref,
    received_ref,
    edge_ref,
    p_inner_ref,
    q_inner_ref,
    sample_ref,
    level_ref,
    split_ref,
):
    width, shots, depth = begun_ref.shape[2:]
    targets = column_ref.shape[1]

    def level(m):
        return begun_ref.at[m] if m < 2 else level_ref.at[m - 2]

    coefficients = CoefficientRows(coef_ref, shots)
    offsets = [0, 0]
    for step in range(2, STEPS + 1):

        def put_row(x, p_new, q_new):
            if step < STEPS:
                level(step)[0, x] = p_new
                level(step)[1, x] = q_new
            else:
                p_inner_ref[x - STEPS] = p_new
                q_inner_ref[x - STEPS] = q_new

        run_step(
            step,
            width,
            level,
            lambda field, x: level(step - 2)[field, x],
            coefficients,
            put_row,
            split_ref,
            offsets[-1],
        )
        offsets.append(offsets[-1] + width - 2 * step)

    for step in range(STEPS):
        for field in range(2):
            for near in range(2):
                edge_ref[0, field, step, near] = level(step)[field, step + near]
                edge_ref[1, field, step, near] = level(step)[field, width - 1 - step - near]

    hot = depth_hot_ref[...]
    first = jnp.dot(begun_split_ref[...], hot, preferred_element_type=jnp.float32)
    found = jnp.dot(split_ref[...], hot, preferred_element_type=jnp.float32)
    column = column_ref[...]
    totals = [jnp.zeros((shots, targets), jnp.float32) for _ in range(STEPS)]
    for x in range(1, width - 1):
        here = column == x
        for step in range(1, STEPS + 1):
            if step <= x < width - step:
                row = (offsets[step - 1] + x - step) * shots
                value = (first if step == 1 else found)[row : row + shots]
                totals[step - 1] += jnp.where(here, value, 0.0)
    for step in range(STEPS):
        sample_ref[step] = totals[step]


def interior(begun, coef, begun_split, depth_hot, column, received):
    width, shots, depth = begun.shape[2:]
    targets = column.shape[1]
    f32 = functools.partial(jax.ShapeDtypeStruct, dtype=jnp.float32)
    out_shape = [
        f32((2, 2, STEPS, 2, shots, depth)),
        f32((width - 2 * STEPS, shots, depth)),
        f32((width - 2 * STEPS, shots, depth)),
        f32((STEPS, shots, targets)),
    ]
    rows = sum(width - 2 * step for step in range(2, STEPS + 1))
    vmem = pl.BlockSpec(memory_space=pltpu.VMEM)
    return pl.pallas_call(
        interior_kernel,
        in_specs=[vmem] * 5 + [pl.BlockSpec(memory_space=pl.ANY)],
        out_specs=[vmem] * len(out_shape),
        out_shape=out_shape,
        scratch_shapes=[
            pltpu.VMEM((STEPS - 2, 2, width, shots, depth), jnp.float32),
            pltpu.VMEM((rows * shots, 2 * depth), jnp.bfloat16),
        ],
        compiler_params=compiler_params(32),
        cost_estimate=pl.CostEstimate(
            flops=MIB, bytes_accessed=MIB, transcendentals=0
        ),
        name="interior",
    )(begun, coef, begun_split, depth_hot, column, received)


def finish_kernel(
    even_ref,
    odd_ref,
    edge_ref,
    prior_edge_ref,
    coef_edge_ref,
    sample_ref,
    depth_hot_ref,
    column_ref,
    list_hot_ref,
    spectra_ref,
    table_ref,
    spectra_out_ref,
    final_ref,
    *rest,
    width,
):
    packed_refs = rest[:-6]
    level_ref, prior_ref, coef_ref, feature_ref, out_ref, out_sem = rest[-6:]
    shots, depth = edge_ref.shape[-2:]
    targets = column_ref.shape[1]
    first = -STEPS
    pair = 2 * shots
    for turn, ref in enumerate((even_ref, odd_ref)):
        side = outer_side(turn)
        for field in range(4):
            both = ref[pl.ds(field * pair, pair), :].astype(jnp.float32)
            value = both[:shots] + both[shots:]
            if field < 2:
                level_ref[side, field, 0, -1 - first] = value
            else:
                prior_ref[side, field - 2, -1 - (1 - STEPS)] = value
        for index, items in enumerate(far_items()):
            both = ref[pl.ds((4 + index) * pair, pair), :].astype(jnp.float32)
            for half, (field, distance) in enumerate(items):
                value = both[half * shots : (half + 1) * shots]
                if field < 2:
                    level_ref[side, field, 0, -1 - distance - first] = value
                else:
                    prior_ref[side, field - 2, -1 - distance - (1 - STEPS)] = value
        params = ref[pl.ds((4 + len(far_items())) * pair, pair), :].astype(jnp.float32)
        for index in range(5):
            far = params[index * (STEPS - 1) : (index + 1) * (STEPS - 1)]
            for j, block in enumerate(blocks(far)):
                coef_ref[side, index, j, pl.ds(0, STEPS - 1), :] = block
    for side in range(2):
        for index in range(5):
            near = coef_edge_ref[side, index, pl.ds(0, STEPS), :]
            for j, block in enumerate(blocks(near)):
                coef_ref[side, index, j, pl.ds(STEPS - 1, STEPS), :] = block
        for field in range(2):
            prior_ref[side, field, STEPS - 1] = prior_edge_ref[side, field]
            for step in range(STEPS):
                for near in range(2):
                    level_ref[side, field, step, step + near - first] = edge_ref[
                        side, field, step, near
                    ]

    for step in range(1, STEPS + 1):
        low = step - STEPS

        for side in range(2):
            coefficients = CoefficientRows(coef_ref.at[side], shots)

            def prior(field):
                if step == 1:
                    return lambda r: prior_ref[side, field, low + r - (1 - STEPS)]
                return lambda r: level_ref[side, field, step - 2, low + r - first]

            def put(r, p_new, q_new):
                if step < STEPS:
                    level_ref[side, 0, step, low + r - first] = p_new
                    level_ref[side, 1, step, low + r - first] = q_new
                else:
                    final_ref[side, 0, r] = p_new
                    final_ref[side, 1, r] = q_new

            advance(
                STEPS,
                lambda r: level_ref[side, 0, step - 1, low + r - first],
                lambda r: level_ref[side, 1, step - 1, low + r - first],
                prior(0),
                prior(1),
                lambda i, r, j: coefficients(i, low + r - (1 - STEPS), j),
                put,
            )

    column = column_ref[...]
    places, values = [], []
    for step in range(1, STEPS + 1):
        for side in range(2):
            for k in range(step):
                places.append((step, k if side == 0 else width - 1 - k))
                if step < STEPS:
                    values.append(level_ref[side, 0, step, k - first])
                else:
                    values.append(final_ref[side, 0, k])
    found = sample_rows(jnp.concatenate(values, 0), depth_hot_ref[...])
    samples = [sample_ref[step] for step in range(STEPS)]
    for index, (step, x) in enumerate(places):
        samples[step - 1] = samples[step - 1] + jnp.where(
            column == x, found[index * shots : (index + 1) * shots], 0.0
        )

    parts = spectra_ref.shape[0] // shots
    lanes = table_ref.shape[-1]
    for s in range(shots):
        for base in range(0, targets, lanes):
            value = spectra_ref[pl.ds(s * parts, parts), pl.ds(base, lanes)]
            for step in range(STEPS):
                value = value + table_ref[step] * samples[step][s : s + 1, base : base + lanes]
            out_ref[pl.ds(s * parts, parts), pl.ds(base, lanes)] = value
            feature_ref[pl.ds(s * parts, parts), pl.ds(base, lanes)] = value.astype(jnp.bfloat16)

    out_copy = pltpu.make_async_copy(out_ref, spectra_out_ref, out_sem)
    out_copy.start()

    owners = len(packed_refs)
    patch = packed_refs[0].shape[1]
    slots = list_hot_ref.shape[0] // (owners * patch)
    half = patch // 2
    row = lax.broadcasted_iota(jnp.int32, (half, patch), 0)
    lane = lax.broadcasted_iota(jnp.int32, (half, patch), 1)
    from_last = (lane < half) & (row > lane)
    for g, packed_ref in enumerate(packed_refs):
        chosen = lax.dot_general(
            list_hot_ref[pl.ds(g * slots * patch, slots * patch), :],
            feature_ref[...],
            NT,
            preferred_element_type=jnp.float32,
        ).astype(jnp.bfloat16)
        diagonals = []
        for s in range(slots):
            mine = chosen[s * patch : (s + 1) * patch]
            gram = lax.dot_general(mine, mine, NT, preferred_element_type=jnp.float32)
            last = pltpu.roll(gram[half:], half, 1)
            packed_ref[pl.ds(s * half, half), :] = jnp.where(from_last, last, gram[:half])
            diagonals.append(jnp.sum(jnp.where(row == lane, last, 0.0), 0, keepdims=True))
        while len(diagonals) % 8:
            diagonals.append(jnp.zeros((1, patch), jnp.float32))
        packed_ref[pl.ds(slots * half, len(diagonals)), :] = jnp.concatenate(diagonals, 0)
    out_copy.wait()


def finish(even, odd, inner, spectra, table, width, owners, slots, patch):
    edge, prior_edge, coef_edge, sample, depth_hot, column, list_hot = inner
    shots, depth = edge.shape[-2:]
    targets = column.shape[1]
    features = spectra.shape[0]
    f32 = functools.partial(jax.ShapeDtypeStruct, dtype=jnp.float32)
    rows = slots * (patch // 2) + -(-slots // 8) * 8
    out_shape = [
        f32((features, targets)),
        f32((2, 2, STEPS, shots, depth)),
        *[f32((rows, patch))] * owners,
    ]
    vmem = pl.BlockSpec(memory_space=pltpu.VMEM)
    return pl.pallas_call(
        functools.partial(finish_kernel, width=width),
        in_specs=[vmem] * 11,
        out_specs=[pl.BlockSpec(memory_space=pl.ANY)] + [vmem] * (len(out_shape) - 1),
        out_shape=out_shape,
        scratch_shapes=[
            pltpu.VMEM((2, 2, STEPS, 2 * STEPS + 1, shots, depth), jnp.float32),
            pltpu.VMEM((2, 2, STEPS, shots, depth), jnp.float32),
            pltpu.VMEM((2, 5, depth // LANES, 2 * STEPS, LANES), jnp.float32),
            pltpu.VMEM((features, targets), jnp.bfloat16),
            pltpu.VMEM((features, targets), jnp.float32),
            pltpu.SemaphoreType.DMA,
        ],
        compiler_params=compiler_params(40),
        name="finish",
    )(
        even,
        odd,
        edge,
        prior_edge,
        coef_edge,
        sample,
        depth_hot,
        column,
        list_hot,
        spectra,
        table,
    )


def assemble_kernel(p_inner_ref, q_inner_ref, final_ref, p_out_ref, q_out_ref):
    width = p_out_ref.shape[1] * TILE
    for field, (inner, out) in enumerate(((p_inner_ref, p_out_ref), (q_inner_ref, q_out_ref))):
        rows = ShotRows(out)
        for k in range(STEPS):
            rows[k] = final_ref[0, field, k]
            rows[width - 1 - k] = final_ref[1, field, k]

        @pl.loop(STEPS, width - STEPS, unroll=4)
        def _(x):
            rows[x] = inner[x - STEPS]


def assemble(p_inner, q_inner, final):
    inner, shots, depth = p_inner.shape
    across, along = (inner + 2 * STEPS) // TILE, depth // LANES
    shape = jax.ShapeDtypeStruct((shots, across, along, TILE, LANES), jnp.float32)
    vmem = pl.BlockSpec(memory_space=pltpu.VMEM)
    return pl.pallas_call(
        assemble_kernel,
        in_specs=[vmem] * 3,
        out_specs=[vmem] * 2,
        out_shape=[shape, shape],
        compiler_params=compiler_params(16),
        cost_estimate=pl.CostEstimate(flops=8 * MIB, bytes_accessed=4 * MIB, transcendentals=0),
        name="assemble",
    )(p_inner, q_inner, final)


def tiles_kernel(counts_ref, *refs, features):
    received, out_ref = refs[:-1], refs[-1]
    slots, patch = out_ref.shape[2], out_ref.shape[3]
    half = patch // 2
    row = lax.broadcasted_iota(jnp.int32, (half, patch), 0)
    lane = lax.broadcasted_iota(jnp.int32, (half, patch), 1)
    live = counts_ref[0, 0]
    total = received[0][...]
    for ref in received[1:]:
        total = total + ref[...]
    for s in range(slots):
        scale = jnp.where(s < live, 1.0 / features, 0.0)
        packed = total[s * half : (s + 1) * half] * scale
        diagonal = total[slots * half + s : slots * half + s + 1] * scale
        turned = jnp.transpose(jnp.concatenate([packed, packed], 0))
        flipped = turned[:half]
        corner = turned[half:]
        out_ref[0, 0, s, pl.ds(0, half), :] = jnp.where(
            (lane < half) & (row > lane), flipped, packed
        )
        last = jnp.where(row > lane, packed, jnp.where(row == lane, diagonal, flipped))
        out_ref[0, 0, s, pl.ds(half, half), :] = jnp.where(
            lane < half, corner, pltpu.roll(last, half, 1)
        )


def tiles(received, patch_counts, slots, features):
    patch = received[0].shape[1]
    return pl.pallas_call(
        functools.partial(tiles_kernel, features=features),
        in_specs=[pl.BlockSpec(memory_space=pltpu.SMEM)]
        + [pl.BlockSpec(memory_space=pltpu.VMEM)] * len(received),
        out_specs=pl.BlockSpec(memory_space=pltpu.VMEM),
        out_shape=jax.ShapeDtypeStruct((1, 1, slots, patch, patch), jnp.float32),
        compiler_params=compiler_params(16),
        name="tiles",
    )(patch_counts, *received)


def shards(
    pressure,
    auxiliary,
    pressure_prior,
    auxiliary_prior,
    courant_sq,
    thomsen_epsilon,
    thomsen_delta,
    tilt_angle,
    frequencies,
    spectra,
    target_cells,
    patch_lists,
    patch_counts,
):
    shots, width, depth = pressure.shape
    _, owners, slots, patch = patch_lists.shape
    fields = [tiled(item) for item in (pressure, auxiliary, pressure_prior, auxiliary_prior)]
    params = (courant_sq, thomsen_epsilon, thomsen_delta, tilt_angle)
    parts, targets = spectra.shape[1:]

    bricks = lax.axis_size("brick")

    def swap(rows, turn):
        pairs = []
        for i in range(turn, bricks - 1, 2):
            pairs += [(i, i + 1), (i + 1, i)]
        return lax.ppermute(rows, "brick", pairs)

    rows = outer_rows(fields, params)
    even = swap(rows, 0)
    message, prior_edge, coef_edge, depth_hot, column, list_hot, *begun = begin(
        fields, params, target_cells, patch_lists, rows
    )
    odd = swap(message, 1)
    edge, p_inner, q_inner, sample = interior(*begun, depth_hot, column, even)

    moments = jnp.arange(1, STEPS + 1, dtype=jnp.float32)
    angle = frequencies[None, :] * moments[:, None]
    table = jnp.concatenate([jnp.cos(angle), -jnp.sin(angle)], 1)
    table = jnp.broadcast_to(table[:, :, None], (STEPS, parts, 128))

    spectra_out, final, *packed = finish(
        even,
        odd,
        (edge, prior_edge, coef_edge, sample, depth_hot, column, list_hot),
        spectra.reshape(shots * parts, targets),
        table,
        width,
        owners,
        slots,
        patch,
    )
    received = packed[:1]
    for k in sorted(range(1, owners), key=lambda k: (k < owners // 2, k)):
        pairs = [(i, int(partner(i, k, owners))) for i in range(owners)]
        received.append(lax.ppermute(packed[k], "shot", pairs))
    pressure_out, auxiliary_out = [untiled(item) for item in assemble(p_inner, q_inner, final)]
    gram_tiles = tiles(received, patch_counts, slots, shots * parts * owners)
    return (pressure_out, auxiliary_out, spectra_out.reshape(spectra.shape), gram_tiles)


def solution(mesh):
    return jax.shard_map(
        shards,
        mesh=mesh,
        in_specs=(
            P("shot", "brick", None),
            P("shot", "brick", None),
            P("shot", "brick", None),
            P("shot", "brick", None),
            P("brick", None),
            P("brick", None),
            P("brick", None),
            P("brick", None),
            P(),
            P("shot", None, "brick"),
            P("brick"),
            P("brick", None, None, None),
            P("brick", "shot"),
        ),
        out_specs=(
            P("shot", "brick", None),
            P("shot", "brick", None),
            P("shot", None, "brick"),
            P("brick", "shot", None, None, None),
        ),
        check_vma=False,
    )
```

```python
import functools
import math

import jax
import jax.numpy as jnp
from jax import lax
from jax.experimental import pallas as pl
from jax.experimental.pallas import tpu as pltpu
from jax.sharding import PartitionSpec as P

STEPS = 4
MIB = 1024 * 1024
NT = (((1,), (1,)), ((), ()))


TILE = 8
LANES = 128


def tiled(field):
    shots, width, depth = field.shape
    parts = field.reshape(shots, width // TILE, TILE, depth // LANES, LANES)
    return parts.transpose(0, 1, 3, 2, 4)


def untiled(parts):
    shots, across, along, tile, lanes = parts.shape
    return parts.transpose(0, 1, 3, 2, 4).reshape(shots, across * tile, along * lanes)


class ShotRows:
    def __init__(self, ref):
        self.shots, self.across, self.along, tile, lanes = ref.shape
        self.stride = self.across * self.along * tile
        self.flat = ref.reshape(self.shots * self.stride, lanes)

    def place(self, x, j):
        if isinstance(x, int):
            start = (x // TILE * self.along + j) * TILE + x % TILE
        else:
            start = (lax.div(x, TILE) * self.along + j) * TILE + lax.rem(x, TILE)
        return pl.ds(start, self.shots, stride=self.stride)

    def __getitem__(self, x):
        return jnp.concatenate([self.flat[self.place(x, j), :] for j in range(self.along)], 1)

    def __setitem__(self, x, row):
        for j in range(self.along):
            self.flat[self.place(x, j), :] = row[:, j * LANES : (j + 1) * LANES]


def compiler_params(mib):
    return pltpu.CompilerParams(vmem_limit_bytes=mib * MIB)


def tilt_coefficients(courant, epsilon, delta, tilt):
    turns = jnp.round(tilt * (2.0 / math.pi))
    rest = (tilt - turns * 1.5703125) - turns * (math.pi / 2 - 1.5703125)
    odd = turns - 2.0 * jnp.floor(turns * 0.5)
    sign = 1.0 - 2.0 * odd
    double = 2.0 * rest
    square = double * double
    sine = double * (
        1.0
        + square
        * (
            -1.0 / 6
            + square
            * (1.0 / 120 + square * (-1.0 / 5040 + square * (1.0 / 362880 - square / 39916800.0)))
        )
    )
    versine = square * (
        0.5
        + square
        * (
            -1.0 / 24
            + square
            * (1.0 / 720 + square * (-1.0 / 40320 + square * (1.0 / 3628800 - square / 479001600.0)))
        )
    )
    sine_sq = jnp.where(odd > 0.5, 1.0 - 0.5 * versine, 0.5 * versine)
    quarter_sin = 0.25 * sign * sine
    gain_p = courant * (1.0 + 2.0 * epsilon)
    gain_q = courant * (1.0 + 2.0 * delta)
    return sine_sq, quarter_sin, courant, gain_p, gain_q


def blocks(row):
    return [row[:, j : j + LANES] for j in range(0, row.shape[1], LANES)]


def depth_terms(row):
    lane = lax.broadcasted_iota(jnp.int32, row[0].shape, 1)
    shallow = [pltpu.roll(block, 1, 1) for block in row]
    deep = [pltpu.roll(block, LANES - 1, 1) for block in row]
    outside = jnp.zeros_like(row[0])
    sums, differences = [], []
    for j in range(len(row)):
        above = jnp.where(lane == 0, shallow[j - 1] if j else outside, shallow[j])
        below = jnp.where(
            lane == LANES - 1, deep[j + 1] if j + 1 < len(row) else outside, deep[j]
        )
        sums.append(below + above)
        differences.append(below - above)
    return sums, differences


def advance(count, p_row, q_row, p_prior, q_prior, coefficient, put):
    p_back, p_here = blocks(p_row(-1)), blocks(p_row(0))
    q_back, q_here = blocks(q_row(-1)), blocks(q_row(0))
    _, p_back_d = depth_terms(p_back)
    _, q_back_d = depth_terms(q_back)
    p_sum, p_here_d = depth_terms(p_here)
    q_sum, q_here_d = depth_terms(q_here)
    for row in range(count):
        p_next, q_next = blocks(p_row(row + 1)), blocks(q_row(row + 1))
        p_next_sum, p_next_d = depth_terms(p_next)
        q_next_sum, q_next_d = depth_terms(q_next)
        p_old, q_old = blocks(p_prior(row)), blocks(q_prior(row))
        p_new, q_new = [], []
        for j in range(len(p_here)):
            sine_sq, quarter_sin, courant, gain_p, gain_q = [coefficient(i, row, j) for i in range(5)]
            twice_p, twice_q = p_here[j] + p_here[j], q_here[j] + q_here[j]
            side = p_next[j] + p_back[j]
            mixed = p_next_d[j] - p_back_d[j]
            across = (side - twice_p) + sine_sq * (p_sum[j] - side) - quarter_sin * mixed
            side = q_next[j] + q_back[j]
            mixed = q_next_d[j] - q_back_d[j]
            along = (q_sum[j] - twice_q) + sine_sq * (side - q_sum[j]) + quarter_sin * mixed
            along = courant * along
            p_new.append((twice_p - p_old[j]) + (gain_p * across + along))
            q_new.append((twice_q - q_old[j]) + (gain_q * across + along))
        put(row, jnp.concatenate(p_new, 1), jnp.concatenate(q_new, 1))
        p_back, p_here, p_back_d, p_here_d, p_sum = p_here, p_next, p_here_d, p_next_d, p_next_sum
        q_back, q_here, q_back_d, q_here_d, q_sum = q_here, q_next, q_here_d, q_next_d, q_next_sum


class CoefficientRows:
    def __init__(self, ref, shots):
        self.shots, (_, self.along, self.rows, lanes) = shots, ref.shape
        self.flat = ref.reshape(ref.shape[0] * self.along * self.rows, lanes)

    def __call__(self, index, row, j):
        place = (index * self.along + j) * self.rows + row
        return self.flat[pl.ds(place, self.shots, stride=0), :]


def split_bf16(values):
    high = values.astype(jnp.bfloat16)
    low = (values - high.astype(jnp.float32)).astype(jnp.bfloat16)
    return high, low


def outer_kernel(*refs):
    sources, outs, (field_ref, param_ref, field_sem, param_sem) = refs[:8], refs[8:10], refs[10:]
    shots, across, along, tile, lanes = sources[0].shape
    depth = along * lanes
    copies = []
    for side in range(2):
        place = side * (across - 1)
        for i in range(4):
            copies.append(
                pltpu.make_async_copy(
                    sources[i].at[:, pl.ds(place, 1), :, pl.ds(side * STEPS, STEPS)],
                    field_ref.at[side, i, :, :, :, pl.ds(side * STEPS, STEPS)],
                    field_sem.at[side, i],
                )
            )
        for i in range(4):
            copies.append(
                pltpu.make_async_copy(
                    sources[4 + i].at[pl.ds(place * tile, tile)],
                    param_ref.at[side, i],
                    param_sem.at[side, i],
                )
            )
    for copy in copies:
        copy.start()
    tiles_by_side = []
    for side in range(2):
        for copy in copies[8 * side : 8 * side + 8]:
            copy.wait()
        terms = tilt_coefficients(*[param_ref[side, i] for i in range(4)])
        rows = []
        for index, term in enumerate(terms):
            term = -term if index == 1 and side == 0 else term
            for distance in reversed(range(STEPS - 1)):
                place = distance if side == 0 else tile - 1 - distance
                rows.append(term[place : place + 1, :])
        while len(rows) < 2 * shots:
            rows.append(jnp.zeros((1, depth), jnp.float32))
        tiles_by_side.append(jnp.concatenate(rows, 0))

    stride = along * tile
    flat = field_ref.reshape(2 * 4 * shots * stride, lanes)
    for turn in range(2):
        side = outer_side(turn)
        out = outs[turn]

        def row(field, distance):
            base = (side * 4 + field) * shots * stride + distance + side * (tile - 1 - 2 * distance)
            return jnp.concatenate(
                [flat[pl.ds(base + j * tile, shots, stride=stride), :] for j in range(along)], 1
            )

        position = 0

        def put(first, second):
            nonlocal position
            out[pl.ds(position, 2 * shots), :] = jnp.concatenate([first, second], 0).astype(
                jnp.bfloat16
            )
            position += 2 * shots

        for field in range(4):
            near = row(field, 0)
            put(near, near - near.astype(jnp.bfloat16).astype(jnp.float32))
        for first, second in far_items():
            put(row(*first), row(*second))
        out[pl.ds(position, 2 * shots), :] = jnp.where(
            side == 1, tiles_by_side[1], tiles_by_side[0]
        ).astype(jnp.bfloat16)


def outer_side(turn):
    return jnp.where(lax.axis_index("brick") % 2 == turn, 1, 0)


def far_items():
    items = []
    for field in range(2):
        items += [(field, distance) for distance in range(1, STEPS)]
    for field in range(2, 4):
        items += [(field, distance) for distance in range(1, STEPS - 1)]
    return list(zip(items[0::2], items[1::2]))


def outer_rows(fields, params):
    shots, across, along, tile, lanes = fields[0].shape
    depth = along * lanes
    rows = 2 * shots * (4 + len(far_items()) + 1)
    shape = jax.ShapeDtypeStruct((rows, depth), jnp.bfloat16)
    return pl.pallas_call(
        outer_kernel,
        in_specs=[pl.BlockSpec(memory_space=pltpu.HBM)] * 8,
        out_specs=[pl.BlockSpec(memory_space=pltpu.VMEM)] * 2,
        out_shape=[shape, shape],
        scratch_shapes=[
            pltpu.VMEM((2, 4, shots, 1, along, tile, lanes), jnp.float32),
            pltpu.VMEM((2, 4, tile, depth), jnp.float32),
            pltpu.SemaphoreType.DMA((2, 4)),
            pltpu.SemaphoreType.DMA((2, 4)),
        ],
        compiler_params=compiler_params(60),
        name="outer_rows",
    )(*fields, *params)


def partner(me, k, count):
    if count & (count - 1):
        return (me + k) % count
    return me ^ k


def owner_of(me, k, owners):
    chips = owners // 2
    chip, core = me // 2, me % 2
    return partner(chip, k % chips, chips) * 2 + (core ^ (k // chips))


def sample_rows(values, one_hot):
    high, low = split_bf16(values)
    return jnp.dot(jnp.concatenate([high, low], 1), one_hot, preferred_element_type=jnp.float32)


def interior_kernel(
    p_ref,
    q_ref,
    pp_ref,
    qq_ref,
    courant_ref,
    epsilon_ref,
    delta_ref,
    tilt_ref,
    cells_ref,
    lists_ref,
    edge_ref,
    prior_edge_ref,
    coef_edge_ref,
    p_inner_ref,
    q_inner_ref,
    sample_ref,
    depth_hot_ref,
    column_ref,
    list_hot_ref,
    level_ref,
    coef_ref,
    split_ref,
):
    shots = p_ref.shape[0]
    width, depth = courant_ref.shape
    along = depth // LANES
    p_rows, q_rows, pp_rows, qq_rows = [ShotRows(ref) for ref in (p_ref, q_ref, pp_ref, qq_ref)]

    @pl.loop(0, width, unroll=4)
    def _(x):
        level_ref[0, 0, x] = p_rows[x]
        level_ref[0, 1, x] = q_rows[x]

    terms = tilt_coefficients(courant_ref[...], epsilon_ref[...], delta_ref[...], tilt_ref[...])
    for index, term in enumerate(terms):
        for j in range(along):
            coef_ref[index, j] = term[:, j * LANES : (j + 1) * LANES]
        for k in range(STEPS):
            coef_edge_ref[0, index, pl.ds(k, 1), :] = term[k : k + 1, :]
            row = term[width - 1 - k : width - k, :]
            coef_edge_ref[1, index, pl.ds(k, 1), :] = -row if index == 1 else row

    one, zero = jnp.bfloat16(1), jnp.bfloat16(0)
    cells = cells_ref[...]
    column = cells // depth
    column_ref[...] = column
    targets = cells.shape[1]
    z_of = jnp.broadcast_to(cells - column * depth, (16, targets)).astype(jnp.int16)
    places = lax.broadcasted_iota(jnp.int16, (16, targets), 0)
    for base in range(0, depth, 16):
        hot = jnp.where(places + jnp.int16(base) == z_of, one, zero)
        depth_hot_ref[pl.ds(base, 16), :] = hot
        depth_hot_ref[pl.ds(depth + base, 16), :] = hot

    owners, slots, patch = lists_ref.shape[1:]
    me = lax.axis_index("shot")
    rows = []
    for k in range(owners):
        lists = lists_ref[0, owner_of(me, k, owners)]
        rows += [lists[s : s + 1, :] for s in range(slots)]
    count = len(rows)
    while len(rows) % 8:
        rows.append(rows[0])
    upright = jnp.transpose(jnp.concatenate(rows, 0).astype(jnp.float32)).astype(jnp.int32)
    lanes = lax.broadcasted_iota(jnp.int16, (patch, LANES), 1)
    for k in range(count):
        wanted = jnp.broadcast_to(upright[:, k : k + 1], (patch, LANES)).astype(jnp.int16)
        for base in range(0, targets, LANES):
            list_hot_ref[pl.ds(k * patch, patch), pl.ds(base, LANES)] = jnp.where(
                lanes + jnp.int16(base) == wanted, one, zero
            )

    for side in range(2):
        x = 0 if side == 0 else width - 1
        prior_edge_ref[side, 0] = pp_rows[x]
        prior_edge_ref[side, 1] = qq_rows[x]

    coefficients = CoefficientRows(coef_ref, shots)
    offsets = [0]
    for step in range(1, STEPS + 1):
        low, high = step, width - step
        chunk = 8 if (high - low) % 8 == 0 else 10
        offset = offsets[-1]
        offsets.append(offset + high - low)

        @pl.loop(0, -(-(high - low) // chunk))
        def _(index):
            at = jnp.minimum(chunk * index, high - low - chunk)
            start = low + at
            held = []

            def put(r, p_new, q_new):
                if step < STEPS:
                    level_ref[step, 0, start + r] = p_new
                    level_ref[step, 1, start + r] = q_new
                else:
                    p_inner_ref[at + r] = p_new
                    q_inner_ref[at + r] = q_new
                held.append(p_new)
                if len(held) == 2:
                    first, rest = split_bf16(jnp.concatenate(held, 0))
                    place = pl.multiple_of((offset + at + r - 1) * shots, 2 * shots)
                    split_ref[pl.ds(place, 2 * shots), pl.ds(0, depth)] = first
                    split_ref[pl.ds(place, 2 * shots), pl.ds(depth, depth)] = rest
                    held.clear()

            advance(
                chunk,
                lambda r: level_ref[step - 1, 0, start + r],
                lambda r: level_ref[step - 1, 1, start + r],
                lambda r: pp_rows[start + r] if step == 1 else level_ref[step - 2, 0, start + r],
                lambda r: qq_rows[start + r] if step == 1 else level_ref[step - 2, 1, start + r],
                lambda i, r, j: coefficients(i, start + r, j),
                put,
            )

    for step in range(STEPS):
        for field in range(2):
            for near in range(2):
                edge_ref[0, field, step, near] = level_ref[step, field, step + near]
                edge_ref[1, field, step, near] = level_ref[step, field, width - 1 - step - near]

    found = jnp.dot(split_ref[...], depth_hot_ref[...], preferred_element_type=jnp.float32)
    totals = [jnp.zeros((shots, targets), jnp.float32) for _ in range(STEPS)]
    for x in range(1, width - 1):
        here = column == x
        for step in range(1, STEPS + 1):
            if step <= x < width - step:
                row = (offsets[step - 1] + x - step) * shots
                totals[step - 1] += jnp.where(here, found[row : row + shots], 0.0)
    for step in range(STEPS):
        sample_ref[step] = totals[step]


def interior(fields, params, target_cells, patch_lists):
    shots = fields[0].shape[0]
    width, depth = params[0].shape
    targets = target_cells.shape[0]
    _, owners, slots, patch = patch_lists.shape
    f32 = functools.partial(jax.ShapeDtypeStruct, dtype=jnp.float32)
    out_shape = [
        f32((2, 2, STEPS, 2, shots, depth)),
        f32((2, 2, shots, depth)),
        f32((2, 5, 8, depth)),
        f32((width - 2 * STEPS, shots, depth)),
        f32((width - 2 * STEPS, shots, depth)),
        f32((STEPS, shots, targets)),
        jax.ShapeDtypeStruct((2 * depth, targets), jnp.bfloat16),
        jax.ShapeDtypeStruct((1, targets), jnp.int32),
        jax.ShapeDtypeStruct((owners * slots * patch, targets), jnp.bfloat16),
    ]
    vmem = pl.BlockSpec(memory_space=pltpu.VMEM)
    return pl.pallas_call(
        interior_kernel,
        in_specs=[vmem] * 10,
        out_specs=[vmem] * len(out_shape),
        out_shape=out_shape,
        scratch_shapes=[
            pltpu.VMEM((STEPS, 2, width, shots, depth), jnp.float32),
            pltpu.VMEM((5, depth // LANES, width, LANES), jnp.float32),
            pltpu.VMEM((STEPS * (width - STEPS - 1) * shots, 2 * depth), jnp.bfloat16),
        ],
        compiler_params=compiler_params(40),
        cost_estimate=pl.CostEstimate(
            flops=200 * STEPS * shots * width * depth, bytes_accessed=8 * MIB, transcendentals=0
        ),
        name="interior",
    )(*fields, *params, target_cells.reshape(1, targets), patch_lists)


def finish_kernel(
    even_ref,
    odd_ref,
    edge_ref,
    prior_edge_ref,
    coef_edge_ref,
    sample_ref,
    depth_hot_ref,
    column_ref,
    list_hot_ref,
    spectra_ref,
    table_ref,
    spectra_out_ref,
    final_ref,
    *rest,
    width,
):
    packed_refs = rest[:-6]
    level_ref, prior_ref, coef_ref, feature_ref, out_ref, out_sem = rest[-6:]
    shots, depth = edge_ref.shape[-2:]
    targets = column_ref.shape[1]
    first = -STEPS
    pair = 2 * shots
    for turn, ref in enumerate((even_ref, odd_ref)):
        side = outer_side(turn)
        for field in range(4):
            both = ref[pl.ds(field * pair, pair), :].astype(jnp.float32)
            value = both[:shots] + both[shots:]
            if field < 2:
                level_ref[side, field, 0, -1 - first] = value
            else:
                prior_ref[side, field - 2, -1 - (1 - STEPS)] = value
        for index, items in enumerate(far_items()):
            both = ref[pl.ds((4 + index) * pair, pair), :].astype(jnp.float32)
            for half, (field, distance) in enumerate(items):
                value = both[half * shots : (half + 1) * shots]
                if field < 2:
                    level_ref[side, field, 0, -1 - distance - first] = value
                else:
                    prior_ref[side, field - 2, -1 - distance - (1 - STEPS)] = value
        params = ref[pl.ds((4 + len(far_items())) * pair, pair), :].astype(jnp.float32)
        for index in range(5):
            far = params[index * (STEPS - 1) : (index + 1) * (STEPS - 1)]
            for j, block in enumerate(blocks(far)):
                coef_ref[side, index, j, pl.ds(0, STEPS - 1), :] = block
    for side in range(2):
        for index in range(5):
            near = coef_edge_ref[side, index, pl.ds(0, STEPS), :]
            for j, block in enumerate(blocks(near)):
                coef_ref[side, index, j, pl.ds(STEPS - 1, STEPS), :] = block
        for field in range(2):
            prior_ref[side, field, STEPS - 1] = prior_edge_ref[side, field]
            for step in range(STEPS):
                for near in range(2):
                    level_ref[side, field, step, step + near - first] = edge_ref[
                        side, field, step, near
                    ]

    for step in range(1, STEPS + 1):
        low = step - STEPS

        for side in range(2):
            coefficients = CoefficientRows(coef_ref.at[side], shots)

            def prior(field):
                if step == 1:
                    return lambda r: prior_ref[side, field, low + r - (1 - STEPS)]
                return lambda r: level_ref[side, field, step - 2, low + r - first]

            def put(r, p_new, q_new):
                if step < STEPS:
                    level_ref[side, 0, step, low + r - first] = p_new
                    level_ref[side, 1, step, low + r - first] = q_new
                else:
                    final_ref[side, 0, r] = p_new
                    final_ref[side, 1, r] = q_new

            advance(
                STEPS,
                lambda r: level_ref[side, 0, step - 1, low + r - first],
                lambda r: level_ref[side, 1, step - 1, low + r - first],
                prior(0),
                prior(1),
                lambda i, r, j: coefficients(i, low + r - (1 - STEPS), j),
                put,
            )

    column = column_ref[...]
    places, values = [], []
    for step in range(1, STEPS + 1):
        for side in range(2):
            for k in range(step):
                places.append((step, k if side == 0 else width - 1 - k))
                if step < STEPS:
                    values.append(level_ref[side, 0, step, k - first])
                else:
                    values.append(final_ref[side, 0, k])
    found = sample_rows(jnp.concatenate(values, 0), depth_hot_ref[...])
    samples = [sample_ref[step] for step in range(STEPS)]
    for index, (step, x) in enumerate(places):
        samples[step - 1] = samples[step - 1] + jnp.where(
            column == x, found[index * shots : (index + 1) * shots], 0.0
        )

    parts = spectra_ref.shape[0] // shots
    lanes = table_ref.shape[-1]
    for s in range(shots):
        for base in range(0, targets, lanes):
            value = spectra_ref[pl.ds(s * parts, parts), pl.ds(base, lanes)]
            for step in range(STEPS):
                value = value + table_ref[step] * samples[step][s : s + 1, base : base + lanes]
            out_ref[pl.ds(s * parts, parts), pl.ds(base, lanes)] = value
            feature_ref[pl.ds(s * parts, parts), pl.ds(base, lanes)] = value.astype(jnp.bfloat16)

    out_copy = pltpu.make_async_copy(out_ref, spectra_out_ref, out_sem)
    out_copy.start()

    chips = len(packed_refs) - 1
    owners = 2 * chips
    size, patch = packed_refs[0].shape
    slots = list_hot_ref.shape[0] // (owners * patch)
    half = patch // 2
    row = lax.broadcasted_iota(jnp.int32, (half, patch), 0)
    lane = lax.broadcasted_iota(jnp.int32, (half, patch), 1)
    from_last = (lane < half) & (row > lane)
    for g in range(owners):
        packed_ref = packed_refs[min(g, chips)]
        base = max(g - chips, 0) * size
        chosen = lax.dot_general(
            list_hot_ref[pl.ds(g * slots * patch, slots * patch), :],
            feature_ref[...],
            NT,
            preferred_element_type=jnp.float32,
        ).astype(jnp.bfloat16)
        diagonals = []
        for s in range(slots):
            mine = chosen[s * patch : (s + 1) * patch]
            gram = lax.dot_general(mine, mine, NT, preferred_element_type=jnp.float32)
            last = pltpu.roll(gram[half:], half, 1)
            packed_ref[pl.ds(base + s * half, half), :] = jnp.where(from_last, last, gram[:half])
            diagonals.append(jnp.sum(jnp.where(row == lane, last, 0.0), 0, keepdims=True))
        while len(diagonals) % 8:
            diagonals.append(jnp.zeros((1, patch), jnp.float32))
        packed_ref[pl.ds(base + slots * half, len(diagonals)), :] = jnp.concatenate(diagonals, 0)
    out_copy.wait()


def finish(even, odd, inner, spectra, table, width, owners, slots, patch):
    edge, prior_edge, coef_edge, sample, depth_hot, column, list_hot = inner
    shots, depth = edge.shape[-2:]
    targets = column.shape[1]
    features = spectra.shape[0]
    f32 = functools.partial(jax.ShapeDtypeStruct, dtype=jnp.float32)
    rows = slots * (patch // 2) + -(-slots // 8) * 8
    out_shape = [
        f32((features, targets)),
        f32((2, 2, STEPS, shots, depth)),
        *[f32((rows, patch))] * (owners // 2),
        f32((owners // 2 * rows, patch)),
    ]
    vmem = pl.BlockSpec(memory_space=pltpu.VMEM)
    return pl.pallas_call(
        functools.partial(finish_kernel, width=width),
        in_specs=[vmem] * 11,
        out_specs=[pl.BlockSpec(memory_space=pl.ANY)] + [vmem] * (len(out_shape) - 1),
        out_shape=out_shape,
        scratch_shapes=[
            pltpu.VMEM((2, 2, STEPS, 2 * STEPS + 1, shots, depth), jnp.float32),
            pltpu.VMEM((2, 2, STEPS, shots, depth), jnp.float32),
            pltpu.VMEM((2, 5, depth // LANES, 2 * STEPS, LANES), jnp.float32),
            pltpu.VMEM((features, targets), jnp.bfloat16),
            pltpu.VMEM((features, targets), jnp.float32),
            pltpu.SemaphoreType.DMA,
        ],
        compiler_params=compiler_params(40),
        name="finish",
    )(
        even,
        odd,
        edge,
        prior_edge,
        coef_edge,
        sample,
        depth_hot,
        column,
        list_hot,
        spectra,
        table,
    )


def assemble_kernel(p_inner_ref, q_inner_ref, final_ref, p_out_ref, q_out_ref):
    width = p_out_ref.shape[1] * TILE
    for field, (inner, out) in enumerate(((p_inner_ref, p_out_ref), (q_inner_ref, q_out_ref))):
        rows = ShotRows(out)
        for k in range(STEPS):
            rows[k] = final_ref[0, field, k]
            rows[width - 1 - k] = final_ref[1, field, k]

        @pl.loop(STEPS, width - STEPS, unroll=4)
        def _(x):
            rows[x] = inner[x - STEPS]


def assemble(p_inner, q_inner, final):
    inner, shots, depth = p_inner.shape
    across, along = (inner + 2 * STEPS) // TILE, depth // LANES
    shape = jax.ShapeDtypeStruct((shots, across, along, TILE, LANES), jnp.float32)
    vmem = pl.BlockSpec(memory_space=pltpu.VMEM)
    return pl.pallas_call(
        assemble_kernel,
        in_specs=[vmem] * 3,
        out_specs=[vmem] * 2,
        out_shape=[shape, shape],
        compiler_params=compiler_params(16),
        cost_estimate=pl.CostEstimate(flops=8 * MIB, bytes_accessed=4 * MIB, transcendentals=0),
        name="assemble",
    )(p_inner, q_inner, final)


def tiles_kernel(counts_ref, *refs, features):
    received, out_ref = refs[:-1], refs[-1]
    slots, patch = out_ref.shape[2], out_ref.shape[3]
    half = patch // 2
    row = lax.broadcasted_iota(jnp.int32, (half, patch), 0)
    lane = lax.broadcasted_iota(jnp.int32, (half, patch), 1)
    live = counts_ref[0, 0]
    total = received[0][...]
    for ref in received[1:]:
        total = total + ref[pl.ds(0, total.shape[0]), :]
    for s in range(slots):
        scale = jnp.where(s < live, 1.0 / features, 0.0)
        packed = total[s * half : (s + 1) * half] * scale
        diagonal = total[slots * half + s : slots * half + s + 1] * scale
        turned = jnp.transpose(jnp.concatenate([packed, packed], 0))
        flipped = turned[:half]
        corner = turned[half:]
        out_ref[0, 0, s, pl.ds(0, half), :] = jnp.where(
            (lane < half) & (row > lane), flipped, packed
        )
        last = jnp.where(row > lane, packed, jnp.where(row == lane, diagonal, flipped))
        out_ref[0, 0, s, pl.ds(half, half), :] = jnp.where(
            lane < half, corner, pltpu.roll(last, half, 1)
        )


def tiles(received, patch_counts, slots, features):
    patch = received[0].shape[1]
    return pl.pallas_call(
        functools.partial(tiles_kernel, features=features),
        in_specs=[pl.BlockSpec(memory_space=pltpu.SMEM)]
        + [pl.BlockSpec(memory_space=pltpu.VMEM)] * len(received),
        out_specs=pl.BlockSpec(memory_space=pltpu.VMEM),
        out_shape=jax.ShapeDtypeStruct((1, 1, slots, patch, patch), jnp.float32),
        compiler_params=compiler_params(16),
        name="tiles",
    )(patch_counts, *received)


def shards(
    pressure,
    auxiliary,
    pressure_prior,
    auxiliary_prior,
    courant_sq,
    thomsen_epsilon,
    thomsen_delta,
    tilt_angle,
    frequencies,
    spectra,
    target_cells,
    patch_lists,
    patch_counts,
):
    shots, width, depth = pressure.shape
    _, owners, slots, patch = patch_lists.shape
    fields = [tiled(item) for item in (pressure, auxiliary, pressure_prior, auxiliary_prior)]
    params = (courant_sq, thomsen_epsilon, thomsen_delta, tilt_angle)
    parts, targets = spectra.shape[1:]

    bricks = lax.axis_size("brick")
    swapped = []
    for turn, rows in enumerate(outer_rows(fields, params)):
        pairs = []
        for i in range(turn, bricks - 1, 2):
            pairs += [(i, i + 1), (i + 1, i)]
        swapped.append(lax.ppermute(rows, "brick", pairs))
    even, odd = swapped

    moments = jnp.arange(1, STEPS + 1, dtype=jnp.float32)
    angle = frequencies[None, :] * moments[:, None]
    table = jnp.concatenate([jnp.cos(angle), -jnp.sin(angle)], 1)
    table = jnp.broadcast_to(table[:, :, None], (STEPS, parts, 128))

    edge, prior_edge, coef_edge, p_inner, q_inner, sample, depth_hot, column, list_hot = interior(
        fields, params, target_cells, patch_lists
    )
    spectra_out, final, *packed = finish(
        even,
        odd,
        (edge, prior_edge, coef_edge, sample, depth_hot, column, list_hot),
        spectra.reshape(shots * parts, targets),
        table,
        width,
        owners,
        slots,
        patch,
    )
    chips = owners // 2
    beside = lax.ppermute(packed[chips], "shot", [(i, i ^ 1) for i in range(owners)])
    received = [packed[0], beside]
    size = packed[0].shape[0]
    for k in range(1, chips):
        both = packed[k] + beside[k * size : (k + 1) * size]
        pairs = [(i, partner(i // 2, k, chips) * 2 + i % 2) for i in range(owners)]
        received.append(lax.ppermute(both, "shot", pairs))
    pressure_out, auxiliary_out = [untiled(item) for item in assemble(p_inner, q_inner, final)]
    gram_tiles = tiles(received, patch_counts, slots, shots * parts * owners)
    return (pressure_out, auxiliary_out, spectra_out.reshape(spectra.shape), gram_tiles)


def solution(mesh):
    return jax.shard_map(
        shards,
        mesh=mesh,
        in_specs=(
            P("shot", "brick", None),
            P("shot", "brick", None),
            P("shot", "brick", None),
            P("shot", "brick", None),
            P("brick", None),
            P("brick", None),
            P("brick", None),
            P("brick", None),
            P(),
            P("shot", None, "brick"),
            P("brick"),
            P("brick", None, None, None),
            P("brick", "shot"),
        ),
        out_specs=(
            P("shot", "brick", None),
            P("shot", "brick", None),
            P("shot", None, "brick"),
            P("brick", "shot", None, None, None),
        ),
        check_vma=False,
    )
```

```python
import functools
import math

import jax
import jax.numpy as jnp
from jax import lax
from jax.experimental import pallas as pl
from jax.experimental.pallas import tpu as pltpu
from jax.sharding import PartitionSpec as P

STEPS = 4
MIB = 1024 * 1024
NT = (((1,), (1,)), ((), ()))


TILE = 8
LANES = 128


def tiled(field):
    shots, width, depth = field.shape
    parts = field.reshape(shots, width // TILE, TILE, depth // LANES, LANES)
    return parts.transpose(0, 1, 3, 2, 4)


def untiled(parts):
    shots, across, along, tile, lanes = parts.shape
    return parts.transpose(0, 1, 3, 2, 4).reshape(shots, across * tile, along * lanes)


class ShotRows:
    def __init__(self, ref):
        self.shots, self.across, self.along, tile, lanes = ref.shape
        self.stride = self.across * self.along * tile
        self.flat = ref.reshape(self.shots * self.stride, lanes)

    def place(self, x, j):
        if isinstance(x, int):
            start = (x // TILE * self.along + j) * TILE + x % TILE
        else:
            start = (lax.div(x, TILE) * self.along + j) * TILE + lax.rem(x, TILE)
        return pl.ds(start, self.shots, stride=self.stride)

    def block(self, x, j):
        return self.flat[self.place(x, j), :]

    def __getitem__(self, x):
        return jnp.concatenate([self.flat[self.place(x, j), :] for j in range(self.along)], 1)

    def __setitem__(self, x, row):
        for j in range(self.along):
            self.flat[self.place(x, j), :] = row[:, j * LANES : (j + 1) * LANES]


def compiler_params(mib):
    return pltpu.CompilerParams(vmem_limit_bytes=mib * MIB)


def tilt_coefficients(courant, epsilon, delta, tilt):
    turns = jnp.round(tilt * (2.0 / math.pi))
    rest = (tilt - turns * 1.5703125) - turns * (math.pi / 2 - 1.5703125)
    odd = turns - 2.0 * jnp.floor(turns * 0.5)
    sign = 1.0 - 2.0 * odd
    double = 2.0 * rest
    square = double * double
    sine = double * (
        1.0
        + square
        * (
            -1.0 / 6
            + square
            * (1.0 / 120 + square * (-1.0 / 5040 + square * (1.0 / 362880 - square / 39916800.0)))
        )
    )
    versine = square * (
        0.5
        + square
        * (
            -1.0 / 24
            + square
            * (1.0 / 720 + square * (-1.0 / 40320 + square * (1.0 / 3628800 - square / 479001600.0)))
        )
    )
    sine_sq = jnp.where(odd > 0.5, 1.0 - 0.5 * versine, 0.5 * versine)
    quarter_sin = 0.25 * sign * sine
    gain_p = courant * (1.0 + 2.0 * epsilon)
    gain_q = courant * (1.0 + 2.0 * delta)
    return sine_sq, quarter_sin, courant, gain_p, gain_q


def blocks(row):
    return [row[:, j : j + LANES] for j in range(0, row.shape[1], LANES)]


def depth_terms(read, row, j, last):
    block = read(row, j)
    lane = lax.broadcasted_iota(jnp.int32, block.shape, 1)
    outside = jnp.zeros_like(block)
    above = pltpu.roll(read(row, j - 1), 1, 1) if j else outside
    below = pltpu.roll(read(row, j + 1), LANES - 1, 1) if j < last else outside
    shallow = jnp.where(lane == 0, above, pltpu.roll(block, 1, 1))
    deep = jnp.where(lane == LANES - 1, below, pltpu.roll(block, LANES - 1, 1))
    return block, deep + shallow, deep - shallow


def advance(count, along, p_row, q_row, p_prior, q_prior, coefficient, put):
    for j in range(along):
        p_terms = functools.partial(depth_terms, p_row, j=j, last=along - 1)
        q_terms = functools.partial(depth_terms, q_row, j=j, last=along - 1)
        p_back, _, p_back_d = p_terms(-1)
        q_back, _, q_back_d = q_terms(-1)
        p_here, p_sum, p_here_d = p_terms(0)
        q_here, q_sum, q_here_d = q_terms(0)
        for row in range(count):
            p_next, p_next_sum, p_next_d = p_terms(row + 1)
            q_next, q_next_sum, q_next_d = q_terms(row + 1)
            sine_sq, quarter_sin, courant, gain_p, gain_q = [coefficient(i, row, j) for i in range(5)]
            twice_p, twice_q = p_here + p_here, q_here + q_here
            side = p_next + p_back
            mixed = p_next_d - p_back_d
            across = (side - twice_p) + sine_sq * (p_sum - side) - quarter_sin * mixed
            side = q_next + q_back
            mixed = q_next_d - q_back_d
            along_q = (q_sum - twice_q) + sine_sq * (side - q_sum) + quarter_sin * mixed
            along_q = courant * along_q
            put(
                row,
                j,
                (twice_p - p_prior(row, j)) + (gain_p * across + along_q),
                (twice_q - q_prior(row, j)) + (gain_q * across + along_q),
            )
            p_back, p_here, p_sum = p_here, p_next, p_next_sum
            p_back_d, p_here_d = p_here_d, p_next_d
            q_back, q_here, q_sum = q_here, q_next, q_next_sum
            q_back_d, q_here_d = q_here_d, q_next_d


def lanes_of(j):
    return pl.ds(j * LANES, LANES)


class CoefficientRows:
    def __init__(self, ref, shots):
        self.shots, (_, self.along, self.rows, lanes) = shots, ref.shape
        self.flat = ref.reshape(ref.shape[0] * self.along * self.rows, lanes)

    def __call__(self, index, row, j):
        place = (index * self.along + j) * self.rows + row
        return self.flat[pl.ds(place, self.shots, stride=0), :]


def split_bf16(values):
    high = values.astype(jnp.bfloat16)
    low = (values - high.astype(jnp.float32)).astype(jnp.bfloat16)
    return high, low


def outer_kernel(*refs):
    sources, outs, (field_ref, param_ref, field_sem, param_sem) = refs[:8], refs[8:10], refs[10:]
    shots, across, along, tile, lanes = sources[0].shape
    depth = along * lanes
    copies = []
    for side in range(2):
        place = side * (across - 1)
        for i in range(4):
            copies.append(
                pltpu.make_async_copy(
                    sources[i].at[:, pl.ds(place, 1), :, pl.ds(side * STEPS, STEPS)],
                    field_ref.at[side, i, :, :, :, pl.ds(side * STEPS, STEPS)],
                    field_sem.at[side, i],
                )
            )
        for i in range(4):
            copies.append(
                pltpu.make_async_copy(
                    sources[4 + i].at[pl.ds(place * tile, tile)],
                    param_ref.at[side, i],
                    param_sem.at[side, i],
                )
            )
    for copy in copies:
        copy.start()
    tiles_by_side = []
    for side in range(2):
        for copy in copies[8 * side : 8 * side + 8]:
            copy.wait()
        terms = tilt_coefficients(*[param_ref[side, i] for i in range(4)])
        rows = []
        for index, term in enumerate(terms):
            term = -term if index == 1 and side == 0 else term
            for distance in reversed(range(STEPS - 1)):
                place = distance if side == 0 else tile - 1 - distance
                rows.append(term[place : place + 1, :])
        while len(rows) < 2 * shots:
            rows.append(jnp.zeros((1, depth), jnp.float32))
        tiles_by_side.append(jnp.concatenate(rows, 0))

    stride = along * tile
    flat = field_ref.reshape(2 * 4 * shots * stride, lanes)
    for turn in range(2):
        side = outer_side(turn)
        out = outs[turn]

        def row(field, distance):
            base = (side * 4 + field) * shots * stride + distance + side * (tile - 1 - 2 * distance)
            return jnp.concatenate(
                [flat[pl.ds(base + j * tile, shots, stride=stride), :] for j in range(along)], 1
            )

        position = 0

        def put(first, second):
            nonlocal position
            out[pl.ds(position, 2 * shots), :] = jnp.concatenate([first, second], 0).astype(
                jnp.bfloat16
            )
            position += 2 * shots

        for field in range(4):
            near = row(field, 0)
            put(near, near - near.astype(jnp.bfloat16).astype(jnp.float32))
        for first, second in far_items():
            put(row(*first), row(*second))
        out[pl.ds(position, 2 * shots), :] = jnp.where(
            side == 1, tiles_by_side[1], tiles_by_side[0]
        ).astype(jnp.bfloat16)


def outer_side(turn):
    return jnp.where(lax.axis_index("brick") % 2 == turn, 1, 0)


def far_items():
    items = []
    for field in range(2):
        items += [(field, distance) for distance in range(1, STEPS)]
    for field in range(2, 4):
        items += [(field, distance) for distance in range(1, STEPS - 1)]
    return list(zip(items[0::2], items[1::2]))


def outer_rows(fields, params):
    shots, across, along, tile, lanes = fields[0].shape
    depth = along * lanes
    rows = 2 * shots * (4 + len(far_items()) + 1)
    shape = jax.ShapeDtypeStruct((rows, depth), jnp.bfloat16)
    return pl.pallas_call(
        outer_kernel,
        in_specs=[pl.BlockSpec(memory_space=pltpu.HBM)] * 8,
        out_specs=[pl.BlockSpec(memory_space=pltpu.VMEM)] * 2,
        out_shape=[shape, shape],
        scratch_shapes=[
            pltpu.VMEM((2, 4, shots, 1, along, tile, lanes), jnp.float32),
            pltpu.VMEM((2, 4, tile, depth), jnp.float32),
            pltpu.SemaphoreType.DMA((2, 4)),
            pltpu.SemaphoreType.DMA((2, 4)),
        ],
        compiler_params=compiler_params(60),
        name="outer_rows",
    )(*fields, *params)


def partner(me, k, count):
    if count & (count - 1):
        return (me + k) % count
    return me ^ k


def owner_of(me, k, owners):
    chips = owners // 2
    chip, core = me // 2, me % 2
    return partner(chip, k % chips, chips) * 2 + (core ^ (k // chips))


def sample_rows(values, one_hot):
    high, low = split_bf16(values)
    return jnp.dot(jnp.concatenate([high, low], 1), one_hot, preferred_element_type=jnp.float32)


def interior_kernel(
    p_ref,
    q_ref,
    pp_ref,
    qq_ref,
    courant_ref,
    epsilon_ref,
    delta_ref,
    tilt_ref,
    cells_ref,
    lists_ref,
    edge_ref,
    prior_edge_ref,
    coef_edge_ref,
    p_inner_ref,
    q_inner_ref,
    sample_ref,
    depth_hot_ref,
    column_ref,
    list_hot_ref,
    level_ref,
    coef_ref,
    split_ref,
):
    shots = p_ref.shape[0]
    width, depth = courant_ref.shape
    along = depth // LANES
    p_rows, q_rows, pp_rows, qq_rows = [ShotRows(ref) for ref in (p_ref, q_ref, pp_ref, qq_ref)]

    @pl.loop(0, width, unroll=4)
    def _(x):
        level_ref[0, 0, x] = p_rows[x]
        level_ref[0, 1, x] = q_rows[x]

    terms = tilt_coefficients(courant_ref[...], epsilon_ref[...], delta_ref[...], tilt_ref[...])
    for index, term in enumerate(terms):
        for j in range(along):
            coef_ref[index, j] = term[:, j * LANES : (j + 1) * LANES]
        for k in range(STEPS):
            coef_edge_ref[0, index, pl.ds(k, 1), :] = term[k : k + 1, :]
            row = term[width - 1 - k : width - k, :]
            coef_edge_ref[1, index, pl.ds(k, 1), :] = -row if index == 1 else row

    one, zero = jnp.bfloat16(1), jnp.bfloat16(0)
    cells = cells_ref[...]
    column = cells // depth
    column_ref[...] = column
    targets = cells.shape[1]
    z_of = jnp.broadcast_to(cells - column * depth, (16, targets)).astype(jnp.int16)
    places = lax.broadcasted_iota(jnp.int16, (16, targets), 0)
    for base in range(0, depth, 16):
        hot = jnp.where(places + jnp.int16(base) == z_of, one, zero)
        depth_hot_ref[pl.ds(base, 16), :] = hot
        depth_hot_ref[pl.ds(depth + base, 16), :] = hot

    owners, slots, patch = lists_ref.shape[1:]
    me = lax.axis_index("shot")
    rows = []
    for k in range(owners):
        lists = lists_ref[0, owner_of(me, k, owners)]
        rows += [lists[s : s + 1, :] for s in range(slots)]
    count = len(rows)
    while len(rows) % 8:
        rows.append(rows[0])
    upright = jnp.transpose(jnp.concatenate(rows, 0).astype(jnp.float32)).astype(jnp.int32)
    lanes = lax.broadcasted_iota(jnp.int16, (patch, LANES), 1)
    for k in range(count):
        wanted = jnp.broadcast_to(upright[:, k : k + 1], (patch, LANES)).astype(jnp.int16)
        for base in range(0, targets, LANES):
            list_hot_ref[pl.ds(k * patch, patch), pl.ds(base, LANES)] = jnp.where(
                lanes + jnp.int16(base) == wanted, one, zero
            )

    for side in range(2):
        x = 0 if side == 0 else width - 1
        prior_edge_ref[side, 0] = pp_rows[x]
        prior_edge_ref[side, 1] = qq_rows[x]

    coefficients = CoefficientRows(coef_ref, shots)
    offsets = [0]
    for step in range(1, STEPS + 1):
        low, high = step, width - step
        chunk = 8 if (high - low) % 8 == 0 else 10
        offset = offsets[-1]
        offsets.append(offset + high - low)

        @pl.loop(0, -(-(high - low) // chunk))
        def _(index):
            at = jnp.minimum(chunk * index, high - low - chunk)
            start = low + at
            held = []

            def put(r, j, p_new, q_new):
                if step < STEPS:
                    level_ref[step, 0, start + r, :, lanes_of(j)] = p_new
                    level_ref[step, 1, start + r, :, lanes_of(j)] = q_new
                else:
                    p_inner_ref[at + r, :, lanes_of(j)] = p_new
                    q_inner_ref[at + r, :, lanes_of(j)] = q_new
                held.append(p_new)
                if len(held) == 2:
                    first, rest = split_bf16(jnp.concatenate(held, 0))
                    place = pl.multiple_of((offset + at + r - 1) * shots, 2 * shots)
                    split_ref[pl.ds(place, 2 * shots), lanes_of(j)] = first
                    split_ref[pl.ds(place, 2 * shots), lanes_of(along + j)] = rest
                    held.clear()

            def current(field):
                return lambda r, j: level_ref[step - 1, field, start + r, :, lanes_of(j)]

            def prior(field):
                if step == 1:
                    rows = (pp_rows, qq_rows)[field]
                    return lambda r, j: rows.block(start + r, j)
                return lambda r, j: level_ref[step - 2, field, start + r, :, lanes_of(j)]

            advance(
                chunk,
                along,
                current(0),
                current(1),
                prior(0),
                prior(1),
                lambda i, r, j: coefficients(i, start + r, j),
                put,
            )

    for step in range(STEPS):
        for field in range(2):
            for near in range(2):
                edge_ref[0, field, step, near] = level_ref[step, field, step + near]
                edge_ref[1, field, step, near] = level_ref[step, field, width - 1 - step - near]

    found = jnp.dot(split_ref[...], depth_hot_ref[...], preferred_element_type=jnp.float32)
    totals = [jnp.zeros((shots, targets), jnp.float32) for _ in range(STEPS)]
    for x in range(1, width - 1):
        here = column == x
        for step in range(1, STEPS + 1):
            if step <= x < width - step:
                row = (offsets[step - 1] + x - step) * shots
                totals[step - 1] += jnp.where(here, found[row : row + shots], 0.0)
    for step in range(STEPS):
        sample_ref[step] = totals[step]


def interior(fields, params, target_cells, patch_lists):
    shots = fields[0].shape[0]
    width, depth = params[0].shape
    targets = target_cells.shape[0]
    _, owners, slots, patch = patch_lists.shape
    f32 = functools.partial(jax.ShapeDtypeStruct, dtype=jnp.float32)
    out_shape = [
        f32((2, 2, STEPS, 2, shots, depth)),
        f32((2, 2, shots, depth)),
        f32((2, 5, 8, depth)),
        f32((width - 2 * STEPS, shots, depth)),
        f32((width - 2 * STEPS, shots, depth)),
        f32((STEPS, shots, targets)),
        jax.ShapeDtypeStruct((2 * depth, targets), jnp.bfloat16),
        jax.ShapeDtypeStruct((1, targets), jnp.int32),
        jax.ShapeDtypeStruct((owners * slots * patch, targets), jnp.bfloat16),
    ]
    vmem = pl.BlockSpec(memory_space=pltpu.VMEM)
    return pl.pallas_call(
        interior_kernel,
        in_specs=[vmem] * 10,
        out_specs=[vmem] * len(out_shape),
        out_shape=out_shape,
        scratch_shapes=[
            pltpu.VMEM((STEPS, 2, width, shots, depth), jnp.float32),
            pltpu.VMEM((5, depth // LANES, width, LANES), jnp.float32),
            pltpu.VMEM((STEPS * (width - STEPS - 1) * shots, 2 * depth), jnp.bfloat16),
        ],
        compiler_params=compiler_params(40),
        cost_estimate=pl.CostEstimate(
            flops=200 * STEPS * shots * width * depth, bytes_accessed=8 * MIB, transcendentals=0
        ),
        name="interior",
    )(*fields, *params, target_cells.reshape(1, targets), patch_lists)


def finish_kernel(
    even_ref,
    odd_ref,
    edge_ref,
    prior_edge_ref,
    coef_edge_ref,
    sample_ref,
    depth_hot_ref,
    column_ref,
    list_hot_ref,
    spectra_ref,
    table_ref,
    spectra_out_ref,
    final_ref,
    *rest,
    width,
):
    packed_refs = rest[:-6]
    level_ref, prior_ref, coef_ref, feature_ref, out_ref, out_sem = rest[-6:]
    shots, depth = edge_ref.shape[-2:]
    targets = column_ref.shape[1]
    first = -STEPS
    pair = 2 * shots
    for turn, ref in enumerate((even_ref, odd_ref)):
        side = outer_side(turn)
        for field in range(4):
            both = ref[pl.ds(field * pair, pair), :].astype(jnp.float32)
            value = both[:shots] + both[shots:]
            if field < 2:
                level_ref[side, field, 0, -1 - first] = value
            else:
                prior_ref[side, field - 2, -1 - (1 - STEPS)] = value
        for index, items in enumerate(far_items()):
            both = ref[pl.ds((4 + index) * pair, pair), :].astype(jnp.float32)
            for half, (field, distance) in enumerate(items):
                value = both[half * shots : (half + 1) * shots]
                if field < 2:
                    level_ref[side, field, 0, -1 - distance - first] = value
                else:
                    prior_ref[side, field - 2, -1 - distance - (1 - STEPS)] = value
        params = ref[pl.ds((4 + len(far_items())) * pair, pair), :].astype(jnp.float32)
        for index in range(5):
            far = params[index * (STEPS - 1) : (index + 1) * (STEPS - 1)]
            for j, block in enumerate(blocks(far)):
                coef_ref[side, index, j, pl.ds(0, STEPS - 1), :] = block
    for side in range(2):
        for index in range(5):
            near = coef_edge_ref[side, index, pl.ds(0, STEPS), :]
            for j, block in enumerate(blocks(near)):
                coef_ref[side, index, j, pl.ds(STEPS - 1, STEPS), :] = block
        for field in range(2):
            prior_ref[side, field, STEPS - 1] = prior_edge_ref[side, field]
            for step in range(STEPS):
                for near in range(2):
                    level_ref[side, field, step, step + near - first] = edge_ref[
                        side, field, step, near
                    ]

    for step in range(1, STEPS + 1):
        low = step - STEPS

        for side in range(2):
            coefficients = CoefficientRows(coef_ref.at[side], shots)

            def current(field):
                return lambda r, j: level_ref[side, field, step - 1, low + r - first, :, lanes_of(j)]

            def prior(field):
                if step == 1:
                    place = low - (1 - STEPS)
                    return lambda r, j: prior_ref[side, field, place + r, :, lanes_of(j)]
                return lambda r, j: level_ref[side, field, step - 2, low + r - first, :, lanes_of(j)]

            def put(r, j, p_new, q_new):
                if step < STEPS:
                    level_ref[side, 0, step, low + r - first, :, lanes_of(j)] = p_new
                    level_ref[side, 1, step, low + r - first, :, lanes_of(j)] = q_new
                else:
                    final_ref[side, 0, r, :, lanes_of(j)] = p_new
                    final_ref[side, 1, r, :, lanes_of(j)] = q_new

            advance(
                STEPS,
                depth // LANES,
                current(0),
                current(1),
                prior(0),
                prior(1),
                lambda i, r, j: coefficients(i, low + r - (1 - STEPS), j),
                put,
            )

    column = column_ref[...]
    places, values = [], []
    for step in range(1, STEPS + 1):
        for side in range(2):
            for k in range(step):
                places.append((step, k if side == 0 else width - 1 - k))
                if step < STEPS:
                    values.append(level_ref[side, 0, step, k - first])
                else:
                    values.append(final_ref[side, 0, k])
    found = sample_rows(jnp.concatenate(values, 0), depth_hot_ref[...])
    samples = [sample_ref[step] for step in range(STEPS)]
    for index, (step, x) in enumerate(places):
        samples[step - 1] = samples[step - 1] + jnp.where(
            column == x, found[index * shots : (index + 1) * shots], 0.0
        )

    parts = spectra_ref.shape[0] // shots
    lanes = table_ref.shape[-1]
    for s in range(shots):
        for base in range(0, targets, lanes):
            value = spectra_ref[pl.ds(s * parts, parts), pl.ds(base, lanes)]
            for step in range(STEPS):
                value = value + table_ref[step] * samples[step][s : s + 1, base : base + lanes]
            out_ref[pl.ds(s * parts, parts), pl.ds(base, lanes)] = value
            feature_ref[pl.ds(s * parts, parts), pl.ds(base, lanes)] = value.astype(jnp.bfloat16)

    out_copy = pltpu.make_async_copy(out_ref, spectra_out_ref, out_sem)
    out_copy.start()

    chips = len(packed_refs) - 1
    owners = 2 * chips
    size, patch = packed_refs[0].shape
    slots = list_hot_ref.shape[0] // (owners * patch)
    half = patch // 2
    row = lax.broadcasted_iota(jnp.int32, (half, patch), 0)
    lane = lax.broadcasted_iota(jnp.int32, (half, patch), 1)
    from_last = (lane < half) & (row > lane)
    for g in range(owners):
        packed_ref = packed_refs[min(g, chips)]
        base = max(g - chips, 0) * size
        chosen = lax.dot_general(
            list_hot_ref[pl.ds(g * slots * patch, slots * patch), :],
            feature_ref[...],
            NT,
            preferred_element_type=jnp.float32,
        ).astype(jnp.bfloat16)
        diagonals = []
        for s in range(slots):
            mine = chosen[s * patch : (s + 1) * patch]
            gram = lax.dot_general(mine, mine, NT, preferred_element_type=jnp.float32)
            last = pltpu.roll(gram[half:], half, 1)
            packed_ref[pl.ds(base + s * half, half), :] = jnp.where(from_last, last, gram[:half])
            diagonals.append(jnp.sum(jnp.where(row == lane, last, 0.0), 0, keepdims=True))
        while len(diagonals) % 8:
            diagonals.append(jnp.zeros((1, patch), jnp.float32))
        packed_ref[pl.ds(base + slots * half, len(diagonals)), :] = jnp.concatenate(diagonals, 0)
    out_copy.wait()


def finish(even, odd, inner, spectra, table, width, owners, slots, patch):
    edge, prior_edge, coef_edge, sample, depth_hot, column, list_hot = inner
    shots, depth = edge.shape[-2:]
    targets = column.shape[1]
    features = spectra.shape[0]
    f32 = functools.partial(jax.ShapeDtypeStruct, dtype=jnp.float32)
    rows = slots * (patch // 2) + -(-slots // 8) * 8
    out_shape = [
        f32((features, targets)),
        f32((2, 2, STEPS, shots, depth)),
        *[f32((rows, patch))] * (owners // 2),
        f32((owners // 2 * rows, patch)),
    ]
    vmem = pl.BlockSpec(memory_space=pltpu.VMEM)
    return pl.pallas_call(
        functools.partial(finish_kernel, width=width),
        in_specs=[vmem] * 11,
        out_specs=[pl.BlockSpec(memory_space=pl.ANY)] + [vmem] * (len(out_shape) - 1),
        out_shape=out_shape,
        scratch_shapes=[
            pltpu.VMEM((2, 2, STEPS, 2 * STEPS + 1, shots, depth), jnp.float32),
            pltpu.VMEM((2, 2, STEPS, shots, depth), jnp.float32),
            pltpu.VMEM((2, 5, depth // LANES, 2 * STEPS, LANES), jnp.float32),
            pltpu.VMEM((features, targets), jnp.bfloat16),
            pltpu.VMEM((features, targets), jnp.float32),
            pltpu.SemaphoreType.DMA,
        ],
        compiler_params=compiler_params(40),
        name="finish",
    )(
        even,
        odd,
        edge,
        prior_edge,
        coef_edge,
        sample,
        depth_hot,
        column,
        list_hot,
        spectra,
        table,
    )


def assemble_kernel(p_inner_ref, q_inner_ref, final_ref, p_out_ref, q_out_ref):
    width = p_out_ref.shape[1] * TILE
    for field, (inner, out) in enumerate(((p_inner_ref, p_out_ref), (q_inner_ref, q_out_ref))):
        rows = ShotRows(out)
        for k in range(STEPS):
            rows[k] = final_ref[0, field, k]
            rows[width - 1 - k] = final_ref[1, field, k]

        @pl.loop(STEPS, width - STEPS, unroll=4)
        def _(x):
            rows[x] = inner[x - STEPS]


def assemble(p_inner, q_inner, final):
    inner, shots, depth = p_inner.shape
    across, along = (inner + 2 * STEPS) // TILE, depth // LANES
    shape = jax.ShapeDtypeStruct((shots, across, along, TILE, LANES), jnp.float32)
    vmem = pl.BlockSpec(memory_space=pltpu.VMEM)
    return pl.pallas_call(
        assemble_kernel,
        in_specs=[vmem] * 3,
        out_specs=[vmem] * 2,
        out_shape=[shape, shape],
        compiler_params=compiler_params(16),
        cost_estimate=pl.CostEstimate(flops=8 * MIB, bytes_accessed=4 * MIB, transcendentals=0),
        name="assemble",
    )(p_inner, q_inner, final)


def tiles_kernel(counts_ref, *refs, features):
    received, out_ref = refs[:-1], refs[-1]
    slots, patch = out_ref.shape[2], out_ref.shape[3]
    half = patch // 2
    row = lax.broadcasted_iota(jnp.int32, (half, patch), 0)
    lane = lax.broadcasted_iota(jnp.int32, (half, patch), 1)
    live = counts_ref[0, 0]
    total = received[0][...]
    for ref in received[1:]:
        total = total + ref[pl.ds(0, total.shape[0]), :]
    for s in range(slots):
        scale = jnp.where(s < live, 1.0 / features, 0.0)
        packed = total[s * half : (s + 1) * half] * scale
        diagonal = total[slots * half + s : slots * half + s + 1] * scale
        turned = jnp.transpose(jnp.concatenate([packed, packed], 0))
        flipped = turned[:half]
        corner = turned[half:]
        out_ref[0, 0, s, pl.ds(0, half), :] = jnp.where(
            (lane < half) & (row > lane), flipped, packed
        )
        last = jnp.where(row > lane, packed, jnp.where(row == lane, diagonal, flipped))
        out_ref[0, 0, s, pl.ds(half, half), :] = jnp.where(
            lane < half, corner, pltpu.roll(last, half, 1)
        )


def tiles(received, patch_counts, slots, features):
    patch = received[0].shape[1]
    return pl.pallas_call(
        functools.partial(tiles_kernel, features=features),
        in_specs=[pl.BlockSpec(memory_space=pltpu.SMEM)]
        + [pl.BlockSpec(memory_space=pltpu.VMEM)] * len(received),
        out_specs=pl.BlockSpec(memory_space=pltpu.VMEM),
        out_shape=jax.ShapeDtypeStruct((1, 1, slots, patch, patch), jnp.float32),
        compiler_params=compiler_params(16),
        name="tiles",
    )(patch_counts, *received)


def shards(
    pressure,
    auxiliary,
    pressure_prior,
    auxiliary_prior,
    courant_sq,
    thomsen_epsilon,
    thomsen_delta,
    tilt_angle,
    frequencies,
    spectra,
    target_cells,
    patch_lists,
    patch_counts,
):
    shots, width, depth = pressure.shape
    _, owners, slots, patch = patch_lists.shape
    fields = [tiled(item) for item in (pressure, auxiliary, pressure_prior, auxiliary_prior)]
    params = (courant_sq, thomsen_epsilon, thomsen_delta, tilt_angle)
    parts, targets = spectra.shape[1:]

    bricks = lax.axis_size("brick")
    swapped = []
    for turn, rows in enumerate(outer_rows(fields, params)):
        pairs = []
        for i in range(turn, bricks - 1, 2):
            pairs += [(i, i + 1), (i + 1, i)]
        swapped.append(lax.ppermute(rows, "brick", pairs))
    even, odd = swapped

    moments = jnp.arange(1, STEPS + 1, dtype=jnp.float32)
    angle = frequencies[None, :] * moments[:, None]
    table = jnp.concatenate([jnp.cos(angle), -jnp.sin(angle)], 1)
    table = jnp.broadcast_to(table[:, :, None], (STEPS, parts, 128))

    edge, prior_edge, coef_edge, p_inner, q_inner, sample, depth_hot, column, list_hot = interior(
        fields, params, target_cells, patch_lists
    )
    spectra_out, final, *packed = finish(
        even,
        odd,
        (edge, prior_edge, coef_edge, sample, depth_hot, column, list_hot),
        spectra.reshape(shots * parts, targets),
        table,
        width,
        owners,
        slots,
        patch,
    )
    chips = owners // 2
    beside = lax.ppermute(packed[chips], "shot", [(i, i ^ 1) for i in range(owners)])
    received = [packed[0], beside]
    size = packed[0].shape[0]
    for k in range(1, chips):
        both = packed[k] + beside[k * size : (k + 1) * size]
        pairs = [(i, partner(i // 2, k, chips) * 2 + i % 2) for i in range(owners)]
        received.append(lax.ppermute(both, "shot", pairs))
    pressure_out, auxiliary_out = [untiled(item) for item in assemble(p_inner, q_inner, final)]
    gram_tiles = tiles(received, patch_counts, slots, shots * parts * owners)
    return (pressure_out, auxiliary_out, spectra_out.reshape(spectra.shape), gram_tiles)


def solution(mesh):
    return jax.shard_map(
        shards,
        mesh=mesh,
        in_specs=(
            P("shot", "brick", None),
            P("shot", "brick", None),
            P("shot", "brick", None),
            P("shot", "brick", None),
            P("brick", None),
            P("brick", None),
            P("brick", None),
            P("brick", None),
            P(),
            P("shot", None, "brick"),
            P("brick"),
            P("brick", None, None, None),
            P("brick", "shot"),
        ),
        out_specs=(
            P("shot", "brick", None),
            P("shot", "brick", None),
            P("shot", None, "brick"),
            P("brick", "shot", None, None, None),
        ),
        check_vma=False,
    )
```

```python
import functools
import math

import jax
import jax.numpy as jnp
from jax import lax
from jax.experimental import pallas as pl
from jax.experimental.pallas import tpu as pltpu
from jax.sharding import PartitionSpec as P

STEPS = 4
MIB = 1024 * 1024
NT = (((1,), (1,)), ((), ()))


TILE = 8
LANES = 128


def tiled(field):
    shots, width, depth = field.shape
    parts = field.reshape(shots, width // TILE, TILE, depth // LANES, LANES)
    return parts.transpose(0, 1, 3, 2, 4)


def untiled(parts):
    shots, across, along, tile, lanes = parts.shape
    return parts.transpose(0, 1, 3, 2, 4).reshape(shots, across * tile, along * lanes)


class ShotRows:
    def __init__(self, ref):
        self.shots, self.across, self.along, tile, lanes = ref.shape
        self.stride = self.across * self.along * tile
        self.flat = ref.reshape(self.shots * self.stride, lanes)

    def place(self, x, j):
        if isinstance(x, int):
            start = (x // TILE * self.along + j) * TILE + x % TILE
        else:
            start = (lax.div(x, TILE) * self.along + j) * TILE + lax.rem(x, TILE)
        return pl.ds(start, self.shots, stride=self.stride)

    def __getitem__(self, x):
        return jnp.concatenate([self.flat[self.place(x, j), :] for j in range(self.along)], 1)

    def __setitem__(self, x, row):
        for j in range(self.along):
            self.flat[self.place(x, j), :] = row[:, j * LANES : (j + 1) * LANES]


def compiler_params(mib):
    return pltpu.CompilerParams(vmem_limit_bytes=mib * MIB)


def tilt_coefficients(courant, epsilon, delta, tilt):
    turns = jnp.round(tilt * (2.0 / math.pi))
    rest = (tilt - turns * 1.5703125) - turns * (math.pi / 2 - 1.5703125)
    odd = turns - 2.0 * jnp.floor(turns * 0.5)
    sign = 1.0 - 2.0 * odd
    double = 2.0 * rest
    square = double * double
    sine = double * (
        1.0
        + square
        * (
            -1.0 / 6
            + square
            * (1.0 / 120 + square * (-1.0 / 5040 + square * (1.0 / 362880 - square / 39916800.0)))
        )
    )
    versine = square * (
        0.5
        + square
        * (
            -1.0 / 24
            + square
            * (1.0 / 720 + square * (-1.0 / 40320 + square * (1.0 / 3628800 - square / 479001600.0)))
        )
    )
    sine_sq = jnp.where(odd > 0.5, 1.0 - 0.5 * versine, 0.5 * versine)
    quarter_sin = 0.25 * sign * sine
    gain_p = courant * (1.0 + 2.0 * epsilon)
    gain_q = courant * (1.0 + 2.0 * delta)
    return sine_sq, quarter_sin, courant, gain_p, gain_q


def blocks(row):
    return [row[:, j : j + LANES] for j in range(0, row.shape[1], LANES)]


def depth_terms(row):
    lane = lax.broadcasted_iota(jnp.int32, row[0].shape, 1)
    shallow = [pltpu.roll(block, 1, 1) for block in row]
    deep = [pltpu.roll(block, LANES - 1, 1) for block in row]
    outside = jnp.zeros_like(row[0])
    sums, differences = [], []
    for j in range(len(row)):
        above = jnp.where(lane == 0, shallow[j - 1] if j else outside, shallow[j])
        below = jnp.where(
            lane == LANES - 1, deep[j + 1] if j + 1 < len(row) else outside, deep[j]
        )
        sums.append(below + above)
        differences.append(below - above)
    return sums, differences


def advance(count, p_row, q_row, p_prior, q_prior, coefficient, put):
    p_back, p_here = blocks(p_row(-1)), blocks(p_row(0))
    q_back, q_here = blocks(q_row(-1)), blocks(q_row(0))
    _, p_back_d = depth_terms(p_back)
    _, q_back_d = depth_terms(q_back)
    p_sum, p_here_d = depth_terms(p_here)
    q_sum, q_here_d = depth_terms(q_here)
    for row in range(count):
        p_next, q_next = blocks(p_row(row + 1)), blocks(q_row(row + 1))
        p_next_sum, p_next_d = depth_terms(p_next)
        q_next_sum, q_next_d = depth_terms(q_next)
        p_old, q_old = blocks(p_prior(row)), blocks(q_prior(row))
        p_new, q_new = [], []
        for j in range(len(p_here)):
            sine_sq, quarter_sin, courant, gain_p, gain_q = [coefficient(i, row, j) for i in range(5)]
            twice_p, twice_q = p_here[j] + p_here[j], q_here[j] + q_here[j]
            side = p_next[j] + p_back[j]
            mixed = p_next_d[j] - p_back_d[j]
            across = (side - twice_p) + sine_sq * (p_sum[j] - side) - quarter_sin * mixed
            side = q_next[j] + q_back[j]
            mixed = q_next_d[j] - q_back_d[j]
            along = (q_sum[j] - twice_q) + sine_sq * (side - q_sum[j]) + quarter_sin * mixed
            along = courant * along
            p_new.append((twice_p - p_old[j]) + (gain_p * across + along))
            q_new.append((twice_q - q_old[j]) + (gain_q * across + along))
        put(row, jnp.concatenate(p_new, 1), jnp.concatenate(q_new, 1))
        p_back, p_here, p_back_d, p_here_d, p_sum = p_here, p_next, p_here_d, p_next_d, p_next_sum
        q_back, q_here, q_back_d, q_here_d, q_sum = q_here, q_next, q_here_d, q_next_d, q_next_sum


class CoefficientRows:
    def __init__(self, ref, shots):
        self.shots, (_, self.along, self.rows, lanes) = shots, ref.shape
        self.flat = ref.reshape(ref.shape[0] * self.along * self.rows, lanes)

    def __call__(self, index, row, j):
        place = (index * self.along + j) * self.rows + row
        return self.flat[pl.ds(place, self.shots, stride=0), :]


def split_bf16(values):
    high = values.astype(jnp.bfloat16)
    low = (values - high.astype(jnp.float32)).astype(jnp.bfloat16)
    return high, low


def outer_kernel(*refs):
    sources, outs, (field_ref, param_ref, field_sem, param_sem) = refs[:8], refs[8:10], refs[10:]
    shots, across, along, tile, lanes = sources[0].shape
    depth = along * lanes
    copies = []
    for side in range(2):
        place = side * (across - 1)
        for i in range(4):
            copies.append(
                pltpu.make_async_copy(
                    sources[i].at[:, pl.ds(place, 1), :, pl.ds(side * STEPS, STEPS)],
                    field_ref.at[side, i, :, :, :, pl.ds(side * STEPS, STEPS)],
                    field_sem.at[side, i],
                )
            )
        for i in range(4):
            copies.append(
                pltpu.make_async_copy(
                    sources[4 + i].at[pl.ds(place * tile, tile)],
                    param_ref.at[side, i],
                    param_sem.at[side, i],
                )
            )
    for copy in copies:
        copy.start()
    tiles_by_side = []
    for side in range(2):
        for copy in copies[8 * side : 8 * side + 8]:
            copy.wait()
        terms = tilt_coefficients(*[param_ref[side, i] for i in range(4)])
        rows = []
        for index, term in enumerate(terms):
            term = -term if index == 1 and side == 0 else term
            for distance in reversed(range(STEPS - 1)):
                place = distance if side == 0 else tile - 1 - distance
                rows.append(term[place : place + 1, :])
        while len(rows) < 2 * shots:
            rows.append(jnp.zeros((1, depth), jnp.float32))
        tiles_by_side.append(jnp.concatenate(rows, 0))

    stride = along * tile
    flat = field_ref.reshape(2 * 4 * shots * stride, lanes)
    for turn in range(2):
        side = outer_side(turn)
        out = outs[turn]

        def row(field, distance):
            base = (side * 4 + field) * shots * stride + distance + side * (tile - 1 - 2 * distance)
            return jnp.concatenate(
                [flat[pl.ds(base + j * tile, shots, stride=stride), :] for j in range(along)], 1
            )

        position = 0

        def put(first, second):
            nonlocal position
            out[pl.ds(position, 2 * shots), :] = jnp.concatenate([first, second], 0).astype(
                jnp.bfloat16
            )
            position += 2 * shots

        for field in range(4):
            near = row(field, 0)
            put(near, near - near.astype(jnp.bfloat16).astype(jnp.float32))
        for first, second in far_items():
            put(row(*first), row(*second))
        out[pl.ds(position, 2 * shots), :] = jnp.where(
            side == 1, tiles_by_side[1], tiles_by_side[0]
        ).astype(jnp.bfloat16)


def outer_side(turn):
    return jnp.where(lax.axis_index("brick") % 2 == turn, 1, 0)


def far_items():
    items = []
    for field in range(2):
        items += [(field, distance) for distance in range(1, STEPS)]
    for field in range(2, 4):
        items += [(field, distance) for distance in range(1, STEPS - 1)]
    return list(zip(items[0::2], items[1::2]))


def outer_rows(fields, params):
    shots, across, along, tile, lanes = fields[0].shape
    depth = along * lanes
    rows = 2 * shots * (4 + len(far_items()) + 1)
    shape = jax.ShapeDtypeStruct((rows, depth), jnp.bfloat16)
    return pl.pallas_call(
        outer_kernel,
        in_specs=[pl.BlockSpec(memory_space=pltpu.HBM)] * 8,
        out_specs=[pl.BlockSpec(memory_space=pltpu.VMEM)] * 2,
        out_shape=[shape, shape],
        scratch_shapes=[
            pltpu.VMEM((2, 4, shots, 1, along, tile, lanes), jnp.float32),
            pltpu.VMEM((2, 4, tile, depth), jnp.float32),
            pltpu.SemaphoreType.DMA((2, 4)),
            pltpu.SemaphoreType.DMA((2, 4)),
        ],
        compiler_params=compiler_params(60),
        name="outer_rows",
    )(*fields, *params)


def partner(me, k, count):
    if count & (count - 1):
        return (me + k) % count
    return me ^ k


def loop_rows(count):
    sizes = range(10, 16, 2)
    return min(sizes, key=lambda size: (-(-count // size) * (size + 1), size))


def owner_of(me, k, owners):
    chips = owners // 2
    chip, core = me // 2, me % 2
    return partner(chip, k % chips, chips) * 2 + (core ^ (k // chips))


def sample_rows(values, one_hot):
    high, low = split_bf16(values)
    return jnp.dot(jnp.concatenate([high, low], 1), one_hot, preferred_element_type=jnp.float32)


def interior_kernel(
    p_ref,
    q_ref,
    pp_ref,
    qq_ref,
    courant_ref,
    epsilon_ref,
    delta_ref,
    tilt_ref,
    cells_ref,
    lists_ref,
    edge_ref,
    prior_edge_ref,
    coef_edge_ref,
    p_inner_ref,
    q_inner_ref,
    sample_ref,
    depth_hot_ref,
    column_ref,
    list_hot_ref,
    level_ref,
    coef_ref,
    split_ref,
):
    shots = p_ref.shape[0]
    width, depth = courant_ref.shape
    along = depth // LANES
    p_rows, q_rows, pp_rows, qq_rows = [ShotRows(ref) for ref in (p_ref, q_ref, pp_ref, qq_ref)]

    @pl.loop(0, width, unroll=4)
    def _(x):
        level_ref[0, 0, x] = p_rows[x]
        level_ref[0, 1, x] = q_rows[x]

    terms = tilt_coefficients(courant_ref[...], epsilon_ref[...], delta_ref[...], tilt_ref[...])
    for index, term in enumerate(terms):
        for j in range(along):
            coef_ref[index, j] = term[:, j * LANES : (j + 1) * LANES]
        for k in range(STEPS):
            coef_edge_ref[0, index, pl.ds(k, 1), :] = term[k : k + 1, :]
            row = term[width - 1 - k : width - k, :]
            coef_edge_ref[1, index, pl.ds(k, 1), :] = -row if index == 1 else row

    one, zero = jnp.bfloat16(1), jnp.bfloat16(0)
    cells = cells_ref[...]
    column = cells // depth
    column_ref[...] = column
    targets = cells.shape[1]
    z_of = jnp.broadcast_to(cells - column * depth, (16, targets)).astype(jnp.int16)
    places = lax.broadcasted_iota(jnp.int16, (16, targets), 0)
    for base in range(0, depth, 16):
        hot = jnp.where(places + jnp.int16(base) == z_of, one, zero)
        depth_hot_ref[pl.ds(base, 16), :] = hot
        depth_hot_ref[pl.ds(depth + base, 16), :] = hot

    owners, slots, patch = lists_ref.shape[1:]
    me = lax.axis_index("shot")
    rows = []
    for k in range(owners):
        lists = lists_ref[0, owner_of(me, k, owners)]
        rows += [lists[s : s + 1, :] for s in range(slots)]
    count = len(rows)
    while len(rows) % 8:
        rows.append(rows[0])
    upright = jnp.transpose(jnp.concatenate(rows, 0).astype(jnp.float32)).astype(jnp.int32)
    lanes = lax.broadcasted_iota(jnp.int16, (patch, LANES), 1)
    for k in range(count):
        wanted = jnp.broadcast_to(upright[:, k : k + 1], (patch, LANES)).astype(jnp.int16)
        for base in range(0, targets, LANES):
            list_hot_ref[pl.ds(k * patch, patch), pl.ds(base, LANES)] = jnp.where(
                lanes + jnp.int16(base) == wanted, one, zero
            )

    for side in range(2):
        x = 0 if side == 0 else width - 1
        prior_edge_ref[side, 0] = pp_rows[x]
        prior_edge_ref[side, 1] = qq_rows[x]

    coefficients = CoefficientRows(coef_ref, shots)
    offsets = [0]
    for step in range(1, STEPS + 1):
        low, high = step, width - step
        chunk = loop_rows(high - low)
        offset = offsets[-1]
        offsets.append(offset + high - low)

        @pl.loop(0, -(-(high - low) // chunk))
        def _(index):
            at = jnp.minimum(chunk * index, high - low - chunk)
            start = low + at
            held = []

            def put(r, p_new, q_new):
                if step < STEPS:
                    level_ref[step, 0, start + r] = p_new
                    level_ref[step, 1, start + r] = q_new
                else:
                    p_inner_ref[at + r] = p_new
                    q_inner_ref[at + r] = q_new
                held.append(p_new)
                if len(held) == 2:
                    first, rest = split_bf16(jnp.concatenate(held, 0))
                    place = pl.multiple_of((offset + at + r - 1) * shots, 2 * shots)
                    split_ref[pl.ds(place, 2 * shots), pl.ds(0, depth)] = first
                    split_ref[pl.ds(place, 2 * shots), pl.ds(depth, depth)] = rest
                    held.clear()

            advance(
                chunk,
                lambda r: level_ref[step - 1, 0, start + r],
                lambda r: level_ref[step - 1, 1, start + r],
                lambda r: pp_rows[start + r] if step == 1 else level_ref[step - 2, 0, start + r],
                lambda r: qq_rows[start + r] if step == 1 else level_ref[step - 2, 1, start + r],
                lambda i, r, j: coefficients(i, start + r, j),
                put,
            )

    for step in range(STEPS):
        for field in range(2):
            for near in range(2):
                edge_ref[0, field, step, near] = level_ref[step, field, step + near]
                edge_ref[1, field, step, near] = level_ref[step, field, width - 1 - step - near]

    found = jnp.dot(split_ref[...], depth_hot_ref[...], preferred_element_type=jnp.float32)
    totals = [jnp.zeros((shots, targets), jnp.float32) for _ in range(STEPS)]
    for x in range(1, width - 1):
        here = column == x
        for step in range(1, STEPS + 1):
            if step <= x < width - step:
                row = (offsets[step - 1] + x - step) * shots
                totals[step - 1] += jnp.where(here, found[row : row + shots], 0.0)
    for step in range(STEPS):
        sample_ref[step] = totals[step]


def interior(fields, params, target_cells, patch_lists):
    shots = fields[0].shape[0]
    width, depth = params[0].shape
    targets = target_cells.shape[0]
    _, owners, slots, patch = patch_lists.shape
    f32 = functools.partial(jax.ShapeDtypeStruct, dtype=jnp.float32)
    out_shape = [
        f32((2, 2, STEPS, 2, shots, depth)),
        f32((2, 2, shots, depth)),
        f32((2, 5, 8, depth)),
        f32((width - 2 * STEPS, shots, depth)),
        f32((width - 2 * STEPS, shots, depth)),
        f32((STEPS, shots, targets)),
        jax.ShapeDtypeStruct((2 * depth, targets), jnp.bfloat16),
        jax.ShapeDtypeStruct((1, targets), jnp.int32),
        jax.ShapeDtypeStruct((owners * slots * patch, targets), jnp.bfloat16),
    ]
    vmem = pl.BlockSpec(memory_space=pltpu.VMEM)
    return pl.pallas_call(
        interior_kernel,
        in_specs=[vmem] * 10,
        out_specs=[vmem] * len(out_shape),
        out_shape=out_shape,
        scratch_shapes=[
            pltpu.VMEM((STEPS, 2, width, shots, depth), jnp.float32),
            pltpu.VMEM((5, depth // LANES, width, LANES), jnp.float32),
            pltpu.VMEM((STEPS * (width - STEPS - 1) * shots, 2 * depth), jnp.bfloat16),
        ],
        compiler_params=compiler_params(40),
        cost_estimate=pl.CostEstimate(
            flops=200 * STEPS * shots * width * depth, bytes_accessed=8 * MIB, transcendentals=0
        ),
        name="interior",
    )(*fields, *params, target_cells.reshape(1, targets), patch_lists)


def packed_rows(slots, patch):
    return slots * (patch // 2) + -(-slots // 8) * 8


def pack_products(list_hot_ref, owner, feature_ref, out_ref, place, slots):
    patch = out_ref.shape[1]
    half = patch // 2
    base = place * packed_rows(slots, patch)
    row = lax.broadcasted_iota(jnp.int32, (half, patch), 0)
    lane = lax.broadcasted_iota(jnp.int32, (half, patch), 1)
    from_last = (lane < half) & (row > lane)
    chosen = lax.dot_general(
        list_hot_ref[pl.ds(owner * slots * patch, slots * patch), :],
        feature_ref[...],
        NT,
        preferred_element_type=jnp.float32,
    ).astype(jnp.bfloat16)
    diagonals = []
    for s in range(slots):
        mine = chosen[s * patch : (s + 1) * patch]
        gram = lax.dot_general(mine, mine, NT, preferred_element_type=jnp.float32)
        last = pltpu.roll(gram[half:], half, 1)
        out_ref[pl.ds(base + s * half, half), :] = jnp.where(from_last, last, gram[:half])
        diagonals.append(jnp.sum(jnp.where(row == lane, last, 0.0), 0, keepdims=True))
    while len(diagonals) % 8:
        diagonals.append(jnp.zeros((1, patch), jnp.float32))
    out_ref[pl.ds(base + slots * half, len(diagonals)), :] = jnp.concatenate(diagonals, 0)


def own_kernel(list_hot_ref, feature_ref, *out_refs, slots):
    for k, out_ref in enumerate(out_refs):
        pack_products(list_hot_ref, k, feature_ref, out_ref, 0, slots)


def own_products(list_hot, features, chips, slots, patch):
    vmem = pl.BlockSpec(memory_space=pltpu.VMEM)
    shape = jax.ShapeDtypeStruct((packed_rows(slots, patch), patch), jnp.float32)
    return pl.pallas_call(
        functools.partial(own_kernel, slots=slots),
        in_specs=[vmem] * 2,
        out_specs=[vmem] * chips,
        out_shape=[shape] * chips,
        compiler_params=compiler_params(24),
        cost_estimate=pl.CostEstimate(flops=512 * MIB, bytes_accessed=2 * MIB, transcendentals=0),
        name="own_products",
    )(list_hot, features)


def finish_kernel(
    even_ref,
    odd_ref,
    edge_ref,
    prior_edge_ref,
    coef_edge_ref,
    sample_ref,
    depth_hot_ref,
    column_ref,
    list_hot_ref,
    spectra_ref,
    table_ref,
    spectra_out_ref,
    final_ref,
    *rest,
    width,
    slots,
):
    feature_ref, beside_ref, level_ref, prior_ref, coef_ref, out_ref, out_sem = rest
    shots, depth = edge_ref.shape[-2:]
    targets = column_ref.shape[1]
    first = -STEPS
    pair = 2 * shots
    for turn, ref in enumerate((even_ref, odd_ref)):
        side = outer_side(turn)
        for field in range(4):
            both = ref[pl.ds(field * pair, pair), :].astype(jnp.float32)
            value = both[:shots] + both[shots:]
            if field < 2:
                level_ref[side, field, 0, -1 - first] = value
            else:
                prior_ref[side, field - 2, -1 - (1 - STEPS)] = value
        for index, items in enumerate(far_items()):
            both = ref[pl.ds((4 + index) * pair, pair), :].astype(jnp.float32)
            for half, (field, distance) in enumerate(items):
                value = both[half * shots : (half + 1) * shots]
                if field < 2:
                    level_ref[side, field, 0, -1 - distance - first] = value
                else:
                    prior_ref[side, field - 2, -1 - distance - (1 - STEPS)] = value
        params = ref[pl.ds((4 + len(far_items())) * pair, pair), :].astype(jnp.float32)
        for index in range(5):
            far = params[index * (STEPS - 1) : (index + 1) * (STEPS - 1)]
            for j, block in enumerate(blocks(far)):
                coef_ref[side, index, j, pl.ds(0, STEPS - 1), :] = block
    for side in range(2):
        for index in range(5):
            near = coef_edge_ref[side, index, pl.ds(0, STEPS), :]
            for j, block in enumerate(blocks(near)):
                coef_ref[side, index, j, pl.ds(STEPS - 1, STEPS), :] = block
        for field in range(2):
            prior_ref[side, field, STEPS - 1] = prior_edge_ref[side, field]
            for step in range(STEPS):
                for near in range(2):
                    level_ref[side, field, step, step + near - first] = edge_ref[
                        side, field, step, near
                    ]

    for step in range(1, STEPS + 1):
        low = step - STEPS

        for side in range(2):
            coefficients = CoefficientRows(coef_ref.at[side], shots)

            def prior(field):
                if step == 1:
                    return lambda r: prior_ref[side, field, low + r - (1 - STEPS)]
                return lambda r: level_ref[side, field, step - 2, low + r - first]

            def put(r, p_new, q_new):
                if step < STEPS:
                    level_ref[side, 0, step, low + r - first] = p_new
                    level_ref[side, 1, step, low + r - first] = q_new
                else:
                    final_ref[side, 0, r] = p_new
                    final_ref[side, 1, r] = q_new

            advance(
                STEPS,
                lambda r: level_ref[side, 0, step - 1, low + r - first],
                lambda r: level_ref[side, 1, step - 1, low + r - first],
                prior(0),
                prior(1),
                lambda i, r, j: coefficients(i, low + r - (1 - STEPS), j),
                put,
            )

    column = column_ref[...]
    places, values = [], []
    for step in range(1, STEPS + 1):
        for side in range(2):
            for k in range(step):
                places.append((step, k if side == 0 else width - 1 - k))
                if step < STEPS:
                    values.append(level_ref[side, 0, step, k - first])
                else:
                    values.append(final_ref[side, 0, k])
    found = sample_rows(jnp.concatenate(values, 0), depth_hot_ref[...])
    samples = [sample_ref[step] for step in range(STEPS)]
    for index, (step, x) in enumerate(places):
        samples[step - 1] = samples[step - 1] + jnp.where(
            column == x, found[index * shots : (index + 1) * shots], 0.0
        )

    parts = spectra_ref.shape[0] // shots
    lanes = table_ref.shape[-1]
    for s in range(shots):
        for base in range(0, targets, lanes):
            value = spectra_ref[pl.ds(s * parts, parts), pl.ds(base, lanes)]
            for step in range(STEPS):
                value = value + table_ref[step] * samples[step][s : s + 1, base : base + lanes]
            out_ref[pl.ds(s * parts, parts), pl.ds(base, lanes)] = value
            feature_ref[pl.ds(s * parts, parts), pl.ds(base, lanes)] = value.astype(jnp.bfloat16)

    out_copy = pltpu.make_async_copy(out_ref, spectra_out_ref, out_sem)
    out_copy.start()

    chips = beside_ref.shape[0] // packed_rows(slots, beside_ref.shape[1])
    for k in range(chips):
        pack_products(list_hot_ref, chips + k, feature_ref, beside_ref, k, slots)
    out_copy.wait()


def finish(even, odd, inner, spectra, table, width, owners, slots, patch):
    edge, prior_edge, coef_edge, sample, depth_hot, column, list_hot = inner
    shots, depth = edge.shape[-2:]
    targets = column.shape[1]
    features = spectra.shape[0]
    f32 = functools.partial(jax.ShapeDtypeStruct, dtype=jnp.float32)
    rows = packed_rows(slots, patch)
    out_shape = [
        f32((features, targets)),
        f32((2, 2, STEPS, shots, depth)),
        jax.ShapeDtypeStruct((features, targets), jnp.bfloat16),
        f32((owners // 2 * rows, patch)),
    ]
    vmem = pl.BlockSpec(memory_space=pltpu.VMEM)
    return pl.pallas_call(
        functools.partial(finish_kernel, width=width, slots=slots),
        in_specs=[vmem] * 11,
        out_specs=[pl.BlockSpec(memory_space=pl.ANY)] + [vmem] * (len(out_shape) - 1),
        out_shape=out_shape,
        scratch_shapes=[
            pltpu.VMEM((2, 2, STEPS, 2 * STEPS + 1, shots, depth), jnp.float32),
            pltpu.VMEM((2, 2, STEPS, shots, depth), jnp.float32),
            pltpu.VMEM((2, 5, depth // LANES, 2 * STEPS, LANES), jnp.float32),
            pltpu.VMEM((features, targets), jnp.float32),
            pltpu.SemaphoreType.DMA,
        ],
        compiler_params=compiler_params(40),
        name="finish",
    )(
        even,
        odd,
        edge,
        prior_edge,
        coef_edge,
        sample,
        depth_hot,
        column,
        list_hot,
        spectra,
        table,
    )


def assemble_kernel(p_inner_ref, q_inner_ref, final_ref, p_out_ref, q_out_ref):
    width = p_out_ref.shape[1] * TILE
    for field, (inner, out) in enumerate(((p_inner_ref, p_out_ref), (q_inner_ref, q_out_ref))):
        rows = ShotRows(out)
        for k in range(STEPS):
            rows[k] = final_ref[0, field, k]
            rows[width - 1 - k] = final_ref[1, field, k]

        @pl.loop(STEPS, width - STEPS, unroll=4)
        def _(x):
            rows[x] = inner[x - STEPS]


def assemble(p_inner, q_inner, final):
    inner, shots, depth = p_inner.shape
    across, along = (inner + 2 * STEPS) // TILE, depth // LANES
    shape = jax.ShapeDtypeStruct((shots, across, along, TILE, LANES), jnp.float32)
    vmem = pl.BlockSpec(memory_space=pltpu.VMEM)
    return pl.pallas_call(
        assemble_kernel,
        in_specs=[vmem] * 3,
        out_specs=[vmem] * 2,
        out_shape=[shape, shape],
        compiler_params=compiler_params(16),
        cost_estimate=pl.CostEstimate(flops=8 * MIB, bytes_accessed=4 * MIB, transcendentals=0),
        name="assemble",
    )(p_inner, q_inner, final)


def tiles_kernel(counts_ref, *refs, features):
    received, out_ref = refs[:-1], refs[-1]
    slots, patch = out_ref.shape[2], out_ref.shape[3]
    half = patch // 2
    row = lax.broadcasted_iota(jnp.int32, (half, patch), 0)
    lane = lax.broadcasted_iota(jnp.int32, (half, patch), 1)
    live = counts_ref[0, 0]
    total = received[0][...]
    for ref in received[1:]:
        total = total + ref[pl.ds(0, total.shape[0]), :]
    for s in range(slots):
        scale = jnp.where(s < live, 1.0 / features, 0.0)
        packed = total[s * half : (s + 1) * half] * scale
        diagonal = total[slots * half + s : slots * half + s + 1] * scale
        turned = jnp.transpose(jnp.concatenate([packed, packed], 0))
        flipped = turned[:half]
        corner = turned[half:]
        out_ref[0, 0, s, pl.ds(0, half), :] = jnp.where(
            (lane < half) & (row > lane), flipped, packed
        )
        last = jnp.where(row > lane, packed, jnp.where(row == lane, diagonal, flipped))
        out_ref[0, 0, s, pl.ds(half, half), :] = jnp.where(
            lane < half, corner, pltpu.roll(last, half, 1)
        )


def tiles(received, patch_counts, slots, features):
    patch = received[0].shape[1]
    return pl.pallas_call(
        functools.partial(tiles_kernel, features=features),
        in_specs=[pl.BlockSpec(memory_space=pltpu.SMEM)]
        + [pl.BlockSpec(memory_space=pltpu.VMEM)] * len(received),
        out_specs=pl.BlockSpec(memory_space=pltpu.VMEM),
        out_shape=jax.ShapeDtypeStruct((1, 1, slots, patch, patch), jnp.float32),
        compiler_params=compiler_params(16),
        name="tiles",
    )(patch_counts, *received)


def shards(
    pressure,
    auxiliary,
    pressure_prior,
    auxiliary_prior,
    courant_sq,
    thomsen_epsilon,
    thomsen_delta,
    tilt_angle,
    frequencies,
    spectra,
    target_cells,
    patch_lists,
    patch_counts,
):
    shots, width, depth = pressure.shape
    _, owners, slots, patch = patch_lists.shape
    fields = [tiled(item) for item in (pressure, auxiliary, pressure_prior, auxiliary_prior)]
    params = (courant_sq, thomsen_epsilon, thomsen_delta, tilt_angle)
    parts, targets = spectra.shape[1:]

    bricks = lax.axis_size("brick")
    swapped = []
    for turn, rows in enumerate(outer_rows(fields, params)):
        pairs = []
        for i in range(turn, bricks - 1, 2):
            pairs += [(i, i + 1), (i + 1, i)]
        swapped.append(lax.ppermute(rows, "brick", pairs))
    even, odd = swapped

    moments = jnp.arange(1, STEPS + 1, dtype=jnp.float32)
    angle = frequencies[None, :] * moments[:, None]
    table = jnp.concatenate([jnp.cos(angle), -jnp.sin(angle)], 1)
    table = jnp.broadcast_to(table[:, :, None], (STEPS, parts, 128))

    edge, prior_edge, coef_edge, p_inner, q_inner, sample, depth_hot, column, list_hot = interior(
        fields, params, target_cells, patch_lists
    )
    spectra_out, final, features, for_beside = finish(
        even,
        odd,
        (edge, prior_edge, coef_edge, sample, depth_hot, column, list_hot),
        spectra.reshape(shots * parts, targets),
        table,
        width,
        owners,
        slots,
        patch,
    )
    chips = owners // 2
    beside = lax.ppermute(for_beside, "shot", [(i, i ^ 1) for i in range(owners)])
    packed = own_products(list_hot, features, chips, slots, patch)
    received = [packed[0], beside]
    size = packed[0].shape[0]
    for k in range(1, chips):
        both = packed[k] + beside[k * size : (k + 1) * size]
        pairs = [(i, partner(i // 2, k, chips) * 2 + i % 2) for i in range(owners)]
        received.append(lax.ppermute(both, "shot", pairs))
    pressure_out, auxiliary_out = [untiled(item) for item in assemble(p_inner, q_inner, final)]
    gram_tiles = tiles(received, patch_counts, slots, shots * parts * owners)
    return (pressure_out, auxiliary_out, spectra_out.reshape(spectra.shape), gram_tiles)


def solution(mesh):
    return jax.shard_map(
        shards,
        mesh=mesh,
        in_specs=(
            P("shot", "brick", None),
            P("shot", "brick", None),
            P("shot", "brick", None),
            P("shot", "brick", None),
            P("brick", None),
            P("brick", None),
            P("brick", None),
            P("brick", None),
            P(),
            P("shot", None, "brick"),
            P("brick"),
            P("brick", None, None, None),
            P("brick", "shot"),
        ),
        out_specs=(
            P("shot", "brick", None),
            P("shot", "brick", None),
            P("shot", None, "brick"),
            P("brick", "shot", None, None, None),
        ),
        check_vma=False,
    )
```

```python
import functools
import math

import jax
import jax.numpy as jnp
from jax import lax
from jax.experimental import pallas as pl
from jax.experimental.pallas import tpu as pltpu
from jax.sharding import PartitionSpec as P

STEPS = 4
MIB = 1024 * 1024
NT = (((1,), (1,)), ((), ()))


TILE = 8
LANES = 128


def tiled(field):
    shots, width, depth = field.shape
    parts = field.reshape(shots, width // TILE, TILE, depth // LANES, LANES)
    return parts.transpose(0, 1, 3, 2, 4)


def untiled(parts):
    shots, across, along, tile, lanes = parts.shape
    return parts.transpose(0, 1, 3, 2, 4).reshape(shots, across * tile, along * lanes)


class ShotRows:
    def __init__(self, ref):
        self.shots, self.across, self.along, tile, lanes = ref.shape
        self.stride = self.across * self.along * tile
        self.flat = ref.reshape(self.shots * self.stride, lanes)

    def place(self, x, j):
        if isinstance(x, int):
            start = (x // TILE * self.along + j) * TILE + x % TILE
        else:
            start = (lax.div(x, TILE) * self.along + j) * TILE + lax.rem(x, TILE)
        return pl.ds(start, self.shots, stride=self.stride)

    def __getitem__(self, x):
        return jnp.concatenate([self.flat[self.place(x, j), :] for j in range(self.along)], 1)

    def __setitem__(self, x, row):
        for j in range(self.along):
            self.flat[self.place(x, j), :] = row[:, j * LANES : (j + 1) * LANES]


def compiler_params(mib):
    return pltpu.CompilerParams(vmem_limit_bytes=mib * MIB)


def tilt_coefficients(courant, epsilon, delta, tilt):
    turns = jnp.round(tilt * (2.0 / math.pi))
    rest = (tilt - turns * 1.5703125) - turns * (math.pi / 2 - 1.5703125)
    odd = turns - 2.0 * jnp.floor(turns * 0.5)
    sign = 1.0 - 2.0 * odd
    double = 2.0 * rest
    square = double * double
    sine = double * (
        1.0
        + square
        * (
            -1.0 / 6
            + square
            * (1.0 / 120 + square * (-1.0 / 5040 + square * (1.0 / 362880 - square / 39916800.0)))
        )
    )
    versine = square * (
        0.5
        + square
        * (
            -1.0 / 24
            + square
            * (1.0 / 720 + square * (-1.0 / 40320 + square * (1.0 / 3628800 - square / 479001600.0)))
        )
    )
    sine_sq = jnp.where(odd > 0.5, 1.0 - 0.5 * versine, 0.5 * versine)
    quarter_sin = 0.25 * sign * sine
    gain_p = courant * (1.0 + 2.0 * epsilon)
    gain_q = courant * (1.0 + 2.0 * delta)
    return sine_sq, quarter_sin, courant, gain_p, gain_q


def blocks(row):
    return [row[:, j : j + LANES] for j in range(0, row.shape[1], LANES)]


def depth_terms(row):
    lane = lax.broadcasted_iota(jnp.int32, row[0].shape, 1)
    shallow = [pltpu.roll(block, 1, 1) for block in row]
    deep = [pltpu.roll(block, LANES - 1, 1) for block in row]
    outside = jnp.zeros_like(row[0])
    sums, differences = [], []
    for j in range(len(row)):
        above = jnp.where(lane == 0, shallow[j - 1] if j else outside, shallow[j])
        below = jnp.where(
            lane == LANES - 1, deep[j + 1] if j + 1 < len(row) else outside, deep[j]
        )
        sums.append(below + above)
        differences.append(below - above)
    return sums, differences


def advance(count, p_row, q_row, p_prior, q_prior, coefficient, put):
    p_back, p_here = blocks(p_row(-1)), blocks(p_row(0))
    q_back, q_here = blocks(q_row(-1)), blocks(q_row(0))
    _, p_back_d = depth_terms(p_back)
    _, q_back_d = depth_terms(q_back)
    p_sum, p_here_d = depth_terms(p_here)
    q_sum, q_here_d = depth_terms(q_here)
    for row in range(count):
        p_next, q_next = blocks(p_row(row + 1)), blocks(q_row(row + 1))
        p_next_sum, p_next_d = depth_terms(p_next)
        q_next_sum, q_next_d = depth_terms(q_next)
        p_old, q_old = blocks(p_prior(row)), blocks(q_prior(row))
        p_new, q_new = [], []
        for j in range(len(p_here)):
            sine_sq, quarter_sin, courant, gain_p, gain_q = [coefficient(i, row, j) for i in range(5)]
            twice_p, twice_q = p_here[j] + p_here[j], q_here[j] + q_here[j]
            side = p_next[j] + p_back[j]
            mixed = p_next_d[j] - p_back_d[j]
            across = (side - twice_p) + sine_sq * (p_sum[j] - side) - quarter_sin * mixed
            side = q_next[j] + q_back[j]
            mixed = q_next_d[j] - q_back_d[j]
            along = (q_sum[j] - twice_q) + sine_sq * (side - q_sum[j]) + quarter_sin * mixed
            along = courant * along
            p_new.append((twice_p - p_old[j]) + (gain_p * across + along))
            q_new.append((twice_q - q_old[j]) + (gain_q * across + along))
        put(row, jnp.concatenate(p_new, 1), jnp.concatenate(q_new, 1))
        p_back, p_here, p_back_d, p_here_d, p_sum = p_here, p_next, p_here_d, p_next_d, p_next_sum
        q_back, q_here, q_back_d, q_here_d, q_sum = q_here, q_next, q_here_d, q_next_d, q_next_sum


class CoefficientRows:
    def __init__(self, ref, shots):
        self.shots, (_, self.along, self.rows, lanes) = shots, ref.shape
        self.flat = ref.reshape(ref.shape[0] * self.along * self.rows, lanes)

    def __call__(self, index, row, j):
        place = (index * self.along + j) * self.rows + row
        return self.flat[pl.ds(place, self.shots, stride=0), :]


def split_bf16(values):
    high = values.astype(jnp.bfloat16)
    low = (values - high.astype(jnp.float32)).astype(jnp.bfloat16)
    return high, low


def outer_kernel(*refs):
    sources, outs, (field_ref, param_ref, field_sem, param_sem) = refs[:8], refs[8:10], refs[10:]
    shots, across, along, tile, lanes = sources[0].shape
    depth = along * lanes
    copies = []
    for side in range(2):
        place = side * (across - 1)
        for i in range(4):
            copies.append(
                pltpu.make_async_copy(
                    sources[i].at[:, pl.ds(place, 1), :, pl.ds(side * STEPS, STEPS)],
                    field_ref.at[side, i, :, :, :, pl.ds(side * STEPS, STEPS)],
                    field_sem.at[side, i],
                )
            )
        for i in range(4):
            copies.append(
                pltpu.make_async_copy(
                    sources[4 + i].at[pl.ds(place * tile, tile)],
                    param_ref.at[side, i],
                    param_sem.at[side, i],
                )
            )
    for copy in copies:
        copy.start()
    tiles_by_side = []
    for side in range(2):
        for copy in copies[8 * side : 8 * side + 8]:
            copy.wait()
        terms = tilt_coefficients(*[param_ref[side, i] for i in range(4)])
        rows = []
        for index, term in enumerate(terms):
            term = -term if index == 1 and side == 0 else term
            for distance in reversed(range(STEPS - 1)):
                place = distance if side == 0 else tile - 1 - distance
                rows.append(term[place : place + 1, :])
        while len(rows) < 2 * shots:
            rows.append(jnp.zeros((1, depth), jnp.float32))
        tiles_by_side.append(jnp.concatenate(rows, 0))

    stride = along * tile
    flat = field_ref.reshape(2 * 4 * shots * stride, lanes)
    for turn in range(2):
        side = outer_side(turn)
        out = outs[turn]

        def row(field, distance):
            base = (side * 4 + field) * shots * stride + distance + side * (tile - 1 - 2 * distance)
            return jnp.concatenate(
                [flat[pl.ds(base + j * tile, shots, stride=stride), :] for j in range(along)], 1
            )

        position = 0

        def put(first, second):
            nonlocal position
            out[pl.ds(position, 2 * shots), :] = jnp.concatenate([first, second], 0).astype(
                jnp.bfloat16
            )
            position += 2 * shots

        for field in range(4):
            near = row(field, 0)
            put(near, near - near.astype(jnp.bfloat16).astype(jnp.float32))
        for first, second in far_items():
            put(row(*first), row(*second))
        out[pl.ds(position, 2 * shots), :] = jnp.where(
            side == 1, tiles_by_side[1], tiles_by_side[0]
        ).astype(jnp.bfloat16)


def outer_side(turn):
    return jnp.where(lax.axis_index("brick") % 2 == turn, 1, 0)


def far_items():
    items = []
    for field in range(2):
        items += [(field, distance) for distance in range(1, STEPS)]
    for field in range(2, 4):
        items += [(field, distance) for distance in range(1, STEPS - 1)]
    return list(zip(items[0::2], items[1::2]))


def outer_rows(fields, params):
    shots, across, along, tile, lanes = fields[0].shape
    depth = along * lanes
    rows = 2 * shots * (4 + len(far_items()) + 1)
    shape = jax.ShapeDtypeStruct((rows, depth), jnp.bfloat16)
    return pl.pallas_call(
        outer_kernel,
        in_specs=[pl.BlockSpec(memory_space=pltpu.HBM)] * 8,
        out_specs=[pl.BlockSpec(memory_space=pltpu.VMEM)] * 2,
        out_shape=[shape, shape],
        scratch_shapes=[
            pltpu.VMEM((2, 4, shots, 1, along, tile, lanes), jnp.float32),
            pltpu.VMEM((2, 4, tile, depth), jnp.float32),
            pltpu.SemaphoreType.DMA((2, 4)),
            pltpu.SemaphoreType.DMA((2, 4)),
        ],
        compiler_params=compiler_params(60),
        name="outer_rows",
    )(*fields, *params)


def partner(me, k, count):
    if count & (count - 1):
        return (me + k) % count
    return me ^ k


def loop_rows(count):
    sizes = range(10, 32, 2)
    return min(sizes, key=lambda size: (-(-count // size) * (size + 1), size))


def owner_of(me, k, owners):
    chips = owners // 2
    chip, core = me // 2, me % 2
    return partner(chip, k % chips, chips) * 2 + (core ^ (k // chips))


def sample_rows(values, one_hot):
    high, low = split_bf16(values)
    return jnp.dot(jnp.concatenate([high, low], 1), one_hot, preferred_element_type=jnp.float32)


def interior_kernel(
    p_ref,
    q_ref,
    pp_ref,
    qq_ref,
    courant_ref,
    epsilon_ref,
    delta_ref,
    tilt_ref,
    cells_ref,
    lists_ref,
    edge_ref,
    prior_edge_ref,
    coef_edge_ref,
    p_inner_ref,
    q_inner_ref,
    sample_ref,
    depth_hot_ref,
    column_ref,
    list_hot_ref,
    level_ref,
    coef_ref,
    split_ref,
):
    shots = p_ref.shape[0]
    width, depth = courant_ref.shape
    along = depth // LANES
    p_rows, q_rows, pp_rows, qq_rows = [ShotRows(ref) for ref in (p_ref, q_ref, pp_ref, qq_ref)]

    @pl.loop(0, width, unroll=4)
    def _(x):
        level_ref[0, 0, x] = p_rows[x]
        level_ref[0, 1, x] = q_rows[x]

    terms = tilt_coefficients(courant_ref[...], epsilon_ref[...], delta_ref[...], tilt_ref[...])
    for index, term in enumerate(terms):
        for j in range(along):
            coef_ref[index, j] = term[:, j * LANES : (j + 1) * LANES]
        for k in range(STEPS):
            coef_edge_ref[0, index, pl.ds(k, 1), :] = term[k : k + 1, :]
            row = term[width - 1 - k : width - k, :]
            coef_edge_ref[1, index, pl.ds(k, 1), :] = -row if index == 1 else row

    one, zero = jnp.bfloat16(1), jnp.bfloat16(0)
    cells = cells_ref[...]
    column = cells // depth
    column_ref[...] = column
    targets = cells.shape[1]
    z_of = jnp.broadcast_to(cells - column * depth, (16, targets)).astype(jnp.int16)
    places = lax.broadcasted_iota(jnp.int16, (16, targets), 0)
    for base in range(0, depth, 16):
        hot = jnp.where(places + jnp.int16(base) == z_of, one, zero)
        depth_hot_ref[pl.ds(base, 16), :] = hot
        depth_hot_ref[pl.ds(depth + base, 16), :] = hot

    owners, slots, patch = lists_ref.shape[1:]
    me = lax.axis_index("shot")
    rows = []
    for k in range(owners):
        lists = lists_ref[0, owner_of(me, k, owners)]
        rows += [lists[s : s + 1, :] for s in range(slots)]
    count = len(rows)
    while len(rows) % 8:
        rows.append(rows[0])
    upright = jnp.transpose(jnp.concatenate(rows, 0).astype(jnp.float32)).astype(jnp.int32)
    lanes = lax.broadcasted_iota(jnp.int16, (patch, LANES), 1)
    for k in range(count):
        wanted = jnp.broadcast_to(upright[:, k : k + 1], (patch, LANES)).astype(jnp.int16)
        for base in range(0, targets, LANES):
            list_hot_ref[pl.ds(k * patch, patch), pl.ds(base, LANES)] = jnp.where(
                lanes + jnp.int16(base) == wanted, one, zero
            )

    for side in range(2):
        x = 0 if side == 0 else width - 1
        prior_edge_ref[side, 0] = pp_rows[x]
        prior_edge_ref[side, 1] = qq_rows[x]

    coefficients = CoefficientRows(coef_ref, shots)
    offsets = [0]
    for step in range(1, STEPS + 1):
        low, high = step, width - step
        chunk = loop_rows(high - low)
        offset = offsets[-1]
        offsets.append(offset + high - low)

        @pl.loop(0, -(-(high - low) // chunk))
        def _(index):
            at = jnp.minimum(chunk * index, high - low - chunk)
            start = low + at
            held = []

            def put(r, p_new, q_new):
                if step < STEPS:
                    level_ref[step, 0, start + r] = p_new
                    level_ref[step, 1, start + r] = q_new
                else:
                    p_inner_ref[at + r] = p_new
                    q_inner_ref[at + r] = q_new
                held.append(p_new)
                if len(held) == 2:
                    first, rest = split_bf16(jnp.concatenate(held, 0))
                    place = pl.multiple_of((offset + at + r - 1) * shots, 2 * shots)
                    split_ref[pl.ds(place, 2 * shots), pl.ds(0, depth)] = first
                    split_ref[pl.ds(place, 2 * shots), pl.ds(depth, depth)] = rest
                    held.clear()

            advance(
                chunk,
                lambda r: level_ref[step - 1, 0, start + r],
                lambda r: level_ref[step - 1, 1, start + r],
                lambda r: pp_rows[start + r] if step == 1 else level_ref[step - 2, 0, start + r],
                lambda r: qq_rows[start + r] if step == 1 else level_ref[step - 2, 1, start + r],
                lambda i, r, j: coefficients(i, start + r, j),
                put,
            )

    for step in range(STEPS):
        for field in range(2):
            for near in range(2):
                edge_ref[0, field, step, near] = level_ref[step, field, step + near]
                edge_ref[1, field, step, near] = level_ref[step, field, width - 1 - step - near]

    found = jnp.dot(split_ref[...], depth_hot_ref[...], preferred_element_type=jnp.float32)
    totals = [jnp.zeros((shots, targets), jnp.float32) for _ in range(STEPS)]
    for x in range(1, width - 1):
        here = column == x
        for step in range(1, STEPS + 1):
            if step <= x < width - step:
                row = (offsets[step - 1] + x - step) * shots
                totals[step - 1] += jnp.where(here, found[row : row + shots], 0.0)
    for step in range(STEPS):
        sample_ref[step] = totals[step]


def interior(fields, params, target_cells, patch_lists):
    shots = fields[0].shape[0]
    width, depth = params[0].shape
    targets = target_cells.shape[0]
    _, owners, slots, patch = patch_lists.shape
    f32 = functools.partial(jax.ShapeDtypeStruct, dtype=jnp.float32)
    out_shape = [
        f32((2, 2, STEPS, 2, shots, depth)),
        f32((2, 2, shots, depth)),
        f32((2, 5, 8, depth)),
        f32((width - 2 * STEPS, shots, depth)),
        f32((width - 2 * STEPS, shots, depth)),
        f32((STEPS, shots, targets)),
        jax.ShapeDtypeStruct((2 * depth, targets), jnp.bfloat16),
        jax.ShapeDtypeStruct((1, targets), jnp.int32),
        jax.ShapeDtypeStruct((owners * slots * patch, targets), jnp.bfloat16),
    ]
    vmem = pl.BlockSpec(memory_space=pltpu.VMEM)
    return pl.pallas_call(
        interior_kernel,
        in_specs=[vmem] * 10,
        out_specs=[vmem] * len(out_shape),
        out_shape=out_shape,
        scratch_shapes=[
            pltpu.VMEM((STEPS, 2, width, shots, depth), jnp.float32),
            pltpu.VMEM((5, depth // LANES, width, LANES), jnp.float32),
            pltpu.VMEM((STEPS * (width - STEPS - 1) * shots, 2 * depth), jnp.bfloat16),
        ],
        compiler_params=compiler_params(40),
        cost_estimate=pl.CostEstimate(
            flops=200 * STEPS * shots * width * depth, bytes_accessed=8 * MIB, transcendentals=0
        ),
        name="interior",
    )(*fields, *params, target_cells.reshape(1, targets), patch_lists)


def packed_rows(slots, patch):
    return slots * (patch // 2) + -(-slots // 8) * 8


def pack_products(list_hot_ref, owner, feature_ref, out_ref, place, slots):
    patch = out_ref.shape[1]
    half = patch // 2
    base = place * packed_rows(slots, patch)
    row = lax.broadcasted_iota(jnp.int32, (half, patch), 0)
    lane = lax.broadcasted_iota(jnp.int32, (half, patch), 1)
    from_last = (lane < half) & (row > lane)
    chosen = lax.dot_general(
        list_hot_ref[pl.ds(owner * slots * patch, slots * patch), :],
        feature_ref[...],
        NT,
        preferred_element_type=jnp.float32,
    ).astype(jnp.bfloat16)
    diagonals = []
    for s in range(slots):
        mine = chosen[s * patch : (s + 1) * patch]
        gram = lax.dot_general(mine, mine, NT, preferred_element_type=jnp.float32)
        last = pltpu.roll(gram[half:], half, 1)
        out_ref[pl.ds(base + s * half, half), :] = jnp.where(from_last, last, gram[:half])
        diagonals.append(jnp.sum(jnp.where(row == lane, last, 0.0), 0, keepdims=True))
    while len(diagonals) % 8:
        diagonals.append(jnp.zeros((1, patch), jnp.float32))
    out_ref[pl.ds(base + slots * half, len(diagonals)), :] = jnp.concatenate(diagonals, 0)


def own_kernel(list_hot_ref, feature_ref, *out_refs, slots):
    for k, out_ref in enumerate(out_refs):
        pack_products(list_hot_ref, k, feature_ref, out_ref, 0, slots)


def own_products(list_hot, features, chips, slots, patch):
    vmem = pl.BlockSpec(memory_space=pltpu.VMEM)
    shape = jax.ShapeDtypeStruct((packed_rows(slots, patch), patch), jnp.float32)
    return pl.pallas_call(
        functools.partial(own_kernel, slots=slots),
        in_specs=[vmem] * 2,
        out_specs=[vmem] * chips,
        out_shape=[shape] * chips,
        compiler_params=compiler_params(24),
        cost_estimate=pl.CostEstimate(flops=512 * MIB, bytes_accessed=2 * MIB, transcendentals=0),
        name="own_products",
    )(list_hot, features)


def finish_kernel(
    even_ref,
    odd_ref,
    edge_ref,
    prior_edge_ref,
    coef_edge_ref,
    sample_ref,
    depth_hot_ref,
    column_ref,
    list_hot_ref,
    spectra_ref,
    table_ref,
    spectra_out_ref,
    final_ref,
    *rest,
    width,
    slots,
):
    feature_ref, beside_ref, level_ref, prior_ref, coef_ref, out_ref, out_sem = rest
    shots, depth = edge_ref.shape[-2:]
    targets = column_ref.shape[1]
    first = -STEPS
    pair = 2 * shots
    for turn, ref in enumerate((even_ref, odd_ref)):
        side = outer_side(turn)
        for field in range(4):
            both = ref[pl.ds(field * pair, pair), :].astype(jnp.float32)
            value = both[:shots] + both[shots:]
            if field < 2:
                level_ref[side, field, 0, -1 - first] = value
            else:
                prior_ref[side, field - 2, -1 - (1 - STEPS)] = value
        for index, items in enumerate(far_items()):
            both = ref[pl.ds((4 + index) * pair, pair), :].astype(jnp.float32)
            for half, (field, distance) in enumerate(items):
                value = both[half * shots : (half + 1) * shots]
                if field < 2:
                    level_ref[side, field, 0, -1 - distance - first] = value
                else:
                    prior_ref[side, field - 2, -1 - distance - (1 - STEPS)] = value
        params = ref[pl.ds((4 + len(far_items())) * pair, pair), :].astype(jnp.float32)
        for index in range(5):
            far = params[index * (STEPS - 1) : (index + 1) * (STEPS - 1)]
            for j, block in enumerate(blocks(far)):
                coef_ref[side, index, j, pl.ds(0, STEPS - 1), :] = block
    for side in range(2):
        for index in range(5):
            near = coef_edge_ref[side, index, pl.ds(0, STEPS), :]
            for j, block in enumerate(blocks(near)):
                coef_ref[side, index, j, pl.ds(STEPS - 1, STEPS), :] = block
        for field in range(2):
            prior_ref[side, field, STEPS - 1] = prior_edge_ref[side, field]
            for step in range(STEPS):
                for near in range(2):
                    level_ref[side, field, step, step + near - first] = edge_ref[
                        side, field, step, near
                    ]

    for step in range(1, STEPS + 1):
        low = step - STEPS

        for side in range(2):
            coefficients = CoefficientRows(coef_ref.at[side], shots)

            def prior(field):
                if step == 1:
                    return lambda r: prior_ref[side, field, low + r - (1 - STEPS)]
                return lambda r: level_ref[side, field, step - 2, low + r - first]

            def put(r, p_new, q_new):
                if step < STEPS:
                    level_ref[side, 0, step, low + r - first] = p_new
                    level_ref[side, 1, step, low + r - first] = q_new
                else:
                    final_ref[side, 0, r] = p_new
                    final_ref[side, 1, r] = q_new

            advance(
                STEPS,
                lambda r: level_ref[side, 0, step - 1, low + r - first],
                lambda r: level_ref[side, 1, step - 1, low + r - first],
                prior(0),
                prior(1),
                lambda i, r, j: coefficients(i, low + r - (1 - STEPS), j),
                put,
            )

    column = column_ref[...]
    places, values = [], []
    for step in range(1, STEPS + 1):
        for side in range(2):
            for k in range(step):
                places.append((step, k if side == 0 else width - 1 - k))
                if step < STEPS:
                    values.append(level_ref[side, 0, step, k - first])
                else:
                    values.append(final_ref[side, 0, k])
    found = sample_rows(jnp.concatenate(values, 0), depth_hot_ref[...])
    samples = [sample_ref[step] for step in range(STEPS)]
    for index, (step, x) in enumerate(places):
        samples[step - 1] = samples[step - 1] + jnp.where(
            column == x, found[index * shots : (index + 1) * shots], 0.0
        )

    parts = spectra_ref.shape[0] // shots
    lanes = table_ref.shape[-1]
    for s in range(shots):
        for base in range(0, targets, lanes):
            value = spectra_ref[pl.ds(s * parts, parts), pl.ds(base, lanes)]
            for step in range(STEPS):
                value = value + table_ref[step] * samples[step][s : s + 1, base : base + lanes]
            out_ref[pl.ds(s * parts, parts), pl.ds(base, lanes)] = value
            feature_ref[pl.ds(s * parts, parts), pl.ds(base, lanes)] = value.astype(jnp.bfloat16)

    out_copy = pltpu.make_async_copy(out_ref, spectra_out_ref, out_sem)
    out_copy.start()

    chips = beside_ref.shape[0] // packed_rows(slots, beside_ref.shape[1])
    for k in range(chips):
        pack_products(list_hot_ref, chips + k, feature_ref, beside_ref, k, slots)
    out_copy.wait()


def finish(even, odd, inner, spectra, table, width, owners, slots, patch):
    edge, prior_edge, coef_edge, sample, depth_hot, column, list_hot = inner
    shots, depth = edge.shape[-2:]
    targets = column.shape[1]
    features = spectra.shape[0]
    f32 = functools.partial(jax.ShapeDtypeStruct, dtype=jnp.float32)
    rows = packed_rows(slots, patch)
    out_shape = [
        f32((features, targets)),
        f32((2, 2, STEPS, shots, depth)),
        jax.ShapeDtypeStruct((features, targets), jnp.bfloat16),
        f32((owners // 2 * rows, patch)),
    ]
    vmem = pl.BlockSpec(memory_space=pltpu.VMEM)
    return pl.pallas_call(
        functools.partial(finish_kernel, width=width, slots=slots),
        in_specs=[vmem] * 11,
        out_specs=[pl.BlockSpec(memory_space=pl.ANY)] + [vmem] * (len(out_shape) - 1),
        out_shape=out_shape,
        scratch_shapes=[
            pltpu.VMEM((2, 2, STEPS, 2 * STEPS + 1, shots, depth), jnp.float32),
            pltpu.VMEM((2, 2, STEPS, shots, depth), jnp.float32),
            pltpu.VMEM((2, 5, depth // LANES, 2 * STEPS, LANES), jnp.float32),
            pltpu.VMEM((features, targets), jnp.float32),
            pltpu.SemaphoreType.DMA,
        ],
        compiler_params=compiler_params(40),
        name="finish",
    )(
        even,
        odd,
        edge,
        prior_edge,
        coef_edge,
        sample,
        depth_hot,
        column,
        list_hot,
        spectra,
        table,
    )


def assemble_kernel(p_inner_ref, q_inner_ref, final_ref, p_out_ref, q_out_ref):
    width = p_out_ref.shape[1] * TILE
    for field, (inner, out) in enumerate(((p_inner_ref, p_out_ref), (q_inner_ref, q_out_ref))):
        rows = ShotRows(out)
        for k in range(STEPS):
            rows[k] = final_ref[0, field, k]
            rows[width - 1 - k] = final_ref[1, field, k]

        @pl.loop(STEPS, width - STEPS, unroll=4)
        def _(x):
            rows[x] = inner[x - STEPS]


def assemble(p_inner, q_inner, final):
    inner, shots, depth = p_inner.shape
    across, along = (inner + 2 * STEPS) // TILE, depth // LANES
    shape = jax.ShapeDtypeStruct((shots, across, along, TILE, LANES), jnp.float32)
    vmem = pl.BlockSpec(memory_space=pltpu.VMEM)
    return pl.pallas_call(
        assemble_kernel,
        in_specs=[vmem] * 3,
        out_specs=[vmem] * 2,
        out_shape=[shape, shape],
        compiler_params=compiler_params(16),
        cost_estimate=pl.CostEstimate(flops=8 * MIB, bytes_accessed=4 * MIB, transcendentals=0),
        name="assemble",
    )(p_inner, q_inner, final)


def tiles_kernel(counts_ref, *refs, features):
    received, out_ref = refs[:-1], refs[-1]
    slots, patch = out_ref.shape[2], out_ref.shape[3]
    half = patch // 2
    row = lax.broadcasted_iota(jnp.int32, (half, patch), 0)
    lane = lax.broadcasted_iota(jnp.int32, (half, patch), 1)
    live = counts_ref[0, 0]
    total = received[0][...]
    for ref in received[1:]:
        total = total + ref[pl.ds(0, total.shape[0]), :]
    for s in range(slots):
        scale = jnp.where(s < live, 1.0 / features, 0.0)
        packed = total[s * half : (s + 1) * half] * scale
        diagonal = total[slots * half + s : slots * half + s + 1] * scale
        turned = jnp.transpose(jnp.concatenate([packed, packed], 0))
        flipped = turned[:half]
        corner = turned[half:]
        out_ref[0, 0, s, pl.ds(0, half), :] = jnp.where(
            (lane < half) & (row > lane), flipped, packed
        )
        last = jnp.where(row > lane, packed, jnp.where(row == lane, diagonal, flipped))
        out_ref[0, 0, s, pl.ds(half, half), :] = jnp.where(
            lane < half, corner, pltpu.roll(last, half, 1)
        )


def tiles(received, patch_counts, slots, features):
    patch = received[0].shape[1]
    return pl.pallas_call(
        functools.partial(tiles_kernel, features=features),
        in_specs=[pl.BlockSpec(memory_space=pltpu.SMEM)]
        + [pl.BlockSpec(memory_space=pltpu.VMEM)] * len(received),
        out_specs=pl.BlockSpec(memory_space=pltpu.VMEM),
        out_shape=jax.ShapeDtypeStruct((1, 1, slots, patch, patch), jnp.float32),
        compiler_params=compiler_params(16),
        name="tiles",
    )(patch_counts, *received)


def shards(
    pressure,
    auxiliary,
    pressure_prior,
    auxiliary_prior,
    courant_sq,
    thomsen_epsilon,
    thomsen_delta,
    tilt_angle,
    frequencies,
    spectra,
    target_cells,
    patch_lists,
    patch_counts,
):
    shots, width, depth = pressure.shape
    _, owners, slots, patch = patch_lists.shape
    fields = [tiled(item) for item in (pressure, auxiliary, pressure_prior, auxiliary_prior)]
    params = (courant_sq, thomsen_epsilon, thomsen_delta, tilt_angle)
    parts, targets = spectra.shape[1:]

    bricks = lax.axis_size("brick")
    swapped = []
    for turn, rows in enumerate(outer_rows(fields, params)):
        pairs = []
        for i in range(turn, bricks - 1, 2):
            pairs += [(i, i + 1), (i + 1, i)]
        swapped.append(lax.ppermute(rows, "brick", pairs))
    even, odd = swapped

    moments = jnp.arange(1, STEPS + 1, dtype=jnp.float32)
    angle = frequencies[None, :] * moments[:, None]
    table = jnp.concatenate([jnp.cos(angle), -jnp.sin(angle)], 1)
    table = jnp.broadcast_to(table[:, :, None], (STEPS, parts, 128))

    edge, prior_edge, coef_edge, p_inner, q_inner, sample, depth_hot, column, list_hot = interior(
        fields, params, target_cells, patch_lists
    )
    spectra_out, final, features, for_beside = finish(
        even,
        odd,
        (edge, prior_edge, coef_edge, sample, depth_hot, column, list_hot),
        spectra.reshape(shots * parts, targets),
        table,
        width,
        owners,
        slots,
        patch,
    )
    chips = owners // 2
    beside = lax.ppermute(for_beside, "shot", [(i, i ^ 1) for i in range(owners)])
    packed = own_products(list_hot, features, chips, slots, patch)
    received = [packed[0], beside]
    size = packed[0].shape[0]
    for k in range(1, chips):
        both = packed[k] + beside[k * size : (k + 1) * size]
        pairs = [(i, partner(i // 2, k, chips) * 2 + i % 2) for i in range(owners)]
        received.append(lax.ppermute(both, "shot", pairs))
    pressure_out, auxiliary_out = [untiled(item) for item in assemble(p_inner, q_inner, final)]
    gram_tiles = tiles(received, patch_counts, slots, shots * parts * owners)
    return (pressure_out, auxiliary_out, spectra_out.reshape(spectra.shape), gram_tiles)


def solution(mesh):
    return jax.shard_map(
        shards,
        mesh=mesh,
        in_specs=(
            P("shot", "brick", None),
            P("shot", "brick", None),
            P("shot", "brick", None),
            P("shot", "brick", None),
            P("brick", None),
            P("brick", None),
            P("brick", None),
            P("brick", None),
            P(),
            P("shot", None, "brick"),
            P("brick"),
            P("brick", None, None, None),
            P("brick", "shot"),
        ),
        out_specs=(
            P("shot", "brick", None),
            P("shot", "brick", None),
            P("shot", None, "brick"),
            P("brick", "shot", None, None, None),
        ),
        check_vma=False,
    )
```

```python
import functools
import math

import jax
import jax.numpy as jnp
from jax import lax
from jax.experimental import pallas as pl
from jax.experimental.pallas import tpu as pltpu
from jax.sharding import PartitionSpec as P

STEPS = 4
MIB = 1024 * 1024
NT = (((1,), (1,)), ((), ()))


TILE = 8
LANES = 128


def tiled(field):
    shots, width, depth = field.shape
    parts = field.reshape(shots, width // TILE, TILE, depth // LANES, LANES)
    return parts.transpose(0, 1, 3, 2, 4)


def untiled(parts):
    shots, across, along, tile, lanes = parts.shape
    return parts.transpose(0, 1, 3, 2, 4).reshape(shots, across * tile, along * lanes)


class ShotRows:
    def __init__(self, ref):
        self.shots, self.across, self.along, tile, lanes = ref.shape
        self.stride = self.across * self.along * tile
        self.flat = ref.reshape(self.shots * self.stride, lanes)

    def place(self, x, j):
        if isinstance(x, int):
            start = (x // TILE * self.along + j) * TILE + x % TILE
        else:
            start = (lax.div(x, TILE) * self.along + j) * TILE + lax.rem(x, TILE)
        return pl.ds(start, self.shots, stride=self.stride)

    def __getitem__(self, x):
        return jnp.concatenate([self.flat[self.place(x, j), :] for j in range(self.along)], 1)

    def __setitem__(self, x, row):
        for j in range(self.along):
            self.flat[self.place(x, j), :] = row[:, j * LANES : (j + 1) * LANES]


def compiler_params(mib):
    return pltpu.CompilerParams(vmem_limit_bytes=mib * MIB)


def tilt_coefficients(courant, epsilon, delta, tilt):
    turns = jnp.round(tilt * (2.0 / math.pi))
    rest = (tilt - turns * 1.5703125) - turns * (math.pi / 2 - 1.5703125)
    odd = turns - 2.0 * jnp.floor(turns * 0.5)
    sign = 1.0 - 2.0 * odd
    double = 2.0 * rest
    square = double * double
    sine = double * (
        1.0
        + square
        * (
            -1.0 / 6
            + square
            * (1.0 / 120 + square * (-1.0 / 5040 + square * (1.0 / 362880 - square / 39916800.0)))
        )
    )
    versine = square * (
        0.5
        + square
        * (
            -1.0 / 24
            + square
            * (1.0 / 720 + square * (-1.0 / 40320 + square * (1.0 / 3628800 - square / 479001600.0)))
        )
    )
    sine_sq = jnp.where(odd > 0.5, 1.0 - 0.5 * versine, 0.5 * versine)
    quarter_sin = 0.25 * sign * sine
    gain_p = courant * (1.0 + 2.0 * epsilon)
    gain_q = courant * (1.0 + 2.0 * delta)
    return sine_sq, quarter_sin, courant, gain_p, gain_q


def blocks(row):
    return [row[:, j : j + LANES] for j in range(0, row.shape[1], LANES)]


def depth_terms(row):
    lane = lax.broadcasted_iota(jnp.int32, row[0].shape, 1)
    shallow = [pltpu.roll(block, 1, 1) for block in row]
    deep = [pltpu.roll(block, LANES - 1, 1) for block in row]
    outside = jnp.zeros_like(row[0])
    sums, differences = [], []
    for j in range(len(row)):
        above = jnp.where(lane == 0, shallow[j - 1] if j else outside, shallow[j])
        below = jnp.where(
            lane == LANES - 1, deep[j + 1] if j + 1 < len(row) else outside, deep[j]
        )
        sums.append(below + above)
        differences.append(below - above)
    return sums, differences


def advance(count, p_row, q_row, p_prior, q_prior, coefficient, put):
    p_back, p_here = blocks(p_row(-1)), blocks(p_row(0))
    q_back, q_here = blocks(q_row(-1)), blocks(q_row(0))
    _, p_back_d = depth_terms(p_back)
    _, q_back_d = depth_terms(q_back)
    p_sum, p_here_d = depth_terms(p_here)
    q_sum, q_here_d = depth_terms(q_here)
    for row in range(count):
        p_next, q_next = blocks(p_row(row + 1)), blocks(q_row(row + 1))
        p_next_sum, p_next_d = depth_terms(p_next)
        q_next_sum, q_next_d = depth_terms(q_next)
        p_old, q_old = blocks(p_prior(row)), blocks(q_prior(row))
        p_new, q_new = [], []
        for j in range(len(p_here)):
            sine_sq, quarter_sin, courant, gain_p, gain_q = [coefficient(i, row, j) for i in range(5)]
            twice_p, twice_q = p_here[j] + p_here[j], q_here[j] + q_here[j]
            side = p_next[j] + p_back[j]
            mixed = p_next_d[j] - p_back_d[j]
            across = (side - twice_p) + sine_sq * (p_sum[j] - side) - quarter_sin * mixed
            side = q_next[j] + q_back[j]
            mixed = q_next_d[j] - q_back_d[j]
            along = (q_sum[j] - twice_q) + sine_sq * (side - q_sum[j]) + quarter_sin * mixed
            along = courant * along
            p_new.append((twice_p - p_old[j]) + (gain_p * across + along))
            q_new.append((twice_q - q_old[j]) + (gain_q * across + along))
        put(row, jnp.concatenate(p_new, 1), jnp.concatenate(q_new, 1))
        p_back, p_here, p_back_d, p_here_d, p_sum = p_here, p_next, p_here_d, p_next_d, p_next_sum
        q_back, q_here, q_back_d, q_here_d, q_sum = q_here, q_next, q_here_d, q_next_d, q_next_sum


class CoefficientRows:
    def __init__(self, ref, shots):
        self.shots, (_, self.along, self.rows, lanes) = shots, ref.shape
        self.flat = ref.reshape(ref.shape[0] * self.along * self.rows, lanes)

    def __call__(self, index, row, j):
        place = (index * self.along + j) * self.rows + row
        return self.flat[pl.ds(place, self.shots, stride=0), :]


def split_bf16(values):
    high = values.astype(jnp.bfloat16)
    low = (values - high.astype(jnp.float32)).astype(jnp.bfloat16)
    return high, low


def outer_kernel(*refs):
    sources, outs, (field_ref, param_ref, field_sem, param_sem) = refs[:8], refs[8:10], refs[10:]
    shots, across, along, tile, lanes = sources[0].shape
    depth = along * lanes
    copies = []
    for side in range(2):
        place = side * (across - 1)
        for i in range(4):
            copies.append(
                pltpu.make_async_copy(
                    sources[i].at[:, pl.ds(place, 1), :, pl.ds(side * STEPS, STEPS)],
                    field_ref.at[side, i, :, :, :, pl.ds(side * STEPS, STEPS)],
                    field_sem.at[side, i],
                )
            )
        for i in range(4):
            copies.append(
                pltpu.make_async_copy(
                    sources[4 + i].at[pl.ds(place * tile, tile)],
                    param_ref.at[side, i],
                    param_sem.at[side, i],
                )
            )
    for copy in copies:
        copy.start()
    tiles_by_side = []
    for side in range(2):
        for copy in copies[8 * side : 8 * side + 8]:
            copy.wait()
        terms = tilt_coefficients(*[param_ref[side, i] for i in range(4)])
        rows = []
        for index, term in enumerate(terms):
            term = -term if index == 1 and side == 0 else term
            for distance in reversed(range(STEPS - 1)):
                place = distance if side == 0 else tile - 1 - distance
                rows.append(term[place : place + 1, :])
        while len(rows) < 2 * shots:
            rows.append(jnp.zeros((1, depth), jnp.float32))
        tiles_by_side.append(jnp.concatenate(rows, 0))

    stride = along * tile
    flat = field_ref.reshape(2 * 4 * shots * stride, lanes)
    for turn in range(2):
        side = outer_side(turn)
        out = outs[turn]

        def row(field, distance):
            base = (side * 4 + field) * shots * stride + distance + side * (tile - 1 - 2 * distance)
            return jnp.concatenate(
                [flat[pl.ds(base + j * tile, shots, stride=stride), :] for j in range(along)], 1
            )

        position = 0

        def put(first, second):
            nonlocal position
            out[pl.ds(position, 2 * shots), :] = jnp.concatenate([first, second], 0).astype(
                jnp.bfloat16
            )
            position += 2 * shots

        for field in range(4):
            near = row(field, 0)
            put(near, near - near.astype(jnp.bfloat16).astype(jnp.float32))
        for first, second in far_items():
            put(row(*first), row(*second))
        out[pl.ds(position, 2 * shots), :] = jnp.where(
            side == 1, tiles_by_side[1], tiles_by_side[0]
        ).astype(jnp.bfloat16)


def outer_side(turn):
    return jnp.where(lax.axis_index("brick") % 2 == turn, 1, 0)


def far_items():
    items = []
    for field in range(2):
        items += [(field, distance) for distance in range(1, STEPS)]
    for field in range(2, 4):
        items += [(field, distance) for distance in range(1, STEPS - 1)]
    return list(zip(items[0::2], items[1::2]))


def outer_rows(fields, params):
    shots, across, along, tile, lanes = fields[0].shape
    depth = along * lanes
    rows = 2 * shots * (4 + len(far_items()) + 1)
    shape = jax.ShapeDtypeStruct((rows, depth), jnp.bfloat16)
    return pl.pallas_call(
        outer_kernel,
        in_specs=[pl.BlockSpec(memory_space=pltpu.HBM)] * 8,
        out_specs=[pl.BlockSpec(memory_space=pltpu.VMEM)] * 2,
        out_shape=[shape, shape],
        scratch_shapes=[
            pltpu.VMEM((2, 4, shots, 1, along, tile, lanes), jnp.float32),
            pltpu.VMEM((2, 4, tile, depth), jnp.float32),
            pltpu.SemaphoreType.DMA((2, 4)),
            pltpu.SemaphoreType.DMA((2, 4)),
        ],
        compiler_params=compiler_params(60),
        name="outer_rows",
    )(*fields, *params)


def partner(me, k, count):
    if count & (count - 1):
        return (me + k) % count
    return me ^ k


def loop_rows(count):
    sizes = range(10, 32, 2)
    return min(sizes, key=lambda size: (-(-count // size) * (size + 1), size))


def owner_of(me, k, owners):
    chips = owners // 2
    chip, core = me // 2, me % 2
    return partner(chip, k % chips, chips) * 2 + (core ^ (k // chips))


def sample_rows(values, one_hot):
    high, low = split_bf16(values)
    return jnp.dot(jnp.concatenate([high, low], 1), one_hot, preferred_element_type=jnp.float32)


def interior_kernel(
    p_ref,
    q_ref,
    pp_ref,
    qq_ref,
    courant_ref,
    epsilon_ref,
    delta_ref,
    tilt_ref,
    cells_ref,
    lists_ref,
    edge_ref,
    prior_edge_ref,
    coef_edge_ref,
    p_inner_ref,
    q_inner_ref,
    sample_ref,
    depth_hot_ref,
    column_ref,
    list_hot_ref,
    level_ref,
    coef_ref,
    split_ref,
):
    shots = p_ref.shape[0]
    width, depth = courant_ref.shape
    along = depth // LANES
    p_rows, q_rows, pp_rows, qq_rows = [ShotRows(ref) for ref in (p_ref, q_ref, pp_ref, qq_ref)]

    for x in range(width):
        level_ref[0, 0, x] = p_rows[x]
        level_ref[0, 1, x] = q_rows[x]

    terms = tilt_coefficients(courant_ref[...], epsilon_ref[...], delta_ref[...], tilt_ref[...])
    for index, term in enumerate(terms):
        for j in range(along):
            coef_ref[index, j] = term[:, j * LANES : (j + 1) * LANES]
        for k in range(STEPS):
            coef_edge_ref[0, index, pl.ds(k, 1), :] = term[k : k + 1, :]
            row = term[width - 1 - k : width - k, :]
            coef_edge_ref[1, index, pl.ds(k, 1), :] = -row if index == 1 else row

    one, zero = jnp.bfloat16(1), jnp.bfloat16(0)
    cells = cells_ref[...]
    column = cells // depth
    column_ref[...] = column
    targets = cells.shape[1]
    z_of = jnp.broadcast_to(cells - column * depth, (16, targets)).astype(jnp.int16)
    places = lax.broadcasted_iota(jnp.int16, (16, targets), 0)
    for base in range(0, depth, 16):
        hot = jnp.where(places + jnp.int16(base) == z_of, one, zero)
        depth_hot_ref[pl.ds(base, 16), :] = hot
        depth_hot_ref[pl.ds(depth + base, 16), :] = hot

    owners, slots, patch = lists_ref.shape[1:]
    me = lax.axis_index("shot")
    rows = []
    for k in range(owners):
        lists = lists_ref[0, owner_of(me, k, owners)]
        rows += [lists[s : s + 1, :] for s in range(slots)]
    count = len(rows)
    while len(rows) % 8:
        rows.append(rows[0])
    upright = jnp.transpose(jnp.concatenate(rows, 0).astype(jnp.float32)).astype(jnp.int32)
    lanes = lax.broadcasted_iota(jnp.int16, (patch, LANES), 1)
    for k in range(count):
        wanted = jnp.broadcast_to(upright[:, k : k + 1], (patch, LANES)).astype(jnp.int16)
        for base in range(0, targets, LANES):
            list_hot_ref[pl.ds(k * patch, patch), pl.ds(base, LANES)] = jnp.where(
                lanes + jnp.int16(base) == wanted, one, zero
            )

    for side in range(2):
        x = 0 if side == 0 else width - 1
        prior_edge_ref[side, 0] = pp_rows[x]
        prior_edge_ref[side, 1] = qq_rows[x]

    coefficients = CoefficientRows(coef_ref, shots)
    offsets = [0]
    for step in range(1, STEPS + 1):
        low, high = step, width - step
        chunk = loop_rows(high - low)
        offset = offsets[-1]
        offsets.append(offset + high - low)

        def run(index):
            at = 0 if chunk == high - low else jnp.minimum(chunk * index, high - low - chunk)
            start = low + at
            held = []

            def put(r, p_new, q_new):
                if step < STEPS:
                    level_ref[step, 0, start + r] = p_new
                    level_ref[step, 1, start + r] = q_new
                else:
                    p_inner_ref[at + r] = p_new
                    q_inner_ref[at + r] = q_new
                held.append(p_new)
                if len(held) == 2:
                    first, rest = split_bf16(jnp.concatenate(held, 0))
                    place = pl.multiple_of((offset + at + r - 1) * shots, 2 * shots)
                    split_ref[pl.ds(place, 2 * shots), pl.ds(0, depth)] = first
                    split_ref[pl.ds(place, 2 * shots), pl.ds(depth, depth)] = rest
                    held.clear()

            advance(
                chunk,
                lambda r: level_ref[step - 1, 0, start + r],
                lambda r: level_ref[step - 1, 1, start + r],
                lambda r: pp_rows[start + r] if step == 1 else level_ref[step - 2, 0, start + r],
                lambda r: qq_rows[start + r] if step == 1 else level_ref[step - 2, 1, start + r],
                lambda i, r, j: coefficients(i, start + r, j),
                put,
            )

        if chunk == high - low:
            run(0)
        else:
            pl.loop(0, -(-(high - low) // chunk))(run)

    for step in range(STEPS):
        for field in range(2):
            for near in range(2):
                edge_ref[0, field, step, near] = level_ref[step, field, step + near]
                edge_ref[1, field, step, near] = level_ref[step, field, width - 1 - step - near]

    found = jnp.dot(split_ref[...], depth_hot_ref[...], preferred_element_type=jnp.float32)
    totals = [jnp.zeros((shots, targets), jnp.float32) for _ in range(STEPS)]
    for x in range(1, width - 1):
        here = column == x
        for step in range(1, STEPS + 1):
            if step <= x < width - step:
                row = (offsets[step - 1] + x - step) * shots
                totals[step - 1] += jnp.where(here, found[row : row + shots], 0.0)
    for step in range(STEPS):
        sample_ref[step] = totals[step]


def interior(fields, params, target_cells, patch_lists):
    shots = fields[0].shape[0]
    width, depth = params[0].shape
    targets = target_cells.shape[0]
    _, owners, slots, patch = patch_lists.shape
    f32 = functools.partial(jax.ShapeDtypeStruct, dtype=jnp.float32)
    out_shape = [
        f32((2, 2, STEPS, 2, shots, depth)),
        f32((2, 2, shots, depth)),
        f32((2, 5, 8, depth)),
        f32((width - 2 * STEPS, shots, depth)),
        f32((width - 2 * STEPS, shots, depth)),
        f32((STEPS, shots, targets)),
        jax.ShapeDtypeStruct((2 * depth, targets), jnp.bfloat16),
        jax.ShapeDtypeStruct((1, targets), jnp.int32),
        jax.ShapeDtypeStruct((owners * slots * patch, targets), jnp.bfloat16),
    ]
    vmem = pl.BlockSpec(memory_space=pltpu.VMEM)
    return pl.pallas_call(
        interior_kernel,
        in_specs=[vmem] * 10,
        out_specs=[vmem] * len(out_shape),
        out_shape=out_shape,
        scratch_shapes=[
            pltpu.VMEM((STEPS, 2, width, shots, depth), jnp.float32),
            pltpu.VMEM((5, depth // LANES, width, LANES), jnp.float32),
            pltpu.VMEM((STEPS * (width - STEPS - 1) * shots, 2 * depth), jnp.bfloat16),
        ],
        compiler_params=compiler_params(40),
        cost_estimate=pl.CostEstimate(
            flops=200 * STEPS * shots * width * depth, bytes_accessed=8 * MIB, transcendentals=0
        ),
        name="interior",
    )(*fields, *params, target_cells.reshape(1, targets), patch_lists)


def packed_rows(slots, patch):
    return slots * (patch // 2) + -(-slots // 8) * 8


def pack_products(list_hot_ref, owner, feature_ref, out_ref, place, slots):
    patch = out_ref.shape[1]
    half = patch // 2
    base = place * packed_rows(slots, patch)
    row = lax.broadcasted_iota(jnp.int32, (half, patch), 0)
    lane = lax.broadcasted_iota(jnp.int32, (half, patch), 1)
    from_last = (lane < half) & (row > lane)
    chosen = lax.dot_general(
        list_hot_ref[pl.ds(owner * slots * patch, slots * patch), :],
        feature_ref[...],
        NT,
        preferred_element_type=jnp.float32,
    ).astype(jnp.bfloat16)
    diagonals = []
    for s in range(slots):
        mine = chosen[s * patch : (s + 1) * patch]
        gram = lax.dot_general(mine, mine, NT, preferred_element_type=jnp.float32)
        last = pltpu.roll(gram[half:], half, 1)
        out_ref[pl.ds(base + s * half, half), :] = jnp.where(from_last, last, gram[:half])
        diagonals.append(jnp.sum(jnp.where(row == lane, last, 0.0), 0, keepdims=True))
    while len(diagonals) % 8:
        diagonals.append(jnp.zeros((1, patch), jnp.float32))
    out_ref[pl.ds(base + slots * half, len(diagonals)), :] = jnp.concatenate(diagonals, 0)


def own_kernel(list_hot_ref, feature_ref, *out_refs, slots):
    for k, out_ref in enumerate(out_refs):
        pack_products(list_hot_ref, k, feature_ref, out_ref, 0, slots)


def own_products(list_hot, features, chips, slots, patch):
    vmem = pl.BlockSpec(memory_space=pltpu.VMEM)
    shape = jax.ShapeDtypeStruct((packed_rows(slots, patch), patch), jnp.float32)
    return pl.pallas_call(
        functools.partial(own_kernel, slots=slots),
        in_specs=[vmem] * 2,
        out_specs=[vmem] * chips,
        out_shape=[shape] * chips,
        compiler_params=compiler_params(24),
        cost_estimate=pl.CostEstimate(flops=512 * MIB, bytes_accessed=2 * MIB, transcendentals=0),
        name="own_products",
    )(list_hot, features)


def finish_kernel(
    even_ref,
    odd_ref,
    edge_ref,
    prior_edge_ref,
    coef_edge_ref,
    sample_ref,
    depth_hot_ref,
    column_ref,
    list_hot_ref,
    spectra_ref,
    table_ref,
    spectra_out_ref,
    final_ref,
    *rest,
    width,
    slots,
):
    feature_ref, beside_ref, level_ref, prior_ref, coef_ref, out_ref, out_sem = rest
    shots, depth = edge_ref.shape[-2:]
    targets = column_ref.shape[1]
    first = -STEPS
    pair = 2 * shots
    for turn, ref in enumerate((even_ref, odd_ref)):
        side = outer_side(turn)
        for field in range(4):
            both = ref[pl.ds(field * pair, pair), :].astype(jnp.float32)
            value = both[:shots] + both[shots:]
            if field < 2:
                level_ref[side, field, 0, -1 - first] = value
            else:
                prior_ref[side, field - 2, -1 - (1 - STEPS)] = value
        for index, items in enumerate(far_items()):
            both = ref[pl.ds((4 + index) * pair, pair), :].astype(jnp.float32)
            for half, (field, distance) in enumerate(items):
                value = both[half * shots : (half + 1) * shots]
                if field < 2:
                    level_ref[side, field, 0, -1 - distance - first] = value
                else:
                    prior_ref[side, field - 2, -1 - distance - (1 - STEPS)] = value
        params = ref[pl.ds((4 + len(far_items())) * pair, pair), :].astype(jnp.float32)
        for index in range(5):
            far = params[index * (STEPS - 1) : (index + 1) * (STEPS - 1)]
            for j, block in enumerate(blocks(far)):
                coef_ref[side, index, j, pl.ds(0, STEPS - 1), :] = block
    for side in range(2):
        for index in range(5):
            near = coef_edge_ref[side, index, pl.ds(0, STEPS), :]
            for j, block in enumerate(blocks(near)):
                coef_ref[side, index, j, pl.ds(STEPS - 1, STEPS), :] = block
        for field in range(2):
            prior_ref[side, field, STEPS - 1] = prior_edge_ref[side, field]
            for step in range(STEPS):
                for near in range(2):
                    level_ref[side, field, step, step + near - first] = edge_ref[
                        side, field, step, near
                    ]

    for step in range(1, STEPS + 1):
        low = step - STEPS

        for side in range(2):
            coefficients = CoefficientRows(coef_ref.at[side], shots)

            def prior(field):
                if step == 1:
                    return lambda r: prior_ref[side, field, low + r - (1 - STEPS)]
                return lambda r: level_ref[side, field, step - 2, low + r - first]

            def put(r, p_new, q_new):
                if step < STEPS:
                    level_ref[side, 0, step, low + r - first] = p_new
                    level_ref[side, 1, step, low + r - first] = q_new
                else:
                    final_ref[side, 0, r] = p_new
                    final_ref[side, 1, r] = q_new

            advance(
                STEPS,
                lambda r: level_ref[side, 0, step - 1, low + r - first],
                lambda r: level_ref[side, 1, step - 1, low + r - first],
                prior(0),
                prior(1),
                lambda i, r, j: coefficients(i, low + r - (1 - STEPS), j),
                put,
            )

    column = column_ref[...]
    places, values = [], []
    for step in range(1, STEPS + 1):
        for side in range(2):
            for k in range(step):
                places.append((step, k if side == 0 else width - 1 - k))
                if step < STEPS:
                    values.append(level_ref[side, 0, step, k - first])
                else:
                    values.append(final_ref[side, 0, k])
    found = sample_rows(jnp.concatenate(values, 0), depth_hot_ref[...])
    samples = [sample_ref[step] for step in range(STEPS)]
    for index, (step, x) in enumerate(places):
        samples[step - 1] = samples[step - 1] + jnp.where(
            column == x, found[index * shots : (index + 1) * shots], 0.0
        )

    parts = spectra_ref.shape[0] // shots
    lanes = table_ref.shape[-1]
    for s in range(shots):
        for base in range(0, targets, lanes):
            value = spectra_ref[pl.ds(s * parts, parts), pl.ds(base, lanes)]
            for step in range(STEPS):
                value = value + table_ref[step] * samples[step][s : s + 1, base : base + lanes]
            out_ref[pl.ds(s * parts, parts), pl.ds(base, lanes)] = value
            feature_ref[pl.ds(s * parts, parts), pl.ds(base, lanes)] = value.astype(jnp.bfloat16)

    out_copy = pltpu.make_async_copy(out_ref, spectra_out_ref, out_sem)
    out_copy.start()

    chips = beside_ref.shape[0] // packed_rows(slots, beside_ref.shape[1])
    for k in range(chips):
        pack_products(list_hot_ref, chips + k, feature_ref, beside_ref, k, slots)
    out_copy.wait()


def finish(even, odd, inner, spectra, table, width, owners, slots, patch):
    edge, prior_edge, coef_edge, sample, depth_hot, column, list_hot = inner
    shots, depth = edge.shape[-2:]
    targets = column.shape[1]
    features = spectra.shape[0]
    f32 = functools.partial(jax.ShapeDtypeStruct, dtype=jnp.float32)
    rows = packed_rows(slots, patch)
    out_shape = [
        f32((features, targets)),
        f32((2, 2, STEPS, shots, depth)),
        jax.ShapeDtypeStruct((features, targets), jnp.bfloat16),
        f32((owners // 2 * rows, patch)),
    ]
    vmem = pl.BlockSpec(memory_space=pltpu.VMEM)
    return pl.pallas_call(
        functools.partial(finish_kernel, width=width, slots=slots),
        in_specs=[vmem] * 11,
        out_specs=[pl.BlockSpec(memory_space=pl.ANY)] + [vmem] * (len(out_shape) - 1),
        out_shape=out_shape,
        scratch_shapes=[
            pltpu.VMEM((2, 2, STEPS, 2 * STEPS + 1, shots, depth), jnp.float32),
            pltpu.VMEM((2, 2, STEPS, shots, depth), jnp.float32),
            pltpu.VMEM((2, 5, depth // LANES, 2 * STEPS, LANES), jnp.float32),
            pltpu.VMEM((features, targets), jnp.float32),
            pltpu.SemaphoreType.DMA,
        ],
        compiler_params=compiler_params(40),
        name="finish",
    )(
        even,
        odd,
        edge,
        prior_edge,
        coef_edge,
        sample,
        depth_hot,
        column,
        list_hot,
        spectra,
        table,
    )


def assemble_kernel(p_inner_ref, q_inner_ref, final_ref, p_out_ref, q_out_ref):
    width = p_out_ref.shape[1] * TILE
    for field, (inner, out) in enumerate(((p_inner_ref, p_out_ref), (q_inner_ref, q_out_ref))):
        rows = ShotRows(out)
        for k in range(STEPS):
            rows[k] = final_ref[0, field, k]
            rows[width - 1 - k] = final_ref[1, field, k]

        @pl.loop(STEPS, width - STEPS, unroll=4)
        def _(x):
            rows[x] = inner[x - STEPS]


def assemble(p_inner, q_inner, final):
    inner, shots, depth = p_inner.shape
    across, along = (inner + 2 * STEPS) // TILE, depth // LANES
    shape = jax.ShapeDtypeStruct((shots, across, along, TILE, LANES), jnp.float32)
    vmem = pl.BlockSpec(memory_space=pltpu.VMEM)
    return pl.pallas_call(
        assemble_kernel,
        in_specs=[vmem] * 3,
        out_specs=[vmem] * 2,
        out_shape=[shape, shape],
        compiler_params=compiler_params(16),
        cost_estimate=pl.CostEstimate(flops=8 * MIB, bytes_accessed=4 * MIB, transcendentals=0),
        name="assemble",
    )(p_inner, q_inner, final)


def tiles_kernel(counts_ref, *refs, features):
    received, out_ref = refs[:-1], refs[-1]
    slots, patch = out_ref.shape[2], out_ref.shape[3]
    half = patch // 2
    row = lax.broadcasted_iota(jnp.int32, (half, patch), 0)
    lane = lax.broadcasted_iota(jnp.int32, (half, patch), 1)
    live = counts_ref[0, 0]
    total = received[0][...]
    for ref in received[1:]:
        total = total + ref[pl.ds(0, total.shape[0]), :]
    for s in range(slots):
        scale = jnp.where(s < live, 1.0 / features, 0.0)
        packed = total[s * half : (s + 1) * half] * scale
        diagonal = total[slots * half + s : slots * half + s + 1] * scale
        turned = jnp.transpose(jnp.concatenate([packed, packed], 0))
        flipped = turned[:half]
        corner = turned[half:]
        out_ref[0, 0, s, pl.ds(0, half), :] = jnp.where(
            (lane < half) & (row > lane), flipped, packed
        )
        last = jnp.where(row > lane, packed, jnp.where(row == lane, diagonal, flipped))
        out_ref[0, 0, s, pl.ds(half, half), :] = jnp.where(
            lane < half, corner, pltpu.roll(last, half, 1)
        )


def tiles(received, patch_counts, slots, features):
    patch = received[0].shape[1]
    return pl.pallas_call(
        functools.partial(tiles_kernel, features=features),
        in_specs=[pl.BlockSpec(memory_space=pltpu.SMEM)]
        + [pl.BlockSpec(memory_space=pltpu.VMEM)] * len(received),
        out_specs=pl.BlockSpec(memory_space=pltpu.VMEM),
        out_shape=jax.ShapeDtypeStruct((1, 1, slots, patch, patch), jnp.float32),
        compiler_params=compiler_params(16),
        name="tiles",
    )(patch_counts, *received)


def shards(
    pressure,
    auxiliary,
    pressure_prior,
    auxiliary_prior,
    courant_sq,
    thomsen_epsilon,
    thomsen_delta,
    tilt_angle,
    frequencies,
    spectra,
    target_cells,
    patch_lists,
    patch_counts,
):
    shots, width, depth = pressure.shape
    _, owners, slots, patch = patch_lists.shape
    fields = [tiled(item) for item in (pressure, auxiliary, pressure_prior, auxiliary_prior)]
    params = (courant_sq, thomsen_epsilon, thomsen_delta, tilt_angle)
    parts, targets = spectra.shape[1:]

    bricks = lax.axis_size("brick")
    swapped = []
    for turn, rows in enumerate(outer_rows(fields, params)):
        pairs = []
        for i in range(turn, bricks - 1, 2):
            pairs += [(i, i + 1), (i + 1, i)]
        swapped.append(lax.ppermute(rows, "brick", pairs))
    even, odd = swapped

    moments = jnp.arange(1, STEPS + 1, dtype=jnp.float32)
    angle = frequencies[None, :] * moments[:, None]
    table = jnp.concatenate([jnp.cos(angle), -jnp.sin(angle)], 1)
    table = jnp.broadcast_to(table[:, :, None], (STEPS, parts, 128))

    edge, prior_edge, coef_edge, p_inner, q_inner, sample, depth_hot, column, list_hot = interior(
        fields, params, target_cells, patch_lists
    )
    spectra_out, final, features, for_beside = finish(
        even,
        odd,
        (edge, prior_edge, coef_edge, sample, depth_hot, column, list_hot),
        spectra.reshape(shots * parts, targets),
        table,
        width,
        owners,
        slots,
        patch,
    )
    chips = owners // 2
    beside = lax.ppermute(for_beside, "shot", [(i, i ^ 1) for i in range(owners)])
    packed = own_products(list_hot, features, chips, slots, patch)
    received = [packed[0], beside]
    size = packed[0].shape[0]
    for k in range(1, chips):
        both = packed[k] + beside[k * size : (k + 1) * size]
        pairs = [(i, partner(i // 2, k, chips) * 2 + i % 2) for i in range(owners)]
        received.append(lax.ppermute(both, "shot", pairs))
    pressure_out, auxiliary_out = [untiled(item) for item in assemble(p_inner, q_inner, final)]
    gram_tiles = tiles(received, patch_counts, slots, shots * parts * owners)
    return (pressure_out, auxiliary_out, spectra_out.reshape(spectra.shape), gram_tiles)


def solution(mesh):
    return jax.shard_map(
        shards,
        mesh=mesh,
        in_specs=(
            P("shot", "brick", None),
            P("shot", "brick", None),
            P("shot", "brick", None),
            P("shot", "brick", None),
            P("brick", None),
            P("brick", None),
            P("brick", None),
            P("brick", None),
            P(),
            P("shot", None, "brick"),
            P("brick"),
            P("brick", None, None, None),
            P("brick", "shot"),
        ),
        out_specs=(
            P("shot", "brick", None),
            P("shot", "brick", None),
            P("shot", None, "brick"),
            P("brick", "shot", None, None, None),
        ),
        check_vma=False,
    )
```

```python
import functools
import math

import jax
import jax.numpy as jnp
from jax import lax
from jax.experimental import pallas as pl
from jax.experimental.pallas import tpu as pltpu
from jax.sharding import PartitionSpec as P

STEPS = 4
MIB = 1024 * 1024
NT = (((1,), (1,)), ((), ()))


TILE = 8
LANES = 128


def tiled(field):
    shots, width, depth = field.shape
    parts = field.reshape(shots, width // TILE, TILE, depth // LANES, LANES)
    return parts.transpose(0, 1, 3, 2, 4)


def untiled(parts):
    shots, across, along, tile, lanes = parts.shape
    return parts.transpose(0, 1, 3, 2, 4).reshape(shots, across * tile, along * lanes)


class ShotRows:
    def __init__(self, ref):
        self.shots, self.across, self.along, tile, lanes = ref.shape
        self.stride = self.across * self.along * tile
        self.flat = ref.reshape(self.shots * self.stride, lanes)

    def place(self, x, j):
        if isinstance(x, int):
            start = (x // TILE * self.along + j) * TILE + x % TILE
        else:
            start = (lax.div(x, TILE) * self.along + j) * TILE + lax.rem(x, TILE)
        return pl.ds(start, self.shots, stride=self.stride)

    def __getitem__(self, x):
        return jnp.concatenate([self.flat[self.place(x, j), :] for j in range(self.along)], 1)

    def __setitem__(self, x, row):
        for j in range(self.along):
            self.flat[self.place(x, j), :] = row[:, j * LANES : (j + 1) * LANES]


def compiler_params(mib):
    return pltpu.CompilerParams(vmem_limit_bytes=mib * MIB)


def tilt_coefficients(courant, epsilon, delta, tilt):
    turns = jnp.round(tilt * (2.0 / math.pi))
    rest = (tilt - turns * 1.5703125) - turns * (math.pi / 2 - 1.5703125)
    odd = turns - 2.0 * jnp.floor(turns * 0.5)
    sign = 1.0 - 2.0 * odd
    double = 2.0 * rest
    square = double * double
    sine = double * (
        1.0
        + square
        * (
            -1.0 / 6
            + square
            * (1.0 / 120 + square * (-1.0 / 5040 + square * (1.0 / 362880 - square / 39916800.0)))
        )
    )
    versine = square * (
        0.5
        + square
        * (
            -1.0 / 24
            + square
            * (1.0 / 720 + square * (-1.0 / 40320 + square * (1.0 / 3628800 - square / 479001600.0)))
        )
    )
    sine_sq = jnp.where(odd > 0.5, 1.0 - 0.5 * versine, 0.5 * versine)
    quarter_sin = 0.25 * sign * sine
    gain_p = courant * (1.0 + 2.0 * epsilon)
    gain_q = courant * (1.0 + 2.0 * delta)
    return sine_sq, quarter_sin, courant, gain_p, gain_q


def blocks(row):
    return [row[:, j : j + LANES] for j in range(0, row.shape[1], LANES)]


def depth_terms(row):
    lane = lax.broadcasted_iota(jnp.int32, row[0].shape, 1)
    shallow = [pltpu.roll(block, 1, 1) for block in row]
    deep = [pltpu.roll(block, LANES - 1, 1) for block in row]
    outside = jnp.zeros_like(row[0])
    sums, differences = [], []
    for j in range(len(row)):
        above = jnp.where(lane == 0, shallow[j - 1] if j else outside, shallow[j])
        below = jnp.where(
            lane == LANES - 1, deep[j + 1] if j + 1 < len(row) else outside, deep[j]
        )
        sums.append(below + above)
        differences.append(below - above)
    return sums, differences


def advance(count, p_row, q_row, p_prior, q_prior, coefficient, put):
    p_back, p_here = blocks(p_row(-1)), blocks(p_row(0))
    q_back, q_here = blocks(q_row(-1)), blocks(q_row(0))
    _, p_back_d = depth_terms(p_back)
    _, q_back_d = depth_terms(q_back)
    p_sum, p_here_d = depth_terms(p_here)
    q_sum, q_here_d = depth_terms(q_here)
    for row in range(count):
        p_next, q_next = blocks(p_row(row + 1)), blocks(q_row(row + 1))
        p_next_sum, p_next_d = depth_terms(p_next)
        q_next_sum, q_next_d = depth_terms(q_next)
        p_old, q_old = blocks(p_prior(row)), blocks(q_prior(row))
        p_new, q_new = [], []
        for j in range(len(p_here)):
            sine_sq, quarter_sin, courant, gain_p, gain_q = [coefficient(i, row, j) for i in range(5)]
            twice_p, twice_q = p_here[j] + p_here[j], q_here[j] + q_here[j]
            side = p_next[j] + p_back[j]
            mixed = p_next_d[j] - p_back_d[j]
            across = (side - twice_p) + sine_sq * (p_sum[j] - side) - quarter_sin * mixed
            side = q_next[j] + q_back[j]
            mixed = q_next_d[j] - q_back_d[j]
            along = (q_sum[j] - twice_q) + sine_sq * (side - q_sum[j]) + quarter_sin * mixed
            along = courant * along
            p_new.append((twice_p - p_old[j]) + (gain_p * across + along))
            q_new.append((twice_q - q_old[j]) + (gain_q * across + along))
        put(row, jnp.concatenate(p_new, 1), jnp.concatenate(q_new, 1))
        p_back, p_here, p_back_d, p_here_d, p_sum = p_here, p_next, p_here_d, p_next_d, p_next_sum
        q_back, q_here, q_back_d, q_here_d, q_sum = q_here, q_next, q_here_d, q_next_d, q_next_sum


class CoefficientRows:
    def __init__(self, ref, shots):
        self.shots, (_, self.along, self.rows, lanes) = shots, ref.shape
        self.flat = ref.reshape(ref.shape[0] * self.along * self.rows, lanes)

    def __call__(self, index, row, j):
        place = (index * self.along + j) * self.rows + row
        return self.flat[pl.ds(place, self.shots, stride=0), :]


def split_bf16(values):
    high = values.astype(jnp.bfloat16)
    low = (values - high.astype(jnp.float32)).astype(jnp.bfloat16)
    return high, low


def outer_kernel(*refs):
    sources, outs, (field_ref, param_ref, field_sem, param_sem) = refs[:8], refs[8:10], refs[10:]
    shots, across, along, tile, lanes = sources[0].shape
    depth = along * lanes
    field_copies, param_copies = [], []
    for side in range(2):
        place = side * (across - 1)
        for i in range(4):
            field_copies.append(
                pltpu.make_async_copy(
                    sources[i].at[:, pl.ds(place, 1), :, pl.ds(side * STEPS, STEPS)],
                    field_ref.at[side, i, :, :, :, pl.ds(side * STEPS, STEPS)],
                    field_sem.at[side, i],
                )
            )
        for i in range(4):
            param_copies.append(
                pltpu.make_async_copy(
                    sources[4 + i].at[pl.ds(place * tile, tile)],
                    param_ref.at[side, i],
                    param_sem.at[side, i],
                )
            )
    for copy in param_copies + field_copies:
        copy.start()
    for copy in param_copies:
        copy.wait()
    tiles_by_side = []
    for side in range(2):
        terms = tilt_coefficients(*[param_ref[side, i] for i in range(4)])
        rows = []
        for index, term in enumerate(terms):
            term = -term if index == 1 and side == 0 else term
            for distance in reversed(range(STEPS - 1)):
                place = distance if side == 0 else tile - 1 - distance
                rows.append(term[place : place + 1, :])
        while len(rows) < 2 * shots:
            rows.append(jnp.zeros((1, depth), jnp.float32))
        tiles_by_side.append(jnp.concatenate(rows, 0))

    for copy in field_copies:
        copy.wait()
    stride = along * tile
    flat = field_ref.reshape(2 * 4 * shots * stride, lanes)
    for turn in range(2):
        side = outer_side(turn)
        out = outs[turn]

        def row(field, distance):
            base = (side * 4 + field) * shots * stride + distance + side * (tile - 1 - 2 * distance)
            return jnp.concatenate(
                [flat[pl.ds(base + j * tile, shots, stride=stride), :] for j in range(along)], 1
            )

        position = 0

        def put(first, second):
            nonlocal position
            out[pl.ds(position, 2 * shots), :] = jnp.concatenate([first, second], 0).astype(
                jnp.bfloat16
            )
            position += 2 * shots

        for field in range(4):
            near = row(field, 0)
            put(near, near - near.astype(jnp.bfloat16).astype(jnp.float32))
        for first, second in far_items():
            put(row(*first), row(*second))
        out[pl.ds(position, 2 * shots), :] = jnp.where(
            side == 1, tiles_by_side[1], tiles_by_side[0]
        ).astype(jnp.bfloat16)


def outer_side(turn):
    return jnp.where(lax.axis_index("brick") % 2 == turn, 1, 0)


def far_items():
    items = []
    for field in range(2):
        items += [(field, distance) for distance in range(1, STEPS)]
    for field in range(2, 4):
        items += [(field, distance) for distance in range(1, STEPS - 1)]
    return list(zip(items[0::2], items[1::2]))


def outer_rows(fields, params):
    shots, across, along, tile, lanes = fields[0].shape
    depth = along * lanes
    rows = 2 * shots * (4 + len(far_items()) + 1)
    shape = jax.ShapeDtypeStruct((rows, depth), jnp.bfloat16)
    return pl.pallas_call(
        outer_kernel,
        in_specs=[pl.BlockSpec(memory_space=pltpu.HBM)] * 8,
        out_specs=[pl.BlockSpec(memory_space=pltpu.VMEM)] * 2,
        out_shape=[shape, shape],
        scratch_shapes=[
            pltpu.VMEM((2, 4, shots, 1, along, tile, lanes), jnp.float32),
            pltpu.VMEM((2, 4, tile, depth), jnp.float32),
            pltpu.SemaphoreType.DMA((2, 4)),
            pltpu.SemaphoreType.DMA((2, 4)),
        ],
        compiler_params=compiler_params(60),
        name="outer_rows",
    )(*fields, *params)


def partner(me, k, count):
    if count & (count - 1):
        return (me + k) % count
    return me ^ k


def loop_rows(count):
    sizes = range(10, 32, 2)
    return min(sizes, key=lambda size: (-(-count // size) * (size + 1), size))


def owner_of(me, k, owners):
    chips = owners // 2
    chip, core = me // 2, me % 2
    return partner(chip, k % chips, chips) * 2 + (core ^ (k // chips))


def sample_rows(values, one_hot):
    high, low = split_bf16(values)
    return jnp.dot(jnp.concatenate([high, low], 1), one_hot, preferred_element_type=jnp.float32)


def interior_kernel(
    p_ref,
    q_ref,
    pp_ref,
    qq_ref,
    courant_ref,
    epsilon_ref,
    delta_ref,
    tilt_ref,
    cells_ref,
    lists_ref,
    edge_ref,
    prior_edge_ref,
    coef_edge_ref,
    p_inner_ref,
    q_inner_ref,
    sample_ref,
    depth_hot_ref,
    column_ref,
    list_hot_ref,
    level_ref,
    coef_ref,
    split_ref,
):
    shots = p_ref.shape[0]
    width, depth = courant_ref.shape
    along = depth // LANES
    p_rows, q_rows, pp_rows, qq_rows = [ShotRows(ref) for ref in (p_ref, q_ref, pp_ref, qq_ref)]

    for x in range(width):
        level_ref[0, 0, x] = p_rows[x]
        level_ref[0, 1, x] = q_rows[x]

    terms = tilt_coefficients(courant_ref[...], epsilon_ref[...], delta_ref[...], tilt_ref[...])
    for index, term in enumerate(terms):
        for j in range(along):
            coef_ref[index, j] = term[:, j * LANES : (j + 1) * LANES]
        for k in range(STEPS):
            coef_edge_ref[0, index, pl.ds(k, 1), :] = term[k : k + 1, :]
            row = term[width - 1 - k : width - k, :]
            coef_edge_ref[1, index, pl.ds(k, 1), :] = -row if index == 1 else row

    one, zero = jnp.bfloat16(1), jnp.bfloat16(0)
    cells = cells_ref[...]
    column = cells // depth
    column_ref[...] = column
    targets = cells.shape[1]
    z_of = jnp.broadcast_to(cells - column * depth, (16, targets)).astype(jnp.int16)
    places = lax.broadcasted_iota(jnp.int16, (16, targets), 0)
    for base in range(0, depth, 16):
        hot = jnp.where(places + jnp.int16(base) == z_of, one, zero)
        depth_hot_ref[pl.ds(base, 16), :] = hot
        depth_hot_ref[pl.ds(depth + base, 16), :] = hot

    owners, slots, patch = lists_ref.shape[1:]
    me = lax.axis_index("shot")
    rows = []
    for k in range(owners):
        lists = lists_ref[0, owner_of(me, k, owners)]
        rows += [lists[s : s + 1, :] for s in range(slots)]
    count = len(rows)
    while len(rows) % 8:
        rows.append(rows[0])
    upright = jnp.transpose(jnp.concatenate(rows, 0).astype(jnp.float32)).astype(jnp.int32)
    lanes = lax.broadcasted_iota(jnp.int16, (patch, LANES), 1)
    for k in range(count):
        wanted = jnp.broadcast_to(upright[:, k : k + 1], (patch, LANES)).astype(jnp.int16)
        for base in range(0, targets, LANES):
            list_hot_ref[pl.ds(k * patch, patch), pl.ds(base, LANES)] = jnp.where(
                lanes + jnp.int16(base) == wanted, one, zero
            )

    for side in range(2):
        x = 0 if side == 0 else width - 1
        prior_edge_ref[side, 0] = pp_rows[x]
        prior_edge_ref[side, 1] = qq_rows[x]

    coefficients = CoefficientRows(coef_ref, shots)
    offsets = [0]
    for step in range(1, STEPS + 1):
        low, high = step, width - step
        chunk = loop_rows(high - low)
        offset = offsets[-1]
        offsets.append(offset + high - low)

        def run(index):
            at = 0 if chunk == high - low else jnp.minimum(chunk * index, high - low - chunk)
            start = low + at
            held = []

            def put(r, p_new, q_new):
                if step < STEPS:
                    level_ref[step, 0, start + r] = p_new
                    level_ref[step, 1, start + r] = q_new
                else:
                    p_inner_ref[at + r] = p_new
                    q_inner_ref[at + r] = q_new
                held.append(p_new)
                if len(held) == 2:
                    first, rest = split_bf16(jnp.concatenate(held, 0))
                    place = pl.multiple_of((offset + at + r - 1) * shots, 2 * shots)
                    split_ref[pl.ds(place, 2 * shots), pl.ds(0, depth)] = first
                    split_ref[pl.ds(place, 2 * shots), pl.ds(depth, depth)] = rest
                    held.clear()

            advance(
                chunk,
                lambda r: level_ref[step - 1, 0, start + r],
                lambda r: level_ref[step - 1, 1, start + r],
                lambda r: pp_rows[start + r] if step == 1 else level_ref[step - 2, 0, start + r],
                lambda r: qq_rows[start + r] if step == 1 else level_ref[step - 2, 1, start + r],
                lambda i, r, j: coefficients(i, start + r, j),
                put,
            )

        if chunk == high - low:
            run(0)
        else:
            pl.loop(0, -(-(high - low) // chunk))(run)

    for step in range(STEPS):
        for field in range(2):
            for near in range(2):
                edge_ref[0, field, step, near] = level_ref[step, field, step + near]
                edge_ref[1, field, step, near] = level_ref[step, field, width - 1 - step - near]

    found = jnp.dot(split_ref[...], depth_hot_ref[...], preferred_element_type=jnp.float32)
    totals = [jnp.zeros((shots, targets), jnp.float32) for _ in range(STEPS)]
    for x in range(1, width - 1):
        here = column == x
        for step in range(1, STEPS + 1):
            if step <= x < width - step:
                row = (offsets[step - 1] + x - step) * shots
                totals[step - 1] += jnp.where(here, found[row : row + shots], 0.0)
    for step in range(STEPS):
        sample_ref[step] = totals[step]


def interior(fields, params, target_cells, patch_lists):
    shots = fields[0].shape[0]
    width, depth = params[0].shape
    targets = target_cells.shape[0]
    _, owners, slots, patch = patch_lists.shape
    f32 = functools.partial(jax.ShapeDtypeStruct, dtype=jnp.float32)
    out_shape = [
        f32((2, 2, STEPS, 2, shots, depth)),
        f32((2, 2, shots, depth)),
        f32((2, 5, 8, depth)),
        f32((width - 2 * STEPS, shots, depth)),
        f32((width - 2 * STEPS, shots, depth)),
        f32((STEPS, shots, targets)),
        jax.ShapeDtypeStruct((2 * depth, targets), jnp.bfloat16),
        jax.ShapeDtypeStruct((1, targets), jnp.int32),
        jax.ShapeDtypeStruct((owners * slots * patch, targets), jnp.bfloat16),
    ]
    vmem = pl.BlockSpec(memory_space=pltpu.VMEM)
    return pl.pallas_call(
        interior_kernel,
        in_specs=[vmem] * 10,
        out_specs=[vmem] * len(out_shape),
        out_shape=out_shape,
        scratch_shapes=[
            pltpu.VMEM((STEPS, 2, width, shots, depth), jnp.float32),
            pltpu.VMEM((5, depth // LANES, width, LANES), jnp.float32),
            pltpu.VMEM((STEPS * (width - STEPS - 1) * shots, 2 * depth), jnp.bfloat16),
        ],
        compiler_params=compiler_params(40),
        cost_estimate=pl.CostEstimate(
            flops=200 * STEPS * shots * width * depth, bytes_accessed=8 * MIB, transcendentals=0
        ),
        name="interior",
    )(*fields, *params, target_cells.reshape(1, targets), patch_lists)


def packed_rows(slots, patch):
    return slots * (patch // 2) + -(-slots // 8) * 8


def pack_products(list_hot_ref, owner, feature_ref, out_ref, place, slots):
    patch = out_ref.shape[1]
    half = patch // 2
    base = place * packed_rows(slots, patch)
    row = lax.broadcasted_iota(jnp.int32, (half, patch), 0)
    lane = lax.broadcasted_iota(jnp.int32, (half, patch), 1)
    from_last = (lane < half) & (row > lane)
    chosen = lax.dot_general(
        list_hot_ref[pl.ds(owner * slots * patch, slots * patch), :],
        feature_ref[...],
        NT,
        preferred_element_type=jnp.float32,
    ).astype(jnp.bfloat16)
    diagonals = []
    for s in range(slots):
        mine = chosen[s * patch : (s + 1) * patch]
        gram = lax.dot_general(mine, mine, NT, preferred_element_type=jnp.float32)
        last = pltpu.roll(gram[half:], half, 1)
        out_ref[pl.ds(base + s * half, half), :] = jnp.where(from_last, last, gram[:half])
        diagonals.append(jnp.sum(jnp.where(row == lane, last, 0.0), 0, keepdims=True))
    while len(diagonals) % 8:
        diagonals.append(jnp.zeros((1, patch), jnp.float32))
    out_ref[pl.ds(base + slots * half, len(diagonals)), :] = jnp.concatenate(diagonals, 0)


def own_kernel(list_hot_ref, feature_ref, *out_refs, slots):
    for k, out_ref in enumerate(out_refs):
        pack_products(list_hot_ref, k, feature_ref, out_ref, 0, slots)


def own_products(list_hot, features, chips, slots, patch):
    vmem = pl.BlockSpec(memory_space=pltpu.VMEM)
    shape = jax.ShapeDtypeStruct((packed_rows(slots, patch), patch), jnp.float32)
    return pl.pallas_call(
        functools.partial(own_kernel, slots=slots),
        in_specs=[vmem] * 2,
        out_specs=[vmem] * chips,
        out_shape=[shape] * chips,
        compiler_params=compiler_params(24),
        cost_estimate=pl.CostEstimate(flops=512 * MIB, bytes_accessed=2 * MIB, transcendentals=0),
        name="own_products",
    )(list_hot, features)


def finish_kernel(
    even_ref,
    odd_ref,
    edge_ref,
    prior_edge_ref,
    coef_edge_ref,
    sample_ref,
    depth_hot_ref,
    column_ref,
    list_hot_ref,
    spectra_ref,
    table_ref,
    spectra_out_ref,
    final_ref,
    *rest,
    width,
    slots,
):
    feature_ref, beside_ref, level_ref, prior_ref, coef_ref, out_ref, out_sem = rest
    shots, depth = edge_ref.shape[-2:]
    targets = column_ref.shape[1]
    first = -STEPS
    pair = 2 * shots
    for turn, ref in enumerate((even_ref, odd_ref)):
        side = outer_side(turn)
        for field in range(4):
            both = ref[pl.ds(field * pair, pair), :].astype(jnp.float32)
            value = both[:shots] + both[shots:]
            if field < 2:
                level_ref[side, field, 0, -1 - first] = value
            else:
                prior_ref[side, field - 2, -1 - (1 - STEPS)] = value
        for index, items in enumerate(far_items()):
            both = ref[pl.ds((4 + index) * pair, pair), :].astype(jnp.float32)
            for half, (field, distance) in enumerate(items):
                value = both[half * shots : (half + 1) * shots]
                if field < 2:
                    level_ref[side, field, 0, -1 - distance - first] = value
                else:
                    prior_ref[side, field - 2, -1 - distance - (1 - STEPS)] = value
        params = ref[pl.ds((4 + len(far_items())) * pair, pair), :].astype(jnp.float32)
        for index in range(5):
            far = params[index * (STEPS - 1) : (index + 1) * (STEPS - 1)]
            for j, block in enumerate(blocks(far)):
                coef_ref[side, index, j, pl.ds(0, STEPS - 1), :] = block
    for side in range(2):
        for index in range(5):
            near = coef_edge_ref[side, index, pl.ds(0, STEPS), :]
            for j, block in enumerate(blocks(near)):
                coef_ref[side, index, j, pl.ds(STEPS - 1, STEPS), :] = block
        for field in range(2):
            prior_ref[side, field, STEPS - 1] = prior_edge_ref[side, field]
            for step in range(STEPS):
                for near in range(2):
                    level_ref[side, field, step, step + near - first] = edge_ref[
                        side, field, step, near
                    ]

    for step in range(1, STEPS + 1):
        low = step - STEPS

        for side in range(2):
            coefficients = CoefficientRows(coef_ref.at[side], shots)

            def prior(field):
                if step == 1:
                    return lambda r: prior_ref[side, field, low + r - (1 - STEPS)]
                return lambda r: level_ref[side, field, step - 2, low + r - first]

            def put(r, p_new, q_new):
                if step < STEPS:
                    level_ref[side, 0, step, low + r - first] = p_new
                    level_ref[side, 1, step, low + r - first] = q_new
                else:
                    final_ref[side, 0, r] = p_new
                    final_ref[side, 1, r] = q_new

            advance(
                STEPS,
                lambda r: level_ref[side, 0, step - 1, low + r - first],
                lambda r: level_ref[side, 1, step - 1, low + r - first],
                prior(0),
                prior(1),
                lambda i, r, j: coefficients(i, low + r - (1 - STEPS), j),
                put,
            )

    column = column_ref[...]
    places, values = [], []
    for step in range(1, STEPS + 1):
        for side in range(2):
            for k in range(step):
                places.append((step, k if side == 0 else width - 1 - k))
                if step < STEPS:
                    values.append(level_ref[side, 0, step, k - first])
                else:
                    values.append(final_ref[side, 0, k])
    found = sample_rows(jnp.concatenate(values, 0), depth_hot_ref[...])
    samples = [sample_ref[step] for step in range(STEPS)]
    for index, (step, x) in enumerate(places):
        samples[step - 1] = samples[step - 1] + jnp.where(
            column == x, found[index * shots : (index + 1) * shots], 0.0
        )

    parts = spectra_ref.shape[0] // shots
    lanes = table_ref.shape[-1]
    for s in range(shots):
        for base in range(0, targets, lanes):
            value = spectra_ref[pl.ds(s * parts, parts), pl.ds(base, lanes)]
            for step in range(STEPS):
                value = value + table_ref[step] * samples[step][s : s + 1, base : base + lanes]
            out_ref[pl.ds(s * parts, parts), pl.ds(base, lanes)] = value
            feature_ref[pl.ds(s * parts, parts), pl.ds(base, lanes)] = value.astype(jnp.bfloat16)

    out_copy = pltpu.make_async_copy(out_ref, spectra_out_ref, out_sem)
    out_copy.start()

    chips = beside_ref.shape[0] // packed_rows(slots, beside_ref.shape[1])
    for k in range(chips):
        pack_products(list_hot_ref, chips + k, feature_ref, beside_ref, k, slots)
    out_copy.wait()


def finish(even, odd, inner, spectra, table, width, owners, slots, patch):
    edge, prior_edge, coef_edge, sample, depth_hot, column, list_hot = inner
    shots, depth = edge.shape[-2:]
    targets = column.shape[1]
    features = spectra.shape[0]
    f32 = functools.partial(jax.ShapeDtypeStruct, dtype=jnp.float32)
    rows = packed_rows(slots, patch)
    out_shape = [
        f32((features, targets)),
        f32((2, 2, STEPS, shots, depth)),
        jax.ShapeDtypeStruct((features, targets), jnp.bfloat16),
        f32((owners // 2 * rows, patch)),
    ]
    vmem = pl.BlockSpec(memory_space=pltpu.VMEM)
    return pl.pallas_call(
        functools.partial(finish_kernel, width=width, slots=slots),
        in_specs=[vmem] * 11,
        out_specs=[pl.BlockSpec(memory_space=pl.ANY)] + [vmem] * (len(out_shape) - 1),
        out_shape=out_shape,
        scratch_shapes=[
            pltpu.VMEM((2, 2, STEPS, 2 * STEPS + 1, shots, depth), jnp.float32),
            pltpu.VMEM((2, 2, STEPS, shots, depth), jnp.float32),
            pltpu.VMEM((2, 5, depth // LANES, 2 * STEPS, LANES), jnp.float32),
            pltpu.VMEM((features, targets), jnp.float32),
            pltpu.SemaphoreType.DMA,
        ],
        compiler_params=compiler_params(40),
        name="finish",
    )(
        even,
        odd,
        edge,
        prior_edge,
        coef_edge,
        sample,
        depth_hot,
        column,
        list_hot,
        spectra,
        table,
    )


def assemble_kernel(p_inner_ref, q_inner_ref, final_ref, p_out_ref, q_out_ref):
    width = p_out_ref.shape[1] * TILE
    for field, (inner, out) in enumerate(((p_inner_ref, p_out_ref), (q_inner_ref, q_out_ref))):
        rows = ShotRows(out)
        for k in range(STEPS):
            rows[k] = final_ref[0, field, k]
            rows[width - 1 - k] = final_ref[1, field, k]

        @pl.loop(STEPS, width - STEPS, unroll=4)
        def _(x):
            rows[x] = inner[x - STEPS]


def assemble(p_inner, q_inner, final):
    inner, shots, depth = p_inner.shape
    across, along = (inner + 2 * STEPS) // TILE, depth // LANES
    shape = jax.ShapeDtypeStruct((shots, across, along, TILE, LANES), jnp.float32)
    vmem = pl.BlockSpec(memory_space=pltpu.VMEM)
    return pl.pallas_call(
        assemble_kernel,
        in_specs=[vmem] * 3,
        out_specs=[vmem] * 2,
        out_shape=[shape, shape],
        compiler_params=compiler_params(16),
        cost_estimate=pl.CostEstimate(flops=8 * MIB, bytes_accessed=4 * MIB, transcendentals=0),
        name="assemble",
    )(p_inner, q_inner, final)


def tiles_kernel(counts_ref, *refs, features):
    received, out_ref = refs[:-1], refs[-1]
    slots, patch = out_ref.shape[2], out_ref.shape[3]
    half = patch // 2
    row = lax.broadcasted_iota(jnp.int32, (half, patch), 0)
    lane = lax.broadcasted_iota(jnp.int32, (half, patch), 1)
    live = counts_ref[0, 0]
    total = received[0][...]
    for ref in received[1:]:
        total = total + ref[pl.ds(0, total.shape[0]), :]
    for s in range(slots):
        scale = jnp.where(s < live, 1.0 / features, 0.0)
        packed = total[s * half : (s + 1) * half] * scale
        diagonal = total[slots * half + s : slots * half + s + 1] * scale
        turned = jnp.transpose(jnp.concatenate([packed, packed], 0))
        flipped = turned[:half]
        corner = turned[half:]
        out_ref[0, 0, s, pl.ds(0, half), :] = jnp.where(
            (lane < half) & (row > lane), flipped, packed
        )
        last = jnp.where(row > lane, packed, jnp.where(row == lane, diagonal, flipped))
        out_ref[0, 0, s, pl.ds(half, half), :] = jnp.where(
            lane < half, corner, pltpu.roll(last, half, 1)
        )


def tiles(received, patch_counts, slots, features):
    patch = received[0].shape[1]
    return pl.pallas_call(
        functools.partial(tiles_kernel, features=features),
        in_specs=[pl.BlockSpec(memory_space=pltpu.SMEM)]
        + [pl.BlockSpec(memory_space=pltpu.VMEM)] * len(received),
        out_specs=pl.BlockSpec(memory_space=pltpu.VMEM),
        out_shape=jax.ShapeDtypeStruct((1, 1, slots, patch, patch), jnp.float32),
        compiler_params=compiler_params(16),
        name="tiles",
    )(patch_counts, *received)


def shards(
    pressure,
    auxiliary,
    pressure_prior,
    auxiliary_prior,
    courant_sq,
    thomsen_epsilon,
    thomsen_delta,
    tilt_angle,
    frequencies,
    spectra,
    target_cells,
    patch_lists,
    patch_counts,
):
    shots, width, depth = pressure.shape
    _, owners, slots, patch = patch_lists.shape
    fields = [tiled(item) for item in (pressure, auxiliary, pressure_prior, auxiliary_prior)]
    params = (courant_sq, thomsen_epsilon, thomsen_delta, tilt_angle)
    parts, targets = spectra.shape[1:]

    bricks = lax.axis_size("brick")
    swapped = []
    for turn, rows in enumerate(outer_rows(fields, params)):
        pairs = []
        for i in range(turn, bricks - 1, 2):
            pairs += [(i, i + 1), (i + 1, i)]
        swapped.append(lax.ppermute(rows, "brick", pairs))
    even, odd = swapped

    moments = jnp.arange(1, STEPS + 1, dtype=jnp.float32)
    angle = frequencies[None, :] * moments[:, None]
    table = jnp.concatenate([jnp.cos(angle), -jnp.sin(angle)], 1)
    table = jnp.broadcast_to(table[:, :, None], (STEPS, parts, 128))

    edge, prior_edge, coef_edge, p_inner, q_inner, sample, depth_hot, column, list_hot = interior(
        fields, params, target_cells, patch_lists
    )
    spectra_out, final, features, for_beside = finish(
        even,
        odd,
        (edge, prior_edge, coef_edge, sample, depth_hot, column, list_hot),
        spectra.reshape(shots * parts, targets),
        table,
        width,
        owners,
        slots,
        patch,
    )
    chips = owners // 2
    beside = lax.ppermute(for_beside, "shot", [(i, i ^ 1) for i in range(owners)])
    packed = own_products(list_hot, features, chips, slots, patch)
    received = [packed[0], beside]
    size = packed[0].shape[0]
    for k in range(1, chips):
        both = packed[k] + beside[k * size : (k + 1) * size]
        pairs = [(i, partner(i // 2, k, chips) * 2 + i % 2) for i in range(owners)]
        received.append(lax.ppermute(both, "shot", pairs))
    pressure_out, auxiliary_out = [untiled(item) for item in assemble(p_inner, q_inner, final)]
    gram_tiles = tiles(received, patch_counts, slots, shots * parts * owners)
    return (pressure_out, auxiliary_out, spectra_out.reshape(spectra.shape), gram_tiles)


def solution(mesh):
    return jax.shard_map(
        shards,
        mesh=mesh,
        in_specs=(
            P("shot", "brick", None),
            P("shot", "brick", None),
            P("shot", "brick", None),
            P("shot", "brick", None),
            P("brick", None),
            P("brick", None),
            P("brick", None),
            P("brick", None),
            P(),
            P("shot", None, "brick"),
            P("brick"),
            P("brick", None, None, None),
            P("brick", "shot"),
        ),
        out_specs=(
            P("shot", "brick", None),
            P("shot", "brick", None),
            P("shot", None, "brick"),
            P("brick", "shot", None, None, None),
        ),
        check_vma=False,
    )
```
